32 devices in a mesh: groups: 2 (over y), latent: 8 (over z, x), layer: 2 (over core).
Axes of the slice: x: 2, y: 2, z: 4, core: 2. Of those that a mesh axis runs over, the one named last changes fastest.
Arguments:
- residual_in: bfloat16 [2, 1024, 2048], P('layer', 'groups', 'latent'), parts along dimension 1, may hold values from -6 to 6
- targets: bfloat16 [2, 1024, 2048], P('layer', 'groups', 'latent'), parts along dimension 1, may hold values from -6 to 6
- enc_weight: bfloat16 [2, 2048, 1024], P('layer', None, 'latent'), may hold values from -0.125 to 0.125
- enc_bias: float32 [2, 1024], P('layer', 'latent'), may hold values from -3 to 3
- dec_same: bfloat16 [2, 1024, 2048], P('layer', 'latent'), may hold values from -0.25 to 0.25
- dec_cross: bfloat16 [1024, 2048], P('latent', 'layer'), may hold values from -0.25 to 0.25
Outputs:
- grad_encoder: float32 [4, 2048, 1024], P(('groups', 'layer'), None, 'latent'), parts along dimension 0
- grad_bias: float32 [4, 1024], P(('groups', 'layer'), 'latent'), parts along dimension 0
- grad_same: float32 [4, 1024, 2048], P(('groups', 'layer'), 'latent'), parts along dimension 0
- grad_cross: float32 [2048, 2048], P(('groups', 'latent'), 'layer'), parts along dimension 0
The draws below stay inside these ranges and needn't reach their ends.
There are 2 independent parts, one for each index of `groups`. The reference program is written for one: setup_inputs(seed, part) draws one part's arguments, and reference() takes and returns one part's arrays. A program takes and returns all parts, laid end to end along the dimension named above; an argument that names none is the same for every part. Nothing has to cross between parts.
All inputs are finite; a program needn't handle non-finite values.
Results may differ from the reference program's by a relative error of at most 0.004.
Values may be sent and summed in bfloat16 or wider, within the bound.
No kernel may reach another device: no remote copies, remote signals or barrier semaphores. Data moves between devices by JAX's collectives and lax.ppermute only.
A program may use at most 64 MiB of HBM per device.

```python
import math
import jax
import jax.numpy as jnp
from jax import lax

D = 2048
F = 1024
LAYERS = 2
TOKENS = 512


def spiked(result, stream_key, source, target, shards_of, factor):
    owner, partner = [(jnp.arange(result.shape[axis_at]) // (result.shape[axis_at] // shards_of)).reshape([-1 if axis == axis_at else 1 for axis in range(result.ndim)]) for axis_at in (source, target)]
    chosen = jax.random.permutation(stream_key, shards_of)[partner]
    strong = (owner == chosen) | (owner == (partner + shards_of // 2) % shards_of)
    return jnp.where(strong, factor * result, result)


def block_levels(key, shape, pieces, smallest, largest):
    def one(dim, shards_of):
        draws = jax.random.uniform(jax.random.fold_in(jax.random.fold_in(key, 6), dim), (shards_of,), jnp.float32, smallest / len(pieces), largest / len(pieces))
        return jnp.repeat(jnp.exp(draws), shape[dim] // shards_of).reshape((-1,) + (1,) * (len(shape) - dim - 1))

    factor_of = one(*pieces[0])
    for cut in pieces[1:]:
        factor_of = factor_of * one(*cut)
    return factor_of


def centred(key, shape, width, limit, cuts=(), dtype=jnp.bfloat16):
    entries = jax.random.normal(key, shape, jnp.float32) * width
    if len(cuts) > 0:
        entries = block_levels(key, shape, cuts, -0.22, 0.18) * entries
    return jnp.clip(entries, min=-limit, max=limit).astype(dtype)


def bell_draw_with(own_key, extent, scale, limit, shards, heavy, held_as=jnp.bfloat16):
    array = scale * jax.random.normal(own_key, extent, jnp.float32)
    if shards:
        array = array * block_levels(own_key, extent, shards, -0.22, 0.18)
    return jnp.clip(spiked(array, jax.random.fold_in(own_key, 3), *heavy), -limit, limit).astype(held_as)


def setup_inputs(seed: int = 0, part: int = 0) -> dict:
    key_of = jax.random.split(jax.random.key(seed), 7)
    part_splits = jax.random.split(jax.random.fold_in(key_of[6], part), 7)
    return {
        "residual_in": centred(part_splits[0], (LAYERS, TOKENS, D), 1.0, 6.0, ((0, 2), (2, 8))),
        "targets": centred(part_splits[1], (LAYERS, TOKENS, D), 1.0, 6.0, ((0, 2), (2, 8))),
        "enc_weight": centred(key_of[2], (LAYERS, D, F), D ** -0.5, 0.125, ((0, 2), (2, 8))),
        "enc_bias": centred(key_of[3], (LAYERS, F), 0.5, 3.0, ((0, 2), (1, 8)), jnp.float32),
        "dec_same": bell_draw_with(key_of[4], (LAYERS, F, D), F ** -0.5, 0.25, ((0, 2), (1, 8)), (1, 2, 8, 2.0)),
        "dec_cross": bell_draw_with(key_of[5], (F, D), F ** -0.5, 0.25, ((0, 8), (1, 2)), (0, 1, 8, 2.0)),
    }


def reference(residual_in, targets, enc_weight, enc_bias, dec_same, dec_cross):
    err_scale = 1.0 / math.sqrt(TOKENS)
    preacts = []
    codes_all = []
    for layer_now in range(2):
        preact = jnp.dot(residual_in[layer_now], enc_weight[layer_now], preferred_element_type=jnp.float32) + enc_bias[layer_now]
        preacts.append(preact)
        codes_all.append(jnp.maximum(preact, 0.0).astype(jnp.bfloat16))
    recon_first = jnp.dot(codes_all[0], dec_same[0], preferred_element_type=jnp.float32)
    recon_second = jnp.dot(codes_all[1], dec_same[1], preferred_element_type=jnp.float32) + jnp.dot(codes_all[0], dec_cross, preferred_element_type=jnp.float32)
    err_first = ((recon_first - targets[0].astype(jnp.float32)) * err_scale).astype(jnp.bfloat16)
    err_second = ((recon_second - targets[1].astype(jnp.float32)) * err_scale).astype(jnp.bfloat16)
    grad_same = jnp.stack([jnp.dot(codes_all[0].T, err_first, preferred_element_type=jnp.float32), jnp.dot(codes_all[1].T, err_second, preferred_element_type=jnp.float32)])
    grad_cross = jnp.dot(codes_all[0].T, err_second, preferred_element_type=jnp.float32)
    codes_first = jnp.dot(err_first, dec_same[0].T, preferred_element_type=jnp.float32) + jnp.dot(err_second, dec_cross.T, preferred_element_type=jnp.float32)
    codes_second = jnp.dot(err_second, dec_same[1].T, preferred_element_type=jnp.float32)
    grad_enc = []
    grad_bias = []
    for layer_now, grad_codes in enumerate([codes_first, codes_second]):
        grad_pre = jnp.where(preacts[layer_now] > 0, grad_codes, 0.0).astype(jnp.bfloat16)
        grad_enc.append(jnp.dot(residual_in[layer_now].T, grad_pre, preferred_element_type=jnp.float32))
        grad_bias.append(lax.optimization_barrier(jnp.sum(grad_pre.astype(jnp.float32), axis=0)))
    return (jnp.stack(grad_enc), jnp.stack(grad_bias), grad_same, grad_cross)
```

```python
import math

import jax
import jax.numpy as jnp
from jax import lax
from jax.sharding import PartitionSpec as P

F32 = jnp.float32
BF16 = jnp.bfloat16
OVER_ROWS = (((0,), (0,)), ((), ()))
OVER_COLS = (((1,), (1,)), ((), ()))
RING_LIMIT = 16


def passed_along(shard, axis, by):
    size = lax.axis_size(axis)
    pairs = [(i, i + by) for i in range(size) if 0 <= i + by < size]
    return lax.ppermute(shard, axis, pairs)


def matmul(a, b, dims=(((1,), (0,)), ((), ()))):
    return lax.dot_general(a, b, dims, preferred_element_type=F32)


def ring_member(place, size):
    place = lax.rem(place + 2 * size, size)
    return jnp.where(place < size // 2, 2 * place, 2 * (size - 1 - place) + 1)


def ring_place(member, size):
    return jnp.where(member % 2 == 0, member // 2, size - 1 - member // 2)


def ring_pairs(size, by):
    order = [2 * p if p < size // 2 else 2 * (size - 1 - p) + 1 for p in range(size)]
    return [(order[p], order[(p + by) % size]) for p in range(size)]


def hop(shard, size, by):
    return lax.ppermute(shard, "latent", ring_pairs(size, by))


def ring_gather(shard, size):
    half = shard.shape[0] // 2
    found = [(0, shard)]
    ahead = behind = shard
    for step in range(1, size // 2):
        ahead, behind = hop(ahead, size, 1), hop(behind, size, -1)
        found += [(-step, ahead), (step, behind)]
    top, bottom = hop(ahead[:half], size, 1), hop(behind[half:], size, -1)
    found.append((size // 2, jnp.concatenate([top, bottom], axis=0)))
    return found


def ring_reduce(partial_of, rows, size):
    half = rows // 2
    far = partial_of(size // 2)
    ahead = hop(far[:half].astype(BF16), size, 1)
    behind = hop(far[half:].astype(BF16), size, -1)
    for step in range(size // 2 - 1, 0, -1):
        plus, minus = partial_of(step), partial_of(-step)
        if step == size // 2 - 1:
            plus = jnp.concatenate([plus[:half] + ahead.astype(F32), plus[half:]], axis=0)
            minus = jnp.concatenate([minus[:half], minus[half:] + behind.astype(F32)], axis=0)
        else:
            plus, minus = plus + ahead.astype(F32), minus + behind.astype(F32)
        ahead, behind = hop(plus.astype(BF16), size, 1), hop(minus.astype(BF16), size, -1)
    return partial_of(0) + (ahead.astype(F32) + behind.astype(F32))


def ring_shards(residual_in, targets, enc_weight, enc_bias, dec_same, dec_cross):
    size = lax.axis_size("latent")
    place = ring_place(lax.axis_index("latent"), size)
    is_first = lax.axis_index("layer") == 0
    rows, wide = residual_in.shape[1:]
    full_width = dec_same.shape[2]
    half_width = full_width // 2
    err_scale = 1.0 / math.sqrt(rows)

    def start_of(offset):
        return ring_member(place + offset, size) * wide

    cross_full = lax.all_gather(dec_cross, "layer", axis=1, tiled=True)
    own_dec = dec_same[0]
    inputs = ring_gather(residual_in[0], size)
    preact = enc_bias
    for offset, shard in inputs:
        preact = preact + matmul(shard, lax.dynamic_slice_in_dim(enc_weight[0], start_of(offset), wide, 0))
    codes_now = jnp.maximum(preact, 0.0).astype(BF16)
    earlier = passed_along(codes_now, "layer", 1)

    def columns(array, offset):
        return lax.dynamic_slice_in_dim(array, start_of(offset), wide, 1)

    def partial_of(offset):
        return matmul(codes_now, columns(own_dec, offset)) + matmul(earlier, columns(cross_full, offset))

    recon = ring_reduce(partial_of, rows, size)
    own_errors = ((recon - targets[0].astype(F32)) * err_scale).astype(BF16)
    found = ring_gather(own_errors, size)
    errors = jnp.zeros((rows, full_width), BF16)
    for offset, shard in found:
        errors = lax.dynamic_update_slice_in_dim(errors, shard, start_of(offset), 1)
    back_cross = matmul(errors, cross_full, OVER_COLS)
    from_next = passed_along(back_cross, "layer", -1)
    grad_full = matmul(earlier, errors, OVER_ROWS)
    returned = passed_along(grad_full[:, :half_width], "layer", -1)
    grad_same = matmul(codes_now, errors, OVER_ROWS)
    grad_cross = jnp.where(is_first, returned, grad_full[:, half_width:])
    grad_codes = matmul(errors, own_dec, OVER_COLS) + from_next
    grad_pre = jnp.where(preact > 0, grad_codes, 0.0).astype(BF16)
    grad_enc = jnp.zeros(enc_weight.shape[1:], F32)
    for offset, shard in inputs:
        grad_enc = lax.dynamic_update_slice_in_dim(grad_enc, matmul(shard, grad_pre, OVER_ROWS), start_of(offset), 0)
    grad_bias = jnp.sum(grad_pre.astype(F32), axis=0)
    return (grad_enc[None], grad_bias[None], grad_same[None], grad_cross)


def wide_shards(residual_in, targets, enc_weight, enc_bias, dec_same, dec_cross):
    is_first = lax.axis_index("layer") == 0
    err_scale = 1.0 / math.sqrt(residual_in.shape[1])
    inputs = lax.all_gather(residual_in[0], "latent", axis=1, tiled=True)
    preact = matmul(inputs, enc_weight[0]) + enc_bias[0]
    codes_now = jnp.maximum(preact, 0.0).astype(BF16)
    earlier = passed_along(codes_now, "layer", 1)
    cross_full = lax.all_gather(dec_cross, "layer", axis=1, tiled=True)
    own_dec = dec_same[0]
    half_width = own_dec.shape[1] // 2
    recon_full = lax.psum(matmul(codes_now, own_dec) + matmul(earlier, cross_full), "latent")
    wanted = lax.all_gather(targets[0], "latent", axis=1, tiled=True)
    errors = ((recon_full - wanted.astype(F32)) * err_scale).astype(BF16)
    grad_same = matmul(codes_now, errors, OVER_ROWS)
    grad_full = matmul(earlier, errors, OVER_ROWS)
    returned = passed_along(grad_full[:, :half_width], "layer", -1)
    grad_cross = jnp.where(is_first, returned, grad_full[:, half_width:])
    from_next = passed_along(matmul(errors, cross_full, OVER_COLS), "layer", -1)
    grad_codes = matmul(errors, own_dec, OVER_COLS) + from_next
    grad_pre = jnp.where(preact > 0, grad_codes, 0.0).astype(BF16)
    grad_enc = matmul(inputs, grad_pre, OVER_ROWS)
    grad_bias = jnp.sum(grad_pre.astype(F32), axis=0)
    return (grad_enc[None], grad_bias[None], grad_same[None], grad_cross)


def solution(mesh):
    size = mesh.shape["latent"]
    placed = (
        P("layer", "groups", "latent"),
        P("layer", "groups", "latent"),
        P("layer", None, "latent"),
        P("layer", "latent"),
        P("layer", "latent", None),
        P("latent", "layer"),
    )
    return jax.shard_map(
        ring_shards if size % 2 == 0 and size <= RING_LIMIT else wide_shards,
        mesh=mesh,
        in_specs=placed,
        out_specs=(
            P(("groups", "layer"), None, "latent"),
            P(("groups", "layer"), "latent"),
            P(("groups", "layer"), "latent", None),
            P(("groups", "latent"), "layer"),
        ),
        check_vma=False,
    )
```

```python
import functools
import math

import jax
import jax.numpy as jnp
from jax import lax
from jax.experimental import pallas as pl
from jax.experimental.pallas import tpu as pltpu
from jax.sharding import PartitionSpec as P

F32 = jnp.float32
BF16 = jnp.bfloat16
OVER_ROWS = (((0,), (0,)), ((), ()))
OVER_COLS = (((1,), (1,)), ((), ()))
RING_LIMIT = 16
VMEM_BYTES = 24 * 1024 * 1024
ENC_PIECES = 4


def passed_along(shard, axis, by):
    size = lax.axis_size(axis)
    pairs = [(i, i + by) for i in range(size) if 0 <= i + by < size]
    return lax.ppermute(shard, axis, pairs)


def matmul(a, b, dims=(((1,), (0,)), ((), ()))):
    return lax.dot_general(a, b, dims, preferred_element_type=F32)


def ring_member(place, size):
    place = lax.rem(place + 2 * size, size)
    return jnp.where(place < size // 2, 2 * place, 2 * (size - 1 - place) + 1)


def ring_place(member, size):
    return jnp.where(member % 2 == 0, member // 2, size - 1 - member // 2)


def ring_pairs(size, by):
    order = [2 * p if p < size // 2 else 2 * (size - 1 - p) + 1 for p in range(size)]
    return [(order[p], order[(p + by) % size]) for p in range(size)]


def hop(shard, size, by):
    return lax.ppermute(shard, "latent", ring_pairs(size, by))


def ring_gather(parts, size):
    found = [[(0, part)] for part in parts]
    ahead, behind = list(parts), list(parts)
    for step in range(1, size // 2):
        for chain in range(2):
            ahead[chain] = hop(ahead[chain], size, 1)
            behind[chain] = hop(behind[chain], size, -1)
            found[chain] += [(-step, ahead[chain]), (step, behind[chain])]
    found[0].append((size // 2, hop(ahead[0], size, 1)))
    found[1].append((size // 2, hop(behind[1], size, -1)))
    return found


def ring_reduce(partial_of, size):
    far = [partial_of(chain, size // 2).astype(BF16) for chain in range(2)]
    ahead = [hop(far[0], size, 1), None]
    behind = [None, hop(far[1], size, -1)]
    for step in range(size // 2 - 1, 0, -1):
        for chain in range(2):
            plus, minus = partial_of(chain, step), partial_of(chain, -step)
            if ahead[chain] is not None:
                plus = plus + ahead[chain].astype(F32)
            if behind[chain] is not None:
                minus = minus + behind[chain].astype(F32)
            ahead[chain] = hop(plus.astype(BF16), size, 1)
            behind[chain] = hop(minus.astype(BF16), size, -1)
    totals = []
    for chain in range(2):
        total = partial_of(chain, 0)
        for arrived in (ahead[chain], behind[chain]):
            if arrived is not None:
                total = total + arrived.astype(F32)
        totals.append(total)
    return totals


def call(kernel, outs, flops, operands, grid=(), out_specs=None, scratch=(), in_vmem=None):
    whole = pl.BlockSpec(memory_space=pltpu.VMEM)
    return pl.pallas_call(
        kernel,
        out_shape=outs,
        grid=grid,
        in_specs=[pl.BlockSpec(memory_space=pltpu.SMEM)] + [whole] * (len(operands) - 1),
        out_specs=out_specs if out_specs is not None else [whole] * len(outs),
        scratch_shapes=list(scratch),
        compiler_params=pltpu.CompilerParams(vmem_limit_bytes=VMEM_BYTES),
        cost_estimate=pl.CostEstimate(flops=flops, bytes_accessed=1 << 20, transcendentals=0),
    )(*operands)


def encode_kernel(starts, *refs):
    *shards, weight, bias, preact, codes = refs
    wide = shards[0].shape[1]
    total = jnp.broadcast_to(bias[...], preact.shape)
    for k, shard in enumerate(shards):
        block = weight[0, pl.ds(pl.multiple_of(starts[k], wide), wide), :]
        total = total + jnp.dot(shard[...], block, preferred_element_type=F32)
    preact[...] = total
    codes[...] = jnp.maximum(total, 0.0).astype(BF16)


def turn_kernel(starts, *refs):
    *shards, turned = refs
    rows, wide = shards[0].shape
    for k in range(len(shards) // 2):
        at = pl.ds(pl.multiple_of(starts[k], wide), wide)
        for chain in range(2):
            turned[at, chain * rows:(chain + 1) * rows] = shards[2 * k + chain][...].T


def back_kernel(starts, *refs):
    *shards, own_dec, cross, back_own, back_cross = refs
    wide = shards[0].shape[1]
    for source, target in ((cross, back_cross), (own_dec, back_own)):
        total = None
        for k, shard in enumerate(shards):
            block = source[:, pl.ds(pl.multiple_of(starts[k], wide), wide)]
            term = lax.dot_general(shard[...], block, OVER_COLS, preferred_element_type=F32)
            total = term if total is None else total + term
        target[...] = total


def outer_kernel(starts, *refs):
    *shards, codes_0, codes_1, earlier_0, earlier_1, same, low, high, errors, turned, turned_earlier = refs
    rows, wide = shards[0].shape
    size = len(shards) // 2

    for chain, (codes, earlier) in enumerate(((codes_0, earlier_0), (codes_1, earlier_1))):
        turned[:, chain * rows:(chain + 1) * rows] = codes[...].T
        turned_earlier[:, chain * rows:(chain + 1) * rows] = earlier[...].T
    for k in range(size):
        at = pl.ds(pl.multiple_of(starts[k], wide), wide)
        for chain in range(2):
            errors[chain * rows:(chain + 1) * rows, at] = shards[2 * k + chain][...]
    half = size // 2
    for k in range(size):
        block = errors[:, k * wide:(k + 1) * wide]
        target = low if k < half else high
        at = (k % half) * wide
        target[:, at:at + wide] = jnp.dot(turned_earlier[...], block, preferred_element_type=F32)
        same[0, :, k * wide:(k + 1) * wide] = jnp.dot(turned[...], block, preferred_element_type=F32)


def enc_kernel(first, turned, pre_0, pre_1, own_0, own_1, next_0, next_1, grad, bias, grad_pre):
    rows = pre_0.shape[0]

    @pl.when(pl.program_id(0) == 0)
    def _():
        total = 0.0
        for chain, (pre, own, later) in enumerate(((pre_0, own_0, next_0), (pre_1, own_1, next_1))):
            value = jnp.where(pre[...] > 0, own[...] + later[...], 0.0).astype(BF16)
            grad_pre[chain * rows:(chain + 1) * rows, :] = value
            total = total + jnp.sum(value.astype(F32), axis=0, keepdims=True)
        bias[...] = total

    height = grad.shape[1]
    at = pl.multiple_of(pl.program_id(0) * height, height)
    grad[0] = jnp.dot(turned[pl.ds(at, height), :], grad_pre[...], preferred_element_type=F32)


def ring_shards(residual_in, targets, enc_weight, enc_bias, dec_same, dec_cross):
    size = lax.axis_size("latent")
    place = ring_place(lax.axis_index("latent"), size)
    is_first = lax.axis_index("layer") == 0
    rows, wide = residual_in.shape[1:]
    deep, lat = enc_weight.shape[1:]
    half = rows // 2
    half_width = deep // 2
    err_scale = 1.0 / math.sqrt(rows)
    shape = jax.ShapeDtypeStruct
    work = 2 * rows * deep * lat

    def start_of(offset):
        return ring_member(place + offset, size) * wide

    def halves(array):
        return [array[:half], array[half:]]

    own_dec = dec_same[0]
    inputs = ring_gather(halves(residual_in[0]), size)
    offsets = [offset for offset, _ in inputs[0]]
    starts = jnp.stack([start_of(offset) for offset in offsets]).astype(jnp.int32)
    cross_full = lax.all_gather(dec_cross, "layer", axis=1, tiled=True)

    preacts, codes, earlier = [], [], []
    for chain in range(2):
        preact, now = call(
            encode_kernel,
            [shape((half, lat), F32), shape((half, lat), BF16)],
            work // 2,
            [starts] + [shard for _, shard in inputs[chain]] + [enc_weight, enc_bias],
        )
        preacts.append(preact)
        codes.append(now)
        earlier.append(passed_along(now, "layer", 1))
    both = [shard for pair in zip(*inputs) for _, shard in pair]
    turned = call(turn_kernel, [shape((deep, rows), BF16)], 0, [starts] + both)[0]

    def columns(array, offset):
        return lax.dynamic_slice_in_dim(array, start_of(offset), wide, 1)

    def partial_of(chain, offset):
        return matmul(codes[chain], columns(own_dec, offset)) + matmul(earlier[chain], columns(cross_full, offset))

    recon = ring_reduce(partial_of, size)
    own_errors = [
        ((total - wanted.astype(F32)) * err_scale).astype(BF16) for total, wanted in zip(recon, halves(targets[0]))
    ]
    errors = ring_gather(own_errors, size)
    back_own, from_next = [], []
    for chain in range(2):
        own, cross = call(
            back_kernel,
            [shape((half, lat), F32), shape((half, lat), F32)],
            work,
            [starts] + [shard for _, shard in errors[chain]] + [own_dec, cross_full],
        )
        back_own.append(own)
        from_next.append(passed_along(cross, "layer", -1))
    both = [shard for pair in zip(*errors) for _, shard in pair]
    grad_same, low, high = call(
        outer_kernel,
        [shape((1, lat, deep), F32), shape((lat, half_width), F32), shape((lat, half_width), F32)],
        2 * work,
        [starts] + both + codes + earlier,
        scratch=[pltpu.VMEM((rows, deep), BF16), pltpu.VMEM((lat, rows), BF16), pltpu.VMEM((lat, rows), BF16)],
    )
    returned = passed_along(low, "layer", -1)
    pieces = ENC_PIECES
    grad_enc, grad_bias = call(
        enc_kernel,
        [shape((1, deep, lat), F32), shape((1, lat), F32)],
        work,
        [starts, turned] + preacts + back_own + from_next,
        grid=(pieces,),
        out_specs=[
            pl.BlockSpec((1, deep // pieces, lat), lambda i: (0, i, 0)),
            pl.BlockSpec((1, lat), lambda i: (0, 0)),
        ],
        scratch=[pltpu.VMEM((rows, lat), BF16)],
    )
    grad_cross = jnp.where(is_first, returned, high)
    return (grad_enc, grad_bias, grad_same, grad_cross)


def wide_shards(residual_in, targets, enc_weight, enc_bias, dec_same, dec_cross):
    is_first = lax.axis_index("layer") == 0
    err_scale = 1.0 / math.sqrt(residual_in.shape[1])
    inputs = lax.all_gather(residual_in[0], "latent", axis=1, tiled=True)
    preact = matmul(inputs, enc_weight[0]) + enc_bias[0]
    codes_now = jnp.maximum(preact, 0.0).astype(BF16)
    earlier = passed_along(codes_now, "layer", 1)
    cross_full = lax.all_gather(dec_cross, "layer", axis=1, tiled=True)
    own_dec = dec_same[0]
    half_width = own_dec.shape[1] // 2
    recon_full = lax.psum(matmul(codes_now, own_dec) + matmul(earlier, cross_full), "latent")
    wanted = lax.all_gather(targets[0], "latent", axis=1, tiled=True)
    errors = ((recon_full - wanted.astype(F32)) * err_scale).astype(BF16)
    grad_same = matmul(codes_now, errors, OVER_ROWS)
    grad_full = matmul(earlier, errors, OVER_ROWS)
    returned = passed_along(grad_full[:, :half_width], "layer", -1)
    grad_cross = jnp.where(is_first, returned, grad_full[:, half_width:])
    from_next = passed_along(matmul(errors, cross_full, OVER_COLS), "layer", -1)
    grad_codes = matmul(errors, own_dec, OVER_COLS) + from_next
    grad_pre = jnp.where(preact > 0, grad_codes, 0.0).astype(BF16)
    grad_enc = matmul(inputs, grad_pre, OVER_ROWS)
    grad_bias = jnp.sum(grad_pre.astype(F32), axis=0)
    return (grad_enc[None], grad_bias[None], grad_same[None], grad_cross)


def solution(mesh):
    size = mesh.shape["latent"]
    placed = (
        P("layer", "groups", "latent"),
        P("layer", "groups", "latent"),
        P("layer", None, "latent"),
        P("layer", "latent"),
        P("layer", "latent", None),
        P("latent", "layer"),
    )
    return jax.shard_map(
        ring_shards if size % 2 == 0 and size <= RING_LIMIT else wide_shards,
        mesh=mesh,
        in_specs=placed,
        out_specs=(
            P(("groups", "layer"), None, "latent"),
            P(("groups", "layer"), "latent"),
            P(("groups", "layer"), "latent", None),
            P(("groups", "latent"), "layer"),
        ),
        check_vma=False,
    )
```

```python
import functools
import math

import jax
import jax.numpy as jnp
from jax import lax
from jax.experimental import pallas as pl
from jax.experimental.pallas import tpu as pltpu
from jax.sharding import PartitionSpec as P

F32 = jnp.float32
BF16 = jnp.bfloat16
OVER_ROWS = (((0,), (0,)), ((), ()))
OVER_COLS = (((1,), (1,)), ((), ()))
RING_LIMIT = 16
VMEM_BYTES = 24 * 1024 * 1024
PIECES = 8


def passed_along(shard, axis, by):
    size = lax.axis_size(axis)
    pairs = [(i, i + by) for i in range(size) if 0 <= i + by < size]
    return lax.ppermute(shard, axis, pairs)


def matmul(a, b, dims=(((1,), (0,)), ((), ()))):
    return lax.dot_general(a, b, dims, preferred_element_type=F32)


def ring_order(size):
    return [2 * p if p < size // 2 else 2 * (size - 1 - p) + 1 for p in range(size)]


def ring_member(place, size):
    place = lax.rem(place + 2 * size, size)
    return jnp.where(place < size // 2, 2 * place, 2 * (size - 1 - place) + 1)


def ring_place(member, size):
    return jnp.where(member % 2 == 0, member // 2, size - 1 - member // 2)


def hop(shard, way):
    size, layers = lax.axis_size("latent"), lax.axis_size("layer")
    order = ring_order(size)
    pairs = []
    for p in range(size):
        for layer in range(layers):
            by = way if layer % 2 == 0 else -way
            pairs.append((order[p] * layers + layer, order[(p + by) % size] * layers + layer))
    return lax.ppermute(shard, ("latent", "layer"), pairs)


def after(value, *others):
    return lax.optimization_barrier((value,) + others)[0]


def call(kernel, outs, flops, operands, spaces=None, out_spaces=None, scratch=(), aliases=None):
    def spec(space):
        return pl.BlockSpec(memory_space=space)

    spaces = spaces or [pltpu.VMEM] * (len(operands) - 1)
    out_spaces = out_spaces or [pltpu.VMEM] * len(outs)
    size = sum(math.prod(x.shape) * x.dtype.itemsize for x in list(operands) + list(outs))
    return pl.pallas_call(
        kernel,
        out_shape=outs,
        in_specs=[spec(pltpu.SMEM)] + [spec(space) for space in spaces],
        out_specs=[spec(space) for space in out_spaces],
        scratch_shapes=list(scratch),
        input_output_aliases=aliases or {},
        compiler_params=pltpu.CompilerParams(vmem_limit_bytes=VMEM_BYTES),
        cost_estimate=pl.CostEstimate(flops=flops, bytes_accessed=size, transcendentals=0),
    )(*operands)


def block_of(starts, slot, wide):
    return pl.ds(pl.multiple_of(starts[slot], wide), wide)


def encode_kernel(slots, last, starts, *refs):
    shards, (weight, before, *outs) = refs[:len(slots)], refs[len(slots):]
    total = jnp.broadcast_to(before[...], outs[0].shape)
    for slot, shard in zip(slots, shards):
        block = weight[0, block_of(starts, slot, shard.shape[1]), :]
        total = total + jnp.dot(shard[...], block, preferred_element_type=F32)
    outs[0][...] = total
    if last:
        outs[1][...] = jnp.maximum(total, 0.0).astype(BF16)


def turn_kernel(starts, *refs):
    *shards, turned = refs
    for slot, shard in enumerate(shards):
        turned[block_of(starts, slot, shard.shape[1]), :] = shard[...].T


def spread_kernel(slots, starts, codes, earlier, own_dec, cross, *outs):
    *partials, codes_t, earlier_t = outs
    both = jnp.concatenate([codes[...], earlier[...]], axis=1)
    for slot, partial in zip(slots, partials):
        at = block_of(starts, slot, partial.shape[1])
        block = jnp.concatenate([own_dec[0, :, at], cross[:, at]], axis=0)
        partial[...] = jnp.dot(both, block, preferred_element_type=F32).astype(partial.dtype)
    codes_t[...] = codes[...].T
    earlier_t[...] = earlier[...].T


def back_kernel(slots, first, starts, *refs):
    count = len(slots)
    shards, (codes_t, earlier_t, own_dec, cross), refs = refs[:count], refs[count:count + 4], refs[count + 4:]
    if not first:
        own_before, next_before = refs[:2]
        refs = refs[5:]
    back_own, back_next, same, low, high, stage, sems = refs
    wide = shards[0].shape[1]
    half_width = low.shape[1]
    own_total = 0.0 if first else own_before[...]
    next_total = 0.0 if first else next_before[...]
    for i, (slot, shard) in enumerate(zip(slots, shards)):
        start = pl.multiple_of(starts[slot], wide)
        error = shard[...]
        stage[0, i] = jnp.dot(codes_t[...], error, preferred_element_type=F32)
        pltpu.make_async_copy(stage.at[0, i], same.at[0, :, pl.ds(start, wide)], sems.at[0, i]).start()
        stage[1, i] = jnp.dot(earlier_t[...], error, preferred_element_type=F32)

        @pl.when(start < half_width)
        def _():
            pltpu.make_async_copy(stage.at[1, i], low.at[:, pl.ds(start, wide)], sems.at[1, i]).start()

        @pl.when(start >= half_width)
        def _():
            there = pl.multiple_of(start - half_width, wide)
            pltpu.make_async_copy(stage.at[1, i], high.at[:, pl.ds(there, wide)], sems.at[1, i]).start()

        at = pl.ds(start, wide)
        next_total = next_total + lax.dot_general(error, cross[:, at], OVER_COLS, preferred_element_type=F32)
        own_total = own_total + lax.dot_general(error, own_dec[0, :, at], OVER_COLS, preferred_element_type=F32)
    back_own[...] = own_total
    back_next[...] = next_total
    for i in range(count):
        pltpu.make_async_copy(stage.at[0, i], same.at[0, :, pl.ds(0, wide)], sems.at[0, i]).wait()
        pltpu.make_async_copy(stage.at[1, i], low.at[:, pl.ds(0, wide)], sems.at[1, i]).wait()


def finish_kernel(starts, turned, preact, back_own, from_next, returned, high, grad, bias, cross, stage, sems, cross_sem):
    pieces, height = stage.shape[:2]
    first = starts[starts.shape[0] - 1] == 0

    @pl.when(first)
    def _():
        pltpu.make_async_copy(returned, cross, cross_sem).start()

    @pl.when(jnp.logical_not(first))
    def _():
        pltpu.make_async_copy(high, cross, cross_sem).start()

    value = jnp.where(preact[...] > 0, back_own[...] + from_next[...], 0.0).astype(BF16)
    for i in range(pieces):
        rows = pl.ds(i * height, height)
        stage[i] = jnp.dot(turned[rows, :], value, preferred_element_type=F32)
        pltpu.make_async_copy(stage.at[i], grad.at[0, rows, :], sems.at[i]).start()
    bias[...] = jnp.sum(value.astype(F32), axis=0, keepdims=True)
    for i in range(pieces):
        pltpu.make_async_copy(stage.at[i], grad.at[0, pl.ds(i * height, height), :], sems.at[i]).wait()
    pltpu.make_async_copy(high, cross, cross_sem).wait()


def ring_shards(residual_in, targets, enc_weight, enc_bias, dec_same, dec_cross):
    size = lax.axis_size("latent")
    reach = size // 2
    place = ring_place(lax.axis_index("latent"), size)
    layer = lax.axis_index("layer")
    sign = jnp.where(layer % 2 == 0, 1, -1)
    rows, wide = residual_in.shape[1:]
    deep, lat = enc_weight.shape[1:]
    half_width = deep // 2
    err_scale = 1.0 / math.sqrt(rows)
    shape = jax.ShapeDtypeStruct
    unit = 2 * rows * wide * lat

    slot_p = {s: 2 * s - 1 for s in range(1, reach)}
    slot_q = {s: 2 * s for s in range(1, reach)}
    far = size - 1
    slot_p[reach] = far
    offsets = [0] * size
    for s in range(1, reach + 1):
        offsets[slot_p[s]] = -s
        if s < reach:
            offsets[slot_q[s]] = s
    starts = jnp.stack([ring_member(place + sign * offset, size) * wide for offset in offsets] + [layer])
    starts = starts.astype(jnp.int32)

    own = residual_in[0]
    inputs = [own] + [None] * (size - 1)
    inputs[slot_p[1]] = hop(own, 1)
    cross_full = lax.all_gather(dec_cross, "layer", axis=1, tiled=True)
    if reach > 1:
        inputs[slot_q[1]] = hop(after(own, cross_full), -1)
    for s in range(2, reach + 1):
        inputs[slot_p[s]] = hop(inputs[slot_p[s - 1]], 1)
        if s < reach:
            inputs[slot_q[s]] = hop(inputs[slot_q[s - 1]], -1)

    early = tuple(range(size - 1))
    part = call(
        functools.partial(encode_kernel, early, False),
        [shape((rows, lat), F32)],
        unit * len(early),
        [starts] + inputs[:-1] + [enc_weight, enc_bias],
    )[0]
    preact, codes = call(
        functools.partial(encode_kernel, (far,), True),
        [shape((rows, lat), F32), shape((rows, lat), BF16)],
        unit,
        [starts, inputs[far], enc_weight, part],
    )
    earlier = passed_along(codes, "layer", 1)

    def columns(array, slot):
        return lax.dynamic_slice_in_dim(array, starts[slot], wide, 1)

    message = (matmul(codes, columns(dec_same[0], far)) + matmul(earlier, columns(cross_full, far))).astype(BF16)
    ahead = hop(message, 1)
    spread = tuple([slot_p[s] for s in range(reach - 1, 0, -1)] + [slot_q[s] for s in range(reach - 1, 0, -1)] + [0])
    *partials, codes_t, earlier_t = call(
        functools.partial(spread_kernel, spread),
        [shape((rows, wide), BF16 if slot == slot_p.get(reach - 1) else F32) for slot in spread]
        + [shape((lat, rows), BF16)] * 2,
        2 * unit * len(spread),
        [starts, codes, earlier, dec_same, cross_full],
    )
    partial = dict(zip(spread, partials))
    turned = call(turn_kernel, [shape((deep, rows), BF16)], unit, [starts] + inputs)[0]
    total = partial[0]
    behind = None
    for s in range(reach - 1, 0, -1):
        going = partial[slot_p[s]]
        if behind is not None:
            going = (going + behind.astype(F32)).astype(BF16)
        behind = hop(going, -1)
        going = (partial[slot_q[s]] + ahead.astype(F32)).astype(BF16)
        if s == 1:
            going = after(going, turned)
        ahead = hop(going, 1)
    total = total + ahead.astype(F32)
    if behind is not None:
        total = total + behind.astype(F32)
    own_errors = ((total - targets[0].astype(F32)) * err_scale).astype(BF16)

    def back(slots, shards, before):
        count = len(slots)
        acc = shape((rows, lat), F32)
        outs = [acc, acc, shape((1, lat, deep), F32), shape((lat, half_width), F32), shape((lat, half_width), F32)]
        operands = [starts] + list(shards) + [codes_t, earlier_t, dec_same, cross_full]
        aliases = {}
        if before is not None:
            aliases = {len(operands) + 2 + i: 2 + i for i in range(3)}
            operands += list(before)
        spaces = [pltpu.VMEM] * (count + 4) + ([] if before is None else [pltpu.VMEM] * 2 + [pl.ANY] * 3)
        return call(
            functools.partial(back_kernel, slots, before is None),
            outs,
            4 * unit * count,
            operands,
            spaces=spaces,
            out_spaces=[pltpu.VMEM] * 2 + [pl.ANY] * 3,
            scratch=[pltpu.VMEM((2, count, lat, wide), F32), pltpu.SemaphoreType.DMA((2, count))],
            aliases=aliases,
        )

    ahead = hop(own_errors, 1)
    done = back((0,), [own_errors], None)
    if reach > 1:
        behind = hop(after(own_errors, done[0]), -1)
    pending = []
    for s in range(1, reach):
        pending += [(slot_p[s], ahead), (slot_q[s], behind)]
        following = after(ahead, done[0])
        if s % 2 == 0 or s == reach - 1:
            done = back(tuple(slot for slot, _ in pending), [shard for _, shard in pending], done)
            pending = []
        ahead = hop(following, 1)
        if s < reach - 1:
            behind = hop(behind, -1)
    back_own, back_next, grad_same, low, high = back((far,), [ahead], done)
    from_next = passed_along(back_next, "layer", -1)
    returned = passed_along(low, "layer", -1)
    height = deep // PIECES
    grad_enc, grad_bias, grad_cross = call(
        finish_kernel,
        [shape((1, deep, lat), F32), shape((1, lat), F32), shape((lat, half_width), F32)],
        unit * size,
        [starts, turned, preact, back_own, from_next, returned, high],
        spaces=[pltpu.VMEM] * 4 + [pl.ANY] * 2,
        out_spaces=[pl.ANY, pltpu.VMEM, pl.ANY],
        scratch=[
            pltpu.VMEM((PIECES, height, lat), F32),
            pltpu.SemaphoreType.DMA((PIECES,)),
            pltpu.SemaphoreType.DMA,
        ],
    )
    return (grad_enc, grad_bias, grad_same, grad_cross)


def wide_shards(residual_in, targets, enc_weight, enc_bias, dec_same, dec_cross):
    is_first = lax.axis_index("layer") == 0
    err_scale = 1.0 / math.sqrt(residual_in.shape[1])
    inputs = lax.all_gather(residual_in[0], "latent", axis=1, tiled=True)
    preact = matmul(inputs, enc_weight[0]) + enc_bias[0]
    codes_now = jnp.maximum(preact, 0.0).astype(BF16)
    earlier = passed_along(codes_now, "layer", 1)
    cross_full = lax.all_gather(dec_cross, "layer", axis=1, tiled=True)
    own_dec = dec_same[0]
    half_width = own_dec.shape[1] // 2
    recon_full = lax.psum(matmul(codes_now, own_dec) + matmul(earlier, cross_full), "latent")
    wanted = lax.all_gather(targets[0], "latent", axis=1, tiled=True)
    errors = ((recon_full - wanted.astype(F32)) * err_scale).astype(BF16)
    grad_same = matmul(codes_now, errors, OVER_ROWS)
    grad_full = matmul(earlier, errors, OVER_ROWS)
    returned = passed_along(grad_full[:, :half_width], "layer", -1)
    grad_cross = jnp.where(is_first, returned, grad_full[:, half_width:])
    from_next = passed_along(matmul(errors, cross_full, OVER_COLS), "layer", -1)
    grad_codes = matmul(errors, own_dec, OVER_COLS) + from_next
    grad_pre = jnp.where(preact > 0, grad_codes, 0.0).astype(BF16)
    grad_enc = matmul(inputs, grad_pre, OVER_ROWS)
    grad_bias = jnp.sum(grad_pre.astype(F32), axis=0)
    return (grad_enc[None], grad_bias[None], grad_same[None], grad_cross)


def solution(mesh):
    size = mesh.shape["latent"]
    placed = (
        P("layer", "groups", "latent"),
        P("layer", "groups", "latent"),
        P("layer", None, "latent"),
        P("layer", "latent"),
        P("layer", "latent", None),
        P("latent", "layer"),
    )
    return jax.shard_map(
        ring_shards if size % 2 == 0 and size <= RING_LIMIT else wide_shards,
        mesh=mesh,
        in_specs=placed,
        out_specs=(
            P(("groups", "layer"), None, "latent"),
            P(("groups", "layer"), "latent"),
            P(("groups", "layer"), "latent", None),
            P(("groups", "latent"), "layer"),
        ),
        check_vma=False,
    )
```

```python
import functools
import math

import jax
import jax.numpy as jnp
from jax import lax
from jax.experimental import pallas as pl
from jax.experimental.pallas import tpu as pltpu
from jax.sharding import PartitionSpec as P

F32 = jnp.float32
BF16 = jnp.bfloat16
OVER_ROWS = (((0,), (0,)), ((), ()))
OVER_COLS = (((1,), (1,)), ((), ()))
RING_LIMIT = 16
VMEM_BYTES = 24 * 1024 * 1024
PIECES = 8
GATHER_BYTES = 512 * 1024


def passed_along(shard, axis, by):
    size = lax.axis_size(axis)
    pairs = [(i, i + by) for i in range(size) if 0 <= i + by < size]
    return lax.ppermute(shard, axis, pairs)


def matmul(a, b, dims=(((1,), (0,)), ((), ()))):
    return lax.dot_general(a, b, dims, preferred_element_type=F32)


def ring_order(size):
    return [2 * p if p < size // 2 else 2 * (size - 1 - p) + 1 for p in range(size)]


def ring_member(place, size):
    place = lax.rem(place + 2 * size, size)
    return jnp.where(place < size // 2, 2 * place, 2 * (size - 1 - place) + 1)


def ring_place(member, size):
    return jnp.where(member % 2 == 0, member // 2, size - 1 - member // 2)


def hop(shard, way):
    size, layers = lax.axis_size("latent"), lax.axis_size("layer")
    order = ring_order(size)
    pairs = []
    for p in range(size):
        for layer in range(layers):
            by = way if layer % 2 == 0 else -way
            pairs.append((order[p] * layers + layer, order[(p + by) % size] * layers + layer))
    return lax.ppermute(shard, ("latent", "layer"), pairs)


def after(value, *others):
    return lax.optimization_barrier((value,) + others)[0]


def call(kernel, outs, flops, operands, spaces=None, out_spaces=None, scratch=(), aliases=None):
    def spec(space):
        return pl.BlockSpec(memory_space=space)

    spaces = spaces or [pltpu.VMEM] * (len(operands) - 1)
    out_spaces = out_spaces or [pltpu.VMEM] * len(outs)
    size = sum(math.prod(x.shape) * x.dtype.itemsize for x in list(operands) + list(outs))
    return pl.pallas_call(
        kernel,
        out_shape=outs,
        in_specs=[spec(pltpu.SMEM)] + [spec(space) for space in spaces],
        out_specs=[spec(space) for space in out_spaces],
        scratch_shapes=list(scratch),
        input_output_aliases=aliases or {},
        compiler_params=pltpu.CompilerParams(vmem_limit_bytes=VMEM_BYTES),
        cost_estimate=pl.CostEstimate(flops=flops, bytes_accessed=size, transcendentals=0),
    )(*operands)


def block_of(starts, slot, wide):
    return pl.ds(pl.multiple_of(starts[slot], wide), wide)


def encode_kernel(starts, *refs):
    *shards, weight, bias, preact, codes = refs
    height = shards[0].shape[0]
    for i, shard in enumerate(shards):
        total = bias[...] + jnp.dot(shard[...], weight[0], preferred_element_type=F32)
        preact[i * height:(i + 1) * height, :] = total
        codes[i * height:(i + 1) * height, :] = jnp.maximum(total, 0.0).astype(BF16)


def turn_kernel(starts, *refs):
    *shards, turned = refs
    height = shards[0].shape[0]
    for i, shard in enumerate(shards):
        turned[:, i * height:(i + 1) * height] = shard[...].T


def spread_kernel(slots, starts, codes, earlier, own_dec, cross, *outs):
    *partials, codes_t, earlier_t = outs
    both = jnp.concatenate([codes[...], earlier[...]], axis=1)
    for slot, partial in zip(slots, partials):
        at = block_of(starts, slot, partial.shape[1])
        block = jnp.concatenate([own_dec[0, :, at], cross[:, at]], axis=0)
        partial[...] = jnp.dot(both, block, preferred_element_type=F32).astype(partial.dtype)
    codes_t[...] = codes[...].T
    earlier_t[...] = earlier[...].T


def back_kernel(slots, first, starts, *refs):
    count = len(slots)
    shards, (codes_t, earlier_t, own_dec, cross), refs = refs[:count], refs[count:count + 4], refs[count + 4:]
    if not first:
        own_before, next_before = refs[:2]
        refs = refs[5:]
    back_own, back_next, same, low, high, stage, sems = refs
    wide = shards[0].shape[1]
    half_width = low.shape[1]
    own_total = 0.0 if first else own_before[...]
    next_total = 0.0 if first else next_before[...]
    for i, (slot, shard) in enumerate(zip(slots, shards)):
        start = pl.multiple_of(starts[slot], wide)
        error = shard[...]
        stage[0, i] = jnp.dot(codes_t[...], error, preferred_element_type=F32)
        pltpu.make_async_copy(stage.at[0, i], same.at[0, :, pl.ds(start, wide)], sems.at[0, i]).start()
        stage[1, i] = jnp.dot(earlier_t[...], error, preferred_element_type=F32)

        @pl.when(start < half_width)
        def _():
            pltpu.make_async_copy(stage.at[1, i], low.at[:, pl.ds(start, wide)], sems.at[1, i]).start()

        @pl.when(start >= half_width)
        def _():
            there = pl.multiple_of(start - half_width, wide)
            pltpu.make_async_copy(stage.at[1, i], high.at[:, pl.ds(there, wide)], sems.at[1, i]).start()

        at = pl.ds(start, wide)
        next_total = next_total + lax.dot_general(error, cross[:, at], OVER_COLS, preferred_element_type=F32)
        own_total = own_total + lax.dot_general(error, own_dec[0, :, at], OVER_COLS, preferred_element_type=F32)
    back_own[...] = own_total
    back_next[...] = next_total
    for i in range(count):
        pltpu.make_async_copy(stage.at[0, i], same.at[0, :, pl.ds(0, wide)], sems.at[0, i]).wait()
        pltpu.make_async_copy(stage.at[1, i], low.at[:, pl.ds(0, wide)], sems.at[1, i]).wait()


def finish_kernel(starts, turned, preact, back_own, from_next, returned, high, grad, bias, cross, stage, sems, cross_sem):
    pieces, height = stage.shape[:2]
    first = starts[starts.shape[0] - 1] == 0

    @pl.when(first)
    def _():
        pltpu.make_async_copy(returned, cross, cross_sem).start()

    @pl.when(jnp.logical_not(first))
    def _():
        pltpu.make_async_copy(high, cross, cross_sem).start()

    value = jnp.where(preact[...] > 0, back_own[...] + from_next[...], 0.0).astype(BF16)
    for i in range(pieces):
        rows = pl.ds(i * height, height)
        stage[i] = jnp.dot(turned[rows, :], value, preferred_element_type=F32)
        pltpu.make_async_copy(stage.at[i], grad.at[0, rows, :], sems.at[i]).start()
    bias[...] = jnp.sum(value.astype(F32), axis=0, keepdims=True)
    for i in range(pieces):
        pltpu.make_async_copy(stage.at[i], grad.at[0, pl.ds(i * height, height), :], sems.at[i]).wait()
    pltpu.make_async_copy(high, cross, cross_sem).wait()


def ring_shards(residual_in, targets, enc_weight, enc_bias, dec_same, dec_cross):
    size = lax.axis_size("latent")
    reach = size // 2
    place = ring_place(lax.axis_index("latent"), size)
    layer = lax.axis_index("layer")
    sign = jnp.where(layer % 2 == 0, 1, -1)
    rows, wide = residual_in.shape[1:]
    deep, lat = enc_weight.shape[1:]
    half_width = deep // 2
    err_scale = 1.0 / math.sqrt(rows)
    shape = jax.ShapeDtypeStruct
    unit = 2 * rows * wide * lat

    slot_p = {s: 2 * s - 1 for s in range(1, reach)}
    slot_q = {s: 2 * s for s in range(1, reach)}
    far = size - 1
    slot_p[reach] = far
    offsets = [0] * size
    for s in range(1, reach + 1):
        offsets[slot_p[s]] = -s
        if s < reach:
            offsets[slot_q[s]] = s
    starts = jnp.stack([ring_member(place + sign * offset, size) * wide for offset in offsets] + [layer])
    starts = starts.astype(jnp.int32)

    cross_full = lax.all_gather(dec_cross, "layer", axis=1, tiled=True)
    count = rows * wide * size * 2 // GATHER_BYTES
    height = rows // count
    inputs = [
        lax.all_gather(residual_in[0, i * height:(i + 1) * height], "latent", axis=1, tiled=True) for i in range(count)
    ]
    preact, codes = call(
        encode_kernel,
        [shape((rows, lat), F32), shape((rows, lat), BF16)],
        unit * size,
        [starts] + inputs + [enc_weight, enc_bias],
    )
    earlier = passed_along(codes, "layer", 1)

    def columns(array, slot):
        return lax.dynamic_slice_in_dim(array, starts[slot], wide, 1)

    message = (matmul(codes, columns(dec_same[0], far)) + matmul(earlier, columns(cross_full, far))).astype(BF16)
    ahead = hop(message, 1)
    spread = tuple([slot_p[s] for s in range(reach - 1, 0, -1)] + [slot_q[s] for s in range(reach - 1, 0, -1)] + [0])
    *partials, codes_t, earlier_t = call(
        functools.partial(spread_kernel, spread),
        [shape((rows, wide), BF16 if slot == slot_p.get(reach - 1) else F32) for slot in spread]
        + [shape((lat, rows), BF16)] * 2,
        2 * unit * len(spread),
        [starts, codes, earlier, dec_same, cross_full],
    )
    partial = dict(zip(spread, partials))
    turned = call(turn_kernel, [shape((deep, rows), BF16)], unit, [starts] + inputs)[0]
    total = partial[0]
    behind = None
    for s in range(reach - 1, 0, -1):
        going = partial[slot_p[s]]
        if behind is not None:
            going = (going + behind.astype(F32)).astype(BF16)
        behind = hop(going, -1)
        going = (partial[slot_q[s]] + ahead.astype(F32)).astype(BF16)
        if s == 1:
            going = after(going, turned)
        ahead = hop(going, 1)
    total = total + ahead.astype(F32)
    if behind is not None:
        total = total + behind.astype(F32)
    own_errors = ((total - targets[0].astype(F32)) * err_scale).astype(BF16)

    def back(slots, shards, before):
        count = len(slots)
        acc = shape((rows, lat), F32)
        outs = [acc, acc, shape((1, lat, deep), F32), shape((lat, half_width), F32), shape((lat, half_width), F32)]
        operands = [starts] + list(shards) + [codes_t, earlier_t, dec_same, cross_full]
        aliases = {}
        if before is not None:
            aliases = {len(operands) + 2 + i: 2 + i for i in range(3)}
            operands += list(before)
        spaces = [pltpu.VMEM] * (count + 4) + ([] if before is None else [pltpu.VMEM] * 2 + [pl.ANY] * 3)
        return call(
            functools.partial(back_kernel, slots, before is None),
            outs,
            4 * unit * count,
            operands,
            spaces=spaces,
            out_spaces=[pltpu.VMEM] * 2 + [pl.ANY] * 3,
            scratch=[pltpu.VMEM((2, count, lat, wide), F32), pltpu.SemaphoreType.DMA((2, count))],
            aliases=aliases,
        )

    ahead = hop(own_errors, 1)
    done = back((0,), [own_errors], None)
    if reach > 1:
        behind = hop(after(own_errors, done[0]), -1)
    pending = []
    for s in range(1, reach):
        pending += [(slot_p[s], ahead), (slot_q[s], behind)]
        following = after(ahead, done[0])
        if s % 2 == 0 or s == reach - 1:
            done = back(tuple(slot for slot, _ in pending), [shard for _, shard in pending], done)
            pending = []
        ahead = hop(following, 1)
        if s < reach - 1:
            behind = hop(behind, -1)
    back_own, back_next, grad_same, low, high = back((far,), [ahead], done)
    from_next = passed_along(back_next, "layer", -1)
    returned = passed_along(low, "layer", -1)
    height = deep // PIECES
    grad_enc, grad_bias, grad_cross = call(
        finish_kernel,
        [shape((1, deep, lat), F32), shape((1, lat), F32), shape((lat, half_width), F32)],
        unit * size,
        [starts, turned, preact, back_own, from_next, returned, high],
        spaces=[pltpu.VMEM] * 4 + [pl.ANY] * 2,
        out_spaces=[pl.ANY, pltpu.VMEM, pl.ANY],
        scratch=[
            pltpu.VMEM((PIECES, height, lat), F32),
            pltpu.SemaphoreType.DMA((PIECES,)),
            pltpu.SemaphoreType.DMA,
        ],
    )
    return (grad_enc, grad_bias, grad_same, grad_cross)


def wide_shards(residual_in, targets, enc_weight, enc_bias, dec_same, dec_cross):
    is_first = lax.axis_index("layer") == 0
    err_scale = 1.0 / math.sqrt(residual_in.shape[1])
    inputs = lax.all_gather(residual_in[0], "latent", axis=1, tiled=True)
    preact = matmul(inputs, enc_weight[0]) + enc_bias[0]
    codes_now = jnp.maximum(preact, 0.0).astype(BF16)
    earlier = passed_along(codes_now, "layer", 1)
    cross_full = lax.all_gather(dec_cross, "layer", axis=1, tiled=True)
    own_dec = dec_same[0]
    half_width = own_dec.shape[1] // 2
    recon_full = lax.psum(matmul(codes_now, own_dec) + matmul(earlier, cross_full), "latent")
    wanted = lax.all_gather(targets[0], "latent", axis=1, tiled=True)
    errors = ((recon_full - wanted.astype(F32)) * err_scale).astype(BF16)
    grad_same = matmul(codes_now, errors, OVER_ROWS)
    grad_full = matmul(earlier, errors, OVER_ROWS)
    returned = passed_along(grad_full[:, :half_width], "layer", -1)
    grad_cross = jnp.where(is_first, returned, grad_full[:, half_width:])
    from_next = passed_along(matmul(errors, cross_full, OVER_COLS), "layer", -1)
    grad_codes = matmul(errors, own_dec, OVER_COLS) + from_next
    grad_pre = jnp.where(preact > 0, grad_codes, 0.0).astype(BF16)
    grad_enc = matmul(inputs, grad_pre, OVER_ROWS)
    grad_bias = jnp.sum(grad_pre.astype(F32), axis=0)
    return (grad_enc[None], grad_bias[None], grad_same[None], grad_cross)


def solution(mesh):
    size = mesh.shape["latent"]
    placed = (
        P("layer", "groups", "latent"),
        P("layer", "groups", "latent"),
        P("layer", None, "latent"),
        P("layer", "latent"),
        P("layer", "latent", None),
        P("latent", "layer"),
    )
    return jax.shard_map(
        ring_shards if size % 2 == 0 and size <= RING_LIMIT else wide_shards,
        mesh=mesh,
        in_specs=placed,
        out_specs=(
            P(("groups", "layer"), None, "latent"),
            P(("groups", "layer"), "latent"),
            P(("groups", "layer"), "latent", None),
            P(("groups", "latent"), "layer"),
        ),
        check_vma=False,
    )
```

```python
import functools
import math

import jax
import jax.numpy as jnp
from jax import lax
from jax.experimental import pallas as pl
from jax.experimental.pallas import tpu as pltpu
from jax.sharding import PartitionSpec as P

F32 = jnp.float32
BF16 = jnp.bfloat16
OVER_ROWS = (((0,), (0,)), ((), ()))
OVER_COLS = (((1,), (1,)), ((), ()))
RING_LIMIT = 16
VMEM_BYTES = 24 * 1024 * 1024
PIECES = 8


def passed_along(shard, axis, by):
    size = lax.axis_size(axis)
    pairs = [(i, i + by) for i in range(size) if 0 <= i + by < size]
    return lax.ppermute(shard, axis, pairs)


def matmul(a, b, dims=(((1,), (0,)), ((), ()))):
    return lax.dot_general(a, b, dims, preferred_element_type=F32)


def ring_order(size):
    return [2 * p if p < size // 2 else 2 * (size - 1 - p) + 1 for p in range(size)]


def ring_member(place, size):
    place = lax.rem(place + 2 * size, size)
    return jnp.where(place < size // 2, 2 * place, 2 * (size - 1 - place) + 1)


def ring_place(member, size):
    return jnp.where(member % 2 == 0, member // 2, size - 1 - member // 2)


def hop(shard, way):
    size, layers = lax.axis_size("latent"), lax.axis_size("layer")
    order = ring_order(size)
    pairs = []
    for p in range(size):
        for layer in range(layers):
            by = way if layer % 2 == 0 else -way
            pairs.append((order[p] * layers + layer, order[(p + by) % size] * layers + layer))
    return lax.ppermute(shard, ("latent", "layer"), pairs)


def after(value, *others):
    return lax.optimization_barrier((value,) + others)[0]


def call(kernel, outs, flops, operands, spaces=None, out_spaces=None, scratch=(), aliases=None):
    def spec(space):
        return pl.BlockSpec(memory_space=space)

    spaces = spaces or [pltpu.VMEM] * (len(operands) - 1)
    out_spaces = out_spaces or [pltpu.VMEM] * len(outs)
    size = sum(math.prod(x.shape) * x.dtype.itemsize for x in list(operands) + list(outs))
    return pl.pallas_call(
        kernel,
        out_shape=outs,
        in_specs=[spec(pltpu.SMEM)] + [spec(space) for space in spaces],
        out_specs=[spec(space) for space in out_spaces],
        scratch_shapes=list(scratch),
        input_output_aliases=aliases or {},
        compiler_params=pltpu.CompilerParams(vmem_limit_bytes=VMEM_BYTES),
        cost_estimate=pl.CostEstimate(flops=flops, bytes_accessed=size, transcendentals=0),
    )(*operands)


def block_of(starts, slot, wide):
    return pl.ds(pl.multiple_of(starts[slot], wide), wide)


def prepare_kernel(starts, own_dec, low_cross, high_cross, weight, stacked, weight_here):
    lat, half_width = high_cross.shape
    stacked[:lat, :] = own_dec[0]
    stacked[lat:, :half_width] = low_cross[...]
    stacked[lat:, half_width:] = high_cross[...]
    weight_here[...] = weight[0]


def encode_kernel(slots, last, starts, *refs):
    shards, (weight, before, *outs) = refs[:len(slots)], refs[len(slots):]
    total = jnp.broadcast_to(before[...], outs[0].shape)
    for slot, shard in zip(slots, shards):
        block = weight[block_of(starts, slot, shard.shape[1]), :]
        total = total + jnp.dot(shard[...], block, preferred_element_type=F32)
    outs[0][...] = total
    if last:
        outs[1][...] = jnp.maximum(total, 0.0).astype(BF16)


def turn_kernel(starts, *refs):
    *shards, turned = refs
    rows, wide = shards[0].shape
    for k in range(len(shards) // 2):
        at = block_of(starts, k, wide)
        for chain in range(2):
            turned[at, chain * rows:(chain + 1) * rows] = shards[2 * k + chain][...].T


def spread_kernel(slots, starts, codes, earlier, stacked, *outs):
    *partials, both_t = outs
    both = jnp.concatenate([codes[...], earlier[...]], axis=1)
    for slot, partial in zip(slots, partials):
        block = stacked[:, block_of(starts, slot, partial.shape[1])]
        partial[...] = jnp.dot(both, block, preferred_element_type=F32).astype(partial.dtype)
    both_t[...] = both.T


def back_products(slots, starts, shards, stacked, both_t, before):
    wide = shards[0].shape[1]
    blocks, totals = [], [None, None] if before is None else [before[0], before[1]]
    for i, slot in enumerate(slots):
        decoder = stacked[:, block_of(starts, slot, wide)]
        block = 0.0
        for chain in range(2):
            error = shards[2 * i + chain][...]
            block = block + jnp.dot(both_t[chain][...], error, preferred_element_type=F32)
            term = lax.dot_general(error, decoder, OVER_COLS, preferred_element_type=F32)
            totals[chain] = term if totals[chain] is None else totals[chain] + term
        blocks.append(block)
    return blocks, totals


def back_kernel(slots, first, starts, *refs):
    count = 2 * len(slots)
    shards, (stacked, *both_t), (*before, outer, back) = refs[:count], refs[count:count + 3], refs[count + 3:]
    blocks, totals = back_products(slots, starts, shards, stacked, both_t, None if first else before[0])
    for i, block in enumerate(blocks):
        outer[i] = block
    for chain in range(2):
        back[chain] = totals[chain]


def last_back_kernel(slots, far, starts, *refs):
    near_refs, (before, same, back_own, sent, high) = refs[:-5], refs[-5:]
    shards, (stacked, *both_t), outers = near_refs[:2], near_refs[2:5], near_refs[5:]
    (block,), totals = back_products((far,), starts, shards, stacked, both_t, before)
    rows, wide = shards[0].shape
    lat = high.shape[1]
    half_width = high.shape[0]
    for chain in range(2):
        back_own[chain * rows:(chain + 1) * rows, :] = totals[chain][:, :lat]
        sent[chain * rows:(chain + 1) * rows, :] = totals[chain][:, lat:]
    same[...] = block[:lat]
    pieces = [(far, block[lat:])]
    for group, outer in zip(slots, outers):
        pieces += [(slot, outer[i, lat:]) for i, slot in enumerate(group)]
    for slot, piece in pieces:
        start = pl.multiple_of(starts[slot], wide)

        @pl.when(start < half_width)
        def _():
            for c in range(0, wide, lat):
                sent[pl.ds(2 * rows + start + c, lat), :] = piece[:, c:c + lat]

        @pl.when(start >= half_width)
        def _():
            for c in range(0, wide, lat):
                high[pl.ds(start - half_width + c, lat), :] = piece[:, c:c + lat]


def finish_kernel(slots, far, starts, *refs):
    turned, pre_0, pre_1, back_own, arrived, high, last_same, *outers = refs[:7 + len(slots)]
    grad, bias, same, cross, stage, value, grad_sems, same_sems, cross_sems = refs[7 + len(slots):]
    pieces, height, lat = stage.shape
    rows = pre_0.shape[0]
    half_width = high.shape[0]
    wide = last_same.shape[1]
    copies = []
    blocks = [(far, last_same)]
    for group, outer in zip(slots, outers):
        blocks += [(slot, outer.at[i, :lat, :]) for i, slot in enumerate(group)]
    for i, (slot, block) in enumerate(blocks):
        copies.append(pltpu.make_async_copy(block, same.at[0, :, block_of(starts, slot, wide)], same_sems.at[i]))
        copies[-1].start()
    first = starts[starts.shape[0] - 1] == 0
    steps = range(half_width // lat)
    for c in steps:
        at = pl.ds(c * lat, lat)

        @pl.when(first)
        def _():
            source = arrived.at[pl.ds(2 * rows + c * lat, lat), :]
            pltpu.make_async_copy(source, cross.at[:, at], cross_sems.at[c]).start()

        @pl.when(jnp.logical_not(first))
        def _():
            pltpu.make_async_copy(high.at[at, :], cross.at[:, at], cross_sems.at[c]).start()

        copies.append(pltpu.make_async_copy(high.at[at, :], cross.at[:, at], cross_sems.at[c]))
    total = 0.0
    for chain, preact in enumerate((pre_0, pre_1)):
        at = slice(chain * rows, (chain + 1) * rows)
        masked = jnp.where(preact[...] > 0, back_own[at, :] + arrived[at, :], 0.0).astype(BF16)
        value[at, :] = masked
        total = total + jnp.sum(masked.astype(F32), axis=0, keepdims=True)
    bias[...] = total
    for i in range(pieces):
        at = pl.ds(i * height, height)
        stage[i] = jnp.dot(turned[at, :], value[...], preferred_element_type=F32)
        copies.append(pltpu.make_async_copy(stage.at[i], grad.at[0, at, :], grad_sems.at[i]))
        copies[-1].start()
    for copy in copies:
        copy.wait()


def ring_shards(residual_in, targets, enc_weight, enc_bias, dec_same, dec_cross):
    size = lax.axis_size("latent")
    reach = size // 2
    place = ring_place(lax.axis_index("latent"), size)
    layer = lax.axis_index("layer")
    sign = jnp.where(layer % 2 == 0, 1, -1)
    rows, wide = residual_in.shape[1:]
    half = rows // 2
    deep, lat = enc_weight.shape[1:]
    half_width = deep // 2
    err_scale = 1.0 / math.sqrt(rows)
    shape = jax.ShapeDtypeStruct
    unit = rows * wide * lat
    chains = (0, 1)

    def halves(array):
        return [array[:half], array[half:]]

    slot_p = {s: 2 * s - 1 for s in range(1, reach)}
    slot_q = {s: 2 * s for s in range(1, reach)}
    far = size - 1
    offsets = [0] * size
    offsets[far] = reach
    for s in range(1, reach):
        offsets[slot_p[s]] = -s
        offsets[slot_q[s]] = s
    starts = jnp.stack([ring_member(place + sign * offset, size) * wide for offset in offsets] + [layer])
    starts = starts.astype(jnp.int32)

    def gather_step(found, s):
        for chain in chains:
            at_p, at_q = (0, 0) if s == 1 else (slot_p[s - 1], slot_q[s - 1])
            if s < reach:
                pair = hop(found[chain][at_p], 1), hop(found[chain][at_q], -1)
                found[chain][slot_p[s]], found[chain][slot_q[s]] = lax.optimization_barrier(pair)
            else:
                found[chain][far] = hop(found[chain][at_q if chain else at_p], -1 if chain else 1)

    inputs = [[part] + [None] * (size - 1) for part in halves(residual_in[0])]
    for s in range(1, reach + 1):
        gather_step(inputs, s)
    low_cross = passed_along(dec_cross, "layer", 1)
    stacked, weight = call(
        prepare_kernel,
        [shape((2 * lat, deep), BF16), shape((deep, lat), BF16)],
        0,
        [starts, dec_same, low_cross, dec_cross, enc_weight],
    )
    early = tuple(range(size - 1))
    preacts, codes, earlier = [], [], []
    for chain in chains:
        part = call(
            functools.partial(encode_kernel, early, False),
            [shape((half, lat), F32)],
            unit * len(early),
            [starts] + inputs[chain][:-1] + [weight, enc_bias],
        )[0]
        preact, now = call(
            functools.partial(encode_kernel, (far,), True),
            [shape((half, lat), F32), shape((half, lat), BF16)],
            unit,
            [starts, inputs[chain][far], weight, part],
        )
        preacts.append(preact)
        codes.append(now)
        earlier.append(passed_along(now, "layer", 1))

    spread = (far,) + tuple(slot for s in range(reach - 1, 0, -1) for slot in (slot_q[s], slot_p[s])) + (0,)
    partial, both_t, ahead, behind = [], [], [], []
    for chain in chains:
        instant = {far, slot_q.get(reach - 1) if chain else slot_p.get(reach - 1)}
        *pieces, turned_codes = call(
            functools.partial(spread_kernel, spread),
            [shape((half, wide), BF16 if slot in instant else F32) for slot in spread]
            + [shape((2 * lat, half), BF16)],
            2 * unit * len(spread),
            [starts, codes[chain], earlier[chain], stacked],
        )
        partial.append(dict(zip(spread, pieces)))
        both_t.append(turned_codes)
    both = [shard for pair in zip(*inputs) for shard in pair]
    turned = call(turn_kernel, [shape((deep, rows), BF16)], unit, [starts] + both)[0]
    ahead = [hop(partial[0][far], 1), None]
    behind = [None, hop(partial[1][far], -1)]
    for s in range(reach - 1, 0, -1):
        for chain in chains:
            plus, minus = partial[chain][slot_q[s]], partial[chain][slot_p[s]]
            if ahead[chain] is not None:
                plus = (plus + ahead[chain].astype(F32)).astype(BF16)
            if behind[chain] is not None:
                minus = (minus + behind[chain].astype(F32)).astype(BF16)
            ahead[chain] = hop(plus, 1)
            behind[chain] = hop(minus, -1)
    errors = []
    for chain, wanted in zip(chains, halves(targets[0])):
        total = partial[chain][0]
        for arrived in (ahead[chain], behind[chain]):
            if arrived is not None:
                total = total + arrived.astype(F32)
        if chain == 1:
            wanted = after(wanted, errors[0][0])
        errors.append([((total - wanted.astype(F32)) * err_scale).astype(BF16)] + [None] * (size - 1))

    def near(slots):
        return [errors[chain][slot] for slot in slots for chain in chains]

    def back(slots, before):
        return call(
            functools.partial(back_kernel, slots, before is None),
            [shape((len(slots), 2 * lat, wide), F32), shape((2, half, 2 * lat), F32)],
            4 * unit * len(slots),
            [starts] + near(slots) + [stacked] + both_t + ([] if before is None else [before]),
        )

    groups, outers, acc, pending = [], [], None, [0]
    for s in range(1, reach + 1):
        gather_step(errors, s)
        if s < reach:
            pending += [slot_p[s], slot_q[s]]
        if s == 1 or s == reach - 1:
            groups.append(tuple(pending))
            outer, acc = back(groups[-1], acc)
            outers.append(outer)
            pending = []
    if not groups:
        groups.append((0,))
        outer, acc = back(groups[-1], acc)
        outers.append(outer)
    last_same, back_own, sent, high = call(
        functools.partial(last_back_kernel, groups, far),
        [
            shape((lat, wide), F32),
            shape((rows, lat), F32),
            shape((rows + half_width, lat), F32),
            shape((half_width, lat), F32),
        ],
        4 * unit,
        [starts] + near((far,)) + [stacked] + both_t + outers + [acc],
    )
    arrived = passed_along(sent, "layer", -1)
    height = deep // PIECES
    grad_enc, grad_bias, grad_same, grad_cross = call(
        functools.partial(finish_kernel, groups, far),
        [
            shape((1, deep, lat), F32),
            shape((1, lat), F32),
            shape((1, lat, deep), F32),
            shape((lat, half_width), F32),
        ],
        2 * unit * size,
        [starts, turned] + preacts + [back_own, arrived, high, last_same] + outers,
        out_spaces=[pl.ANY, pltpu.VMEM, pl.ANY, pl.ANY],
        scratch=[
            pltpu.VMEM((PIECES, height, lat), F32),
            pltpu.VMEM((rows, lat), BF16),
            pltpu.SemaphoreType.DMA((PIECES,)),
            pltpu.SemaphoreType.DMA((size,)),
            pltpu.SemaphoreType.DMA((half_width // lat,)),
        ],
    )
    return (grad_enc, grad_bias, grad_same, grad_cross)


def wide_shards(residual_in, targets, enc_weight, enc_bias, dec_same, dec_cross):
    is_first = lax.axis_index("layer") == 0
    err_scale = 1.0 / math.sqrt(residual_in.shape[1])
    inputs = lax.all_gather(residual_in[0], "latent", axis=1, tiled=True)
    preact = matmul(inputs, enc_weight[0]) + enc_bias[0]
    codes_now = jnp.maximum(preact, 0.0).astype(BF16)
    earlier = passed_along(codes_now, "layer", 1)
    cross_full = lax.all_gather(dec_cross, "layer", axis=1, tiled=True)
    own_dec = dec_same[0]
    half_width = own_dec.shape[1] // 2
    recon_full = lax.psum(matmul(codes_now, own_dec) + matmul(earlier, cross_full), "latent")
    wanted = lax.all_gather(targets[0], "latent", axis=1, tiled=True)
    errors = ((recon_full - wanted.astype(F32)) * err_scale).astype(BF16)
    grad_same = matmul(codes_now, errors, OVER_ROWS)
    grad_full = matmul(earlier, errors, OVER_ROWS)
    returned = passed_along(grad_full[:, :half_width], "layer", -1)
    grad_cross = jnp.where(is_first, returned, grad_full[:, half_width:])
    from_next = passed_along(matmul(errors, cross_full, OVER_COLS), "layer", -1)
    grad_codes = matmul(errors, own_dec, OVER_COLS) + from_next
    grad_pre = jnp.where(preact > 0, grad_codes, 0.0).astype(BF16)
    grad_enc = matmul(inputs, grad_pre, OVER_ROWS)
    grad_bias = jnp.sum(grad_pre.astype(F32), axis=0)
    return (grad_enc[None], grad_bias[None], grad_same[None], grad_cross)


def solution(mesh):
    size = mesh.shape["latent"]
    placed = (
        P("layer", "groups", "latent"),
        P("layer", "groups", "latent"),
        P("layer", None, "latent"),
        P("layer", "latent"),
        P("layer", "latent", None),
        P("latent", "layer"),
    )
    return jax.shard_map(
        ring_shards if size % 2 == 0 and size <= RING_LIMIT else wide_shards,
        mesh=mesh,
        in_specs=placed,
        out_specs=(
            P(("groups", "layer"), None, "latent"),
            P(("groups", "layer"), "latent"),
            P(("groups", "layer"), "latent", None),
            P(("groups", "latent"), "layer"),
        ),
        check_vma=False,
    )
```

```python
import functools
import math

import jax
import jax.numpy as jnp
from jax import lax
from jax.experimental import pallas as pl
from jax.experimental.pallas import tpu as pltpu
from jax.sharding import PartitionSpec as P

F32 = jnp.float32
BF16 = jnp.bfloat16
OVER_ROWS = (((0,), (0,)), ((), ()))
OVER_COLS = (((1,), (1,)), ((), ()))
GRID_SIZES = (2, 4, 8, 16)
VMEM_BYTES = 24 * 1024 * 1024
PIECES = 8


def passed_along(shard, axis, by):
    size = lax.axis_size(axis)
    pairs = [(i, i + by) for i in range(size) if 0 <= i + by < size]
    return lax.ppermute(shard, axis, pairs)


def matmul(a, b, dims=(((1,), (0,)), ((), ()))):
    return lax.dot_general(a, b, dims, preferred_element_type=F32)


def hop(shard, mask):
    return lax.ppermute(shard, "latent", [(i, i ^ mask) for i in range(lax.axis_size("latent"))])


def after(value, *others):
    return lax.optimization_barrier((value,) + others)[0]


def call(kernel, outs, flops, operands, spaces=None, out_spaces=None, scratch=(), aliases=None):
    def spec(space):
        return pl.BlockSpec(memory_space=space)

    spaces = spaces or [pltpu.VMEM] * (len(operands) - 1)
    out_spaces = out_spaces or [pltpu.VMEM] * len(outs)
    size = sum(math.prod(x.shape) * x.dtype.itemsize for x in list(operands) + list(outs))
    return pl.pallas_call(
        kernel,
        out_shape=outs,
        in_specs=[spec(pltpu.SMEM)] + [spec(space) for space in spaces],
        out_specs=[spec(space) for space in out_spaces],
        scratch_shapes=list(scratch),
        input_output_aliases=aliases or {},
        compiler_params=pltpu.CompilerParams(vmem_limit_bytes=VMEM_BYTES),
        cost_estimate=pl.CostEstimate(flops=flops, bytes_accessed=size, transcendentals=0),
    )(*operands)


def block_of(starts, slot, wide):
    return pl.ds(pl.multiple_of(starts[slot], wide), wide)


def prepare_kernel(starts, own_dec, low_cross, high_cross, weight, stacked, weight_here):
    lat, half_width = high_cross.shape
    stacked[:lat, :] = own_dec[0]
    stacked[lat:, :half_width] = low_cross[...]
    stacked[lat:, half_width:] = high_cross[...]
    weight_here[...] = weight[0]


def encode_kernel(slots, last, starts, *refs):
    shards, (weight, before, *outs) = refs[:len(slots)], refs[len(slots):]
    total = jnp.broadcast_to(before[...], outs[0].shape)
    for slot, shard in zip(slots, shards):
        block = weight[block_of(starts, slot, shard.shape[1]), :]
        total = total + jnp.dot(shard[...], block, preferred_element_type=F32)
    outs[0][...] = total
    if last:
        outs[1][...] = jnp.maximum(total, 0.0).astype(BF16)


def turn_kernel(starts, *refs):
    *shards, turned = refs
    for slot, shard in enumerate(shards):
        turned[block_of(starts, slot, shard.shape[1]), :] = shard[...].T


def spread_kernel(slots, starts, codes, earlier, stacked, *partials):
    both = jnp.concatenate([codes[...], earlier[...]], axis=1)
    for slot, partial in zip(slots, partials):
        block = stacked[:, block_of(starts, slot, partial.shape[1])]
        partial[...] = jnp.dot(both, block, preferred_element_type=F32).astype(partial.dtype)
    if len(partials) > len(slots):
        partials[-1][...] = both.T


def back_products(slots, starts, shards, stacked, both_t, before):
    blocks, total = [], before
    for slot, shard in zip(slots, shards):
        error = shard[...]
        decoder = stacked[:, block_of(starts, slot, error.shape[1])]
        blocks.append(jnp.dot(both_t[...], error, preferred_element_type=F32))
        term = lax.dot_general(error, decoder, OVER_COLS, preferred_element_type=F32)
        total = term if total is None else total + term
    return blocks, total


def back_kernel(slots, first, starts, *refs):
    count = len(slots)
    shards, (stacked, both_t), (*before, outer, back) = refs[:count], refs[count:count + 2], refs[count + 2:]
    blocks, total = back_products(slots, starts, shards, stacked, both_t, None if first else before[0][...])
    for i, block in enumerate(blocks):
        outer[i] = block
    back[...] = total


def last_back_kernel(slots, far, starts, *refs):
    shard, stacked, both_t, *outers, before, same, back_own, sent, high = refs
    (block,), total = back_products((far,), starts, (shard,), stacked, both_t, before[...])
    rows, wide = shard.shape
    half_width, lat = high.shape
    back_own[...] = total[:, :lat]
    sent[:rows, :] = total[:, lat:]
    same[...] = block[:lat]
    pieces = [(far, block[lat:])]
    for group, outer in zip(slots, outers):
        pieces += [(slot, outer[i, lat:]) for i, slot in enumerate(group)]
    for slot, piece in pieces:
        start = pl.multiple_of(starts[slot], wide)

        @pl.when(start < half_width)
        def _():
            for c in range(0, wide, lat):
                sent[pl.ds(rows + start + c, lat), :] = piece[:, c:c + lat]

        @pl.when(start >= half_width)
        def _():
            for c in range(0, wide, lat):
                high[pl.ds(start - half_width + c, lat), :] = piece[:, c:c + lat]


def finish_kernel(slots, far, starts, *refs):
    turned, preact, back_own, arrived, high, last_same, *outers = refs[:6 + len(slots)]
    grad, bias, same, cross, stage, grad_sems, same_sems, cross_sems = refs[6 + len(slots):]
    pieces, height, lat = stage.shape
    rows = preact.shape[0]
    half_width = high.shape[0]
    wide = last_same.shape[1]
    copies = []
    blocks = [(far, last_same)]
    for group, outer in zip(slots, outers):
        blocks += [(slot, outer.at[i, :lat, :]) for i, slot in enumerate(group)]
    for i, (slot, block) in enumerate(blocks):
        copies.append(pltpu.make_async_copy(block, same.at[0, :, block_of(starts, slot, wide)], same_sems.at[i]))
        copies[-1].start()
    first = starts[starts.shape[0] - 1] == 0
    for c in range(half_width // lat):
        at = pl.ds(c * lat, lat)

        @pl.when(first)
        def _():
            source = arrived.at[pl.ds(rows + c * lat, lat), :]
            pltpu.make_async_copy(source, cross.at[:, at], cross_sems.at[c]).start()

        @pl.when(jnp.logical_not(first))
        def _():
            pltpu.make_async_copy(high.at[at, :], cross.at[:, at], cross_sems.at[c]).start()

        copies.append(pltpu.make_async_copy(high.at[at, :], cross.at[:, at], cross_sems.at[c]))
    value = jnp.where(preact[...] > 0, back_own[...] + arrived[:rows, :], 0.0).astype(BF16)
    for i in range(pieces):
        at = pl.ds(i * height, height)
        stage[i] = jnp.dot(turned[at, :], value, preferred_element_type=F32)
        copies.append(pltpu.make_async_copy(stage.at[i], grad.at[0, at, :], grad_sems.at[i]))
        copies[-1].start()
    bias[...] = jnp.sum(value.astype(F32), axis=0, keepdims=True)
    for copy in copies:
        copy.wait()


def grid_shards(residual_in, targets, enc_weight, enc_bias, dec_same, dec_cross):
    size = lax.axis_size("latent")
    tall = size // 2
    member = lax.axis_index("latent")
    layer = lax.axis_index("layer")
    rows, wide = residual_in.shape[1:]
    deep, lat = enc_weight.shape[1:]
    half_width = deep // 2
    err_scale = 1.0 / math.sqrt(rows)
    shape = jax.ShapeDtypeStruct
    unit = 2 * rows * wide * lat

    starts = jnp.stack([(member ^ (2 * (j % tall) + j // tall)) * wide for j in range(size)] + [layer])
    starts = starts.astype(jnp.int32)
    along = [1] + list(range(tall - 1, 1, -1)) if tall > 1 else []
    last = tall + (along[-1] if along else 0)

    def gather(own, ready=None):
        found = [own] + [None] * (size - 1)
        for k in along:
            found[k] = hop(own, 2 * k)
        found[tall] = hop(own, 1)
        for k in along:
            passing = found[k]
            if ready is not None and k == along[-1]:
                passing = after(passing, ready)
            found[tall + k] = hop(passing, 1)
        return found

    low_cross = passed_along(dec_cross, "layer", 1)
    stacked, weight = call(
        prepare_kernel,
        [shape((2 * lat, deep), BF16), shape((deep, lat), BF16)],
        0,
        [starts, dec_same, low_cross, dec_cross, enc_weight],
    )
    inputs = gather(residual_in[0], stacked)
    early = tuple(slot for slot in range(size) if slot != last)
    part = call(
        functools.partial(encode_kernel, early, False),
        [shape((rows, lat), F32)],
        unit * len(early),
        [starts] + [inputs[slot] for slot in early] + [weight, enc_bias],
    )[0]
    preact, codes = call(
        functools.partial(encode_kernel, (last,), True),
        [shape((rows, lat), F32), shape((rows, lat), BF16)],
        unit,
        [starts, inputs[last], weight, part],
    )
    earlier = passed_along(codes, "layer", 1)

    across = tuple(tall + k for k in reversed([0] + along)) if along else (tall,)
    messages = call(
        functools.partial(spread_kernel, across),
        [shape((rows, wide), BF16)] * len(across),
        2 * unit * len(across),
        [starts, codes, earlier, stacked],
    )
    arrived = {slot - tall: hop(message, 1) for slot, message in zip(across, messages)}
    column = tuple(range(tall))
    *partials, both_t = call(
        functools.partial(spread_kernel, column),
        [shape((rows, wide), F32)] * tall + [shape((2 * lat, rows), BF16)],
        2 * unit * tall,
        [starts, codes, earlier, stacked],
    )
    summed = {}
    for k in reversed(along):
        summed[k] = hop((partials[k] + arrived[k].astype(F32)).astype(BF16), 2 * k)
    total = partials[0] + arrived[0].astype(F32)
    for k in along:
        total = total + summed[k].astype(F32)
    own_errors = ((total - targets[0].astype(F32)) * err_scale).astype(BF16)

    errors = gather(own_errors)
    turned = call(turn_kernel, [shape((deep, rows), BF16)], unit, [starts] + inputs)[0]

    def back(slots, before):
        return call(
            functools.partial(back_kernel, slots, before is None),
            [shape((len(slots), 2 * lat, wide), F32), shape((rows, 2 * lat), F32)],
            4 * unit * len(slots),
            [starts] + [errors[slot] for slot in slots] + [stacked, both_t] + ([] if before is None else [before]),
        )

    first_group = (0,) + tuple(along[:1])
    if last != tall:
        first_group += (tall,)
    groups = [first_group, tuple(slot for slot in range(size) if slot not in first_group and slot != last)]
    groups = [group for group in groups if group]
    outers, acc = [], None
    for group in groups:
        outer, acc = back(group, acc)
        outers.append(outer)
    last_same, back_own, sent, high = call(
        functools.partial(last_back_kernel, groups, last),
        [
            shape((lat, wide), F32),
            shape((rows, lat), F32),
            shape((rows + half_width, lat), F32),
            shape((half_width, lat), F32),
        ],
        4 * unit,
        [starts, errors[last], stacked, both_t] + outers + [acc],
    )
    returned = passed_along(sent, "layer", -1)
    height = deep // PIECES
    grad_enc, grad_bias, grad_same, grad_cross = call(
        functools.partial(finish_kernel, groups, last),
        [
            shape((1, deep, lat), F32),
            shape((1, lat), F32),
            shape((1, lat, deep), F32),
            shape((lat, half_width), F32),
        ],
        unit * size,
        [starts, turned, preact, back_own, returned, high, last_same] + outers,
        out_spaces=[pl.ANY, pltpu.VMEM, pl.ANY, pl.ANY],
        scratch=[
            pltpu.VMEM((PIECES, height, lat), F32),
            pltpu.SemaphoreType.DMA((PIECES,)),
            pltpu.SemaphoreType.DMA((size,)),
            pltpu.SemaphoreType.DMA((half_width // lat,)),
        ],
    )
    return (grad_enc, grad_bias, grad_same, grad_cross)


def wide_shards(residual_in, targets, enc_weight, enc_bias, dec_same, dec_cross):
    is_first = lax.axis_index("layer") == 0
    err_scale = 1.0 / math.sqrt(residual_in.shape[1])
    inputs = lax.all_gather(residual_in[0], "latent", axis=1, tiled=True)
    preact = matmul(inputs, enc_weight[0]) + enc_bias[0]
    codes_now = jnp.maximum(preact, 0.0).astype(BF16)
    earlier = passed_along(codes_now, "layer", 1)
    cross_full = lax.all_gather(dec_cross, "layer", axis=1, tiled=True)
    own_dec = dec_same[0]
    half_width = own_dec.shape[1] // 2
    recon_full = lax.psum(matmul(codes_now, own_dec) + matmul(earlier, cross_full), "latent")
    wanted = lax.all_gather(targets[0], "latent", axis=1, tiled=True)
    errors = ((recon_full - wanted.astype(F32)) * err_scale).astype(BF16)
    grad_same = matmul(codes_now, errors, OVER_ROWS)
    grad_full = matmul(earlier, errors, OVER_ROWS)
    returned = passed_along(grad_full[:, :half_width], "layer", -1)
    grad_cross = jnp.where(is_first, returned, grad_full[:, half_width:])
    from_next = passed_along(matmul(errors, cross_full, OVER_COLS), "layer", -1)
    grad_codes = matmul(errors, own_dec, OVER_COLS) + from_next
    grad_pre = jnp.where(preact > 0, grad_codes, 0.0).astype(BF16)
    grad_enc = matmul(inputs, grad_pre, OVER_ROWS)
    grad_bias = jnp.sum(grad_pre.astype(F32), axis=0)
    return (grad_enc[None], grad_bias[None], grad_same[None], grad_cross)


def solution(mesh):
    size = mesh.shape["latent"]
    placed = (
        P("layer", "groups", "latent"),
        P("layer", "groups", "latent"),
        P("layer", None, "latent"),
        P("layer", "latent"),
        P("layer", "latent", None),
        P("latent", "layer"),
    )
    return jax.shard_map(
        grid_shards if size in GRID_SIZES else wide_shards,
        mesh=mesh,
        in_specs=placed,
        out_specs=(
            P(("groups", "layer"), None, "latent"),
            P(("groups", "layer"), "latent"),
            P(("groups", "layer"), "latent", None),
            P(("groups", "latent"), "layer"),
        ),
        check_vma=False,
    )
```

```python
import functools
import math

import jax
import jax.numpy as jnp
from jax import lax
from jax.experimental import pallas as pl
from jax.experimental.pallas import tpu as pltpu
from jax.sharding import PartitionSpec as P

F32 = jnp.float32
BF16 = jnp.bfloat16
OVER_ROWS = (((0,), (0,)), ((), ()))
OVER_COLS = (((1,), (1,)), ((), ()))
RING_LIMIT = 16
VMEM_BYTES = 24 * 1024 * 1024
PIECES = 8


def passed_along(shard, axis, by):
    size = lax.axis_size(axis)
    pairs = [(i, i + by) for i in range(size) if 0 <= i + by < size]
    return lax.ppermute(shard, axis, pairs)


def matmul(a, b, dims=(((1,), (0,)), ((), ()))):
    return lax.dot_general(a, b, dims, preferred_element_type=F32)


def ring_order(size):
    return [2 * p if p < size // 2 else 2 * (size - 1 - p) + 1 for p in range(size)]


def ring_member(place, size):
    place = lax.rem(place + 2 * size, size)
    return jnp.where(place < size // 2, 2 * place, 2 * (size - 1 - place) + 1)


def ring_place(member, size):
    return jnp.where(member % 2 == 0, member // 2, size - 1 - member // 2)


def hop(shard, way):
    size, layers = lax.axis_size("latent"), lax.axis_size("layer")
    order = ring_order(size)
    pairs = []
    for p in range(size):
        for layer in range(layers):
            by = way if layer % 2 == 0 else -way
            pairs.append((order[p] * layers + layer, order[(p + by) % size] * layers + layer))
    return lax.ppermute(shard, ("latent", "layer"), pairs)


def after(value, *others):
    return lax.optimization_barrier((value,) + others)[0]


def call(kernel, outs, flops, operands, spaces=None, out_spaces=None, scratch=(), aliases=None):
    def spec(space):
        return pl.BlockSpec(memory_space=space)

    spaces = spaces or [pltpu.VMEM] * (len(operands) - 1)
    out_spaces = out_spaces or [pltpu.VMEM] * len(outs)
    size = sum(math.prod(x.shape) * x.dtype.itemsize for x in list(operands) + list(outs))
    return pl.pallas_call(
        kernel,
        out_shape=outs,
        in_specs=[spec(pltpu.SMEM)] + [spec(space) for space in spaces],
        out_specs=[spec(space) for space in out_spaces],
        scratch_shapes=list(scratch),
        input_output_aliases=aliases or {},
        compiler_params=pltpu.CompilerParams(vmem_limit_bytes=VMEM_BYTES),
        cost_estimate=pl.CostEstimate(flops=flops, bytes_accessed=size, transcendentals=0),
    )(*operands)


def block_of(starts, slot, wide):
    return pl.ds(pl.multiple_of(starts[slot], wide), wide)


def prepare_kernel(starts, own_dec, low_cross, high_cross, weight, stacked, weight_here, sems):
    lat, half_width = high_cross.shape
    copies = [
        pltpu.make_async_copy(own_dec.at[0], stacked.at[:lat, :], sems.at[0]),
        pltpu.make_async_copy(low_cross, stacked.at[lat:, :half_width], sems.at[1]),
        pltpu.make_async_copy(high_cross, stacked.at[lat:, half_width:], sems.at[2]),
        pltpu.make_async_copy(weight.at[0], weight_here, sems.at[3]),
    ]
    for copy in copies:
        copy.start()
    for copy in copies:
        copy.wait()


def encode_kernel(slots, last, starts, *refs):
    count = 2 * len(slots)
    shards, (weight, before, *outs) = refs[:count], refs[count:]
    rows, wide = shards[0].shape
    for chain in range(2):
        at = slice(chain * rows, (chain + 1) * rows)
        total = before[at, :] if last else jnp.broadcast_to(before[...], (rows, before.shape[1]))
        for i, slot in enumerate(slots):
            block = weight[block_of(starts, slot, wide), :]
            total = total + jnp.dot(shards[2 * i + chain][...], block, preferred_element_type=F32)
        outs[0][at, :] = total
        if last:
            outs[1][at, :] = jnp.maximum(total, 0.0).astype(BF16)


def turn_kernel(starts, *refs):
    *shards, turned = refs
    rows, wide = shards[0].shape
    for k in range(len(shards) // 2):
        at = block_of(starts, k, wide)
        for chain in range(2):
            turned[at, chain * rows:(chain + 1) * rows] = shards[2 * k + chain][...].T


def spread_kernel(chain, slots, starts, codes, earlier, stacked, *partials):
    rows = codes.shape[0] // 2
    at = slice(chain * rows, (chain + 1) * rows)
    both = jnp.concatenate([codes[at, :], earlier[at, :]], axis=1)
    for slot, partial in zip(slots, partials):
        block = stacked[:, block_of(starts, slot, partial.shape[1])]
        partial[...] = jnp.dot(both, block, preferred_element_type=F32).astype(partial.dtype)
    if len(partials) > len(slots):
        partials[-1][...] = both.T


def back_products(slots, starts, shards, stacked, both_t, before):
    wide = shards[0].shape[1]
    blocks, totals = [], [None, None] if before is None else [before[0], before[1]]
    for i, slot in enumerate(slots):
        decoder = stacked[:, block_of(starts, slot, wide)]
        block = 0.0
        for chain in range(2):
            error = shards[2 * i + chain][...]
            block = block + jnp.dot(both_t[chain][...], error, preferred_element_type=F32)
            term = lax.dot_general(error, decoder, OVER_COLS, preferred_element_type=F32)
            totals[chain] = term if totals[chain] is None else totals[chain] + term
        blocks.append(block)
    return blocks, totals


def back_kernel(slots, first, starts, *refs):
    count = 2 * len(slots)
    shards, (stacked, *both_t), (*before, outer, back) = refs[:count], refs[count:count + 3], refs[count + 3:]
    blocks, totals = back_products(slots, starts, shards, stacked, both_t, None if first else before[0])
    for i, block in enumerate(blocks):
        outer[i] = block
    for chain in range(2):
        back[chain] = totals[chain]


def last_back_kernel(slots, far, starts, *refs):
    near_refs, (before, same, back_own, sent, high) = refs[:-5], refs[-5:]
    shards, (stacked, *both_t), outers = near_refs[:2], near_refs[2:5], near_refs[5:]
    (block,), totals = back_products((far,), starts, shards, stacked, both_t, before)
    rows, wide = shards[0].shape
    lat = high.shape[1]
    half_width = high.shape[0]
    for chain in range(2):
        back_own[chain * rows:(chain + 1) * rows, :] = totals[chain][:, :lat]
        sent[chain * rows:(chain + 1) * rows, :] = totals[chain][:, lat:]
    same[...] = block[:lat]
    pieces = [(far, block[lat:])]
    for group, outer in zip(slots, outers):
        pieces += [(slot, outer[i, lat:]) for i, slot in enumerate(group)]
    for slot, piece in pieces:
        start = pl.multiple_of(starts[slot], wide)

        @pl.when(start < half_width)
        def _():
            for c in range(0, wide, lat):
                sent[pl.ds(2 * rows + start + c, lat), :] = piece[:, c:c + lat]

        @pl.when(start >= half_width)
        def _():
            for c in range(0, wide, lat):
                high[pl.ds(start - half_width + c, lat), :] = piece[:, c:c + lat]


def finish_kernel(slots, far, starts, *refs):
    turned, preact, back_own, arrived, high, last_same, *outers = refs[:6 + len(slots)]
    grad, bias, same, cross, stage, grad_sems, same_sems, cross_sems = refs[6 + len(slots):]
    pieces, height, lat = stage.shape
    rows = preact.shape[0]
    half_width = high.shape[0]
    wide = last_same.shape[1]
    copies = []
    blocks = [(far, last_same)]
    for group, outer in zip(slots, outers):
        blocks += [(slot, outer.at[i, :lat, :]) for i, slot in enumerate(group)]
    for i, (slot, block) in enumerate(blocks):
        copies.append(pltpu.make_async_copy(block, same.at[0, :, block_of(starts, slot, wide)], same_sems.at[i]))
        copies[-1].start()
    first = starts[starts.shape[0] - 1] == 0
    for c in range(half_width // lat):
        at = pl.ds(c * lat, lat)

        @pl.when(first)
        def _():
            source = arrived.at[pl.ds(rows + c * lat, lat), :]
            pltpu.make_async_copy(source, cross.at[:, at], cross_sems.at[c]).start()

        @pl.when(jnp.logical_not(first))
        def _():
            pltpu.make_async_copy(high.at[at, :], cross.at[:, at], cross_sems.at[c]).start()

        copies.append(pltpu.make_async_copy(high.at[at, :], cross.at[:, at], cross_sems.at[c]))
    value = jnp.where(preact[...] > 0, back_own[...] + arrived[:rows, :], 0.0).astype(BF16)
    for i in range(pieces):
        at = pl.ds(i * height, height)
        stage[i] = jnp.dot(turned[at, :], value, preferred_element_type=F32)
        copies.append(pltpu.make_async_copy(stage.at[i], grad.at[0, at, :], grad_sems.at[i]))
        copies[-1].start()
    bias[...] = jnp.sum(value.astype(F32), axis=0, keepdims=True)
    for copy in copies:
        copy.wait()


def ring_shards(residual_in, targets, enc_weight, enc_bias, dec_same, dec_cross):
    size = lax.axis_size("latent")
    reach = size // 2
    place = ring_place(lax.axis_index("latent"), size)
    layer = lax.axis_index("layer")
    sign = jnp.where(layer % 2 == 0, 1, -1)
    rows, wide = residual_in.shape[1:]
    half = rows // 2
    deep, lat = enc_weight.shape[1:]
    half_width = deep // 2
    err_scale = 1.0 / math.sqrt(rows)
    shape = jax.ShapeDtypeStruct
    unit = rows * wide * lat
    chains = (0, 1)

    def halves(array):
        return [array[:half], array[half:]]

    slot_p = {s: 2 * s - 1 for s in range(1, reach)}
    slot_q = {s: 2 * s for s in range(1, reach)}
    far = size - 1
    offsets = [0] * size
    offsets[far] = reach
    for s in range(1, reach):
        offsets[slot_p[s]] = -s
        offsets[slot_q[s]] = s
    starts = jnp.stack([ring_member(place + sign * offset, size) * wide for offset in offsets] + [layer])
    starts = starts.astype(jnp.int32)

    def gather_step(found, s):
        for chain in chains:
            at_p, at_q = (0, 0) if s == 1 else (slot_p[s - 1], slot_q[s - 1])
            if s < reach:
                pair = hop(found[chain][at_p], 1), hop(found[chain][at_q], -1)
                if s == 1:
                    pair = lax.optimization_barrier(pair)
                found[chain][slot_p[s]], found[chain][slot_q[s]] = pair
            else:
                found[chain][far] = hop(found[chain][at_q if chain else at_p], -1 if chain else 1)

    inputs = [[part] + [None] * (size - 1) for part in halves(residual_in[0])]
    low_cross = passed_along(dec_cross, "layer", 1)
    stacked, weight = call(
        prepare_kernel,
        [shape((2 * lat, deep), BF16), shape((deep, lat), BF16)],
        0,
        [starts, dec_same, low_cross, dec_cross, enc_weight],
        spaces=[pl.ANY] * 4,
        scratch=[pltpu.SemaphoreType.DMA((4,))],
    )
    for s in range(1, reach + 1):
        if s == reach and reach > 1:
            inputs[0][slot_p[s - 1]] = after(inputs[0][slot_p[s - 1]], stacked)
        gather_step(inputs, s)

    def both_chains(found, slots):
        return [found[chain][slot] for slot in slots for chain in chains]

    early = tuple(range(size - 1))
    part = call(
        functools.partial(encode_kernel, early, False),
        [shape((rows, lat), F32)],
        2 * unit * len(early),
        [starts] + both_chains(inputs, early) + [weight, enc_bias],
    )[0]
    preact, codes = call(
        functools.partial(encode_kernel, (far,), True),
        [shape((rows, lat), F32), shape((rows, lat), BF16)],
        2 * unit,
        [starts] + both_chains(inputs, (far,)) + [weight, part],
    )
    earlier = passed_along(codes, "layer", 1)

    def spread(chain, slots, dtype, turned):
        return call(
            functools.partial(spread_kernel, chain, slots),
            [shape((half, wide), dtype) for _ in slots] + ([shape((2 * lat, half), BF16)] if turned else []),
            2 * unit * len(slots),
            [starts, codes, earlier, stacked],
        )

    first = [(far, slot_p[reach - 1]), (far, slot_q[reach - 1])] if reach > 1 else [(far,), (far,)]
    partial, both_t = [], []
    ahead, behind = [None, None], [None, None]
    for chain in chains:
        rest = tuple(slot for slot in range(size) if slot not in first[chain])
        instant = dict(zip(first[chain], spread(chain, first[chain], BF16, False)))
        *pieces, turned_codes = spread(chain, rest, F32, True)
        partial.append({**dict(zip(rest, pieces)), **instant})
        both_t.append(turned_codes)
    ahead[0], behind[1] = hop(partial[0][far], 1), hop(partial[1][far], -1)
    for s in range(reach - 1, 0, -1):
        for chain in chains:
            plus, minus = partial[chain][slot_q[s]], partial[chain][slot_p[s]]
            if ahead[chain] is not None:
                plus = (plus + ahead[chain].astype(F32)).astype(BF16)
            if behind[chain] is not None:
                minus = (minus + behind[chain].astype(F32)).astype(BF16)
            ahead[chain] = hop(plus, 1)
            behind[chain] = hop(minus, -1)
    errors = []
    for chain, wanted in zip(chains, halves(targets[0])):
        total = partial[chain][0]
        for arrived in (ahead[chain], behind[chain]):
            if arrived is not None:
                total = total + arrived.astype(F32)
        if chain == 1:
            wanted = after(wanted, errors[0][0])
        errors.append([((total - wanted.astype(F32)) * err_scale).astype(BF16)] + [None] * (size - 1))

    def back(slots, before):
        return call(
            functools.partial(back_kernel, slots, before is None),
            [shape((len(slots), 2 * lat, wide), F32), shape((2, half, 2 * lat), F32)],
            4 * unit * len(slots),
            [starts] + both_chains(errors, slots) + [stacked] + both_t + ([] if before is None else [before]),
        )

    groups, outers, acc, pending = [], [], None, [0]
    for s in range(1, reach + 1):
        gather_step(errors, s)
        if s < reach:
            pending += [slot_p[s], slot_q[s]]
        if s == 1 or s == reach - 1:
            groups.append(tuple(pending))
            outer, acc = back(groups[-1], acc)
            outers.append(outer)
            pending = []
    last_same, back_own, sent, high = call(
        functools.partial(last_back_kernel, groups, far),
        [
            shape((lat, wide), F32),
            shape((rows, lat), F32),
            shape((rows + half_width, lat), F32),
            shape((half_width, lat), F32),
        ],
        4 * unit,
        [starts] + both_chains(errors, (far,)) + [stacked] + both_t + outers + [acc],
    )
    returned = passed_along(sent, "layer", -1)
    turned = call(turn_kernel, [shape((deep, rows), BF16)], unit, [starts] + both_chains(inputs, range(size)))[0]
    height = deep // PIECES
    grad_enc, grad_bias, grad_same, grad_cross = call(
        functools.partial(finish_kernel, groups, far),
        [
            shape((1, deep, lat), F32),
            shape((1, lat), F32),
            shape((1, lat, deep), F32),
            shape((lat, half_width), F32),
        ],
        2 * unit * size,
        [starts, turned, preact, back_own, returned, high, last_same] + outers,
        out_spaces=[pl.ANY, pltpu.VMEM, pl.ANY, pl.ANY],
        scratch=[
            pltpu.VMEM((PIECES, height, lat), F32),
            pltpu.SemaphoreType.DMA((PIECES,)),
            pltpu.SemaphoreType.DMA((size,)),
            pltpu.SemaphoreType.DMA((half_width // lat,)),
        ],
    )
    return (grad_enc, grad_bias, grad_same, grad_cross)


def wide_shards(residual_in, targets, enc_weight, enc_bias, dec_same, dec_cross):
    is_first = lax.axis_index("layer") == 0
    err_scale = 1.0 / math.sqrt(residual_in.shape[1])
    inputs = lax.all_gather(residual_in[0], "latent", axis=1, tiled=True)
    preact = matmul(inputs, enc_weight[0]) + enc_bias[0]
    codes_now = jnp.maximum(preact, 0.0).astype(BF16)
    earlier = passed_along(codes_now, "layer", 1)
    cross_full = lax.all_gather(dec_cross, "layer", axis=1, tiled=True)
    own_dec = dec_same[0]
    half_width = own_dec.shape[1] // 2
    recon_full = lax.psum(matmul(codes_now, own_dec) + matmul(earlier, cross_full), "latent")
    wanted = lax.all_gather(targets[0], "latent", axis=1, tiled=True)
    errors = ((recon_full - wanted.astype(F32)) * err_scale).astype(BF16)
    grad_same = matmul(codes_now, errors, OVER_ROWS)
    grad_full = matmul(earlier, errors, OVER_ROWS)
    returned = passed_along(grad_full[:, :half_width], "layer", -1)
    grad_cross = jnp.where(is_first, returned, grad_full[:, half_width:])
    from_next = passed_along(matmul(errors, cross_full, OVER_COLS), "layer", -1)
    grad_codes = matmul(errors, own_dec, OVER_COLS) + from_next
    grad_pre = jnp.where(preact > 0, grad_codes, 0.0).astype(BF16)
    grad_enc = matmul(inputs, grad_pre, OVER_ROWS)
    grad_bias = jnp.sum(grad_pre.astype(F32), axis=0)
    return (grad_enc[None], grad_bias[None], grad_same[None], grad_cross)


def solution(mesh):
    size = mesh.shape["latent"]
    placed = (
        P("layer", "groups", "latent"),
        P("layer", "groups", "latent"),
        P("layer", None, "latent"),
        P("layer", "latent"),
        P("layer", "latent", None),
        P("latent", "layer"),
    )
    return jax.shard_map(
        ring_shards if size % 2 == 0 and size <= RING_LIMIT else wide_shards,
        mesh=mesh,
        in_specs=placed,
        out_specs=(
            P(("groups", "layer"), None, "latent"),
            P(("groups", "layer"), "latent"),
            P(("groups", "layer"), "latent", None),
            P(("groups", "latent"), "layer"),
        ),
        check_vma=False,
    )
```

```python
import functools
import math

import jax
import jax.numpy as jnp
from jax import lax
from jax.experimental import pallas as pl
from jax.experimental.pallas import tpu as pltpu
from jax.sharding import PartitionSpec as P

F32 = jnp.float32
BF16 = jnp.bfloat16
OVER_ROWS = (((0,), (0,)), ((), ()))
OVER_COLS = (((1,), (1,)), ((), ()))
RING_LIMIT = 16
VMEM_BYTES = 24 * 1024 * 1024
PIECES = 8


def passed_along(shard, axis, by):
    size = lax.axis_size(axis)
    pairs = [(i, i + by) for i in range(size) if 0 <= i + by < size]
    return lax.ppermute(shard, axis, pairs)


def matmul(a, b, dims=(((1,), (0,)), ((), ()))):
    return lax.dot_general(a, b, dims, preferred_element_type=F32)


def ring_order(size):
    return [2 * p if p < size // 2 else 2 * (size - 1 - p) + 1 for p in range(size)]


def ring_member(place, size):
    place = lax.rem(place + 2 * size, size)
    return jnp.where(place < size // 2, 2 * place, 2 * (size - 1 - place) + 1)


def ring_place(member, size):
    return jnp.where(member % 2 == 0, member // 2, size - 1 - member // 2)


def hop(shard, way):
    size = lax.axis_size("latent")
    order = ring_order(size)
    return lax.ppermute(shard, "latent", [(order[p], order[(p + way) % size]) for p in range(size)])


def after(value, *others):
    return lax.optimization_barrier((value,) + others)[0]


def call(kernel, outs, flops, operands, spaces=None, out_spaces=None, scratch=(), aliases=None):
    def spec(space):
        return pl.BlockSpec(memory_space=space)

    spaces = spaces or [pltpu.VMEM] * (len(operands) - 1)
    out_spaces = out_spaces or [pltpu.VMEM] * len(outs)
    return pl.pallas_call(
        kernel,
        out_shape=outs,
        in_specs=[spec(pltpu.SMEM)] + [spec(space) for space in spaces],
        out_specs=[spec(space) for space in out_spaces],
        scratch_shapes=list(scratch),
        input_output_aliases=aliases or {},
        compiler_params=pltpu.CompilerParams(vmem_limit_bytes=VMEM_BYTES),
        cost_estimate=pl.CostEstimate(flops=flops, bytes_accessed=1024, transcendentals=0),
    )(*operands)


def block_of(starts, slot, wide):
    return pl.ds(pl.multiple_of(starts[slot], wide), wide)


def encode_kernel(slots, last, starts, *refs):
    count = 2 * len(slots)
    shards, (weight, before, *outs) = refs[:count], refs[count:]
    rows, wide = shards[0].shape
    for chain in range(2):
        at = slice(chain * rows, (chain + 1) * rows)
        total = before[at, :] if last else jnp.broadcast_to(before[...], (rows, before.shape[1]))
        for i, slot in enumerate(slots):
            block = weight[0, block_of(starts, slot, wide), :]
            total = total + jnp.dot(shards[2 * i + chain][...], block, preferred_element_type=F32)
        outs[0][at, :] = total
        if last:
            outs[1][at, :] = jnp.maximum(total, 0.0).astype(BF16)


def turn_kernel(starts, *refs):
    *shards, turned = refs
    rows, wide = shards[0].shape
    for k in range(len(shards) // 2):
        at = block_of(starts, k, wide)
        for chain in range(2):
            turned[at, chain * rows:(chain + 1) * rows] = shards[2 * k + chain][...].T


def spread_kernel(slots, starts, codes, earlier, stacked, *outs):
    rows = codes.shape[0] // 2
    outs = list(outs)
    for chain in range(2):
        at = slice(chain * rows, (chain + 1) * rows)
        both = jnp.concatenate([codes[at, :], earlier[at, :]], axis=1)
        for slot in slots:
            partial = outs.pop(0)
            block = stacked[:, block_of(starts, slot, partial.shape[1])]
            partial[...] = jnp.dot(both, block, preferred_element_type=F32).astype(partial.dtype)
        if len(outs) > (1 - chain) * len(slots):
            outs.pop(0)[...] = both.T


def back_products(slots, starts, shards, stacked, both_t, before):
    wide = shards[0].shape[1]
    blocks, totals = [], [None, None] if before is None else [before[0], before[1]]
    for i, slot in enumerate(slots):
        decoder = stacked[:, block_of(starts, slot, wide)]
        block = 0.0
        for chain in range(2):
            error = shards[2 * i + chain][...]
            block = block + jnp.dot(both_t[chain][...], error, preferred_element_type=F32)
            term = lax.dot_general(error, decoder, OVER_COLS, preferred_element_type=F32)
            totals[chain] = term if totals[chain] is None else totals[chain] + term
        blocks.append(block)
    return blocks, totals


def back_kernel(slots, first, starts, *refs):
    count = 2 * len(slots)
    shards, (stacked, *both_t), (*before, outer, back) = refs[:count], refs[count:count + 3], refs[count + 3:]
    blocks, totals = back_products(slots, starts, shards, stacked, both_t, None if first else before[0])
    for i, block in enumerate(blocks):
        outer[i] = block
    for chain in range(2):
        back[chain] = totals[chain]


def last_back_kernel(slots, far, starts, *refs):
    near_refs, (before, same, back_own, sent, high) = refs[:-5], refs[-5:]
    shards, (stacked, *both_t), outers = near_refs[:2], near_refs[2:5], near_refs[5:]
    (block,), totals = back_products((far,), starts, shards, stacked, both_t, before)
    rows, wide = shards[0].shape
    lat = high.shape[1]
    half_width = high.shape[0]
    for chain in range(2):
        back_own[chain * rows:(chain + 1) * rows, :] = totals[chain][:, :lat]
        sent[chain * rows:(chain + 1) * rows, :] = totals[chain][:, lat:]
    same[...] = block[:lat]
    pieces = [(far, block[lat:])]
    for group, outer in zip(slots, outers):
        pieces += [(slot, outer[i, lat:]) for i, slot in enumerate(group)]
    for slot, piece in pieces:
        start = pl.multiple_of(starts[slot], wide)

        @pl.when(start < half_width)
        def _():
            for c in range(0, wide, lat):
                sent[pl.ds(2 * rows + start + c, lat), :] = piece[:, c:c + lat]

        @pl.when(start >= half_width)
        def _():
            for c in range(0, wide, lat):
                high[pl.ds(start - half_width + c, lat), :] = piece[:, c:c + lat]


def finish_kernel(slots, far, starts, *refs):
    turned, preact, back_own, arrived, high, last_same, *outers = refs[:6 + len(slots)]
    grad, bias, same, cross, stage, grad_sems, same_sems, cross_sems = refs[6 + len(slots):]
    pieces, height, lat = stage.shape
    rows = preact.shape[0]
    half_width = high.shape[0]
    wide = last_same.shape[1]
    copies = []
    blocks = [(far, last_same)]
    for group, outer in zip(slots, outers):
        blocks += [(slot, outer.at[i, :lat, :]) for i, slot in enumerate(group)]
    for i, (slot, block) in enumerate(blocks):
        copies.append(pltpu.make_async_copy(block, same.at[0, :, block_of(starts, slot, wide)], same_sems.at[i]))
        copies[-1].start()
    first = starts[starts.shape[0] - 1] == 0
    for c in range(half_width // lat):
        at = pl.ds(c * lat, lat)

        @pl.when(first)
        def _():
            source = arrived.at[pl.ds(rows + c * lat, lat), :]
            pltpu.make_async_copy(source, cross.at[:, at], cross_sems.at[c]).start()

        @pl.when(jnp.logical_not(first))
        def _():
            pltpu.make_async_copy(high.at[at, :], cross.at[:, at], cross_sems.at[c]).start()

        copies.append(pltpu.make_async_copy(high.at[at, :], cross.at[:, at], cross_sems.at[c]))
    value = jnp.where(preact[...] > 0, back_own[...] + arrived[:rows, :], 0.0).astype(BF16)
    for i in range(pieces):
        at = pl.ds(i * height, height)
        stage[i] = jnp.dot(turned[at, :], value, preferred_element_type=F32)
        copies.append(pltpu.make_async_copy(stage.at[i], grad.at[0, at, :], grad_sems.at[i]))
        copies[-1].start()
    bias[...] = jnp.sum(value.astype(F32), axis=0, keepdims=True)
    for copy in copies:
        copy.wait()


def ring_shards(residual_in, targets, enc_weight, enc_bias, dec_same, dec_cross):
    size = lax.axis_size("latent")
    reach = size // 2
    place = ring_place(lax.axis_index("latent"), size)
    layer = lax.axis_index("layer")
    rows, wide = residual_in.shape[1:]
    half = rows // 2
    deep, lat = enc_weight.shape[1:]
    half_width = deep // 2
    err_scale = 1.0 / math.sqrt(rows)
    shape = jax.ShapeDtypeStruct
    unit = rows * wide * lat
    chains = (0, 1)

    def halves(array):
        return [array[:half], array[half:]]

    slot_p = {s: 2 * s - 1 for s in range(1, reach)}
    slot_q = {s: 2 * s for s in range(1, reach)}
    far = size - 1
    offsets = [0] * size
    offsets[far] = reach
    for s in range(1, reach):
        offsets[slot_p[s]] = -s
        offsets[slot_q[s]] = s
    starts = jnp.stack([ring_member(place + offset, size) * wide for offset in offsets] + [layer])
    starts = starts.astype(jnp.int32)

    def gather_step(found, s, ready=None):
        for chain in chains:
            at_p, at_q = (0, 0) if s == 1 else (slot_p[s - 1], slot_q[s - 1])
            if s < reach:
                ahead, behind = found[chain][at_p], found[chain][at_q]
                if ready is not None:
                    ahead, behind = (after(ahead, ready), behind) if chain else (ahead, after(behind, ready))
                found[chain][slot_p[s]], found[chain][slot_q[s]] = hop(ahead, 1), hop(behind, -1)
            else:
                found[chain][far] = hop(found[chain][at_q if chain else at_p], -1 if chain else 1)

    inputs = [[part] + [None] * (size - 1) for part in halves(residual_in[0])]
    low_cross = passed_along(after(dec_cross, inputs[0][0]), "layer", 1)
    stacked = jnp.concatenate([dec_same[0], jnp.concatenate([low_cross, dec_cross], axis=1)], axis=0)
    for s in range(1, reach + 1):
        if s == reach and reach > 1:
            inputs[0][slot_p[s - 1]] = after(inputs[0][slot_p[s - 1]], stacked)
        gather_step(inputs, s, low_cross if s == 1 else None)

    def both_chains(found, slots):
        return [found[chain][slot] for slot in slots for chain in chains]

    early = tuple(range(size - 1))
    part = call(
        functools.partial(encode_kernel, early, False),
        [shape((rows, lat), F32)],
        2 * unit * len(early),
        [starts] + both_chains(inputs, early) + [enc_weight, enc_bias],
    )[0]
    preact, codes = call(
        functools.partial(encode_kernel, (far,), True),
        [shape((rows, lat), F32), shape((rows, lat), BF16)],
        2 * unit,
        [starts] + both_chains(inputs, (far,)) + [enc_weight, part],
    )
    earlier = passed_along(codes, "layer", 1)

    def spread(slots, dtypes, turned):
        outs = []
        for chain in chains:
            outs += [shape((half, wide), dtypes[chain].get(slot, F32)) for slot in slots]
            outs += [shape((2 * lat, half), BF16)] if turned else []
        found = call(
            functools.partial(spread_kernel, slots), outs, 4 * unit * len(slots), [starts, codes, earlier, stacked]
        )
        return found[:len(outs) // 2], found[len(outs) // 2:]

    rest = tuple(slot for slot in range(size) if slot != far)
    instant = ({far: BF16, slot_p.get(reach - 1): BF16}, {far: BF16, slot_q.get(reach - 1): BF16})
    far_0, far_1 = spread((far,), instant, False)
    ahead, behind = [hop(far_0[0], 1), None], [None, hop(far_1[0], -1)]
    partial, both_t = [], []
    for pieces in spread(rest, instant, True):
        partial.append(dict(zip(rest, pieces)))
        both_t.append(pieces[-1])
    for s in range(reach - 1, 0, -1):
        for chain in chains:
            plus, minus = partial[chain][slot_q[s]], partial[chain][slot_p[s]]
            if ahead[chain] is not None:
                plus = (plus + ahead[chain].astype(F32)).astype(BF16)
            if behind[chain] is not None:
                minus = (minus + behind[chain].astype(F32)).astype(BF16)
            ahead[chain] = hop(plus, 1)
            behind[chain] = hop(minus, -1)
    errors = []
    for chain, wanted in zip(chains, halves(targets[0])):
        total = partial[chain][0]
        for arrived in (ahead[chain], behind[chain]):
            if arrived is not None:
                total = total + arrived.astype(F32)
        if chain == 1:
            wanted = after(wanted, errors[0][0])
        errors.append([((total - wanted.astype(F32)) * err_scale).astype(BF16)] + [None] * (size - 1))

    def back(slots, before):
        return call(
            functools.partial(back_kernel, slots, before is None),
            [shape((len(slots), 2 * lat, wide), F32), shape((2, half, 2 * lat), F32)],
            4 * unit * len(slots),
            [starts] + both_chains(errors, slots) + [stacked] + both_t + ([] if before is None else [before]),
        )

    groups, outers, acc, pending = [], [], None, [0]
    for s in range(1, reach + 1):
        gather_step(errors, s)
        if s < reach:
            pending += [slot_p[s], slot_q[s]]
        if s == 1 or s == reach - 1:
            groups.append(tuple(pending))
            outer, acc = back(groups[-1], acc)
            outers.append(outer)
            pending = []
    last_same, back_own, sent, high = call(
        functools.partial(last_back_kernel, groups, far),
        [
            shape((lat, wide), F32),
            shape((rows, lat), F32),
            shape((rows + half_width, lat), F32),
            shape((half_width, lat), F32),
        ],
        4 * unit,
        [starts] + both_chains(errors, (far,)) + [stacked] + both_t + outers + [acc],
    )
    returned = passed_along(sent, "layer", -1)
    turned = call(turn_kernel, [shape((deep, rows), BF16)], unit, [starts] + both_chains(inputs, range(size)))[0]
    height = deep // PIECES
    grad_enc, grad_bias, grad_same, grad_cross = call(
        functools.partial(finish_kernel, groups, far),
        [
            shape((1, deep, lat), F32),
            shape((1, lat), F32),
            shape((1, lat, deep), F32),
            shape((lat, half_width), F32),
        ],
        2 * unit * size,
        [starts, turned, preact, back_own, returned, high, last_same] + outers,
        out_spaces=[pl.ANY, pltpu.VMEM, pl.ANY, pl.ANY],
        scratch=[
            pltpu.VMEM((PIECES, height, lat), F32),
            pltpu.SemaphoreType.DMA((PIECES,)),
            pltpu.SemaphoreType.DMA((size,)),
            pltpu.SemaphoreType.DMA((half_width // lat,)),
        ],
    )
    return (grad_enc, grad_bias, grad_same, grad_cross)


def wide_shards(residual_in, targets, enc_weight, enc_bias, dec_same, dec_cross):
    is_first = lax.axis_index("layer") == 0
    err_scale = 1.0 / math.sqrt(residual_in.shape[1])
    inputs = lax.all_gather(residual_in[0], "latent", axis=1, tiled=True)
    preact = matmul(inputs, enc_weight[0]) + enc_bias[0]
    codes_now = jnp.maximum(preact, 0.0).astype(BF16)
    earlier = passed_along(codes_now, "layer", 1)
    cross_full = lax.all_gather(dec_cross, "layer", axis=1, tiled=True)
    own_dec = dec_same[0]
    half_width = own_dec.shape[1] // 2
    recon_full = lax.psum(matmul(codes_now, own_dec) + matmul(earlier, cross_full), "latent")
    wanted = lax.all_gather(targets[0], "latent", axis=1, tiled=True)
    errors = ((recon_full - wanted.astype(F32)) * err_scale).astype(BF16)
    grad_same = matmul(codes_now, errors, OVER_ROWS)
    grad_full = matmul(earlier, errors, OVER_ROWS)
    returned = passed_along(grad_full[:, :half_width], "layer", -1)
    grad_cross = jnp.where(is_first, returned, grad_full[:, half_width:])
    from_next = passed_along(matmul(errors, cross_full, OVER_COLS), "layer", -1)
    grad_codes = matmul(errors, own_dec, OVER_COLS) + from_next
    grad_pre = jnp.where(preact > 0, grad_codes, 0.0).astype(BF16)
    grad_enc = matmul(inputs, grad_pre, OVER_ROWS)
    grad_bias = jnp.sum(grad_pre.astype(F32), axis=0)
    return (grad_enc[None], grad_bias[None], grad_same[None], grad_cross)


def solution(mesh):
    size = mesh.shape["latent"]
    placed = (
        P("layer", "groups", "latent"),
        P("layer", "groups", "latent"),
        P("layer", None, "latent"),
        P("layer", "latent"),
        P("layer", "latent", None),
        P("latent", "layer"),
    )
    return jax.shard_map(
        ring_shards if size % 2 == 0 and size <= RING_LIMIT else wide_shards,
        mesh=mesh,
        in_specs=placed,
        out_specs=(
            P(("groups", "layer"), None, "latent"),
            P(("groups", "layer"), "latent"),
            P(("groups", "layer"), "latent", None),
            P(("groups", "latent"), "layer"),
        ),
        check_vma=False,
    )
```

```python
import functools
import math

import jax
import jax.numpy as jnp
from jax import lax
from jax.experimental import pallas as pl
from jax.experimental.pallas import tpu as pltpu
from jax.sharding import PartitionSpec as P

F32 = jnp.float32
BF16 = jnp.bfloat16
OVER_ROWS = (((0,), (0,)), ((), ()))
OVER_COLS = (((1,), (1,)), ((), ()))
RING_LIMIT = 16
VMEM_BYTES = 24 * 1024 * 1024
PIECES = 8


def passed_along(shard, axis, by):
    size = lax.axis_size(axis)
    pairs = [(i, i + by) for i in range(size) if 0 <= i + by < size]
    return lax.ppermute(shard, axis, pairs)


def matmul(a, b, dims=(((1,), (0,)), ((), ()))):
    return lax.dot_general(a, b, dims, preferred_element_type=F32)


def ring_order(size):
    return [2 * p if p < size // 2 else 2 * (size - 1 - p) + 1 for p in range(size)]


def ring_member(place, size):
    place = lax.rem(place + 2 * size, size)
    return jnp.where(place < size // 2, 2 * place, 2 * (size - 1 - place) + 1)


def ring_place(member, size):
    return jnp.where(member % 2 == 0, member // 2, size - 1 - member // 2)


def hop(shard, way):
    size = lax.axis_size("latent")
    order = ring_order(size)
    return lax.ppermute(shard, "latent", [(order[p], order[(p + way) % size]) for p in range(size)])


def after(value, *others):
    return lax.optimization_barrier((value,) + others)[0]


def call(kernel, outs, flops, operands, spaces=None, out_spaces=None, scratch=(), aliases=None):
    def spec(space):
        return pl.BlockSpec(memory_space=space)

    spaces = spaces or [pltpu.VMEM] * (len(operands) - 1)
    out_spaces = out_spaces or [pltpu.VMEM] * len(outs)
    return pl.pallas_call(
        kernel,
        out_shape=outs,
        in_specs=[spec(pltpu.SMEM)] + [spec(space) for space in spaces],
        out_specs=[spec(space) for space in out_spaces],
        scratch_shapes=list(scratch),
        input_output_aliases=aliases or {},
        compiler_params=pltpu.CompilerParams(vmem_limit_bytes=VMEM_BYTES),
        cost_estimate=pl.CostEstimate(flops=flops, bytes_accessed=1024, transcendentals=0),
    )(*operands)


def block_of(starts, slot, wide):
    return pl.ds(pl.multiple_of(starts[slot], wide), wide)


def encode_kernel(slots, first, last, starts, *refs):
    count = 2 * len(slots)
    shards, (weight, before, *outs) = refs[:count], refs[count:]
    rows, wide = shards[0].shape
    for chain in range(2):
        at = slice(chain * rows, (chain + 1) * rows)
        total = jnp.broadcast_to(before[...], (rows, before.shape[1])) if first else before[at, :]
        for i, slot in enumerate(slots):
            block = weight[0, block_of(starts, slot, wide), :]
            total = total + jnp.dot(shards[2 * i + chain][...], block, preferred_element_type=F32)
        outs[0][at, :] = total
        if last:
            outs[1][at, :] = jnp.maximum(total, 0.0).astype(BF16)


def turn_kernel(starts, *refs):
    *shards, turned = refs
    rows, wide = shards[0].shape
    for k in range(len(shards) // 2):
        at = block_of(starts, k, wide)
        for chain in range(2):
            turned[at, chain * rows:(chain + 1) * rows] = shards[2 * k + chain][...].T


def spread_kernel(slots, starts, codes, earlier, stacked, *outs):
    rows = codes.shape[0] // 2
    outs = list(outs)
    for chain in range(2):
        at = slice(chain * rows, (chain + 1) * rows)
        both = jnp.concatenate([codes[at, :], earlier[at, :]], axis=1)
        for slot in slots:
            partial = outs.pop(0)
            block = stacked[:, block_of(starts, slot, partial.shape[1])]
            partial[...] = jnp.dot(both, block, preferred_element_type=F32).astype(partial.dtype)
        if len(outs) > (1 - chain) * len(slots):
            outs.pop(0)[...] = both.T


def back_products(slots, starts, shards, stacked, both_t, before):
    wide = shards[0].shape[1]
    blocks, totals = [], [None, None] if before is None else [before[0], before[1]]
    for i, slot in enumerate(slots):
        decoder = stacked[:, block_of(starts, slot, wide)]
        block = 0.0
        for chain in range(2):
            error = shards[2 * i + chain][...]
            block = block + jnp.dot(both_t[chain][...], error, preferred_element_type=F32)
            term = lax.dot_general(error, decoder, OVER_COLS, preferred_element_type=F32)
            totals[chain] = term if totals[chain] is None else totals[chain] + term
        blocks.append(block)
    return blocks, totals


def back_kernel(slots, first, starts, *refs):
    count = 2 * len(slots)
    shards, (stacked, *both_t), (*before, outer, back) = refs[:count], refs[count:count + 3], refs[count + 3:]
    blocks, totals = back_products(slots, starts, shards, stacked, both_t, None if first else before[0])
    for i, block in enumerate(blocks):
        outer[i] = block
    for chain in range(2):
        back[chain] = totals[chain]


def last_back_kernel(slots, far, starts, *refs):
    near_refs, (before, same, back_own, sent, high) = refs[:-5], refs[-5:]
    shards, (stacked, *both_t), outers = near_refs[:2], near_refs[2:5], near_refs[5:]
    (block,), totals = back_products((far,), starts, shards, stacked, both_t, before)
    rows, wide = shards[0].shape
    lat = high.shape[1]
    half_width = high.shape[0]
    for chain in range(2):
        back_own[chain * rows:(chain + 1) * rows, :] = totals[chain][:, :lat]
        sent[chain * rows:(chain + 1) * rows, :] = totals[chain][:, lat:]
    same[...] = block[:lat]
    pieces = [(far, block[lat:])]
    for group, outer in zip(slots, outers):
        pieces += [(slot, outer[i, lat:]) for i, slot in enumerate(group)]
    for slot, piece in pieces:
        start = pl.multiple_of(starts[slot], wide)

        @pl.when(start < half_width)
        def _():
            for c in range(0, wide, lat):
                sent[pl.ds(2 * rows + start + c, lat), :] = piece[:, c:c + lat]

        @pl.when(start >= half_width)
        def _():
            for c in range(0, wide, lat):
                high[pl.ds(start - half_width + c, lat), :] = piece[:, c:c + lat]


def finish_kernel(slots, far, starts, *refs):
    turned, preact, back_own, arrived, high, last_same, *outers = refs[:6 + len(slots)]
    grad, bias, same, cross, stage, grad_sems, same_sems, cross_sems = refs[6 + len(slots):]
    pieces, height, lat = stage.shape
    rows = preact.shape[0]
    half_width = high.shape[0]
    wide = last_same.shape[1]
    copies = []
    blocks = [(far, last_same)]
    for group, outer in zip(slots, outers):
        blocks += [(slot, outer.at[i, :lat, :]) for i, slot in enumerate(group)]
    for i, (slot, block) in enumerate(blocks):
        copies.append(pltpu.make_async_copy(block, same.at[0, :, block_of(starts, slot, wide)], same_sems.at[i]))
        copies[-1].start()
    first = starts[starts.shape[0] - 1] == 0
    for c in range(half_width // lat):
        at = pl.ds(c * lat, lat)

        @pl.when(first)
        def _():
            source = arrived.at[pl.ds(rows + c * lat, lat), :]
            pltpu.make_async_copy(source, cross.at[:, at], cross_sems.at[c]).start()

        @pl.when(jnp.logical_not(first))
        def _():
            pltpu.make_async_copy(high.at[at, :], cross.at[:, at], cross_sems.at[c]).start()

        copies.append(pltpu.make_async_copy(high.at[at, :], cross.at[:, at], cross_sems.at[c]))
    value = jnp.where(preact[...] > 0, back_own[...] + arrived[:rows, :], 0.0).astype(BF16)
    for i in range(pieces):
        at = pl.ds(i * height, height)
        stage[i] = jnp.dot(turned[at, :], value, preferred_element_type=F32)
        copies.append(pltpu.make_async_copy(stage.at[i], grad.at[0, at, :], grad_sems.at[i]))
        copies[-1].start()
    bias[...] = jnp.sum(value.astype(F32), axis=0, keepdims=True)
    for copy in copies:
        copy.wait()


def ring_shards(residual_in, targets, enc_weight, enc_bias, dec_same, dec_cross):
    size = lax.axis_size("latent")
    reach = size // 2
    place = ring_place(lax.axis_index("latent"), size)
    layer = lax.axis_index("layer")
    rows, wide = residual_in.shape[1:]
    half = rows // 2
    deep, lat = enc_weight.shape[1:]
    half_width = deep // 2
    err_scale = 1.0 / math.sqrt(rows)
    shape = jax.ShapeDtypeStruct
    unit = rows * wide * lat
    chains = (0, 1)

    def halves(array):
        return [array[:half], array[half:]]

    slot_p = {s: 2 * s - 1 for s in range(1, reach)}
    slot_q = {s: 2 * s for s in range(1, reach)}
    far = size - 1
    offsets = [0] * size
    offsets[far] = reach
    for s in range(1, reach):
        offsets[slot_p[s]] = -s
        offsets[slot_q[s]] = s
    starts = jnp.stack([ring_member(place + offset, size) * wide for offset in offsets] + [layer])
    starts = starts.astype(jnp.int32)

    urgent, later = ((0, 1), (1, -1)), ((0, -1), (1, 1))

    def gather_step(found, s, ready=None):
        for chain, way in urgent + later if s < reach else urgent:
            slots = slot_p if way == 1 else slot_q
            shard = found[chain][slots[s - 1] if s > 1 else 0]
            if ready is not None and (chain, way) in later:
                shard = after(shard, ready)
            found[chain][slots[s] if s < reach else far] = hop(shard, way)

    def both_chains(found, slots):
        return [found[chain][slot] for slot in slots for chain in chains]

    def encode(slots, before):
        first, last = slots[0] == 0, slots[-1] == far
        return call(
            functools.partial(encode_kernel, slots, first, last),
            [shape((rows, lat), F32)] + ([shape((rows, lat), BF16)] if last else []),
            2 * unit * len(slots),
            [starts] + both_chains(inputs, slots) + [enc_weight, before],
        )

    front = residual_in[0, :half]
    inputs = [[front] + [None] * (size - 1), [after(residual_in, front)[0, half:]] + [None] * (size - 1)]
    part = encode((0,), enc_bias)[0]
    for s in range(1, reach + 1):
        gather_step(inputs, s, part if s == 1 else None)
    low_cross = passed_along(after(dec_cross, inputs[0][slot_p.get(1, far)]), "layer", 1)
    stacked = jnp.concatenate([dec_same[0], jnp.concatenate([low_cross, dec_cross], axis=1)], axis=0)
    if size > 2:
        part = encode(tuple(range(1, far)), after(part, stacked))[0]
    preact, codes = encode((far,), part)
    earlier = passed_along(codes, "layer", 1)

    def spread(slots, dtypes, turned):
        outs = []
        for chain in chains:
            outs += [shape((half, wide), dtypes[chain].get(slot, F32)) for slot in slots]
            outs += [shape((2 * lat, half), BF16)] if turned else []
        found = call(
            functools.partial(spread_kernel, slots), outs, 4 * unit * len(slots), [starts, codes, earlier, stacked]
        )
        return found[:len(outs) // 2], found[len(outs) // 2:]

    rest = tuple(slot for slot in range(size) if slot != far)
    instant = ({far: BF16, slot_p.get(reach - 1): BF16}, {far: BF16, slot_q.get(reach - 1): BF16})
    far_0, far_1 = spread((far,), instant, False)
    moving = {(0, 1): hop(far_0[0], 1), (1, -1): hop(far_1[0], -1)}
    partial, both_t = [], []
    for pieces in spread(rest, instant, True):
        partial.append(dict(zip(rest, pieces)))
        both_t.append(pieces[-1])
    before = []
    for s in range(reach - 1, 0, -1):
        landed = [moving[loop] for loop in urgent]
        for chain, way in urgent + later:
            message = partial[chain][slot_q[s] if way == 1 else slot_p[s]]
            if (chain, way) in moving:
                message = (message + moving[chain, way].astype(F32)).astype(BF16)
            if (chain, way) in later and before:
                message = after(message, *before)
            moving[chain, way] = hop(message, way)
        before = landed
    errors = []
    for chain, wanted in zip(chains, halves(targets[0])):
        total = partial[chain][0]
        for way in (1, -1):
            if (chain, way) in moving:
                total = total + moving[chain, way].astype(F32)
        if chain == 1:
            wanted = after(wanted, errors[0][0])
        errors.append([((total - wanted.astype(F32)) * err_scale).astype(BF16)] + [None] * (size - 1))

    def back(slots, before):
        return call(
            functools.partial(back_kernel, slots, before is None),
            [shape((len(slots), 2 * lat, wide), F32), shape((2, half, 2 * lat), F32)],
            4 * unit * len(slots),
            [starts] + both_chains(errors, slots) + [stacked] + both_t + ([] if before is None else [before]),
        )

    groups, outers, acc, pending = [], [], None, [0]
    for s in range(1, reach + 1):
        gather_step(errors, s)
        if s < reach:
            pending += [slot_p[s], slot_q[s]]
        if s == 1 or s == reach - 1:
            groups.append(tuple(pending))
            outer, acc = back(groups[-1], acc)
            outers.append(outer)
            pending = []
    last_same, back_own, sent, high = call(
        functools.partial(last_back_kernel, groups, far),
        [
            shape((lat, wide), F32),
            shape((rows, lat), F32),
            shape((rows + half_width, lat), F32),
            shape((half_width, lat), F32),
        ],
        4 * unit,
        [starts] + both_chains(errors, (far,)) + [stacked] + both_t + outers + [acc],
    )
    returned = passed_along(sent, "layer", -1)
    turned = call(turn_kernel, [shape((deep, rows), BF16)], unit, [starts] + both_chains(inputs, range(size)))[0]
    height = deep // PIECES
    grad_enc, grad_bias, grad_same, grad_cross = call(
        functools.partial(finish_kernel, groups, far),
        [
            shape((1, deep, lat), F32),
            shape((1, lat), F32),
            shape((1, lat, deep), F32),
            shape((lat, half_width), F32),
        ],
        2 * unit * size,
        [starts, turned, preact, back_own, returned, high, last_same] + outers,
        out_spaces=[pl.ANY, pltpu.VMEM, pl.ANY, pl.ANY],
        scratch=[
            pltpu.VMEM((PIECES, height, lat), F32),
            pltpu.SemaphoreType.DMA((PIECES,)),
            pltpu.SemaphoreType.DMA((size,)),
            pltpu.SemaphoreType.DMA((half_width // lat,)),
        ],
    )
    return (grad_enc, grad_bias, grad_same, grad_cross)


def wide_shards(residual_in, targets, enc_weight, enc_bias, dec_same, dec_cross):
    is_first = lax.axis_index("layer") == 0
    err_scale = 1.0 / math.sqrt(residual_in.shape[1])
    inputs = lax.all_gather(residual_in[0], "latent", axis=1, tiled=True)
    preact = matmul(inputs, enc_weight[0]) + enc_bias[0]
    codes_now = jnp.maximum(preact, 0.0).astype(BF16)
    earlier = passed_along(codes_now, "layer", 1)
    cross_full = lax.all_gather(dec_cross, "layer", axis=1, tiled=True)
    own_dec = dec_same[0]
    half_width = own_dec.shape[1] // 2
    recon_full = lax.psum(matmul(codes_now, own_dec) + matmul(earlier, cross_full), "latent")
    wanted = lax.all_gather(targets[0], "latent", axis=1, tiled=True)
    errors = ((recon_full - wanted.astype(F32)) * err_scale).astype(BF16)
    grad_same = matmul(codes_now, errors, OVER_ROWS)
    grad_full = matmul(earlier, errors, OVER_ROWS)
    returned = passed_along(grad_full[:, :half_width], "layer", -1)
    grad_cross = jnp.where(is_first, returned, grad_full[:, half_width:])
    from_next = passed_along(matmul(errors, cross_full, OVER_COLS), "layer", -1)
    grad_codes = matmul(errors, own_dec, OVER_COLS) + from_next
    grad_pre = jnp.where(preact > 0, grad_codes, 0.0).astype(BF16)
    grad_enc = matmul(inputs, grad_pre, OVER_ROWS)
    grad_bias = jnp.sum(grad_pre.astype(F32), axis=0)
    return (grad_enc[None], grad_bias[None], grad_same[None], grad_cross)


def solution(mesh):
    size = mesh.shape["latent"]
    placed = (
        P("layer", "groups", "latent"),
        P("layer", "groups", "latent"),
        P("layer", None, "latent"),
        P("layer", "latent"),
        P("layer", "latent", None),
        P("latent", "layer"),
    )
    return jax.shard_map(
        ring_shards if size % 2 == 0 and size <= RING_LIMIT else wide_shards,
        mesh=mesh,
        in_specs=placed,
        out_specs=(
            P(("groups", "layer"), None, "latent"),
            P(("groups", "layer"), "latent"),
            P(("groups", "layer"), "latent", None),
            P(("groups", "latent"), "layer"),
        ),
        check_vma=False,
    )
```

```python
import functools
import math

import jax
import jax.numpy as jnp
from jax import lax
from jax.experimental import pallas as pl
from jax.experimental.pallas import tpu as pltpu
from jax.sharding import PartitionSpec as P

F32 = jnp.float32
BF16 = jnp.bfloat16
OVER_ROWS = (((0,), (0,)), ((), ()))
OVER_COLS = (((1,), (1,)), ((), ()))
RING_LIMIT = 16
VMEM_BYTES = 24 * 1024 * 1024
PIECES = 8


def passed_along(shard, axis, by):
    size = lax.axis_size(axis)
    pairs = [(i, i + by) for i in range(size) if 0 <= i + by < size]
    return lax.ppermute(shard, axis, pairs)


def matmul(a, b, dims=(((1,), (0,)), ((), ()))):
    return lax.dot_general(a, b, dims, preferred_element_type=F32)


def ring_order(size):
    return [2 * p if p < size // 2 else 2 * (size - 1 - p) + 1 for p in range(size)]


def ring_member(place, size):
    place = lax.rem(place + 2 * size, size)
    return jnp.where(place < size // 2, 2 * place, 2 * (size - 1 - place) + 1)


def ring_place(member, size):
    return jnp.where(member % 2 == 0, member // 2, size - 1 - member // 2)


def hop(shard, way):
    size = lax.axis_size("latent")
    order = ring_order(size)
    return lax.ppermute(shard, "latent", [(order[p], order[(p + way) % size]) for p in range(size)])


def after(value, *others):
    return lax.optimization_barrier((value,) + others)[0]


def call(kernel, outs, flops, operands, spaces=None, out_spaces=None, scratch=(), aliases=None):
    def spec(space):
        return pl.BlockSpec(memory_space=space)

    spaces = spaces or [pltpu.VMEM] * (len(operands) - 1)
    out_spaces = out_spaces or [pltpu.VMEM] * len(outs)
    return pl.pallas_call(
        kernel,
        out_shape=outs,
        in_specs=[spec(pltpu.SMEM)] + [spec(space) for space in spaces],
        out_specs=[spec(space) for space in out_spaces],
        scratch_shapes=list(scratch),
        input_output_aliases=aliases or {},
        compiler_params=pltpu.CompilerParams(vmem_limit_bytes=VMEM_BYTES),
        cost_estimate=pl.CostEstimate(flops=flops, bytes_accessed=1024, transcendentals=0),
    )(*operands)


def block_of(starts, slot, wide):
    return pl.ds(pl.multiple_of(starts[slot], wide), wide)


def encode_kernel(slots, first, last, starts, *refs):
    count = 2 * len(slots)
    shards, (weight, before, *outs) = refs[:count], refs[count:]
    rows, wide = shards[0].shape
    for chain in range(2):
        at = slice(chain * rows, (chain + 1) * rows)
        total = jnp.broadcast_to(before[...], (rows, before.shape[1])) if first else before[at, :]
        for i, slot in enumerate(slots):
            block = weight[0, block_of(starts, slot, wide), :]
            total = total + jnp.dot(shards[2 * i + chain][...], block, preferred_element_type=F32)
        outs[0][at, :] = total
        if last:
            outs[1][at, :] = jnp.maximum(total, 0.0).astype(BF16)


def turn_own_kernel(starts, *refs):
    *shards, turned = refs
    rows = shards[0].shape[0]
    for chain, shard in enumerate(shards):
        turned[:, chain * rows:(chain + 1) * rows] = shard[...].T


def turn_kernel(starts, own, *refs):
    *shards, turned = refs
    rows, wide = shards[0].shape
    turned[block_of(starts, 0, wide), :] = own[...]
    for k in range(len(shards) // 2):
        at = block_of(starts, k + 1, wide)
        for chain in range(2):
            turned[at, chain * rows:(chain + 1) * rows] = shards[2 * k + chain][...].T


def spread_kernel(slots, starts, codes, earlier, stacked, *outs):
    rows = codes.shape[0] // 2
    outs = list(outs)
    for chain in range(2):
        at = slice(chain * rows, (chain + 1) * rows)
        both = jnp.concatenate([codes[at, :], earlier[at, :]], axis=1)
        for slot in slots:
            partial = outs.pop(0)
            block = stacked[:, block_of(starts, slot, partial.shape[1])]
            partial[...] = jnp.dot(both, block, preferred_element_type=F32).astype(partial.dtype)
        if len(outs) > (1 - chain) * len(slots):
            outs.pop(0)[...] = both.T


def back_products(slots, starts, shards, stacked, both_t, before):
    wide = shards[0].shape[1]
    blocks, totals = [], [None, None] if before is None else [before[0], before[1]]
    for i, slot in enumerate(slots):
        decoder = stacked[:, block_of(starts, slot, wide)]
        block = 0.0
        for chain in range(2):
            error = shards[2 * i + chain][...]
            block = block + jnp.dot(both_t[chain][...], error, preferred_element_type=F32)
            term = lax.dot_general(error, decoder, OVER_COLS, preferred_element_type=F32)
            totals[chain] = term if totals[chain] is None else totals[chain] + term
        blocks.append(block)
    return blocks, totals


def back_kernel(slots, first, starts, *refs):
    count = 2 * len(slots)
    shards, (stacked, *both_t), (*before, outer, back) = refs[:count], refs[count:count + 3], refs[count + 3:]
    blocks, totals = back_products(slots, starts, shards, stacked, both_t, None if first else before[0])
    for i, block in enumerate(blocks):
        outer[i] = block
    for chain in range(2):
        back[chain] = totals[chain]


def last_back_kernel(slots, far, starts, *refs):
    near_refs, (before, same, back_own, sent, high) = refs[:-5], refs[-5:]
    shards, (stacked, *both_t), outers = near_refs[:2], near_refs[2:5], near_refs[5:]
    (block,), totals = back_products((far,), starts, shards, stacked, both_t, before)
    rows, wide = shards[0].shape
    lat = high.shape[1]
    half_width = high.shape[0]
    for chain in range(2):
        back_own[chain * rows:(chain + 1) * rows, :] = totals[chain][:, :lat]
        sent[chain * rows:(chain + 1) * rows, :] = totals[chain][:, lat:]
    same[...] = block[:lat]
    pieces = [(far, block[lat:])]
    for group, outer in zip(slots, outers):
        pieces += [(slot, outer[i, lat:]) for i, slot in enumerate(group)]
    for slot, piece in pieces:
        start = pl.multiple_of(starts[slot], wide)

        @pl.when(start < half_width)
        def _():
            for c in range(0, wide, lat):
                sent[pl.ds(2 * rows + start + c, lat), :] = piece[:, c:c + lat]

        @pl.when(start >= half_width)
        def _():
            for c in range(0, wide, lat):
                high[pl.ds(start - half_width + c, lat), :] = piece[:, c:c + lat]


def place_kernel(slots, far, starts, *refs):
    last, *outers, same, sems = refs
    lat, wide = last.shape
    blocks = [(far, last)]
    for group, outer in zip(slots, outers):
        blocks += [(slot, outer.at[i, :lat, :]) for i, slot in enumerate(group)]
    copies = []
    for i, (slot, block) in enumerate(blocks):
        copies.append(pltpu.make_async_copy(block, same.at[0, :, block_of(starts, slot, wide)], sems.at[i]))
        copies[-1].start()
    for copy in copies:
        copy.wait()


def finish_kernel(starts, turned, preact, back_own, arrived, high, grad, bias, cross, stage, grad_sems, cross_sems):
    pieces, height, lat = stage.shape
    rows = preact.shape[0]
    half_width = high.shape[0]
    copies = []
    first = starts[starts.shape[0] - 1] == 0
    for c in range(half_width // lat):
        at = pl.ds(c * lat, lat)

        @pl.when(first)
        def _():
            source = arrived.at[pl.ds(rows + c * lat, lat), :]
            pltpu.make_async_copy(source, cross.at[:, at], cross_sems.at[c]).start()

        @pl.when(jnp.logical_not(first))
        def _():
            pltpu.make_async_copy(high.at[at, :], cross.at[:, at], cross_sems.at[c]).start()

        copies.append(pltpu.make_async_copy(high.at[at, :], cross.at[:, at], cross_sems.at[c]))
    value = jnp.where(preact[...] > 0, back_own[...] + arrived[:rows, :], 0.0).astype(BF16)
    for i in range(pieces):
        at = pl.ds(i * height, height)
        stage[i] = jnp.dot(turned[at, :], value, preferred_element_type=F32)
        copies.append(pltpu.make_async_copy(stage.at[i], grad.at[0, at, :], grad_sems.at[i]))
        copies[-1].start()
    bias[...] = jnp.sum(value.astype(F32), axis=0, keepdims=True)
    for copy in copies:
        copy.wait()


def ring_shards(residual_in, targets, enc_weight, enc_bias, dec_same, dec_cross):
    size = lax.axis_size("latent")
    reach = size // 2
    place = ring_place(lax.axis_index("latent"), size)
    layer = lax.axis_index("layer")
    rows, wide = residual_in.shape[1:]
    half = rows // 2
    deep, lat = enc_weight.shape[1:]
    half_width = deep // 2
    err_scale = 1.0 / math.sqrt(rows)
    shape = jax.ShapeDtypeStruct
    unit = rows * wide * lat
    chains = (0, 1)

    def halves(array):
        return [array[:half], array[half:]]

    slot_p = {s: 2 * s - 1 for s in range(1, reach)}
    slot_q = {s: 2 * s for s in range(1, reach)}
    far = size - 1
    offsets = [0] * size
    offsets[far] = reach
    for s in range(1, reach):
        offsets[slot_p[s]] = -s
        offsets[slot_q[s]] = s
    starts = jnp.stack([ring_member(place + offset, size) * wide for offset in offsets] + [layer])
    starts = starts.astype(jnp.int32)

    urgent, later = ((0, 1), (1, -1)), ((0, -1), (1, 1))

    def gather_step(found, s, ready=None):
        for chain, way in urgent + later if s < reach else urgent:
            slots = slot_p if way == 1 else slot_q
            shard = found[chain][slots[s - 1] if s > 1 else 0]
            if ready is not None and (chain, way) in later:
                shard = after(shard, ready)
            found[chain][slots[s] if s < reach else far] = hop(shard, way)

    def both_chains(found, slots):
        return [found[chain][slot] for slot in slots for chain in chains]

    def encode(slots, before):
        first, last = slots[0] == 0, slots[-1] == far
        return call(
            functools.partial(encode_kernel, slots, first, last),
            [shape((rows, lat), F32)] + ([shape((rows, lat), BF16)] if last else []),
            2 * unit * len(slots),
            [starts] + both_chains(inputs, slots) + [enc_weight, before],
        )

    inputs = [[part] + [None] * (size - 1) for part in halves(residual_in[0])]
    turned_own = call(
        turn_own_kernel, [shape((wide, rows), BF16)], 0, [starts] + both_chains(inputs, (0,))
    )[0]
    for s in range(1, reach + 1):
        gather_step(inputs, s, turned_own if s == 1 else None)
    low_cross = passed_along(after(dec_cross, inputs[0][slot_p.get(1, far)]), "layer", 1)
    stacked = jnp.concatenate([dec_same[0], jnp.concatenate([low_cross, dec_cross], axis=1)], axis=0)
    part = encode(tuple(range(far)), after(enc_bias, stacked))[0]
    preact, codes = encode((far,), part)
    earlier = passed_along(codes, "layer", 1)

    def spread(slots, dtypes, turned):
        outs = []
        for chain in chains:
            outs += [shape((half, wide), dtypes[chain].get(slot, F32)) for slot in slots]
            outs += [shape((2 * lat, half), BF16)] if turned else []
        found = call(
            functools.partial(spread_kernel, slots), outs, 4 * unit * len(slots), [starts, codes, earlier, stacked]
        )
        return found[:len(outs) // 2], found[len(outs) // 2:]

    rest = tuple(slot for slot in range(size) if slot != far)
    instant = ({far: BF16, slot_p.get(reach - 1): BF16}, {far: BF16, slot_q.get(reach - 1): BF16})
    far_0, far_1 = spread((far,), instant, False)
    moving = {(0, 1): hop(far_0[0], 1), (1, -1): hop(far_1[0], -1)}
    partial, both_t = [], []
    for pieces in spread(rest, instant, True):
        partial.append(dict(zip(rest, pieces)))
        both_t.append(pieces[-1])
    before = []
    for s in range(reach - 1, 0, -1):
        landed = [moving[loop] for loop in urgent]
        for chain, way in urgent + later:
            message = partial[chain][slot_q[s] if way == 1 else slot_p[s]]
            if (chain, way) in moving:
                message = (message + moving[chain, way].astype(F32)).astype(BF16)
            if (chain, way) in later and before:
                message = after(message, *before)
            moving[chain, way] = hop(message, way)
        before = landed
    errors = []
    for chain, wanted in zip(chains, halves(targets[0])):
        total = partial[chain][0]
        for way in (1, -1):
            if (chain, way) in moving:
                total = total + moving[chain, way].astype(F32)
        if chain == 1:
            wanted = after(wanted, errors[0][0])
        errors.append([((total - wanted.astype(F32)) * err_scale).astype(BF16)] + [None] * (size - 1))

    def back(slots, before):
        return call(
            functools.partial(back_kernel, slots, before is None),
            [shape((len(slots), 2 * lat, wide), F32), shape((2, half, 2 * lat), F32)],
            4 * unit * len(slots),
            [starts] + both_chains(errors, slots) + [stacked] + both_t + ([] if before is None else [before]),
        )

    groups, outers, acc, pending = [], [], None, [0]
    arrived = [inputs[0][1]] if size == 2 else [after(inputs[0][1], errors[1][0])]
    turned = call(
        turn_kernel,
        [shape((deep, rows), BF16)],
        0,
        [starts, turned_own] + arrived + both_chains(inputs, range(1, size))[1:],
    )[0]
    for s in range(1, reach + 1):
        gather_step(errors, s, turned if s == 2 else None)
        if s < reach:
            pending += [slot_p[s], slot_q[s]]
        if s == 1 or s == reach - 1:
            groups.append(tuple(pending))
            outer, acc = back(groups[-1], acc)
            outers.append(outer)
            pending = []
    last_same, back_own, sent, high = call(
        functools.partial(last_back_kernel, groups, far),
        [
            shape((lat, wide), F32),
            shape((rows, lat), F32),
            shape((rows + half_width, lat), F32),
            shape((half_width, lat), F32),
        ],
        4 * unit,
        [starts] + both_chains(errors, (far,)) + [stacked] + both_t + outers + [acc],
    )
    returned = passed_along(sent, "layer", -1)
    grad_same = call(
        functools.partial(place_kernel, groups, far),
        [shape((1, lat, deep), F32)],
        0,
        [starts, last_same] + outers,
        out_spaces=[pl.ANY],
        scratch=[pltpu.SemaphoreType.DMA((size,))],
    )[0]
    height = deep // PIECES
    grad_enc, grad_bias, grad_cross = call(
        finish_kernel,
        [shape((1, deep, lat), F32), shape((1, lat), F32), shape((lat, half_width), F32)],
        2 * unit * size,
        [starts, turned, preact, back_own, returned, high],
        out_spaces=[pl.ANY, pltpu.VMEM, pl.ANY],
        scratch=[
            pltpu.VMEM((PIECES, height, lat), F32),
            pltpu.SemaphoreType.DMA((PIECES,)),
            pltpu.SemaphoreType.DMA((half_width // lat,)),
        ],
    )
    return (grad_enc, grad_bias, grad_same, grad_cross)


def wide_shards(residual_in, targets, enc_weight, enc_bias, dec_same, dec_cross):
    is_first = lax.axis_index("layer") == 0
    err_scale = 1.0 / math.sqrt(residual_in.shape[1])
    inputs = lax.all_gather(residual_in[0], "latent", axis=1, tiled=True)
    preact = matmul(inputs, enc_weight[0]) + enc_bias[0]
    codes_now = jnp.maximum(preact, 0.0).astype(BF16)
    earlier = passed_along(codes_now, "layer", 1)
    cross_full = lax.all_gather(dec_cross, "layer", axis=1, tiled=True)
    own_dec = dec_same[0]
    half_width = own_dec.shape[1] // 2
    recon_full = lax.psum(matmul(codes_now, own_dec) + matmul(earlier, cross_full), "latent")
    wanted = lax.all_gather(targets[0], "latent", axis=1, tiled=True)
    errors = ((recon_full - wanted.astype(F32)) * err_scale).astype(BF16)
    grad_same = matmul(codes_now, errors, OVER_ROWS)
    grad_full = matmul(earlier, errors, OVER_ROWS)
    returned = passed_along(grad_full[:, :half_width], "layer", -1)
    grad_cross = jnp.where(is_first, returned, grad_full[:, half_width:])
    from_next = passed_along(matmul(errors, cross_full, OVER_COLS), "layer", -1)
    grad_codes = matmul(errors, own_dec, OVER_COLS) + from_next
    grad_pre = jnp.where(preact > 0, grad_codes, 0.0).astype(BF16)
    grad_enc = matmul(inputs, grad_pre, OVER_ROWS)
    grad_bias = jnp.sum(grad_pre.astype(F32), axis=0)
    return (grad_enc[None], grad_bias[None], grad_same[None], grad_cross)


def solution(mesh):
    size = mesh.shape["latent"]
    placed = (
        P("layer", "groups", "latent"),
        P("layer", "groups", "latent"),
        P("layer", None, "latent"),
        P("layer", "latent"),
        P("layer", "latent", None),
        P("latent", "layer"),
    )
    return jax.shard_map(
        ring_shards if size % 2 == 0 and size <= RING_LIMIT else wide_shards,
        mesh=mesh,
        in_specs=placed,
        out_specs=(
            P(("groups", "layer"), None, "latent"),
            P(("groups", "layer"), "latent"),
            P(("groups", "layer"), "latent", None),
            P(("groups", "latent"), "layer"),
        ),
        check_vma=False,
    )
```

```python
import functools
import math

import jax
import jax.numpy as jnp
from jax import lax
from jax.experimental import pallas as pl
from jax.experimental.pallas import tpu as pltpu
from jax.sharding import PartitionSpec as P

F32 = jnp.float32
BF16 = jnp.bfloat16
OVER_ROWS = (((0,), (0,)), ((), ()))
OVER_COLS = (((1,), (1,)), ((), ()))
RING_LIMIT = 16
VMEM_BYTES = 24 * 1024 * 1024
PIECES = 8


def passed_along(shard, axis, by):
    size = lax.axis_size(axis)
    pairs = [(i, i + by) for i in range(size) if 0 <= i + by < size]
    return lax.ppermute(shard, axis, pairs)


def matmul(a, b, dims=(((1,), (0,)), ((), ()))):
    return lax.dot_general(a, b, dims, preferred_element_type=F32)


def ring_order(size):
    return [2 * p if p < size // 2 else 2 * (size - 1 - p) + 1 for p in range(size)]


def ring_member(place, size):
    place = lax.rem(place + 2 * size, size)
    return jnp.where(place < size // 2, 2 * place, 2 * (size - 1 - place) + 1)


def ring_place(member, size):
    return jnp.where(member % 2 == 0, member // 2, size - 1 - member // 2)


def hop(shard, way):
    size, layers = lax.axis_size("latent"), lax.axis_size("layer")
    order = ring_order(size)
    pairs = []
    for p in range(size):
        for layer in range(layers):
            by = way if layer % 2 == 0 else -way
            pairs.append((order[p] * layers + layer, order[(p + by) % size] * layers + layer))
    return lax.ppermute(shard, ("latent", "layer"), pairs)


def after(value, *others):
    return lax.optimization_barrier((value,) + others)[0]


def call(kernel, outs, flops, operands, spaces=None, out_spaces=None, scratch=(), aliases=None):
    def spec(space):
        return pl.BlockSpec(memory_space=space)

    spaces = spaces or [pltpu.VMEM] * (len(operands) - 1)
    out_spaces = out_spaces or [pltpu.VMEM] * len(outs)
    return pl.pallas_call(
        kernel,
        out_shape=outs,
        in_specs=[spec(pltpu.SMEM)] + [spec(space) for space in spaces],
        out_specs=[spec(space) for space in out_spaces],
        scratch_shapes=list(scratch),
        input_output_aliases=aliases or {},
        compiler_params=pltpu.CompilerParams(vmem_limit_bytes=VMEM_BYTES),
        cost_estimate=pl.CostEstimate(flops=flops, bytes_accessed=1024, transcendentals=0),
    )(*operands)


def block_of(starts, slot, wide):
    return pl.ds(pl.multiple_of(starts[slot], wide), wide)


def encode_kernel(slots, first, last, starts, *refs):
    count = 2 * len(slots)
    shards, (weight, before, *outs) = refs[:count], refs[count:]
    rows, wide = shards[0].shape
    for chain in range(2):
        at = slice(chain * rows, (chain + 1) * rows)
        total = jnp.broadcast_to(before[...], (rows, before.shape[1])) if first else before[at, :]
        for i, slot in enumerate(slots):
            block = weight[0, block_of(starts, slot, wide), :]
            total = total + jnp.dot(shards[2 * i + chain][...], block, preferred_element_type=F32)
        outs[0][at, :] = total
        if last:
            outs[1][at, :] = jnp.maximum(total, 0.0).astype(BF16)


def turn_own_kernel(starts, *refs):
    *shards, turned = refs
    rows = shards[0].shape[0]
    for chain, shard in enumerate(shards):
        turned[:, chain * rows:(chain + 1) * rows] = shard[...].T


def turn_kernel(starts, own, *refs):
    *shards, turned = refs
    rows, wide = shards[0].shape
    turned[block_of(starts, 0, wide), :] = own[...]
    for k in range(len(shards) // 2):
        at = block_of(starts, k + 1, wide)
        for chain in range(2):
            turned[at, chain * rows:(chain + 1) * rows] = shards[2 * k + chain][...].T


def spread_kernel(slots, starts, codes, earlier, stacked, *outs):
    rows = codes.shape[0] // 2
    outs = list(outs)
    for chain in range(2):
        at = slice(chain * rows, (chain + 1) * rows)
        both = jnp.concatenate([codes[at, :], earlier[at, :]], axis=1)
        for slot in slots:
            partial = outs.pop(0)
            block = stacked[:, block_of(starts, slot, partial.shape[1])]
            partial[...] = jnp.dot(both, block, preferred_element_type=F32).astype(partial.dtype)
        if len(outs) > (1 - chain) * len(slots):
            outs.pop(0)[...] = both.T


def back_products(slots, starts, shards, stacked, both_t, before):
    wide = shards[0].shape[1]
    blocks, totals = [], [None, None] if before is None else [before[0], before[1]]
    for i, slot in enumerate(slots):
        decoder = stacked[:, block_of(starts, slot, wide)]
        block = 0.0
        for chain in range(2):
            error = shards[2 * i + chain][...]
            block = block + jnp.dot(both_t[chain][...], error, preferred_element_type=F32)
            term = lax.dot_general(error, decoder, OVER_COLS, preferred_element_type=F32)
            totals[chain] = term if totals[chain] is None else totals[chain] + term
        blocks.append(block)
    return blocks, totals


def back_kernel(slots, first, starts, *refs):
    count = 2 * len(slots)
    shards, (stacked, *both_t), (*before, outer, back) = refs[:count], refs[count:count + 3], refs[count + 3:]
    blocks, totals = back_products(slots, starts, shards, stacked, both_t, None if first else before[0])
    for i, block in enumerate(blocks):
        outer[i] = block
    for chain in range(2):
        back[chain] = totals[chain]


def last_back_kernel(slots, far, starts, *refs):
    near_refs, (before, same, back_own, sent, high) = refs[:-5], refs[-5:]
    shards, (stacked, *both_t), outers = near_refs[:2], near_refs[2:5], near_refs[5:]
    (block,), totals = back_products((far,), starts, shards, stacked, both_t, before)
    rows, wide = shards[0].shape
    lat = high.shape[1]
    half_width = high.shape[0]
    for chain in range(2):
        back_own[chain * rows:(chain + 1) * rows, :] = totals[chain][:, :lat]
        sent[chain * rows:(chain + 1) * rows, :] = totals[chain][:, lat:]
    same[...] = block[:lat]
    pieces = [(far, block[lat:])]
    for group, outer in zip(slots, outers):
        pieces += [(slot, outer[i, lat:]) for i, slot in enumerate(group)]
    for slot, piece in pieces:
        start = pl.multiple_of(starts[slot], wide)

        @pl.when(start < half_width)
        def _():
            for c in range(0, wide, lat):
                sent[pl.ds(2 * rows + start + c, lat), :] = piece[:, c:c + lat]

        @pl.when(start >= half_width)
        def _():
            for c in range(0, wide, lat):
                high[pl.ds(start - half_width + c, lat), :] = piece[:, c:c + lat]


def place_kernel(slots, far, starts, *refs):
    last, *outers, same, sems = refs
    lat, wide = last.shape
    blocks = [(far, last)]
    for group, outer in zip(slots, outers):
        blocks += [(slot, outer.at[i, :lat, :]) for i, slot in enumerate(group)]
    copies = []
    for i, (slot, block) in enumerate(blocks):
        copies.append(pltpu.make_async_copy(block, same.at[0, :, block_of(starts, slot, wide)], sems.at[i]))
        copies[-1].start()
    for copy in copies:
        copy.wait()


def finish_kernel(starts, turned, preact, back_own, arrived, high, grad, bias, cross, stage, grad_sems, cross_sems):
    pieces, height, lat = stage.shape
    rows = preact.shape[0]
    half_width = high.shape[0]
    copies = []
    first = starts[starts.shape[0] - 1] == 0
    for c in range(half_width // lat):
        at = pl.ds(c * lat, lat)

        @pl.when(first)
        def _():
            source = arrived.at[pl.ds(rows + c * lat, lat), :]
            pltpu.make_async_copy(source, cross.at[:, at], cross_sems.at[c]).start()

        @pl.when(jnp.logical_not(first))
        def _():
            pltpu.make_async_copy(high.at[at, :], cross.at[:, at], cross_sems.at[c]).start()

        copies.append(pltpu.make_async_copy(high.at[at, :], cross.at[:, at], cross_sems.at[c]))
    value = jnp.where(preact[...] > 0, back_own[...] + arrived[:rows, :], 0.0).astype(BF16)
    for i in range(pieces):
        at = pl.ds(i * height, height)
        stage[i] = jnp.dot(turned[at, :], value, preferred_element_type=F32)
        copies.append(pltpu.make_async_copy(stage.at[i], grad.at[0, at, :], grad_sems.at[i]))
        copies[-1].start()
    bias[...] = jnp.sum(value.astype(F32), axis=0, keepdims=True)
    for copy in copies:
        copy.wait()


def ring_shards(residual_in, targets, enc_weight, enc_bias, dec_same, dec_cross):
    size = lax.axis_size("latent")
    reach = size // 2
    place = ring_place(lax.axis_index("latent"), size)
    layer = lax.axis_index("layer")
    sign = jnp.where(layer % 2 == 0, 1, -1)
    rows, wide = residual_in.shape[1:]
    half = rows // 2
    deep, lat = enc_weight.shape[1:]
    half_width = deep // 2
    err_scale = 1.0 / math.sqrt(rows)
    shape = jax.ShapeDtypeStruct
    unit = rows * wide * lat
    chains = (0, 1)

    def halves(array):
        return [array[:half], array[half:]]

    slot_p = {s: 2 * s - 1 for s in range(1, reach)}
    slot_q = {s: 2 * s for s in range(1, reach)}
    far = size - 1
    offsets = [0] * size
    offsets[far] = reach
    for s in range(1, reach):
        offsets[slot_p[s]] = -s
        offsets[slot_q[s]] = s
    starts = jnp.stack([ring_member(place + sign * offset, size) * wide for offset in offsets] + [layer])
    starts = starts.astype(jnp.int32)

    urgent, later = ((0, 1), (1, -1)), ((1, 1), (0, -1))

    def gather_step(found, s, ready=None):
        for chain, way in urgent + later if s < reach else urgent:
            slots = slot_p if way == 1 else slot_q
            shard = found[chain][slots[s - 1] if s > 1 else 0]
            if ready is not None and (chain, way) in later:
                shard = after(shard, ready)
            found[chain][slots[s] if s < reach else far] = hop(shard, way)

    def both_chains(found, slots):
        return [found[chain][slot] for slot in slots for chain in chains]

    def encode(slots, before):
        first, last = slots[0] == 0, slots[-1] == far
        return call(
            functools.partial(encode_kernel, slots, first, last),
            [shape((rows, lat), F32)] + ([shape((rows, lat), BF16)] if last else []),
            2 * unit * len(slots),
            [starts] + both_chains(inputs, slots) + [enc_weight, before],
        )

    inputs = [[part] + [None] * (size - 1) for part in halves(residual_in[0])]
    turned_own = call(
        turn_own_kernel, [shape((wide, rows), BF16)], 0, [starts] + both_chains(inputs, (0,))
    )[0]
    for s in range(1, reach + 1):
        gather_step(inputs, s, turned_own if s == 1 else None)
    low_cross = passed_along(after(dec_cross, inputs[0][slot_p.get(1, far)]), "layer", 1)
    stacked = jnp.concatenate([dec_same[0], jnp.concatenate([low_cross, dec_cross], axis=1)], axis=0)
    part = encode(tuple(range(far)), after(enc_bias, stacked))[0]
    preact, codes = encode((far,), part)
    earlier = passed_along(codes, "layer", 1)

    def spread(slots, dtypes, turned):
        outs = []
        for chain in chains:
            outs += [shape((half, wide), dtypes[chain].get(slot, F32)) for slot in slots]
            outs += [shape((2 * lat, half), BF16)] if turned else []
        found = call(
            functools.partial(spread_kernel, slots), outs, 4 * unit * len(slots), [starts, codes, earlier, stacked]
        )
        return found[:len(outs) // 2], found[len(outs) // 2:]

    rest = tuple(slot for slot in range(size) if slot != far)
    instant = ({far: BF16, slot_p.get(reach - 1): BF16}, {far: BF16, slot_q.get(reach - 1): BF16})
    far_0, far_1 = spread((far,), instant, False)
    moving = {(0, 1): hop(far_0[0], 1), (1, -1): hop(far_1[0], -1)}
    partial, both_t = [], []
    for pieces in spread(rest, instant, True):
        partial.append(dict(zip(rest, pieces)))
        both_t.append(pieces[-1])
    before = []
    for s in range(reach - 1, 0, -1):
        landed = [moving[loop] for loop in urgent]
        for chain, way in urgent + later:
            message = partial[chain][slot_q[s] if way == 1 else slot_p[s]]
            if (chain, way) in moving:
                message = (message + moving[chain, way].astype(F32)).astype(BF16)
            if (chain, way) in later and before:
                message = after(message, *before)
            moving[chain, way] = hop(message, way)
        before = landed
    errors = []
    for chain, wanted in zip(chains, halves(targets[0])):
        total = partial[chain][0]
        for way in (1, -1):
            if (chain, way) in moving:
                total = total + moving[chain, way].astype(F32)
        if chain == 1:
            wanted = after(wanted, errors[0][0])
        errors.append([((total - wanted.astype(F32)) * err_scale).astype(BF16)] + [None] * (size - 1))

    def back(slots, before):
        return call(
            functools.partial(back_kernel, slots, before is None),
            [shape((len(slots), 2 * lat, wide), F32), shape((2, half, 2 * lat), F32)],
            4 * unit * len(slots),
            [starts] + both_chains(errors, slots) + [stacked] + both_t + ([] if before is None else [before]),
        )

    groups, outers, acc, pending = [], [], None, [0]
    arrived = [inputs[0][1]] if size == 2 else [after(inputs[0][1], errors[1][0])]
    turned = call(
        turn_kernel,
        [shape((deep, rows), BF16)],
        0,
        [starts, turned_own] + arrived + both_chains(inputs, range(1, size))[1:],
    )[0]
    for s in range(1, reach + 1):
        gather_step(errors, s, turned if s == 2 else None)
        if s < reach:
            pending += [slot_p[s], slot_q[s]]
        if s == 1 or s == reach - 1:
            groups.append(tuple(pending))
            outer, acc = back(groups[-1], acc)
            outers.append(outer)
            pending = []
    last_same, back_own, sent, high = call(
        functools.partial(last_back_kernel, groups, far),
        [
            shape((lat, wide), F32),
            shape((rows, lat), F32),
            shape((rows + half_width, lat), F32),
            shape((half_width, lat), F32),
        ],
        4 * unit,
        [starts] + both_chains(errors, (far,)) + [stacked] + both_t + outers + [acc],
    )
    returned = passed_along(sent, "layer", -1)
    grad_same = call(
        functools.partial(place_kernel, groups, far),
        [shape((1, lat, deep), F32)],
        0,
        [starts, last_same] + outers,
        out_spaces=[pl.ANY],
        scratch=[pltpu.SemaphoreType.DMA((size,))],
    )[0]
    height = deep // PIECES
    grad_enc, grad_bias, grad_cross = call(
        finish_kernel,
        [shape((1, deep, lat), F32), shape((1, lat), F32), shape((lat, half_width), F32)],
        2 * unit * size,
        [starts, turned, preact, back_own, returned, high],
        out_spaces=[pl.ANY, pltpu.VMEM, pl.ANY],
        scratch=[
            pltpu.VMEM((PIECES, height, lat), F32),
            pltpu.SemaphoreType.DMA((PIECES,)),
            pltpu.SemaphoreType.DMA((half_width // lat,)),
        ],
    )
    return (grad_enc, grad_bias, grad_same, grad_cross)


def wide_shards(residual_in, targets, enc_weight, enc_bias, dec_same, dec_cross):
    is_first = lax.axis_index("layer") == 0
    err_scale = 1.0 / math.sqrt(residual_in.shape[1])
    inputs = lax.all_gather(residual_in[0], "latent", axis=1, tiled=True)
    preact = matmul(inputs, enc_weight[0]) + enc_bias[0]
    codes_now = jnp.maximum(preact, 0.0).astype(BF16)
    earlier = passed_along(codes_now, "layer", 1)
    cross_full = lax.all_gather(dec_cross, "layer", axis=1, tiled=True)
    own_dec = dec_same[0]
    half_width = own_dec.shape[1] // 2
    recon_full = lax.psum(matmul(codes_now, own_dec) + matmul(earlier, cross_full), "latent")
    wanted = lax.all_gather(targets[0], "latent", axis=1, tiled=True)
    errors = ((recon_full - wanted.astype(F32)) * err_scale).astype(BF16)
    grad_same = matmul(codes_now, errors, OVER_ROWS)
    grad_full = matmul(earlier, errors, OVER_ROWS)
    returned = passed_along(grad_full[:, :half_width], "layer", -1)
    grad_cross = jnp.where(is_first, returned, grad_full[:, half_width:])
    from_next = passed_along(matmul(errors, cross_full, OVER_COLS), "layer", -1)
    grad_codes = matmul(errors, own_dec, OVER_COLS) + from_next
    grad_pre = jnp.where(preact > 0, grad_codes, 0.0).astype(BF16)
    grad_enc = matmul(inputs, grad_pre, OVER_ROWS)
    grad_bias = jnp.sum(grad_pre.astype(F32), axis=0)
    return (grad_enc[None], grad_bias[None], grad_same[None], grad_cross)


def solution(mesh):
    size = mesh.shape["latent"]
    placed = (
        P("layer", "groups", "latent"),
        P("layer", "groups", "latent"),
        P("layer", None, "latent"),
        P("layer", "latent"),
        P("layer", "latent", None),
        P("latent", "layer"),
    )
    return jax.shard_map(
        ring_shards if size % 2 == 0 and size <= RING_LIMIT else wide_shards,
        mesh=mesh,
        in_specs=placed,
        out_specs=(
            P(("groups", "layer"), None, "latent"),
            P(("groups", "layer"), "latent"),
            P(("groups", "layer"), "latent", None),
            P(("groups", "latent"), "layer"),
        ),
        check_vma=False,
    )
```

```python
import functools
import math

import jax
import jax.numpy as jnp
from jax import lax
from jax.experimental import pallas as pl
from jax.experimental.pallas import tpu as pltpu
from jax.sharding import PartitionSpec as P

F32 = jnp.float32
BF16 = jnp.bfloat16
OVER_ROWS = (((0,), (0,)), ((), ()))
OVER_COLS = (((1,), (1,)), ((), ()))
RING_LIMIT = 16
VMEM_BYTES = 24 * 1024 * 1024
PIECES = 8


def passed_along(shard, axis, by):
    size = lax.axis_size(axis)
    pairs = [(i, i + by) for i in range(size) if 0 <= i + by < size]
    return lax.ppermute(shard, axis, pairs)


def matmul(a, b, dims=(((1,), (0,)), ((), ()))):
    return lax.dot_general(a, b, dims, preferred_element_type=F32)


def ring_order(size):
    return [2 * p if p < size // 2 else 2 * (size - 1 - p) + 1 for p in range(size)]


def ring_member(place, size):
    place = lax.rem(place + 2 * size, size)
    return jnp.where(place < size // 2, 2 * place, 2 * (size - 1 - place) + 1)


def ring_place(member, size):
    return jnp.where(member % 2 == 0, member // 2, size - 1 - member // 2)


def hop(shard, way):
    size, layers = lax.axis_size("latent"), lax.axis_size("layer")
    order = ring_order(size)
    pairs = []
    for p in range(size):
        for layer in range(layers):
            by = way if layer % 2 == 0 else -way
            pairs.append((order[p] * layers + layer, order[(p + by) % size] * layers + layer))
    return lax.ppermute(shard, ("latent", "layer"), pairs)


def after(value, *others):
    return lax.optimization_barrier((value,) + others)[0]


def call(kernel, outs, flops, operands, spaces=None, out_spaces=None, scratch=(), aliases=None):
    def spec(space):
        return pl.BlockSpec(memory_space=space)

    spaces = spaces or [pltpu.VMEM] * (len(operands) - 1)
    out_spaces = out_spaces or [pltpu.VMEM] * len(outs)
    return pl.pallas_call(
        kernel,
        out_shape=outs,
        in_specs=[spec(pltpu.SMEM)] + [spec(space) for space in spaces],
        out_specs=[spec(space) for space in out_spaces],
        scratch_shapes=list(scratch),
        input_output_aliases=aliases or {},
        compiler_params=pltpu.CompilerParams(vmem_limit_bytes=VMEM_BYTES),
        cost_estimate=pl.CostEstimate(flops=flops, bytes_accessed=1024, transcendentals=0),
    )(*operands)


def block_of(starts, slot, wide):
    return pl.ds(pl.multiple_of(starts[slot], wide), wide)


def encode_kernel(slots, first, last, starts, *refs):
    count = 2 * len(slots)
    shards, (weight, before, *outs) = refs[:count], refs[count:]
    rows, wide = shards[0].shape
    for chain in range(2):
        at = slice(chain * rows, (chain + 1) * rows)
        total = jnp.broadcast_to(before[...], (rows, before.shape[1])) if first else before[at, :]
        for i, slot in enumerate(slots):
            block = weight[0, block_of(starts, slot, wide), :]
            total = total + jnp.dot(shards[2 * i + chain][...], block, preferred_element_type=F32)
        outs[0][at, :] = total
        if last:
            outs[1][at, :] = jnp.maximum(total, 0.0).astype(BF16)


def turn_own_kernel(starts, shard, *refs):
    refs[-1][...] = shard[...].T


def turn_kernel(starts, own_0, own_1, *refs):
    *shards, turned = refs
    rows, wide = shards[0].shape
    for chain, own in enumerate((own_0, own_1)):
        turned[block_of(starts, 0, wide), chain * rows:(chain + 1) * rows] = own[...]
    for k in range(len(shards) // 2):
        at = block_of(starts, k + 1, wide)
        for chain in range(2):
            turned[at, chain * rows:(chain + 1) * rows] = shards[2 * k + chain][...].T


def spread_kernel(slots, starts, codes, earlier, stacked, *outs):
    rows = codes.shape[0] // 2
    outs = list(outs)
    for chain in range(2):
        at = slice(chain * rows, (chain + 1) * rows)
        both = jnp.concatenate([codes[at, :], earlier[at, :]], axis=1)
        for slot in slots:
            partial = outs.pop(0)
            block = stacked[:, block_of(starts, slot, partial.shape[1])]
            partial[...] = jnp.dot(both, block, preferred_element_type=F32).astype(partial.dtype)
        if len(outs) > (1 - chain) * len(slots):
            outs.pop(0)[...] = both.T


def back_products(slots, starts, shards, stacked, both_t, before):
    wide = shards[0].shape[1]
    blocks, totals = [], [None, None] if before is None else [before[0], before[1]]
    for i, slot in enumerate(slots):
        decoder = stacked[:, block_of(starts, slot, wide)]
        block = 0.0
        for chain in range(2):
            error = shards[2 * i + chain][...]
            block = block + jnp.dot(both_t[chain][...], error, preferred_element_type=F32)
            term = lax.dot_general(error, decoder, OVER_COLS, preferred_element_type=F32)
            totals[chain] = term if totals[chain] is None else totals[chain] + term
        blocks.append(block)
    return blocks, totals


def back_kernel(slots, first, starts, *refs):
    count = 2 * len(slots)
    shards, (stacked, *both_t), (*before, outer, back) = refs[:count], refs[count:count + 3], refs[count + 3:]
    blocks, totals = back_products(slots, starts, shards, stacked, both_t, None if first else before[0])
    for i, block in enumerate(blocks):
        outer[i] = block
    for chain in range(2):
        back[chain] = totals[chain]


def last_back_kernel(slots, far, starts, *refs):
    near_refs, (before, same, back_own, sent, high) = refs[:-5], refs[-5:]
    shards, (stacked, *both_t), outers = near_refs[:2], near_refs[2:5], near_refs[5:]
    (block,), totals = back_products((far,), starts, shards, stacked, both_t, before)
    rows, wide = shards[0].shape
    lat = high.shape[1]
    half_width = high.shape[0]
    for chain in range(2):
        back_own[chain * rows:(chain + 1) * rows, :] = totals[chain][:, :lat]
        sent[chain * rows:(chain + 1) * rows, :] = totals[chain][:, lat:]
    same[...] = block[:lat]
    pieces = [(far, block[lat:])]
    for group, outer in zip(slots, outers):
        pieces += [(slot, outer[i, lat:]) for i, slot in enumerate(group)]
    for slot, piece in pieces:
        start = pl.multiple_of(starts[slot], wide)

        @pl.when(start < half_width)
        def _():
            for c in range(0, wide, lat):
                sent[pl.ds(2 * rows + start + c, lat), :] = piece[:, c:c + lat]

        @pl.when(start >= half_width)
        def _():
            for c in range(0, wide, lat):
                high[pl.ds(start - half_width + c, lat), :] = piece[:, c:c + lat]


def place_kernel(slots, far, starts, *refs):
    last, *outers, same, sems = refs
    lat, wide = last.shape
    blocks = [(far, last)]
    for group, outer in zip(slots, outers):
        blocks += [(slot, outer.at[i, :lat, :]) for i, slot in enumerate(group)]
    copies = []
    for i, (slot, block) in enumerate(blocks):
        copies.append(pltpu.make_async_copy(block, same.at[0, :, block_of(starts, slot, wide)], sems.at[i]))
        copies[-1].start()
    for copy in copies:
        copy.wait()


def finish_kernel(starts, turned, preact, back_own, arrived, high, grad, bias, cross, stage, grad_sems, cross_sems):
    pieces, height, lat = stage.shape
    rows = preact.shape[0]
    half_width = high.shape[0]
    copies = []
    first = starts[starts.shape[0] - 1] == 0
    for c in range(half_width // lat):
        at = pl.ds(c * lat, lat)

        @pl.when(first)
        def _():
            source = arrived.at[pl.ds(rows + c * lat, lat), :]
            pltpu.make_async_copy(source, cross.at[:, at], cross_sems.at[c]).start()

        @pl.when(jnp.logical_not(first))
        def _():
            pltpu.make_async_copy(high.at[at, :], cross.at[:, at], cross_sems.at[c]).start()

        copies.append(pltpu.make_async_copy(high.at[at, :], cross.at[:, at], cross_sems.at[c]))
    value = jnp.where(preact[...] > 0, back_own[...] + arrived[:rows, :], 0.0).astype(BF16)
    for i in range(pieces):
        at = pl.ds(i * height, height)
        stage[i] = jnp.dot(turned[at, :], value, preferred_element_type=F32)
        copies.append(pltpu.make_async_copy(stage.at[i], grad.at[0, at, :], grad_sems.at[i]))
        copies[-1].start()
    bias[...] = jnp.sum(value.astype(F32), axis=0, keepdims=True)
    for copy in copies:
        copy.wait()


def ring_shards(residual_in, targets, enc_weight, enc_bias, dec_same, dec_cross):
    size = lax.axis_size("latent")
    reach = size // 2
    place = ring_place(lax.axis_index("latent"), size)
    layer = lax.axis_index("layer")
    sign = jnp.where(layer % 2 == 0, 1, -1)
    rows, wide = residual_in.shape[1:]
    half = rows // 2
    deep, lat = enc_weight.shape[1:]
    half_width = deep // 2
    err_scale = 1.0 / math.sqrt(rows)
    shape = jax.ShapeDtypeStruct
    unit = rows * wide * lat
    chains = (0, 1)

    def halves(array):
        return [array[:half], array[half:]]

    slot_p = {s: 2 * s - 1 for s in range(1, reach)}
    slot_q = {s: 2 * s for s in range(1, reach)}
    far = size - 1
    offsets = [0] * size
    offsets[far] = reach
    for s in range(1, reach):
        offsets[slot_p[s]] = -s
        offsets[slot_q[s]] = s
    starts = jnp.stack([ring_member(place + sign * offset, size) * wide for offset in offsets] + [layer])
    starts = starts.astype(jnp.int32)

    urgent, later = ((0, 1), (1, -1)), ((0, -1), (1, 1))

    def gather_step(found, s, ready=None):
        for chain, way in urgent + later if s < reach else urgent:
            slots = slot_p if way == 1 else slot_q
            shard = found[chain][slots[s - 1] if s > 1 else 0]
            if ready is not None and (chain, way) in later:
                shard = after(shard, ready[chain])
            found[chain][slots[s] if s < reach else far] = hop(shard, way)

    def both_chains(found, slots):
        return [found[chain][slot] for slot in slots for chain in chains]

    def encode(slots, before):
        first, last = slots[0] == 0, slots[-1] == far
        return call(
            functools.partial(encode_kernel, slots, first, last),
            [shape((rows, lat), F32)] + ([shape((rows, lat), BF16)] if last else []),
            2 * unit * len(slots),
            [starts] + both_chains(inputs, slots) + [enc_weight, before],
        )

    inputs = [[part] + [None] * (size - 1) for part in halves(residual_in[0])]
    turned_own = []
    for chain in chains:
        source = inputs[chain][0] if chain == 0 else after(inputs[chain][0], turned_own[0])
        turned_own += call(turn_own_kernel, [shape((wide, half), BF16)], 0, [starts, source])
    for s in range(1, reach + 1):
        gather_step(inputs, s, turned_own if s == 1 else None)
    low_cross = passed_along(after(dec_cross, inputs[0][slot_p.get(1, far)]), "layer", 1)
    stacked = jnp.concatenate([dec_same[0], jnp.concatenate([low_cross, dec_cross], axis=1)], axis=0)
    part = encode(tuple(range(far)), after(enc_bias, stacked))[0]
    preact, codes = encode((far,), part)
    earlier = passed_along(codes, "layer", 1)

    def spread(slots, dtypes, turned):
        outs = []
        for chain in chains:
            outs += [shape((half, wide), dtypes[chain].get(slot, F32)) for slot in slots]
            outs += [shape((2 * lat, half), BF16)] if turned else []
        found = call(
            functools.partial(spread_kernel, slots), outs, 4 * unit * len(slots), [starts, codes, earlier, stacked]
        )
        return found[:len(outs) // 2], found[len(outs) // 2:]

    rest = tuple(slot for slot in range(size) if slot != far)
    instant = ({far: BF16, slot_p.get(reach - 1): BF16}, {far: BF16, slot_q.get(reach - 1): BF16})
    far_0, far_1 = spread((far,), instant, False)
    moving = {(0, 1): hop(far_0[0], 1), (1, -1): hop(far_1[0], -1)}
    partial, both_t = [], []
    for pieces in spread(rest, instant, True):
        partial.append(dict(zip(rest, pieces)))
        both_t.append(pieces[-1])
    before = []
    for s in range(reach - 1, 0, -1):
        landed = [moving[loop] for loop in urgent]
        for chain, way in urgent + later:
            message = partial[chain][slot_q[s] if way == 1 else slot_p[s]]
            if (chain, way) in moving:
                message = (message + moving[chain, way].astype(F32)).astype(BF16)
            if (chain, way) in later and before:
                message = after(message, *before)
            moving[chain, way] = hop(message, way)
        before = landed
    errors = []
    for chain, wanted in zip(chains, halves(targets[0])):
        total = partial[chain][0]
        for way in (1, -1):
            if (chain, way) in moving:
                total = total + moving[chain, way].astype(F32)
        if chain == 1:
            wanted = after(wanted, errors[0][0])
        errors.append([((total - wanted.astype(F32)) * err_scale).astype(BF16)] + [None] * (size - 1))

    def back(slots, before, decoders):
        return call(
            functools.partial(back_kernel, slots, before is None),
            [shape((len(slots), 2 * lat, wide), F32), shape((2, half, 2 * lat), F32)],
            4 * unit * len(slots),
            [starts] + both_chains(errors, slots) + [decoders] + both_t + ([] if before is None else [before]),
        )

    groups, outers, acc, pending = [], [], None, [0]
    arrived = [after(inputs[0][1], errors[1][0])]
    turned = call(
        turn_kernel,
        [shape((deep, rows), BF16)],
        0,
        [starts] + turned_own + arrived + both_chains(inputs, range(1, size))[1:],
    )[0]
    groups = [(0,), tuple(range(1, far))] if reach > 1 else [(0,)]
    outer, acc = back(groups[0], None, stacked)
    outers = [outer]
    for s in range(1, reach + 1):
        gather_step(errors, s, (turned, turned) if s == 2 else None)
    if reach > 1:
        outer, acc = back(groups[1], acc, stacked)
        outers.append(outer)
    last_same, back_own, sent, high = call(
        functools.partial(last_back_kernel, groups, far),
        [
            shape((lat, wide), F32),
            shape((rows, lat), F32),
            shape((rows + half_width, lat), F32),
            shape((half_width, lat), F32),
        ],
        4 * unit,
        [starts] + both_chains(errors, (far,)) + [stacked] + both_t + outers + [acc],
    )
    returned = passed_along(sent, "layer", -1)
    grad_same = call(
        functools.partial(place_kernel, groups, far),
        [shape((1, lat, deep), F32)],
        0,
        [starts, last_same] + outers,
        out_spaces=[pl.ANY],
        scratch=[pltpu.SemaphoreType.DMA((size,))],
    )[0]
    height = deep // PIECES
    grad_enc, grad_bias, grad_cross = call(
        finish_kernel,
        [shape((1, deep, lat), F32), shape((1, lat), F32), shape((lat, half_width), F32)],
        2 * unit * size,
        [starts, turned, preact, back_own, returned, high],
        out_spaces=[pl.ANY, pltpu.VMEM, pl.ANY],
        scratch=[
            pltpu.VMEM((PIECES, height, lat), F32),
            pltpu.SemaphoreType.DMA((PIECES,)),
            pltpu.SemaphoreType.DMA((half_width // lat,)),
        ],
    )
    return (grad_enc, grad_bias, grad_same, grad_cross)


def wide_shards(residual_in, targets, enc_weight, enc_bias, dec_same, dec_cross):
    is_first = lax.axis_index("layer") == 0
    err_scale = 1.0 / math.sqrt(residual_in.shape[1])
    inputs = lax.all_gather(residual_in[0], "latent", axis=1, tiled=True)
    preact = matmul(inputs, enc_weight[0]) + enc_bias[0]
    codes_now = jnp.maximum(preact, 0.0).astype(BF16)
    earlier = passed_along(codes_now, "layer", 1)
    cross_full = lax.all_gather(dec_cross, "layer", axis=1, tiled=True)
    own_dec = dec_same[0]
    half_width = own_dec.shape[1] // 2
    recon_full = lax.psum(matmul(codes_now, own_dec) + matmul(earlier, cross_full), "latent")
    wanted = lax.all_gather(targets[0], "latent", axis=1, tiled=True)
    errors = ((recon_full - wanted.astype(F32)) * err_scale).astype(BF16)
    grad_same = matmul(codes_now, errors, OVER_ROWS)
    grad_full = matmul(earlier, errors, OVER_ROWS)
    returned = passed_along(grad_full[:, :half_width], "layer", -1)
    grad_cross = jnp.where(is_first, returned, grad_full[:, half_width:])
    from_next = passed_along(matmul(errors, cross_full, OVER_COLS), "layer", -1)
    grad_codes = matmul(errors, own_dec, OVER_COLS) + from_next
    grad_pre = jnp.where(preact > 0, grad_codes, 0.0).astype(BF16)
    grad_enc = matmul(inputs, grad_pre, OVER_ROWS)
    grad_bias = jnp.sum(grad_pre.astype(F32), axis=0)
    return (grad_enc[None], grad_bias[None], grad_same[None], grad_cross)


def solution(mesh):
    size = mesh.shape["latent"]
    placed = (
        P("layer", "groups", "latent"),
        P("layer", "groups", "latent"),
        P("layer", None, "latent"),
        P("layer", "latent"),
        P("layer", "latent", None),
        P("latent", "layer"),
    )
    return jax.shard_map(
        ring_shards if size % 2 == 0 and size <= RING_LIMIT else wide_shards,
        mesh=mesh,
        in_specs=placed,
        out_specs=(
            P(("groups", "layer"), None, "latent"),
            P(("groups", "layer"), "latent"),
            P(("groups", "layer"), "latent", None),
            P(("groups", "latent"), "layer"),
        ),
        check_vma=False,
    )
```

```python
import functools
import math

import jax
import jax.numpy as jnp
from jax import lax
from jax.experimental import pallas as pl
from jax.experimental.pallas import tpu as pltpu
from jax.sharding import PartitionSpec as P

F32 = jnp.float32
BF16 = jnp.bfloat16
OVER_ROWS = (((0,), (0,)), ((), ()))
OVER_COLS = (((1,), (1,)), ((), ()))
RING_LIMIT = 16
VMEM_BYTES = 24 * 1024 * 1024
PIECES = 8


def passed_along(shard, axis, by):
    size = lax.axis_size(axis)
    pairs = [(i, i + by) for i in range(size) if 0 <= i + by < size]
    return lax.ppermute(shard, axis, pairs)


def matmul(a, b, dims=(((1,), (0,)), ((), ()))):
    return lax.dot_general(a, b, dims, preferred_element_type=F32)


def ring_order(size):
    return [2 * p if p < size // 2 else 2 * (size - 1 - p) + 1 for p in range(size)]


def ring_member(place, size):
    place = lax.rem(place + 2 * size, size)
    return jnp.where(place < size // 2, 2 * place, 2 * (size - 1 - place) + 1)


def ring_place(member, size):
    return jnp.where(member % 2 == 0, member // 2, size - 1 - member // 2)


def hop(shard, way):
    size, layers = lax.axis_size("latent"), lax.axis_size("layer")
    order = ring_order(size)
    pairs = []
    for p in range(size):
        for layer in range(layers):
            by = way if layer % 2 == 0 else -way
            pairs.append((order[p] * layers + layer, order[(p + by) % size] * layers + layer))
    return lax.ppermute(shard, ("latent", "layer"), pairs)


def after(value, *others):
    return lax.optimization_barrier((value,) + others)[0]


def call(kernel, outs, flops, operands, spaces=None, out_spaces=None, scratch=(), aliases=None):
    def spec(space):
        return pl.BlockSpec(memory_space=space)

    spaces = spaces or [pltpu.VMEM] * (len(operands) - 1)
    out_spaces = out_spaces or [pltpu.VMEM] * len(outs)
    return pl.pallas_call(
        kernel,
        out_shape=outs,
        in_specs=[spec(pltpu.SMEM)] + [spec(space) for space in spaces],
        out_specs=[spec(space) for space in out_spaces],
        scratch_shapes=list(scratch),
        input_output_aliases=aliases or {},
        compiler_params=pltpu.CompilerParams(vmem_limit_bytes=VMEM_BYTES),
        cost_estimate=pl.CostEstimate(flops=flops, bytes_accessed=1024, transcendentals=0),
    )(*operands)


def block_of(starts, slot, wide):
    return pl.ds(pl.multiple_of(starts[slot], wide), wide)


def encode_kernel(slots, first, last, starts, *refs):
    count = 2 * len(slots)
    shards, (weight, before, *outs) = refs[:count], refs[count:]
    rows, wide = shards[0].shape
    for chain in range(2):
        at = slice(chain * rows, (chain + 1) * rows)
        total = jnp.broadcast_to(before[...], (rows, before.shape[1])) if first else before[at, :]
        for i, slot in enumerate(slots):
            block = weight[0, block_of(starts, slot, wide), :]
            total = total + jnp.dot(shards[2 * i + chain][...], block, preferred_element_type=F32)
        outs[0][at, :] = total
        if last:
            outs[1][at, :] = jnp.maximum(total, 0.0).astype(BF16)


def turn_own_kernel(starts, shard, *refs):
    refs[-1][...] = shard[...].T


def turn_kernel(starts, own_0, own_1, *refs):
    *shards, turned = refs
    rows, wide = shards[0].shape
    for chain, own in enumerate((own_0, own_1)):
        turned[block_of(starts, 0, wide), chain * rows:(chain + 1) * rows] = own[...]
    for k in range(len(shards) // 2):
        at = block_of(starts, k + 1, wide)
        for chain in range(2):
            turned[at, chain * rows:(chain + 1) * rows] = shards[2 * k + chain][...].T


def spread_kernel(slots, starts, codes, earlier, stacked, *outs):
    rows = codes.shape[0] // 2
    outs = list(outs)
    for chain in range(2):
        at = slice(chain * rows, (chain + 1) * rows)
        both = jnp.concatenate([codes[at, :], earlier[at, :]], axis=1)
        for slot in slots:
            partial = outs.pop(0)
            block = stacked[:, block_of(starts, slot, partial.shape[1])]
            partial[...] = jnp.dot(both, block, preferred_element_type=F32).astype(partial.dtype)
        if len(outs) > (1 - chain) * len(slots):
            outs.pop(0)[...] = both.T


def back_products(slots, starts, shards, stacked, both_t, before):
    wide = shards[0].shape[1]
    blocks, totals = [], [None, None] if before is None else [before[0], before[1]]
    for i, slot in enumerate(slots):
        decoder = stacked[:, block_of(starts, slot, wide)]
        block = 0.0
        for chain in range(2):
            error = shards[2 * i + chain][...]
            block = block + jnp.dot(both_t[chain][...], error, preferred_element_type=F32)
            term = lax.dot_general(error, decoder, OVER_COLS, preferred_element_type=F32)
            totals[chain] = term if totals[chain] is None else totals[chain] + term
        blocks.append(block)
    return blocks, totals


def back_kernel(slots, first, starts, *refs):
    count = 2 * len(slots)
    shards, (stacked, *both_t), (*before, outer, back) = refs[:count], refs[count:count + 3], refs[count + 3:]
    blocks, totals = back_products(slots, starts, shards, stacked, both_t, None if first else before[0])
    for i, block in enumerate(blocks):
        outer[i] = block
    for chain in range(2):
        back[chain] = totals[chain]


def last_back_kernel(slots, far, starts, *refs):
    near_refs, (before, same, back_own, sent, high) = refs[:-5], refs[-5:]
    shards, (stacked, *both_t), outers = near_refs[:2], near_refs[2:5], near_refs[5:]
    (block,), totals = back_products((far,), starts, shards, stacked, both_t, before)
    rows, wide = shards[0].shape
    lat = high.shape[1]
    half_width = high.shape[0]
    for chain in range(2):
        back_own[chain * rows:(chain + 1) * rows, :] = totals[chain][:, :lat]
        sent[chain * rows:(chain + 1) * rows, :] = totals[chain][:, lat:]
    same[...] = block[:lat]
    pieces = [(far, block[lat:])]
    for group, outer in zip(slots, outers):
        pieces += [(slot, outer[i, lat:]) for i, slot in enumerate(group)]
    for slot, piece in pieces:
        start = pl.multiple_of(starts[slot], wide)

        @pl.when(start < half_width)
        def _():
            for c in range(0, wide, lat):
                sent[pl.ds(2 * rows + start + c, lat), :] = piece[:, c:c + lat]

        @pl.when(start >= half_width)
        def _():
            for c in range(0, wide, lat):
                high[pl.ds(start - half_width + c, lat), :] = piece[:, c:c + lat]


def place_kernel(slots, far, starts, *refs):
    last, *outers, same, sems = refs
    lat, wide = last.shape
    blocks = [(far, last)]
    for group, outer in zip(slots, outers):
        blocks += [(slot, outer.at[i, :lat, :]) for i, slot in enumerate(group)]
    copies = []
    for i, (slot, block) in enumerate(blocks):
        copies.append(pltpu.make_async_copy(block, same.at[0, :, block_of(starts, slot, wide)], sems.at[i]))
        copies[-1].start()
    for copy in copies:
        copy.wait()


def finish_kernel(starts, turned, preact, back_own, arrived, high, grad, bias, cross, stage, grad_sems, cross_sems):
    pieces, height, lat = stage.shape
    rows = preact.shape[0]
    half_width = high.shape[0]
    copies = []
    first = starts[starts.shape[0] - 1] == 0
    for c in range(half_width // lat):
        at = pl.ds(c * lat, lat)

        @pl.when(first)
        def _():
            source = arrived.at[pl.ds(rows + c * lat, lat), :]
            pltpu.make_async_copy(source, cross.at[:, at], cross_sems.at[c]).start()

        @pl.when(jnp.logical_not(first))
        def _():
            pltpu.make_async_copy(high.at[at, :], cross.at[:, at], cross_sems.at[c]).start()

        copies.append(pltpu.make_async_copy(high.at[at, :], cross.at[:, at], cross_sems.at[c]))
    value = jnp.where(preact[...] > 0, back_own[...] + arrived[:rows, :], 0.0).astype(BF16)
    for i in range(pieces):
        at = pl.ds(i * height, height)
        stage[i] = jnp.dot(turned[at, :], value, preferred_element_type=F32)
        copies.append(pltpu.make_async_copy(stage.at[i], grad.at[0, at, :], grad_sems.at[i]))
        copies[-1].start()
    bias[...] = jnp.sum(value.astype(F32), axis=0, keepdims=True)
    for copy in copies:
        copy.wait()


def ring_shards(residual_in, targets, enc_weight, enc_bias, dec_same, dec_cross):
    size = lax.axis_size("latent")
    reach = size // 2
    place = ring_place(lax.axis_index("latent"), size)
    layer = lax.axis_index("layer")
    sign = jnp.where(layer % 2 == 0, 1, -1)
    rows, wide = residual_in.shape[1:]
    half = rows // 2
    deep, lat = enc_weight.shape[1:]
    half_width = deep // 2
    err_scale = 1.0 / math.sqrt(rows)
    shape = jax.ShapeDtypeStruct
    unit = rows * wide * lat
    chains = (0, 1)

    def halves(array):
        return [array[:half], array[half:]]

    slot_p = {s: 2 * s - 1 for s in range(1, reach)}
    slot_q = {s: 2 * s for s in range(1, reach)}
    far = size - 1
    offsets = [0] * size
    offsets[far] = reach
    for s in range(1, reach):
        offsets[slot_p[s]] = -s
        offsets[slot_q[s]] = s
    starts = jnp.stack([ring_member(place + sign * offset, size) * wide for offset in offsets] + [layer])
    starts = starts.astype(jnp.int32)

    urgent, later = ((0, 1), (1, -1)), ((0, -1), (1, 1))

    def gather_step(found, s, ready=None):
        for chain, way in urgent + later if s < reach else urgent:
            slots = slot_p if way == 1 else slot_q
            shard = found[chain][slots[s - 1] if s > 1 else 0]
            if ready is not None and (chain, way) in later:
                shard = after(shard, ready[chain])
            found[chain][slots[s] if s < reach else far] = hop(shard, way)

    def both_chains(found, slots):
        return [found[chain][slot] for slot in slots for chain in chains]

    def encode(slots, before):
        first, last = slots[0] == 0, slots[-1] == far
        return call(
            functools.partial(encode_kernel, slots, first, last),
            [shape((rows, lat), F32)] + ([shape((rows, lat), BF16)] if last else []),
            2 * unit * len(slots),
            [starts] + both_chains(inputs, slots) + [enc_weight, before],
        )

    inputs = [[part] + [None] * (size - 1) for part in halves(residual_in[0])]
    turned_own = []
    for chain in chains:
        source = inputs[chain][0]
        turned_own += call(turn_own_kernel, [shape((wide, half), BF16)], 0, [starts, source])
    for s in range(1, reach + 1):
        gather_step(inputs, s, turned_own if s == 1 else None)
    low_cross = passed_along(after(dec_cross, inputs[0][slot_p.get(1, far)]), "layer", 1)
    stacked = jnp.concatenate([dec_same[0], jnp.concatenate([low_cross, dec_cross], axis=1)], axis=0)
    part = encode(tuple(range(far)), after(enc_bias, stacked))[0]
    preact, codes = encode((far,), part)
    earlier = passed_along(codes, "layer", 1)

    def spread(slots, dtypes, turned):
        outs = []
        for chain in chains:
            outs += [shape((half, wide), dtypes[chain].get(slot, F32)) for slot in slots]
            outs += [shape((2 * lat, half), BF16)] if turned else []
        found = call(
            functools.partial(spread_kernel, slots), outs, 4 * unit * len(slots), [starts, codes, earlier, stacked]
        )
        return found[:len(outs) // 2], found[len(outs) // 2:]

    rest = tuple(slot for slot in range(size) if slot != far)
    instant = ({far: BF16, slot_p.get(reach - 1): BF16}, {far: BF16, slot_q.get(reach - 1): BF16})
    far_0, far_1 = spread((far,), instant, False)
    moving = {(0, 1): hop(far_0[0], 1), (1, -1): hop(far_1[0], -1)}
    partial, both_t = [], []
    for pieces in spread(rest, instant, True):
        partial.append(dict(zip(rest, pieces)))
        both_t.append(pieces[-1])
    before = []
    for s in range(reach - 1, 0, -1):
        landed = [moving[loop] for loop in urgent]
        for chain, way in urgent + later:
            message = partial[chain][slot_q[s] if way == 1 else slot_p[s]]
            if (chain, way) in moving:
                message = (message + moving[chain, way].astype(F32)).astype(BF16)
            if (chain, way) in later and before:
                message = after(message, *before)
            moving[chain, way] = hop(message, way)
        before = landed
    errors = []
    for chain, wanted in zip(chains, halves(targets[0])):
        total = partial[chain][0]
        for way in (1, -1):
            if (chain, way) in moving:
                total = total + moving[chain, way].astype(F32)
        if chain == 1:
            wanted = after(wanted, codes)
        errors.append([((total - wanted.astype(F32)) * err_scale).astype(BF16)] + [None] * (size - 1))

    def back(slots, before):
        return call(
            functools.partial(back_kernel, slots, before is None),
            [shape((len(slots), 2 * lat, wide), F32), shape((2, half, 2 * lat), F32)],
            4 * unit * len(slots),
            [starts] + both_chains(errors, slots) + [stacked] + both_t + ([] if before is None else [before]),
        )

    groups, outers, acc, pending = [], [], None, [0]
    arrived = [after(inputs[0][1], errors[1][0])]
    turned = call(
        turn_kernel,
        [shape((deep, rows), BF16)],
        0,
        [starts] + turned_own + arrived + both_chains(inputs, range(1, size))[1:],
    )[0]
    for s in range(1, reach + 1):
        gather_step(errors, s, (turned, turned) if s == 2 else None)
    cut = 1 + 2 * min(1, reach - 1)
    groups = [group for group in (tuple(range(cut)), tuple(range(cut, far))) if group]
    outers, acc = [], None
    for group in groups:
        outer, acc = back(group, acc)
        outers.append(outer)
    last_same, back_own, sent, high = call(
        functools.partial(last_back_kernel, groups, far),
        [
            shape((lat, wide), F32),
            shape((rows, lat), F32),
            shape((rows + half_width, lat), F32),
            shape((half_width, lat), F32),
        ],
        4 * unit,
        [starts] + both_chains(errors, (far,)) + [stacked] + both_t + outers + [acc],
    )
    returned = passed_along(sent, "layer", -1)
    grad_same = call(
        functools.partial(place_kernel, groups, far),
        [shape((1, lat, deep), F32)],
        0,
        [starts, last_same] + outers,
        out_spaces=[pl.ANY],
        scratch=[pltpu.SemaphoreType.DMA((size,))],
    )[0]
    height = deep // PIECES
    grad_enc, grad_bias, grad_cross = call(
        finish_kernel,
        [shape((1, deep, lat), F32), shape((1, lat), F32), shape((lat, half_width), F32)],
        2 * unit * size,
        [starts, turned, preact, back_own, returned, high],
        out_spaces=[pl.ANY, pltpu.VMEM, pl.ANY],
        scratch=[
            pltpu.VMEM((PIECES, height, lat), F32),
            pltpu.SemaphoreType.DMA((PIECES,)),
            pltpu.SemaphoreType.DMA((half_width // lat,)),
        ],
    )
    return (grad_enc, grad_bias, grad_same, grad_cross)


def wide_shards(residual_in, targets, enc_weight, enc_bias, dec_same, dec_cross):
    is_first = lax.axis_index("layer") == 0
    err_scale = 1.0 / math.sqrt(residual_in.shape[1])
    inputs = lax.all_gather(residual_in[0], "latent", axis=1, tiled=True)
    preact = matmul(inputs, enc_weight[0]) + enc_bias[0]
    codes_now = jnp.maximum(preact, 0.0).astype(BF16)
    earlier = passed_along(codes_now, "layer", 1)
    cross_full = lax.all_gather(dec_cross, "layer", axis=1, tiled=True)
    own_dec = dec_same[0]
    half_width = own_dec.shape[1] // 2
    recon_full = lax.psum(matmul(codes_now, own_dec) + matmul(earlier, cross_full), "latent")
    wanted = lax.all_gather(targets[0], "latent", axis=1, tiled=True)
    errors = ((recon_full - wanted.astype(F32)) * err_scale).astype(BF16)
    grad_same = matmul(codes_now, errors, OVER_ROWS)
    grad_full = matmul(earlier, errors, OVER_ROWS)
    returned = passed_along(grad_full[:, :half_width], "layer", -1)
    grad_cross = jnp.where(is_first, returned, grad_full[:, half_width:])
    from_next = passed_along(matmul(errors, cross_full, OVER_COLS), "layer", -1)
    grad_codes = matmul(errors, own_dec, OVER_COLS) + from_next
    grad_pre = jnp.where(preact > 0, grad_codes, 0.0).astype(BF16)
    grad_enc = matmul(inputs, grad_pre, OVER_ROWS)
    grad_bias = jnp.sum(grad_pre.astype(F32), axis=0)
    return (grad_enc[None], grad_bias[None], grad_same[None], grad_cross)


def solution(mesh):
    size = mesh.shape["latent"]
    placed = (
        P("layer", "groups", "latent"),
        P("layer", "groups", "latent"),
        P("layer", None, "latent"),
        P("layer", "latent"),
        P("layer", "latent", None),
        P("latent", "layer"),
    )
    return jax.shard_map(
        ring_shards if size % 2 == 0 and size <= RING_LIMIT else wide_shards,
        mesh=mesh,
        in_specs=placed,
        out_specs=(
            P(("groups", "layer"), None, "latent"),
            P(("groups", "layer"), "latent"),
            P(("groups", "layer"), "latent", None),
            P(("groups", "latent"), "layer"),
        ),
        check_vma=False,
    )
```

```python
import functools
import math

import jax
import jax.numpy as jnp
from jax import lax
from jax.experimental import pallas as pl
from jax.experimental.pallas import tpu as pltpu
from jax.sharding import PartitionSpec as P

F32 = jnp.float32
BF16 = jnp.bfloat16
OVER_ROWS = (((0,), (0,)), ((), ()))
OVER_COLS = (((1,), (1,)), ((), ()))
RING_LIMIT = 16
VMEM_BYTES = 24 * 1024 * 1024
PIECES = 4


def passed_along(shard, axis, by):
    size = lax.axis_size(axis)
    pairs = [(i, i + by) for i in range(size) if 0 <= i + by < size]
    return lax.ppermute(shard, axis, pairs)


def matmul(a, b, dims=(((1,), (0,)), ((), ()))):
    return lax.dot_general(a, b, dims, preferred_element_type=F32)


def ring_order(size):
    return [2 * p if p < size // 2 else 2 * (size - 1 - p) + 1 for p in range(size)]


def ring_member(place, size):
    place = lax.rem(place + 2 * size, size)
    return jnp.where(place < size // 2, 2 * place, 2 * (size - 1 - place) + 1)


def ring_place(member, size):
    return jnp.where(member % 2 == 0, member // 2, size - 1 - member // 2)


def hop(shard, way):
    size, layers = lax.axis_size("latent"), lax.axis_size("layer")
    order = ring_order(size)
    pairs = []
    for p in range(size):
        for layer in range(layers):
            by = way if layer % 2 == 0 else -way
            pairs.append((order[p] * layers + layer, order[(p + by) % size] * layers + layer))
    return lax.ppermute(shard, ("latent", "layer"), pairs)


def after(value, *others):
    return lax.optimization_barrier((value,) + others)[0]


def call(kernel, outs, flops, operands, spaces=None, out_spaces=None, scratch=(), aliases=None):
    def spec(space):
        return pl.BlockSpec(memory_space=space)

    spaces = spaces or [pltpu.VMEM] * (len(operands) - 1)
    out_spaces = out_spaces or [pltpu.VMEM] * len(outs)
    return pl.pallas_call(
        kernel,
        out_shape=outs,
        in_specs=[spec(pltpu.SMEM)] + [spec(space) for space in spaces],
        out_specs=[spec(space) for space in out_spaces],
        scratch_shapes=list(scratch),
        input_output_aliases=aliases or {},
        compiler_params=pltpu.CompilerParams(vmem_limit_bytes=VMEM_BYTES),
        cost_estimate=pl.CostEstimate(flops=flops, bytes_accessed=1024, transcendentals=0),
    )(*operands)


def block_of(starts, slot, wide):
    return pl.ds(pl.multiple_of(starts[slot], wide), wide)


def encode_kernel(slots, first, last, starts, *refs):
    count = 2 * len(slots)
    shards, (weight, before, *outs) = refs[:count], refs[count:]
    rows, wide = shards[0].shape
    for chain in range(2):
        at = slice(chain * rows, (chain + 1) * rows)
        total = jnp.broadcast_to(before[...], (rows, before.shape[1])) if first else before[at, :]
        for i, slot in enumerate(slots):
            block = weight[0, block_of(starts, slot, wide), :]
            total = total + jnp.dot(shards[2 * i + chain][...], block, preferred_element_type=F32)
        outs[0][at, :] = total
        if last:
            outs[1][at, :] = jnp.maximum(total, 0.0).astype(BF16)


def turn_own_kernel(starts, shard, *refs):
    refs[-1][...] = shard[...].T


def turn_kernel(starts, own_0, own_1, *refs):
    *shards, turned = refs
    rows, wide = shards[0].shape
    for chain, own in enumerate((own_0, own_1)):
        turned[block_of(starts, 0, wide), chain * rows:(chain + 1) * rows] = own[...]
    for k in range(len(shards) // 2):
        at = block_of(starts, k + 1, wide)
        for chain in range(2):
            turned[at, chain * rows:(chain + 1) * rows] = shards[2 * k + chain][...].T


def spread_kernel(slots, starts, codes, earlier, stacked, *outs):
    rows = codes.shape[0] // 2
    outs = list(outs)
    for chain in range(2):
        at = slice(chain * rows, (chain + 1) * rows)
        both = jnp.concatenate([codes[at, :], earlier[at, :]], axis=1)
        for slot in slots:
            partial = outs.pop(0)
            block = stacked[:, block_of(starts, slot, partial.shape[1])]
            partial[...] = jnp.dot(both, block, preferred_element_type=F32).astype(partial.dtype)
        if len(outs) > (1 - chain) * len(slots):
            outs.pop(0)[...] = both.T


def back_products(slots, starts, shards, stacked, both_t, before):
    wide = shards[0].shape[1]
    blocks, totals = [], [None, None] if before is None else [before[0], before[1]]
    for i, slot in enumerate(slots):
        decoder = stacked[:, block_of(starts, slot, wide)]
        block = 0.0
        for chain in range(2):
            error = shards[2 * i + chain][...]
            block = block + jnp.dot(both_t[chain][...], error, preferred_element_type=F32)
            term = lax.dot_general(error, decoder, OVER_COLS, preferred_element_type=F32)
            totals[chain] = term if totals[chain] is None else totals[chain] + term
        blocks.append(block)
    return blocks, totals


def back_kernel(slots, first, starts, *refs):
    count = 2 * len(slots)
    shards, (stacked, *both_t), (*before, outer, back) = refs[:count], refs[count:count + 3], refs[count + 3:]
    blocks, totals = back_products(slots, starts, shards, stacked, both_t, None if first else before[0])
    for i, block in enumerate(blocks):
        outer[i] = block
    for chain in range(2):
        back[chain] = totals[chain]


def last_back_kernel(slots, far, starts, *refs):
    near_refs, (before, same, back_own, sent, high) = refs[:-5], refs[-5:]
    shards, (stacked, *both_t), outers = near_refs[:2], near_refs[2:5], near_refs[5:]
    (block,), totals = back_products((far,), starts, shards, stacked, both_t, before)
    rows, wide = shards[0].shape
    lat = high.shape[1]
    half_width = high.shape[0]
    for chain in range(2):
        back_own[chain * rows:(chain + 1) * rows, :] = totals[chain][:, :lat]
        sent[chain * rows:(chain + 1) * rows, :] = totals[chain][:, lat:].astype(BF16)
    same[...] = block[:lat]
    pieces = [(far, block[lat:])]
    for group, outer in zip(slots, outers):
        pieces += [(slot, outer[i, lat:]) for i, slot in enumerate(group)]
    for slot, piece in pieces:
        start = pl.multiple_of(starts[slot], wide)

        @pl.when(start < half_width)
        def _():
            for c in range(0, wide, lat):
                sent[pl.ds(2 * rows + start + c, lat), :] = piece[:, c:c + lat].astype(BF16)

        @pl.when(start >= half_width)
        def _():
            for c in range(0, wide, lat):
                high[pl.ds(start - half_width + c, lat), :] = piece[:, c:c + lat]


def place_kernel(slots, far, starts, *refs):
    last, *outers, same, sems = refs
    lat, wide = last.shape
    blocks = [(far, last)]
    for group, outer in zip(slots, outers):
        blocks += [(slot, outer.at[i, :lat, :]) for i, slot in enumerate(group)]
    copies = []
    for i, (slot, block) in enumerate(blocks):
        copies.append(pltpu.make_async_copy(block, same.at[0, :, block_of(starts, slot, wide)], sems.at[i]))
        copies[-1].start()
    for copy in copies:
        copy.wait()


def finish_kernel(
    starts, turned, preact, back_own, arrived, high, grad, bias, cross, stage, cross_stage, grad_sems, cross_sems
):
    pieces, height, lat = stage.shape
    rows = preact.shape[0]
    half_width = high.shape[0]
    copies = []
    first = starts[starts.shape[0] - 1] == 0
    cross_stage[...] = jnp.where(first, arrived[rows:, :].astype(F32), high[...])
    for c in range(half_width // lat):
        at = pl.ds(c * lat, lat)
        copies.append(pltpu.make_async_copy(cross_stage.at[at, :], cross.at[:, at], cross_sems.at[c]))
        copies[-1].start()
    value = jnp.where(preact[...] > 0, back_own[...] + arrived[:rows, :].astype(F32), 0.0).astype(BF16)
    for i in range(pieces):
        at = pl.ds(i * height, height)
        stage[i] = jnp.dot(turned[at, :], value, preferred_element_type=F32)
        copies.append(pltpu.make_async_copy(stage.at[i], grad.at[0, at, :], grad_sems.at[i]))
        copies[-1].start()
    bias[...] = jnp.sum(value.astype(F32), axis=0, keepdims=True)
    for copy in copies:
        copy.wait()


def ring_shards(residual_in, targets, enc_weight, enc_bias, dec_same, dec_cross):
    size = lax.axis_size("latent")
    reach = size // 2
    place = ring_place(lax.axis_index("latent"), size)
    layer = lax.axis_index("layer")
    sign = jnp.where(layer % 2 == 0, 1, -1)
    rows, wide = residual_in.shape[1:]
    half = rows // 2
    deep, lat = enc_weight.shape[1:]
    half_width = deep // 2
    err_scale = 1.0 / math.sqrt(rows)
    shape = jax.ShapeDtypeStruct
    unit = rows * wide * lat
    chains = (0, 1)

    def halves(array):
        return [array[:half], array[half:]]

    slot_p = {s: 2 * s - 1 for s in range(1, reach)}
    slot_q = {s: 2 * s for s in range(1, reach)}
    far = size - 1
    offsets = [0] * size
    offsets[far] = reach
    for s in range(1, reach):
        offsets[slot_p[s]] = -s
        offsets[slot_q[s]] = s
    starts = jnp.stack([ring_member(place + sign * offset, size) * wide for offset in offsets] + [layer])
    starts = starts.astype(jnp.int32)

    urgent, later = ((0, -1), (1, 1)), ((0, 1), (1, -1))

    def gather_step(found, s, ready=None):
        for chain, way in urgent + later if s < reach else urgent:
            slots = slot_p if way == 1 else slot_q
            shard = found[chain][slots[s - 1] if s > 1 else 0]
            if ready is not None and (chain, way) in later:
                shard = after(shard, ready[chain])
            found[chain][slots[s] if s < reach else far] = hop(shard, way)

    def both_chains(found, slots):
        return [found[chain][slot] for slot in slots for chain in chains]

    def encode(slots, before):
        first, last = slots[0] == 0, slots[-1] == far
        return call(
            functools.partial(encode_kernel, slots, first, last),
            [shape((rows, lat), F32)] + ([shape((rows, lat), BF16)] if last else []),
            2 * unit * len(slots),
            [starts] + both_chains(inputs, slots) + [enc_weight, before],
        )

    inputs = [[part] + [None] * (size - 1) for part in halves(residual_in[0])]
    turned_own = []
    for chain in chains:
        source = inputs[chain][0]
        turned_own += call(turn_own_kernel, [shape((wide, half), BF16)], 0, [starts, source])
    for s in range(1, reach + 1):
        gather_step(inputs, s, turned_own if s == 1 else None)
    low_cross = passed_along(after(dec_cross, inputs[0][slot_p.get(1, far)]), "layer", 1)
    stacked = jnp.concatenate([dec_same[0], jnp.concatenate([low_cross, dec_cross], axis=1)], axis=0)
    part = encode(tuple(range(far)), after(enc_bias, stacked))[0]
    preact, codes = encode((far,), part)
    earlier = passed_along(codes, "layer", 1)

    def spread(slots, dtypes, turned):
        outs = []
        for chain in chains:
            outs += [shape((half, wide), dtypes[chain].get(slot, F32)) for slot in slots]
            outs += [shape((2 * lat, half), BF16)] if turned else []
        found = call(
            functools.partial(spread_kernel, slots), outs, 4 * unit * len(slots), [starts, codes, earlier, stacked]
        )
        return found[:len(outs) // 2], found[len(outs) // 2:]

    rest = tuple(slot for slot in range(size) if slot != far)
    instant = tuple({far: BF16, (slot_q if way == 1 else slot_p).get(reach - 1): BF16} for _, way in later)
    far_0, far_1 = spread((far,), instant, False)
    moving = {loop: hop(message, loop[1]) for loop, message in zip(urgent, (far_0[0], far_1[0]))}
    partial, both_t = [], []
    for pieces in spread(rest, instant, True):
        partial.append(dict(zip(rest, pieces)))
        both_t.append(pieces[-1])
    before = []
    for s in range(reach - 1, 0, -1):
        landed = [moving[loop] for loop in urgent]
        for chain, way in urgent + later:
            message = partial[chain][slot_q[s] if way == 1 else slot_p[s]]
            if (chain, way) in moving:
                message = (message + moving[chain, way].astype(F32)).astype(BF16)
            if (chain, way) in later and before:
                message = after(message, *before)
            moving[chain, way] = hop(message, way)
        before = landed
    errors = []
    for chain, wanted in zip(chains, halves(targets[0])):
        total = partial[chain][0]
        for way in (1, -1):
            if (chain, way) in moving:
                total = total + moving[chain, way].astype(F32)
        if chain == 1:
            wanted = after(wanted, codes)
        errors.append([((total - wanted.astype(F32)) * err_scale).astype(BF16)] + [None] * (size - 1))

    def back(slots, before):
        return call(
            functools.partial(back_kernel, slots, before is None),
            [shape((len(slots), 2 * lat, wide), F32), shape((2, half, 2 * lat), F32)],
            4 * unit * len(slots),
            [starts] + both_chains(errors, slots) + [stacked] + both_t + ([] if before is None else [before]),
        )

    groups, outers, acc, pending = [], [], None, [0]
    arrived = [after(inputs[0][1], errors[1][0])]
    turned = call(
        turn_kernel,
        [shape((deep, rows), BF16)],
        0,
        [starts] + turned_own + arrived + both_chains(inputs, range(1, size))[1:],
    )[0]
    for s in range(1, reach + 1):
        gather_step(errors, s, (turned, turned) if s == 2 else None)
    cut = 1 + 2 * min(1, reach - 1)
    groups = [group for group in (tuple(range(cut)), tuple(range(cut, far))) if group]
    outers, acc = [], None
    for group in groups:
        outer, acc = back(group, acc)
        outers.append(outer)
    last_same, back_own, sent, high = call(
        functools.partial(last_back_kernel, groups, far),
        [
            shape((lat, wide), F32),
            shape((rows, lat), F32),
            shape((rows + half_width, lat), BF16),
            shape((half_width, lat), F32),
        ],
        4 * unit,
        [starts] + both_chains(errors, (far,)) + [stacked] + both_t + outers + [acc],
    )
    returned = passed_along(sent, "layer", -1)
    grad_same = call(
        functools.partial(place_kernel, groups, far),
        [shape((1, lat, deep), F32)],
        0,
        [starts, last_same] + outers,
        out_spaces=[pl.ANY],
        scratch=[pltpu.SemaphoreType.DMA((size,))],
    )[0]
    height = deep // PIECES
    grad_enc, grad_bias, grad_cross = call(
        finish_kernel,
        [shape((1, deep, lat), F32), shape((1, lat), F32), shape((lat, half_width), F32)],
        2 * unit * size,
        [starts, turned, preact, back_own, returned, high],
        out_spaces=[pl.ANY, pltpu.VMEM, pl.ANY],
        scratch=[
            pltpu.VMEM((PIECES, height, lat), F32),
            pltpu.VMEM((half_width, lat), F32),
            pltpu.SemaphoreType.DMA((PIECES,)),
            pltpu.SemaphoreType.DMA((half_width // lat,)),
        ],
    )
    return (grad_enc, grad_bias, grad_same, grad_cross)


def wide_shards(residual_in, targets, enc_weight, enc_bias, dec_same, dec_cross):
    is_first = lax.axis_index("layer") == 0
    err_scale = 1.0 / math.sqrt(residual_in.shape[1])
    inputs = lax.all_gather(residual_in[0], "latent", axis=1, tiled=True)
    preact = matmul(inputs, enc_weight[0]) + enc_bias[0]
    codes_now = jnp.maximum(preact, 0.0).astype(BF16)
    earlier = passed_along(codes_now, "layer", 1)
    cross_full = lax.all_gather(dec_cross, "layer", axis=1, tiled=True)
    own_dec = dec_same[0]
    half_width = own_dec.shape[1] // 2
    recon_full = lax.psum(matmul(codes_now, own_dec) + matmul(earlier, cross_full), "latent")
    wanted = lax.all_gather(targets[0], "latent", axis=1, tiled=True)
    errors = ((recon_full - wanted.astype(F32)) * err_scale).astype(BF16)
    grad_same = matmul(codes_now, errors, OVER_ROWS)
    grad_full = matmul(earlier, errors, OVER_ROWS)
    returned = passed_along(grad_full[:, :half_width], "layer", -1)
    grad_cross = jnp.where(is_first, returned, grad_full[:, half_width:])
    from_next = passed_along(matmul(errors, cross_full, OVER_COLS), "layer", -1)
    grad_codes = matmul(errors, own_dec, OVER_COLS) + from_next
    grad_pre = jnp.where(preact > 0, grad_codes, 0.0).astype(BF16)
    grad_enc = matmul(inputs, grad_pre, OVER_ROWS)
    grad_bias = jnp.sum(grad_pre.astype(F32), axis=0)
    return (grad_enc[None], grad_bias[None], grad_same[None], grad_cross)


def solution(mesh):
    size = mesh.shape["latent"]
    placed = (
        P("layer", "groups", "latent"),
        P("layer", "groups", "latent"),
        P("layer", None, "latent"),
        P("layer", "latent"),
        P("layer", "latent", None),
        P("latent", "layer"),
    )
    return jax.shard_map(
        ring_shards if size % 2 == 0 and size <= RING_LIMIT else wide_shards,
        mesh=mesh,
        in_specs=placed,
        out_specs=(
            P(("groups", "layer"), None, "latent"),
            P(("groups", "layer"), "latent"),
            P(("groups", "layer"), "latent", None),
            P(("groups", "latent"), "layer"),
        ),
        check_vma=False,
    )
```

```python
import functools
import math

import jax
import jax.numpy as jnp
from jax import lax
from jax.experimental import pallas as pl
from jax.experimental.pallas import tpu as pltpu
from jax.sharding import PartitionSpec as P

F32 = jnp.float32
BF16 = jnp.bfloat16
OVER_ROWS = (((0,), (0,)), ((), ()))
OVER_COLS = (((1,), (1,)), ((), ()))
RING_LIMIT = 16
VMEM_BYTES = 24 * 1024 * 1024
PIECES = 8


def passed_along(shard, axis, by):
    size = lax.axis_size(axis)
    pairs = [(i, i + by) for i in range(size) if 0 <= i + by < size]
    return lax.ppermute(shard, axis, pairs)


def matmul(a, b, dims=(((1,), (0,)), ((), ()))):
    return lax.dot_general(a, b, dims, preferred_element_type=F32)


def ring_order(size):
    return [2 * p if p < size // 2 else 2 * (size - 1 - p) + 1 for p in range(size)]


def ring_member(place, size):
    place = lax.rem(place + 2 * size, size)
    return jnp.where(place < size // 2, 2 * place, 2 * (size - 1 - place) + 1)


def ring_place(member, size):
    return jnp.where(member % 2 == 0, member // 2, size - 1 - member // 2)


def hop(shard, way):
    size, layers = lax.axis_size("latent"), lax.axis_size("layer")
    order = ring_order(size)
    pairs = []
    for p in range(size):
        for layer in range(layers):
            by = way if layer % 2 == 0 else -way
            pairs.append((order[p] * layers + layer, order[(p + by) % size] * layers + layer))
    return lax.ppermute(shard, ("latent", "layer"), pairs)


def after(value, *others):
    return lax.optimization_barrier((value,) + others)[0]


def call(kernel, outs, flops, operands, spaces=None, out_spaces=None, scratch=(), aliases=None):
    def spec(space):
        return pl.BlockSpec(memory_space=space)

    spaces = spaces or [pltpu.VMEM] * (len(operands) - 1)
    out_spaces = out_spaces or [pltpu.VMEM] * len(outs)
    return pl.pallas_call(
        kernel,
        out_shape=outs,
        in_specs=[spec(pltpu.SMEM)] + [spec(space) for space in spaces],
        out_specs=[spec(space) for space in out_spaces],
        scratch_shapes=list(scratch),
        input_output_aliases=aliases or {},
        compiler_params=pltpu.CompilerParams(vmem_limit_bytes=VMEM_BYTES),
        cost_estimate=pl.CostEstimate(flops=flops, bytes_accessed=1024, transcendentals=0),
    )(*operands)


def block_of(starts, slot, wide):
    return pl.ds(pl.multiple_of(starts[slot], wide), wide)


def encode_kernel(slots, first, last, starts, *refs):
    count = 2 * len(slots)
    shards, (weight, before, *outs) = refs[:count], refs[count:]
    rows, wide = shards[0].shape
    for chain in range(2):
        at = slice(chain * rows, (chain + 1) * rows)
        total = jnp.broadcast_to(before[...], (rows, before.shape[1])) if first else before[at, :]
        for i, slot in enumerate(slots):
            block = weight[0, block_of(starts, slot, wide), :]
            total = total + jnp.dot(shards[2 * i + chain][...], block, preferred_element_type=F32)
        outs[0][at, :] = total
        if last:
            outs[1][at, :] = jnp.maximum(total, 0.0).astype(BF16)


def turn_own_kernel(starts, shard, *refs):
    refs[-1][...] = shard[...].T


def turn_kernel(starts, own_0, own_1, *refs):
    *shards, turned = refs
    rows, wide = shards[0].shape
    for chain, own in enumerate((own_0, own_1)):
        turned[block_of(starts, 0, wide), chain * rows:(chain + 1) * rows] = own[...]
    for k in range(len(shards) // 2):
        at = block_of(starts, k + 1, wide)
        for chain in range(2):
            turned[at, chain * rows:(chain + 1) * rows] = shards[2 * k + chain][...].T


def spread_kernel(slots, starts, codes, earlier, stacked, *outs):
    rows = codes.shape[0] // 2
    outs = list(outs)
    for chain in range(2):
        at = slice(chain * rows, (chain + 1) * rows)
        both = jnp.concatenate([codes[at, :], earlier[at, :]], axis=1)
        for slot in slots:
            partial = outs.pop(0)
            block = stacked[:, block_of(starts, slot, partial.shape[1])]
            partial[...] = jnp.dot(both, block, preferred_element_type=F32).astype(partial.dtype)
        if len(outs) > (1 - chain) * len(slots):
            outs.pop(0)[...] = both.T


def back_products(slots, starts, shards, stacked, both_t, before):
    wide = shards[0].shape[1]
    blocks, totals = [], [None, None] if before is None else [before[0], before[1]]
    for i, slot in enumerate(slots):
        decoder = stacked[:, block_of(starts, slot, wide)]
        block = 0.0
        for chain in range(2):
            error = shards[2 * i + chain][...]
            block = block + jnp.dot(both_t[chain][...], error, preferred_element_type=F32)
            term = lax.dot_general(error, decoder, OVER_COLS, preferred_element_type=F32)
            totals[chain] = term if totals[chain] is None else totals[chain] + term
        blocks.append(block)
    return blocks, totals


def back_kernel(slots, first, starts, *refs):
    count = 2 * len(slots)
    shards, (stacked, *both_t), (*before, outer, back) = refs[:count], refs[count:count + 3], refs[count + 3:]
    blocks, totals = back_products(slots, starts, shards, stacked, both_t, None if first else before[0])
    for i, block in enumerate(blocks):
        outer[i] = block
    for chain in range(2):
        back[chain] = totals[chain]


def cross_back_kernel(slots, far, starts, *refs):
    shards, (stacked, *both_t), outers, (before, sent, high) = refs[:2], refs[2:5], refs[5:-3], refs[-3:]
    rows, wide = shards[0].shape
    half_width, lat = high.shape

    @pl.when(starts[starts.shape[0] - 1] != 0)
    def _():
        decoder = stacked[lat:, block_of(starts, far, wide)]
        last = 0.0
        for chain in range(2):
            error = shards[chain][...]
            last = last + jnp.dot(both_t[chain][lat:, :], error, preferred_element_type=F32)
            term = lax.dot_general(error, decoder, OVER_COLS, preferred_element_type=F32)
            sent[chain * rows:(chain + 1) * rows, :] = (before[chain, :, lat:] + term).astype(BF16)
        pieces = [(far, last)]
        for group, outer in zip(slots, outers):
            pieces += [(slot, outer[i, lat:]) for i, slot in enumerate(group)]
        for slot, piece in pieces:
            start = pl.multiple_of(starts[slot], wide)

            @pl.when(start < half_width)
            def _():
                for c in range(0, wide, lat):
                    sent[pl.ds(2 * rows + start + c, lat), :] = piece[:, c:c + lat].astype(BF16)

            @pl.when(start >= half_width)
            def _():
                for c in range(0, wide, lat):
                    high[pl.ds(start - half_width + c, lat), :] = piece[:, c:c + lat]


def own_back_kernel(slots, far, starts, *refs):
    shards, (stacked, *both_t), refs = refs[:2], refs[2:5], refs[5:]
    outers, (before, back_own, same, last, sems) = refs[:-5], refs[-5:]
    rows, wide = shards[0].shape
    lat = back_own.shape[1]
    blocks = []
    for group, outer in zip(slots, outers):
        blocks += [(slot, outer.at[i, :lat, :]) for i, slot in enumerate(group)]
    blocks.append((far, last))
    copies = []
    for i, (slot, block) in enumerate(blocks):
        copies.append(pltpu.make_async_copy(block, same.at[0, :, block_of(starts, slot, wide)], sems.at[i]))
    for copy in copies[:-1]:
        copy.start()
    decoder = stacked[:lat, block_of(starts, far, wide)]
    total = 0.0
    for chain in range(2):
        error = shards[chain][...]
        total = total + jnp.dot(both_t[chain][:lat, :], error, preferred_element_type=F32)
        term = lax.dot_general(error, decoder, OVER_COLS, preferred_element_type=F32)
        back_own[chain * rows:(chain + 1) * rows, :] = before[chain, :, :lat] + term
    last[...] = total
    copies[-1].start()
    for copy in copies:
        copy.wait()


def finish_kernel(
    starts, turned, preact, back_own, arrived, high, grad, bias, cross, stage, cross_stage, grad_sems, cross_sems
):
    pieces, height, lat = stage.shape
    rows = preact.shape[0]
    half_width = high.shape[0]
    copies = []
    first = starts[starts.shape[0] - 1] == 0

    @pl.when(first)
    def _():
        cross_stage[...] = arrived[rows:, :].astype(F32)

    @pl.when(jnp.logical_not(first))
    def _():
        cross_stage[...] = high[...]

    for c in range(half_width // lat):
        at = pl.ds(c * lat, lat)
        copies.append(pltpu.make_async_copy(cross_stage.at[at, :], cross.at[:, at], cross_sems.at[c]))
        copies[-1].start()
    value = jnp.where(preact[...] > 0, back_own[...] + arrived[:rows, :].astype(F32), 0.0).astype(BF16)
    for i in range(pieces):
        at = pl.ds(i * height, height)
        stage[i] = jnp.dot(turned[at, :], value, preferred_element_type=F32)
        copies.append(pltpu.make_async_copy(stage.at[i], grad.at[0, at, :], grad_sems.at[i]))
        copies[-1].start()
    bias[...] = jnp.sum(value.astype(F32), axis=0, keepdims=True)
    for copy in copies:
        copy.wait()


def ring_shards(residual_in, targets, enc_weight, enc_bias, dec_same, dec_cross):
    size = lax.axis_size("latent")
    reach = size // 2
    place = ring_place(lax.axis_index("latent"), size)
    layer = lax.axis_index("layer")
    sign = jnp.where(layer % 2 == 0, 1, -1)
    rows, wide = residual_in.shape[1:]
    half = rows // 2
    deep, lat = enc_weight.shape[1:]
    half_width = deep // 2
    err_scale = 1.0 / math.sqrt(rows)
    shape = jax.ShapeDtypeStruct
    unit = rows * wide * lat
    chains = (0, 1)

    def halves(array):
        return [array[:half], array[half:]]

    slot_p = {s: 2 * s - 1 for s in range(1, reach)}
    slot_q = {s: 2 * s for s in range(1, reach)}
    far = size - 1
    offsets = [0] * size
    offsets[far] = reach
    for s in range(1, reach):
        offsets[slot_p[s]] = -s
        offsets[slot_q[s]] = s
    starts = jnp.stack([ring_member(place + sign * offset, size) * wide for offset in offsets] + [layer])
    starts = starts.astype(jnp.int32)

    urgent, later = ((0, -1), (1, 1)), ((0, 1), (1, -1))

    def gather_step(found, s, ready=None):
        for chain, way in urgent + later if s < reach else urgent:
            slots = slot_p if way == 1 else slot_q
            shard = found[chain][slots[s - 1] if s > 1 else 0]
            if ready is not None and (chain, way) in later:
                shard = after(shard, ready[chain])
            found[chain][slots[s] if s < reach else far] = hop(shard, way)

    def both_chains(found, slots):
        return [found[chain][slot] for slot in slots for chain in chains]

    def encode(slots, before):
        first, last = slots[0] == 0, slots[-1] == far
        return call(
            functools.partial(encode_kernel, slots, first, last),
            [shape((rows, lat), F32)] + ([shape((rows, lat), BF16)] if last else []),
            2 * unit * len(slots),
            [starts] + both_chains(inputs, slots) + [enc_weight, before],
        )

    inputs = [[part] + [None] * (size - 1) for part in halves(residual_in[0])]
    turned_own = []
    for chain in chains:
        source = inputs[chain][0]
        turned_own += call(turn_own_kernel, [shape((wide, half), BF16)], 0, [starts, source])
    for s in range(1, reach + 1):
        gather_step(inputs, s, turned_own if s == 1 else None)
    low_cross = passed_along(after(dec_cross, inputs[0][slot_p.get(1, far)]), "layer", 1)
    stacked = jnp.concatenate([dec_same[0], jnp.concatenate([low_cross, dec_cross], axis=1)], axis=0)
    part = encode(tuple(range(far)), after(enc_bias, stacked))[0]
    preact, codes = encode((far,), part)
    earlier = passed_along(codes, "layer", 1)

    def spread(slots, dtypes, turned):
        outs = []
        for chain in chains:
            outs += [shape((half, wide), dtypes[chain].get(slot, F32)) for slot in slots]
            outs += [shape((2 * lat, half), BF16)] if turned else []
        found = call(
            functools.partial(spread_kernel, slots), outs, 4 * unit * len(slots), [starts, codes, earlier, stacked]
        )
        return found[:len(outs) // 2], found[len(outs) // 2:]

    rest = tuple(slot for slot in range(size) if slot != far)
    instant = tuple({far: BF16, (slot_q if way == 1 else slot_p).get(reach - 1): BF16} for _, way in later)
    far_0, far_1 = spread((far,), instant, False)
    moving = {loop: hop(message, loop[1]) for loop, message in zip(urgent, (far_0[0], far_1[0]))}
    partial, both_t = [], []
    for pieces in spread(rest, instant, True):
        partial.append(dict(zip(rest, pieces)))
        both_t.append(pieces[-1])
    before = []
    for s in range(reach - 1, 0, -1):
        landed = [moving[loop] for loop in urgent]
        for chain, way in urgent + later:
            message = partial[chain][slot_q[s] if way == 1 else slot_p[s]]
            if (chain, way) in moving:
                message = (message + moving[chain, way].astype(F32)).astype(BF16)
            if (chain, way) in later and before:
                message = after(message, *before)
            moving[chain, way] = hop(message, way)
        before = landed
    errors = []
    for chain, wanted in zip(chains, halves(targets[0])):
        total = partial[chain][0]
        for way in (1, -1):
            if (chain, way) in moving:
                total = total + moving[chain, way].astype(F32)
        if chain == 1:
            wanted = after(wanted, codes)
        errors.append([((total - wanted.astype(F32)) * err_scale).astype(BF16)] + [None] * (size - 1))

    def back(slots, before):
        return call(
            functools.partial(back_kernel, slots, before is None),
            [shape((len(slots), 2 * lat, wide), F32), shape((2, half, 2 * lat), F32)],
            4 * unit * len(slots),
            [starts] + both_chains(errors, slots) + [stacked] + both_t + ([] if before is None else [before]),
        )

    groups, outers, acc, pending = [], [], None, [0]
    arrived = [after(inputs[0][1], errors[1][0])]
    turned = call(
        turn_kernel,
        [shape((deep, rows), BF16)],
        0,
        [starts] + turned_own + arrived + both_chains(inputs, range(1, size))[1:],
    )[0]
    for s in range(1, reach + 1):
        gather_step(errors, s, (turned, turned) if s == 2 else None)
    cut = 1 + 2 * min(1, reach - 1)
    groups = [group for group in (tuple(range(cut)), tuple(range(cut, far))) if group]
    outers, acc = [], None
    for group in groups:
        outer, acc = back(group, acc)
        outers.append(outer)
    last = both_chains(errors, (far,)) + [stacked] + both_t + outers + [acc]
    sent, high = call(
        functools.partial(cross_back_kernel, groups, far),
        [shape((rows + half_width, lat), BF16), shape((half_width, lat), F32)],
        0,
        [starts] + last,
    )
    returned = passed_along(sent, "layer", -1)
    back_own, grad_same = call(
        functools.partial(own_back_kernel, groups, far),
        [shape((rows, lat), F32), shape((1, lat, deep), F32)],
        0,
        [starts] + last,
        out_spaces=[pltpu.VMEM, pl.ANY],
        scratch=[pltpu.VMEM((lat, wide), F32), pltpu.SemaphoreType.DMA((size,))],
    )
    height = deep // PIECES
    grad_enc, grad_bias, grad_cross = call(
        finish_kernel,
        [shape((1, deep, lat), F32), shape((1, lat), F32), shape((lat, half_width), F32)],
        2 * unit * size,
        [starts, turned, preact, back_own, returned, high],
        out_spaces=[pl.ANY, pltpu.VMEM, pl.ANY],
        scratch=[
            pltpu.VMEM((PIECES, height, lat), F32),
            pltpu.VMEM((half_width, lat), F32),
            pltpu.SemaphoreType.DMA((PIECES,)),
            pltpu.SemaphoreType.DMA((half_width // lat,)),
        ],
    )
    return (grad_enc, grad_bias, grad_same, grad_cross)


def wide_shards(residual_in, targets, enc_weight, enc_bias, dec_same, dec_cross):
    is_first = lax.axis_index("layer") == 0
    err_scale = 1.0 / math.sqrt(residual_in.shape[1])
    inputs = lax.all_gather(residual_in[0], "latent", axis=1, tiled=True)
    preact = matmul(inputs, enc_weight[0]) + enc_bias[0]
    codes_now = jnp.maximum(preact, 0.0).astype(BF16)
    earlier = passed_along(codes_now, "layer", 1)
    cross_full = lax.all_gather(dec_cross, "layer", axis=1, tiled=True)
    own_dec = dec_same[0]
    half_width = own_dec.shape[1] // 2
    recon_full = lax.psum(matmul(codes_now, own_dec) + matmul(earlier, cross_full), "latent")
    wanted = lax.all_gather(targets[0], "latent", axis=1, tiled=True)
    errors = ((recon_full - wanted.astype(F32)) * err_scale).astype(BF16)
    grad_same = matmul(codes_now, errors, OVER_ROWS)
    grad_full = matmul(earlier, errors, OVER_ROWS)
    returned = passed_along(grad_full[:, :half_width], "layer", -1)
    grad_cross = jnp.where(is_first, returned, grad_full[:, half_width:])
    from_next = passed_along(matmul(errors, cross_full, OVER_COLS), "layer", -1)
    grad_codes = matmul(errors, own_dec, OVER_COLS) + from_next
    grad_pre = jnp.where(preact > 0, grad_codes, 0.0).astype(BF16)
    grad_enc = matmul(inputs, grad_pre, OVER_ROWS)
    grad_bias = jnp.sum(grad_pre.astype(F32), axis=0)
    return (grad_enc[None], grad_bias[None], grad_same[None], grad_cross)


def solution(mesh):
    size = mesh.shape["latent"]
    placed = (
        P("layer", "groups", "latent"),
        P("layer", "groups", "latent"),
        P("layer", None, "latent"),
        P("layer", "latent"),
        P("layer", "latent", None),
        P("latent", "layer"),
    )
    return jax.shard_map(
        ring_shards if size % 2 == 0 and size <= RING_LIMIT else wide_shards,
        mesh=mesh,
        in_specs=placed,
        out_specs=(
            P(("groups", "layer"), None, "latent"),
            P(("groups", "layer"), "latent"),
            P(("groups", "layer"), "latent", None),
            P(("groups", "latent"), "layer"),
        ),
        check_vma=False,
    )
```

```python
import functools
import math

import jax
import jax.numpy as jnp
from jax import lax
from jax.experimental import pallas as pl
from jax.experimental.pallas import tpu as pltpu
from jax.sharding import PartitionSpec as P

F32 = jnp.float32
BF16 = jnp.bfloat16
OVER_ROWS = (((0,), (0,)), ((), ()))
OVER_COLS = (((1,), (1,)), ((), ()))
RING_LIMIT = 16
VMEM_BYTES = 24 * 1024 * 1024
PIECES = 8


def passed_along(shard, axis, by):
    size = lax.axis_size(axis)
    pairs = [(i, i + by) for i in range(size) if 0 <= i + by < size]
    return lax.ppermute(shard, axis, pairs)


def matmul(a, b, dims=(((1,), (0,)), ((), ()))):
    return lax.dot_general(a, b, dims, preferred_element_type=F32)


def ring_order(size):
    return [2 * p if p < size // 2 else 2 * (size - 1 - p) + 1 for p in range(size)]


def ring_member(place, size):
    place = lax.rem(place + 2 * size, size)
    return jnp.where(place < size // 2, 2 * place, 2 * (size - 1 - place) + 1)


def ring_place(member, size):
    return jnp.where(member % 2 == 0, member // 2, size - 1 - member // 2)


def hop(shard, way):
    size, layers = lax.axis_size("latent"), lax.axis_size("layer")
    order = ring_order(size)
    pairs = []
    for p in range(size):
        for layer in range(layers):
            by = way if layer % 2 == 0 else -way
            pairs.append((order[p] * layers + layer, order[(p + by) % size] * layers + layer))
    return lax.ppermute(shard, ("latent", "layer"), pairs)


def after(value, *others):
    return lax.optimization_barrier((value,) + others)[0]


def call(kernel, outs, flops, operands, spaces=None, out_spaces=None, scratch=(), aliases=None):
    def spec(space):
        return pl.BlockSpec(memory_space=space)

    spaces = spaces or [pltpu.VMEM] * (len(operands) - 1)
    out_spaces = out_spaces or [pltpu.VMEM] * len(outs)
    return pl.pallas_call(
        kernel,
        out_shape=outs,
        in_specs=[spec(pltpu.SMEM)] + [spec(space) for space in spaces],
        out_specs=[spec(space) for space in out_spaces],
        scratch_shapes=list(scratch),
        input_output_aliases=aliases or {},
        compiler_params=pltpu.CompilerParams(vmem_limit_bytes=VMEM_BYTES),
        cost_estimate=pl.CostEstimate(flops=flops, bytes_accessed=1024, transcendentals=0),
    )(*operands)


def block_of(starts, slot, wide):
    return pl.ds(pl.multiple_of(starts[slot], wide), wide)


def encode_kernel(slots, first, last, starts, *refs):
    count = 2 * len(slots)
    shards, (weight, before, *outs) = refs[:count], refs[count:]
    rows, wide = shards[0].shape
    for chain in range(2):
        at = slice(chain * rows, (chain + 1) * rows)
        total = jnp.broadcast_to(before[...], (rows, before.shape[1])) if first else before[at, :]
        for i, slot in enumerate(slots):
            block = weight[0, block_of(starts, slot, wide), :]
            total = total + jnp.dot(shards[2 * i + chain][...], block, preferred_element_type=F32)
        outs[0][at, :] = total
        if last:
            outs[1][at, :] = jnp.maximum(total, 0.0).astype(BF16)


def turn_own_kernel(starts, shard, *refs):
    refs[-1][...] = shard[...].T


def turn_kernel(starts, own_0, own_1, *refs):
    *shards, turned = refs
    rows, wide = shards[0].shape
    for chain, own in enumerate((own_0, own_1)):
        turned[block_of(starts, 0, wide), chain * rows:(chain + 1) * rows] = own[...]
    for k in range(len(shards) // 2):
        at = block_of(starts, k + 1, wide)
        for chain in range(2):
            turned[at, chain * rows:(chain + 1) * rows] = shards[2 * k + chain][...].T


def spread_kernel(slots, starts, codes, earlier, stacked, *outs):
    rows = codes.shape[0] // 2
    outs = list(outs)
    for chain in range(2):
        at = slice(chain * rows, (chain + 1) * rows)
        both = jnp.concatenate([codes[at, :], earlier[at, :]], axis=1)
        for slot in slots:
            partial = outs.pop(0)
            block = stacked[:, block_of(starts, slot, partial.shape[1])]
            partial[...] = jnp.dot(both, block, preferred_element_type=F32).astype(partial.dtype)
        if len(outs) > (1 - chain) * len(slots):
            outs.pop(0)[...] = both.T


def back_products(slots, starts, shards, stacked, both_t, before):
    wide = shards[0].shape[1]
    blocks, totals = [], [None, None] if before is None else [before[0], before[1]]
    for i, slot in enumerate(slots):
        decoder = stacked[:, block_of(starts, slot, wide)]
        block = 0.0
        for chain in range(2):
            error = shards[2 * i + chain][...]
            block = block + jnp.dot(both_t[chain][...], error, preferred_element_type=F32)
            term = lax.dot_general(error, decoder, OVER_COLS, preferred_element_type=F32)
            totals[chain] = term if totals[chain] is None else totals[chain] + term
        blocks.append(block)
    return blocks, totals


def back_kernel(slots, first, starts, *refs):
    count = 2 * len(slots)
    shards, (stacked, *both_t), (*before, outer, back) = refs[:count], refs[count:count + 3], refs[count + 3:]
    blocks, totals = back_products(slots, starts, shards, stacked, both_t, None if first else before[0])
    for i, block in enumerate(blocks):
        outer[i] = block
    for chain in range(2):
        back[chain] = totals[chain]


def cross_back_kernel(slots, far, starts, *refs):
    shards, (stacked, *both_t), outers, (before, sent, high) = refs[:2], refs[2:5], refs[5:-3], refs[-3:]
    rows, wide = shards[0].shape
    half_width, lat = high.shape

    @pl.when(starts[starts.shape[0] - 1] != 0)
    def _():
        decoder = stacked[lat:, block_of(starts, far, wide)]
        last = 0.0
        for chain in range(2):
            error = shards[chain][...]
            last = last + jnp.dot(both_t[chain][lat:, :], error, preferred_element_type=F32)
            term = lax.dot_general(error, decoder, OVER_COLS, preferred_element_type=F32)
            sent[chain * rows:(chain + 1) * rows, :] = (before[chain, :, lat:] + term).astype(BF16)
        pieces = [(far, last)]
        for group, outer in zip(slots, outers):
            pieces += [(slot, outer[i, lat:]) for i, slot in enumerate(group)]
        for slot, piece in pieces:
            start = pl.multiple_of(starts[slot], wide)

            @pl.when(start < half_width)
            def _():
                for c in range(0, wide, lat):
                    sent[pl.ds(2 * rows + start + c, lat), :] = piece[:, c:c + lat].astype(BF16)

            @pl.when(start >= half_width)
            def _():
                for c in range(0, wide, lat):
                    high[pl.ds(start - half_width + c, lat), :] = piece[:, c:c + lat]


def own_back_kernel(slots, far, starts, *refs):
    shards, (stacked, *both_t), refs = refs[:2], refs[2:5], refs[5:]
    outers, (before, back_own, same, last, sems) = refs[:-5], refs[-5:]
    rows, wide = shards[0].shape
    lat = back_own.shape[1]
    blocks = []
    for group, outer in zip(slots, outers):
        blocks += [(slot, outer.at[i, :lat, :]) for i, slot in enumerate(group)]
    blocks.append((far, last))
    copies = []
    for i, (slot, block) in enumerate(blocks):
        copies.append(pltpu.make_async_copy(block, same.at[0, :, block_of(starts, slot, wide)], sems.at[i]))
    for copy in copies[:-1]:
        copy.start()
    decoder = stacked[:lat, block_of(starts, far, wide)]
    total = 0.0
    for chain in range(2):
        error = shards[chain][...]
        total = total + jnp.dot(both_t[chain][:lat, :], error, preferred_element_type=F32)
        term = lax.dot_general(error, decoder, OVER_COLS, preferred_element_type=F32)
        back_own[chain * rows:(chain + 1) * rows, :] = before[chain, :, :lat] + term
    last[...] = total
    copies[-1].start()
    for copy in copies:
        copy.wait()


def finish_kernel(
    starts, turned, preact, back_own, arrived, high, grad, bias, cross, stage, cross_stage, grad_sems, cross_sems
):
    pieces, height, lat = stage.shape
    rows = preact.shape[0]
    half_width = high.shape[0]
    copies = []
    first = starts[starts.shape[0] - 1] == 0

    @pl.when(first)
    def _():
        cross_stage[...] = arrived[rows:, :].astype(F32)

    @pl.when(jnp.logical_not(first))
    def _():
        cross_stage[...] = high[...]

    for c in range(half_width // lat):
        at = pl.ds(c * lat, lat)
        copies.append(pltpu.make_async_copy(cross_stage.at[at, :], cross.at[:, at], cross_sems.at[c]))
        copies[-1].start()
    value = jnp.where(preact[...] > 0, back_own[...] + arrived[:rows, :].astype(F32), 0.0).astype(BF16)
    for i in range(pieces):
        at = pl.ds(i * height, height)
        stage[i] = jnp.dot(turned[at, :], value, preferred_element_type=F32)
        copies.append(pltpu.make_async_copy(stage.at[i], grad.at[0, at, :], grad_sems.at[i]))
        copies[-1].start()
    bias[...] = jnp.sum(value.astype(F32), axis=0, keepdims=True)
    for copy in copies:
        copy.wait()


def ring_shards(residual_in, targets, enc_weight, enc_bias, dec_same, dec_cross):
    size = lax.axis_size("latent")
    reach = size // 2
    place = ring_place(lax.axis_index("latent"), size)
    layer = lax.axis_index("layer")
    sign = jnp.where(layer % 2 == 0, 1, -1)
    rows, wide = residual_in.shape[1:]
    half = rows // 2
    deep, lat = enc_weight.shape[1:]
    half_width = deep // 2
    err_scale = 1.0 / math.sqrt(rows)
    shape = jax.ShapeDtypeStruct
    unit = rows * wide * lat
    chains = (0, 1)

    def halves(array):
        return [array[:half], array[half:]]

    slot_p = {s: 2 * s - 1 for s in range(1, reach)}
    slot_q = {s: 2 * s for s in range(1, reach)}
    far = size - 1
    offsets = [0] * size
    offsets[far] = reach
    for s in range(1, reach):
        offsets[slot_p[s]] = -s
        offsets[slot_q[s]] = s
    starts = jnp.stack([ring_member(place + sign * offset, size) * wide for offset in offsets] + [layer])
    starts = starts.astype(jnp.int32)

    urgent, later = ((0, -1), (1, 1)), ((0, 1), (1, -1))

    def gather_step(found, s, ready=None):
        for chain, way in urgent + later if s < reach else urgent:
            slots = slot_p if way == 1 else slot_q
            shard = found[chain][slots[s - 1] if s > 1 else 0]
            if ready is not None and (chain, way) in later:
                shard = after(shard, ready[chain])
            found[chain][slots[s] if s < reach else far] = hop(shard, way)

    def both_chains(found, slots):
        return [found[chain][slot] for slot in slots for chain in chains]

    def encode(slots, before):
        first, last = slots[0] == 0, slots[-1] == far
        return call(
            functools.partial(encode_kernel, slots, first, last),
            [shape((rows, lat), F32)] + ([shape((rows, lat), BF16)] if last else []),
            2 * unit * len(slots),
            [starts] + both_chains(inputs, slots) + [enc_weight, before],
        )

    inputs = [[part] + [None] * (size - 1) for part in halves(residual_in[0])]
    turned_own = []
    for chain in chains:
        source = inputs[chain][0]
        turned_own += call(turn_own_kernel, [shape((wide, half), BF16)], 0, [starts, source])
    for s in range(1, reach + 1):
        gather_step(inputs, s, turned_own if s == 1 else None)
    low_cross = passed_along(after(dec_cross, inputs[0][slot_p.get(1, far)]), "layer", 1)
    stacked = jnp.concatenate([dec_same[0], jnp.concatenate([low_cross, dec_cross], axis=1)], axis=0)
    part = encode(tuple(range(far)), after(enc_bias, stacked))[0]
    preact, codes = encode((far,), part)
    earlier = passed_along(codes, "layer", 1)

    def spread(slots, dtypes, turned):
        outs = []
        for chain in chains:
            outs += [shape((half, wide), dtypes[chain].get(slot, F32)) for slot in slots]
            outs += [shape((2 * lat, half), BF16)] if turned else []
        found = call(
            functools.partial(spread_kernel, slots), outs, 4 * unit * len(slots), [starts, codes, earlier, stacked]
        )
        return found[:len(outs) // 2], found[len(outs) // 2:]

    rest = tuple(slot for slot in range(size) if slot != far)
    instant = tuple({far: BF16, (slot_q if way == 1 else slot_p).get(reach - 1): BF16} for _, way in later)
    far_0, far_1 = spread((far,), instant, False)
    moving = {loop: hop(message, loop[1]) for loop, message in zip(urgent, (far_0[0], far_1[0]))}
    partial, both_t = [], []
    for pieces in spread(rest, instant, True):
        partial.append(dict(zip(rest, pieces)))
        both_t.append(pieces[-1])
    before = []
    for s in range(reach - 1, 0, -1):
        landed = [moving[loop] for loop in urgent]
        for chain, way in urgent + later:
            message = partial[chain][slot_q[s] if way == 1 else slot_p[s]]
            if (chain, way) in moving:
                message = (message + moving[chain, way].astype(F32)).astype(BF16)
            if (chain, way) in later and before:
                message = after(message, *before)
            moving[chain, way] = hop(message, way)
        before = landed
    errors = []
    for chain, wanted in zip(chains, halves(targets[0])):
        total = partial[chain][0]
        for way in (1, -1):
            if (chain, way) in moving:
                total = total + moving[chain, way].astype(F32)
        if chain == 1:
            wanted = after(wanted, codes)
        errors.append([((total - wanted.astype(F32)) * err_scale).astype(BF16)] + [None] * (size - 1))

    def back(slots, before):
        return call(
            functools.partial(back_kernel, slots, before is None),
            [shape((len(slots), 2 * lat, wide), F32), shape((2, half, 2 * lat), F32)],
            4 * unit * len(slots),
            [starts] + both_chains(errors, slots) + [stacked] + both_t + ([] if before is None else [before]),
        )

    groups, outers, acc, pending = [], [], None, [0]
    arrived = [after(inputs[0][1], errors[1][0])]
    turned = call(
        turn_kernel,
        [shape((deep, rows), BF16)],
        0,
        [starts] + turned_own + arrived + both_chains(inputs, range(1, size))[1:],
    )[0]
    groups = [group for group in ((0,), tuple(range(1, far))) if group]
    outer, acc = back(groups[0], None)
    outers = [outer]
    for s in range(1, reach + 1):
        gather_step(errors, s, (turned, acc) if s == 1 else None)
    for group in groups[1:]:
        outer, acc = back(group, acc)
        outers.append(outer)
    last = both_chains(errors, (far,)) + [stacked] + both_t + outers + [acc]
    sent, high = call(
        functools.partial(cross_back_kernel, groups, far),
        [shape((rows + half_width, lat), BF16), shape((half_width, lat), F32)],
        0,
        [starts] + last,
    )
    returned = passed_along(sent, "layer", -1)
    back_own, grad_same = call(
        functools.partial(own_back_kernel, groups, far),
        [shape((rows, lat), F32), shape((1, lat, deep), F32)],
        0,
        [starts] + last,
        out_spaces=[pltpu.VMEM, pl.ANY],
        scratch=[pltpu.VMEM((lat, wide), F32), pltpu.SemaphoreType.DMA((size,))],
    )
    height = deep // PIECES
    grad_enc, grad_bias, grad_cross = call(
        finish_kernel,
        [shape((1, deep, lat), F32), shape((1, lat), F32), shape((lat, half_width), F32)],
        2 * unit * size,
        [starts, turned, preact, back_own, returned, high],
        out_spaces=[pl.ANY, pltpu.VMEM, pl.ANY],
        scratch=[
            pltpu.VMEM((PIECES, height, lat), F32),
            pltpu.VMEM((half_width, lat), F32),
            pltpu.SemaphoreType.DMA((PIECES,)),
            pltpu.SemaphoreType.DMA((half_width // lat,)),
        ],
    )
    return (grad_enc, grad_bias, grad_same, grad_cross)


def wide_shards(residual_in, targets, enc_weight, enc_bias, dec_same, dec_cross):
    is_first = lax.axis_index("layer") == 0
    err_scale = 1.0 / math.sqrt(residual_in.shape[1])
    inputs = lax.all_gather(residual_in[0], "latent", axis=1, tiled=True)
    preact = matmul(inputs, enc_weight[0]) + enc_bias[0]
    codes_now = jnp.maximum(preact, 0.0).astype(BF16)
    earlier = passed_along(codes_now, "layer", 1)
    cross_full = lax.all_gather(dec_cross, "layer", axis=1, tiled=True)
    own_dec = dec_same[0]
    half_width = own_dec.shape[1] // 2
    recon_full = lax.psum(matmul(codes_now, own_dec) + matmul(earlier, cross_full), "latent")
    wanted = lax.all_gather(targets[0], "latent", axis=1, tiled=True)
    errors = ((recon_full - wanted.astype(F32)) * err_scale).astype(BF16)
    grad_same = matmul(codes_now, errors, OVER_ROWS)
    grad_full = matmul(earlier, errors, OVER_ROWS)
    returned = passed_along(grad_full[:, :half_width], "layer", -1)
    grad_cross = jnp.where(is_first, returned, grad_full[:, half_width:])
    from_next = passed_along(matmul(errors, cross_full, OVER_COLS), "layer", -1)
    grad_codes = matmul(errors, own_dec, OVER_COLS) + from_next
    grad_pre = jnp.where(preact > 0, grad_codes, 0.0).astype(BF16)
    grad_enc = matmul(inputs, grad_pre, OVER_ROWS)
    grad_bias = jnp.sum(grad_pre.astype(F32), axis=0)
    return (grad_enc[None], grad_bias[None], grad_same[None], grad_cross)


def solution(mesh):
    size = mesh.shape["latent"]
    placed = (
        P("layer", "groups", "latent"),
        P("layer", "groups", "latent"),
        P("layer", None, "latent"),
        P("layer", "latent"),
        P("layer", "latent", None),
        P("latent", "layer"),
    )
    return jax.shard_map(
        ring_shards if size % 2 == 0 and size <= RING_LIMIT else wide_shards,
        mesh=mesh,
        in_specs=placed,
        out_specs=(
            P(("groups", "layer"), None, "latent"),
            P(("groups", "layer"), "latent"),
            P(("groups", "layer"), "latent", None),
            P(("groups", "latent"), "layer"),
        ),
        check_vma=False,
    )
```

```python
import functools
import math

import jax
import jax.numpy as jnp
from jax import lax
from jax.experimental import pallas as pl
from jax.experimental.pallas import tpu as pltpu
from jax.sharding import PartitionSpec as P

F32 = jnp.float32
BF16 = jnp.bfloat16
OVER_ROWS = (((0,), (0,)), ((), ()))
OVER_COLS = (((1,), (1,)), ((), ()))
RING_LIMIT = 16
VMEM_BYTES = 24 * 1024 * 1024
PIECES = 8
URGENT = 5 * 10**9


def passed_along(shard, axis, by):
    size = lax.axis_size(axis)
    pairs = [(i, i + by) for i in range(size) if 0 <= i + by < size]
    return lax.ppermute(shard, axis, pairs)


def matmul(a, b, dims=(((1,), (0,)), ((), ()))):
    return lax.dot_general(a, b, dims, preferred_element_type=F32)


def ring_order(size):
    return [2 * p if p < size // 2 else 2 * (size - 1 - p) + 1 for p in range(size)]


def ring_member(place, size):
    place = lax.rem(place + 2 * size, size)
    return jnp.where(place < size // 2, 2 * place, 2 * (size - 1 - place) + 1)


def ring_place(member, size):
    return jnp.where(member % 2 == 0, member // 2, size - 1 - member // 2)


def hop(shard, way, only=None):
    size, layers = lax.axis_size("latent"), lax.axis_size("layer")
    order = ring_order(size)
    pairs = []
    for p in range(size):
        for layer in only or range(layers):
            by = way if layer % 2 == 0 else -way
            pairs.append((order[p] * layers + layer, order[(p + by) % size] * layers + layer))
    return lax.ppermute(shard, ("latent", "layer"), pairs)


def after(value, *others):
    return lax.optimization_barrier((value,) + others)[0]


def call(kernel, outs, flops, operands, spaces=None, out_spaces=None, scratch=(), aliases=None, weight=0):
    def spec(space):
        return pl.BlockSpec(memory_space=space)

    spaces = spaces or [pltpu.VMEM] * (len(operands) - 1)
    out_spaces = out_spaces or [pltpu.VMEM] * len(outs)
    return pl.pallas_call(
        kernel,
        out_shape=outs,
        in_specs=[spec(pltpu.SMEM)] + [spec(space) for space in spaces],
        out_specs=[spec(space) for space in out_spaces],
        scratch_shapes=list(scratch),
        input_output_aliases=aliases or {},
        compiler_params=pltpu.CompilerParams(vmem_limit_bytes=VMEM_BYTES),
        cost_estimate=pl.CostEstimate(flops=flops + weight, bytes_accessed=1024, transcendentals=0),
    )(*operands)


def block_of(starts, slot, wide):
    return pl.ds(pl.multiple_of(starts[slot], wide), wide)


def encode_kernel(slots, first, last, starts, *refs):
    count = 2 * len(slots)
    shards, (weight, before, *outs) = refs[:count], refs[count:]
    rows, wide = shards[0].shape
    for chain in range(2):
        at = slice(chain * rows, (chain + 1) * rows)
        total = jnp.broadcast_to(before[...], (rows, before.shape[1])) if first else before[at, :]
        for i, slot in enumerate(slots):
            block = weight[0, block_of(starts, slot, wide), :]
            total = total + jnp.dot(shards[2 * i + chain][...], block, preferred_element_type=F32)
        outs[0][at, :] = total
        if last:
            outs[1][at, :] = jnp.maximum(total, 0.0).astype(BF16)


def turn_own_kernel(starts, shard, *refs):
    refs[-1][...] = shard[...].T


def turn_kernel(starts, own_0, own_1, *refs):
    *shards, turned = refs
    rows, wide = shards[0].shape
    for chain, own in enumerate((own_0, own_1)):
        turned[block_of(starts, 0, wide), chain * rows:(chain + 1) * rows] = own[...]
    for k in range(len(shards) // 2):
        at = block_of(starts, k + 1, wide)
        for chain in range(2):
            turned[at, chain * rows:(chain + 1) * rows] = shards[2 * k + chain][...].T


def spread_kernel(slots, starts, codes, earlier, stacked, *outs):
    rows = codes.shape[0] // 2
    outs = list(outs)
    for chain in range(2):
        at = slice(chain * rows, (chain + 1) * rows)
        both = jnp.concatenate([codes[at, :], earlier[at, :]], axis=1)
        for slot in slots:
            partial = outs.pop(0)
            block = stacked[:, block_of(starts, slot, partial.shape[1])]
            partial[...] = jnp.dot(both, block, preferred_element_type=F32).astype(partial.dtype)
        if len(outs) > (1 - chain) * len(slots):
            outs.pop(0)[...] = both.T


def back_products(slots, starts, shards, stacked, both_t, before):
    wide = shards[0].shape[1]
    blocks, totals = [], [None, None] if before is None else [before[0], before[1]]
    for i, slot in enumerate(slots):
        decoder = stacked[:, block_of(starts, slot, wide)]
        block = 0.0
        for chain in range(2):
            error = shards[2 * i + chain][...]
            block = block + jnp.dot(both_t[chain][...], error, preferred_element_type=F32)
            term = lax.dot_general(error, decoder, OVER_COLS, preferred_element_type=F32)
            totals[chain] = term if totals[chain] is None else totals[chain] + term
        blocks.append(block)
    return blocks, totals


def back_kernel(slots, first, starts, *refs):
    count = 2 * len(slots)
    shards, (stacked, *both_t), (*before, outer, back) = refs[:count], refs[count:count + 3], refs[count + 3:]
    blocks, totals = back_products(slots, starts, shards, stacked, both_t, None if first else before[0])
    for i, block in enumerate(blocks):
        outer[i] = block
    for chain in range(2):
        back[chain] = totals[chain]


def cross_back_kernel(slots, far, starts, *refs):
    shards, (stacked, *both_t), outers, (before, sent, high) = refs[:2], refs[2:5], refs[5:-3], refs[-3:]
    rows, wide = shards[0].shape
    half_width, lat = high.shape

    @pl.when(starts[starts.shape[0] - 1] != 0)
    def _():
        decoder = stacked[lat:, block_of(starts, far, wide)]
        last = 0.0
        for chain in range(2):
            error = shards[chain][...]
            last = last + jnp.dot(both_t[chain][lat:, :], error, preferred_element_type=F32)
            term = lax.dot_general(error, decoder, OVER_COLS, preferred_element_type=F32)
            sent[chain * rows:(chain + 1) * rows, :] = (before[chain, :, lat:] + term).astype(BF16)
        pieces = [(far, last)]
        for group, outer in zip(slots, outers):
            pieces += [(slot, outer[i, lat:]) for i, slot in enumerate(group)]
        for slot, piece in pieces:
            start = pl.multiple_of(starts[slot], wide)

            @pl.when(start < half_width)
            def _():
                for c in range(0, wide, lat):
                    sent[pl.ds(2 * rows + start + c, lat), :] = piece[:, c:c + lat].astype(BF16)

            @pl.when(start >= half_width)
            def _():
                for c in range(0, wide, lat):
                    high[pl.ds(start - half_width + c, lat), :] = piece[:, c:c + lat]


def own_back_kernel(slots, far, starts, *refs):
    firsts, laters, (stacked, *both_t), refs = refs[:2], refs[2:4], refs[4:7], refs[7:]
    outers, (before, back_own, same, last, sems) = refs[:-5], refs[-5:]
    rows, wide = firsts[0].shape
    lat = back_own.shape[1]
    first = starts[starts.shape[0] - 1] == 0
    blocks = []
    for group, outer in zip(slots, outers):
        blocks += [(slot, outer.at[i, :lat, :]) for i, slot in enumerate(group)]
    blocks.append((far, last))
    copies = []
    for i, (slot, block) in enumerate(blocks):
        copies.append(pltpu.make_async_copy(block, same.at[0, :, block_of(starts, slot, wide)], sems.at[i]))
    for copy in copies[:-1]:
        copy.start()
    decoder = stacked[:lat, block_of(starts, far, wide)]
    total = 0.0
    for chain in range(2):
        error = jnp.where(first, firsts[chain][...], laters[chain][...])
        total = total + jnp.dot(both_t[chain][:lat, :], error, preferred_element_type=F32)
        term = lax.dot_general(error, decoder, OVER_COLS, preferred_element_type=F32)
        back_own[chain * rows:(chain + 1) * rows, :] = before[chain, :, :lat] + term
    last[...] = total
    copies[-1].start()
    for copy in copies:
        copy.wait()


def finish_kernel(
    starts, turned, preact, back_own, arrived, high, grad, bias, cross, stage, cross_stage, grad_sems, cross_sems
):
    pieces, height, lat = stage.shape
    rows = preact.shape[0]
    half_width = high.shape[0]
    copies = []
    first = starts[starts.shape[0] - 1] == 0

    @pl.when(first)
    def _():
        cross_stage[...] = arrived[rows:, :].astype(F32)

    @pl.when(jnp.logical_not(first))
    def _():
        cross_stage[...] = high[...]

    for c in range(half_width // lat):
        at = pl.ds(c * lat, lat)
        copies.append(pltpu.make_async_copy(cross_stage.at[at, :], cross.at[:, at], cross_sems.at[c]))
        copies[-1].start()
    value = jnp.where(preact[...] > 0, back_own[...] + arrived[:rows, :].astype(F32), 0.0).astype(BF16)
    for i in range(pieces):
        at = pl.ds(i * height, height)
        stage[i] = jnp.dot(turned[at, :], value, preferred_element_type=F32)
        copies.append(pltpu.make_async_copy(stage.at[i], grad.at[0, at, :], grad_sems.at[i]))
        copies[-1].start()
    bias[...] = jnp.sum(value.astype(F32), axis=0, keepdims=True)
    for copy in copies:
        copy.wait()


def ring_shards(residual_in, targets, enc_weight, enc_bias, dec_same, dec_cross):
    size = lax.axis_size("latent")
    reach = size // 2
    place = ring_place(lax.axis_index("latent"), size)
    layer = lax.axis_index("layer")
    sign = jnp.where(layer % 2 == 0, 1, -1)
    rows, wide = residual_in.shape[1:]
    half = rows // 2
    deep, lat = enc_weight.shape[1:]
    half_width = deep // 2
    err_scale = 1.0 / math.sqrt(rows)
    shape = jax.ShapeDtypeStruct
    unit = rows * wide * lat
    chains = (0, 1)

    def halves(array):
        return [array[:half], array[half:]]

    slot_p = {s: 2 * s - 1 for s in range(1, reach)}
    slot_q = {s: 2 * s for s in range(1, reach)}
    far = size - 1
    offsets = [0] * size
    offsets[far] = reach
    for s in range(1, reach):
        offsets[slot_p[s]] = -s
        offsets[slot_q[s]] = s
    starts = jnp.stack([ring_member(place + sign * offset, size) * wide for offset in offsets] + [layer])
    starts = starts.astype(jnp.int32)

    urgent, later = ((0, -1), (1, 1)), ((0, 1), (1, -1))

    def gather_step(found, s, ready=None, split=None):
        for chain, way in urgent + later if s < reach else urgent:
            slots = slot_p if way == 1 else slot_q
            shard = found[chain][slots[s - 1] if s > 1 else 0]
            if ready is not None and (chain, way) in later:
                shard = after(shard, ready[chain])
            if split and s == reach:
                found[chain][far] = hop(shard, way, (0,)), hop(shard, way, split)
            else:
                found[chain][slots[s] if s < reach else far] = hop(shard, way)

    def both_chains(found, slots):
        return [found[chain][slot] for slot in slots for chain in chains]

    def encode(slots, before):
        first, last = slots[0] == 0, slots[-1] == far
        return call(
            functools.partial(encode_kernel, slots, first, last),
            [shape((rows, lat), F32)] + ([shape((rows, lat), BF16)] if last else []),
            2 * unit * len(slots),
            [starts] + both_chains(inputs, slots) + [enc_weight, before],
        )

    inputs = [[part] + [None] * (size - 1) for part in halves(residual_in[0])]
    turned_own = []
    for chain in chains:
        source = inputs[chain][0]
        turned_own += call(turn_own_kernel, [shape((wide, half), BF16)], 0, [starts, source])
    for s in range(1, reach + 1):
        gather_step(inputs, s, turned_own if s == 1 else None)
    low_cross = passed_along(after(dec_cross, inputs[0][slot_p.get(1, far)]), "layer", 1)
    stacked = jnp.concatenate([dec_same[0], jnp.concatenate([low_cross, dec_cross], axis=1)], axis=0)
    part = encode(tuple(range(far)), after(enc_bias, stacked))[0]
    preact, codes = encode((far,), part)
    earlier = passed_along(codes, "layer", 1)

    def spread(slots, dtypes, turned):
        outs = []
        for chain in chains:
            outs += [shape((half, wide), dtypes[chain].get(slot, F32)) for slot in slots]
            outs += [shape((2 * lat, half), BF16)] if turned else []
        found = call(
            functools.partial(spread_kernel, slots), outs, 4 * unit * len(slots), [starts, codes, earlier, stacked]
        )
        return found[:len(outs) // 2], found[len(outs) // 2:]

    rest = tuple(slot for slot in range(size) if slot != far)
    instant = tuple({far: BF16, (slot_q if way == 1 else slot_p).get(reach - 1): BF16} for _, way in later)
    far_0, far_1 = spread((far,), instant, False)
    moving = {loop: hop(message, loop[1]) for loop, message in zip(urgent, (far_0[0], far_1[0]))}
    partial, both_t = [], []
    for pieces in spread(rest, instant, True):
        partial.append(dict(zip(rest, pieces)))
        both_t.append(pieces[-1])
    before = []
    for s in range(reach - 1, 0, -1):
        landed = [moving[loop] for loop in urgent]
        for chain, way in urgent + later:
            message = partial[chain][slot_q[s] if way == 1 else slot_p[s]]
            if (chain, way) in moving:
                message = (message + moving[chain, way].astype(F32)).astype(BF16)
            if (chain, way) in later and before:
                message = after(message, *before)
            moving[chain, way] = hop(message, way)
        before = landed
    errors = []
    for chain, wanted in zip(chains, halves(targets[0])):
        total = partial[chain][0]
        for way in (1, -1):
            if (chain, way) in moving:
                total = total + moving[chain, way].astype(F32)
        if chain == 1:
            wanted = after(wanted, codes)
        errors.append([((total - wanted.astype(F32)) * err_scale).astype(BF16)] + [None] * (size - 1))

    def back(slots, before):
        return call(
            functools.partial(back_kernel, slots, before is None),
            [shape((len(slots), 2 * lat, wide), F32), shape((2, half, 2 * lat), F32)],
            4 * unit * len(slots),
            [starts] + both_chains(errors, slots) + [stacked] + both_t + ([] if before is None else [before]),
        )

    groups, outers, acc, pending = [], [], None, [0]
    arrived = [after(inputs[0][1], errors[1][0])]
    turned = call(
        turn_kernel,
        [shape((deep, rows), BF16)],
        0,
        [starts] + turned_own + arrived + both_chains(inputs, range(1, size))[1:],
    )[0]
    later_layers = tuple(range(1, lax.axis_size("layer")))
    for s in range(1, reach + 1):
        gather_step(errors, s, (turned, turned) if s == 2 else None, later_layers)
    cut = 1 + 2 * min(1, reach - 1)
    groups = [group for group in (tuple(range(cut)), tuple(range(cut, far))) if group]
    outers, acc = [], None
    for group in groups:
        outer, acc = back(group, acc)
        outers.append(outer)
    far_first, far_later = zip(errors[0][far], errors[1][far])
    others = [stacked] + both_t + outers + [acc]
    sent, high = call(
        functools.partial(cross_back_kernel, groups, far),
        [shape((rows + half_width, lat), BF16), shape((half_width, lat), F32)],
        0,
        [starts] + list(far_later) + others,
    )
    returned = passed_along(sent, "layer", -1)
    back_own, grad_same = call(
        functools.partial(own_back_kernel, groups, far),
        [shape((rows, lat), F32), shape((1, lat, deep), F32)],
        0,
        [starts] + list(far_first) + list(far_later) + others,
        out_spaces=[pltpu.VMEM, pl.ANY],
        scratch=[pltpu.VMEM((lat, wide), F32), pltpu.SemaphoreType.DMA((size,))],
        weight=URGENT,
    )
    height = deep // PIECES
    grad_enc, grad_bias, grad_cross = call(
        finish_kernel,
        [shape((1, deep, lat), F32), shape((1, lat), F32), shape((lat, half_width), F32)],
        2 * unit * size,
        [starts, turned, preact, back_own, returned, high],
        out_spaces=[pl.ANY, pltpu.VMEM, pl.ANY],
        scratch=[
            pltpu.VMEM((PIECES, height, lat), F32),
            pltpu.VMEM((half_width, lat), F32),
            pltpu.SemaphoreType.DMA((PIECES,)),
            pltpu.SemaphoreType.DMA((half_width // lat,)),
        ],
    )
    return (grad_enc, grad_bias, grad_same, grad_cross)


def wide_shards(residual_in, targets, enc_weight, enc_bias, dec_same, dec_cross):
    is_first = lax.axis_index("layer") == 0
    err_scale = 1.0 / math.sqrt(residual_in.shape[1])
    inputs = lax.all_gather(residual_in[0], "latent", axis=1, tiled=True)
    preact = matmul(inputs, enc_weight[0]) + enc_bias[0]
    codes_now = jnp.maximum(preact, 0.0).astype(BF16)
    earlier = passed_along(codes_now, "layer", 1)
    cross_full = lax.all_gather(dec_cross, "layer", axis=1, tiled=True)
    own_dec = dec_same[0]
    half_width = own_dec.shape[1] // 2
    recon_full = lax.psum(matmul(codes_now, own_dec) + matmul(earlier, cross_full), "latent")
    wanted = lax.all_gather(targets[0], "latent", axis=1, tiled=True)
    errors = ((recon_full - wanted.astype(F32)) * err_scale).astype(BF16)
    grad_same = matmul(codes_now, errors, OVER_ROWS)
    grad_full = matmul(earlier, errors, OVER_ROWS)
    returned = passed_along(grad_full[:, :half_width], "layer", -1)
    grad_cross = jnp.where(is_first, returned, grad_full[:, half_width:])
    from_next = passed_along(matmul(errors, cross_full, OVER_COLS), "layer", -1)
    grad_codes = matmul(errors, own_dec, OVER_COLS) + from_next
    grad_pre = jnp.where(preact > 0, grad_codes, 0.0).astype(BF16)
    grad_enc = matmul(inputs, grad_pre, OVER_ROWS)
    grad_bias = jnp.sum(grad_pre.astype(F32), axis=0)
    return (grad_enc[None], grad_bias[None], grad_same[None], grad_cross)


def solution(mesh):
    size = mesh.shape["latent"]
    placed = (
        P("layer", "groups", "latent"),
        P("layer", "groups", "latent"),
        P("layer", None, "latent"),
        P("layer", "latent"),
        P("layer", "latent", None),
        P("latent", "layer"),
    )
    return jax.shard_map(
        ring_shards if size % 2 == 0 and size <= RING_LIMIT else wide_shards,
        mesh=mesh,
        in_specs=placed,
        out_specs=(
            P(("groups", "layer"), None, "latent"),
            P(("groups", "layer"), "latent"),
            P(("groups", "layer"), "latent", None),
            P(("groups", "latent"), "layer"),
        ),
        check_vma=False,
    )
```

```python
import functools
import math

import jax
import jax.numpy as jnp
from jax import lax
from jax.experimental import pallas as pl
from jax.experimental.pallas import tpu as pltpu
from jax.sharding import PartitionSpec as P

F32 = jnp.float32
BF16 = jnp.bfloat16
OVER_ROWS = (((0,), (0,)), ((), ()))
OVER_COLS = (((1,), (1,)), ((), ()))
RING_LIMIT = 16
VMEM_BYTES = 24 * 1024 * 1024
PIECES = 8


def passed_along(shard, axis, by):
    size = lax.axis_size(axis)
    pairs = [(i, i + by) for i in range(size) if 0 <= i + by < size]
    return lax.ppermute(shard, axis, pairs)


def matmul(a, b, dims=(((1,), (0,)), ((), ()))):
    return lax.dot_general(a, b, dims, preferred_element_type=F32)


def ring_order(size):
    return [2 * p if p < size // 2 else 2 * (size - 1 - p) + 1 for p in range(size)]


def ring_member(place, size):
    place = lax.rem(place + 2 * size, size)
    return jnp.where(place < size // 2, 2 * place, 2 * (size - 1 - place) + 1)


def ring_place(member, size):
    return jnp.where(member % 2 == 0, member // 2, size - 1 - member // 2)


def hop(shard, way):
    size, layers = lax.axis_size("latent"), lax.axis_size("layer")
    order = ring_order(size)
    pairs = []
    for p in range(size):
        for layer in range(layers):
            by = way if layer % 2 == 0 else -way
            pairs.append((order[p] * layers + layer, order[(p + by) % size] * layers + layer))
    return lax.ppermute(shard, ("latent", "layer"), pairs)


def after(value, *others):
    return lax.optimization_barrier((value,) + others)[0]


def call(kernel, outs, flops, operands, spaces=None, out_spaces=None, scratch=(), aliases=None):
    def spec(space):
        return pl.BlockSpec(memory_space=space)

    spaces = spaces or [pltpu.VMEM] * (len(operands) - 1)
    out_spaces = out_spaces or [pltpu.VMEM] * len(outs)
    return pl.pallas_call(
        kernel,
        out_shape=outs,
        in_specs=[spec(pltpu.SMEM)] + [spec(space) for space in spaces],
        out_specs=[spec(space) for space in out_spaces],
        scratch_shapes=list(scratch),
        input_output_aliases=aliases or {},
        compiler_params=pltpu.CompilerParams(vmem_limit_bytes=VMEM_BYTES),
        cost_estimate=pl.CostEstimate(flops=flops, bytes_accessed=1024, transcendentals=0),
    )(*operands)


def block_of(starts, slot, wide):
    return pl.ds(pl.multiple_of(starts[slot], wide), wide)


def encode_kernel(slots, first, last, starts, *refs):
    count = 2 * len(slots)
    shards, (weight, before, *outs) = refs[:count], refs[count:]
    rows, wide = shards[0].shape
    for chain in range(2):
        at = slice(chain * rows, (chain + 1) * rows)
        total = jnp.broadcast_to(before[...], (rows, before.shape[1])) if first else before[at, :]
        for i, slot in enumerate(slots):
            block = weight[0, block_of(starts, slot, wide), :]
            total = total + jnp.dot(shards[2 * i + chain][...], block, preferred_element_type=F32)
        outs[0][at, :] = total
        if last:
            outs[1][at, :] = jnp.maximum(total, 0.0).astype(BF16)


def turn_own_kernel(starts, shard, *refs):
    refs[-1][...] = shard[...].T


def turn_kernel(starts, own_0, own_1, *refs):
    *shards, turned = refs
    rows, wide = shards[0].shape
    for chain, own in enumerate((own_0, own_1)):
        turned[block_of(starts, 0, wide), chain * rows:(chain + 1) * rows] = own[...]
    for k in range(len(shards) // 2):
        at = block_of(starts, k + 1, wide)
        for chain in range(2):
            turned[at, chain * rows:(chain + 1) * rows] = shards[2 * k + chain][...].T


def spread_kernel(slots, starts, codes, earlier, stacked, *outs):
    rows = codes.shape[0] // 2
    outs = list(outs)
    for chain in range(2):
        at = slice(chain * rows, (chain + 1) * rows)
        both = jnp.concatenate([codes[at, :], earlier[at, :]], axis=1)
        for slot in slots:
            partial = outs.pop(0)
            block = stacked[:, block_of(starts, slot, partial.shape[1])]
            partial[...] = jnp.dot(both, block, preferred_element_type=F32).astype(partial.dtype)
        if len(outs) > (1 - chain) * len(slots):
            outs.pop(0)[...] = both.T


def back_products(slots, starts, shards, stacked, both_t, before):
    wide = shards[0].shape[1]
    blocks, totals = [], [None, None] if before is None else [before[0], before[1]]
    for i, slot in enumerate(slots):
        decoder = stacked[:, block_of(starts, slot, wide)]
        block = 0.0
        for chain in range(2):
            error = shards[2 * i + chain][...]
            block = block + jnp.dot(both_t[chain][...], error, preferred_element_type=F32)
            term = lax.dot_general(error, decoder, OVER_COLS, preferred_element_type=F32)
            totals[chain] = term if totals[chain] is None else totals[chain] + term
        blocks.append(block)
    return blocks, totals


def back_kernel(slots, first, starts, *refs):
    count = 2 * len(slots)
    shards, (stacked, *both_t), (*before, outer, back) = refs[:count], refs[count:count + 3], refs[count + 3:]
    blocks, totals = back_products(slots, starts, shards, stacked, both_t, None if first else before[0])
    for i, block in enumerate(blocks):
        outer[i] = block
    for chain in range(2):
        back[chain] = totals[chain]


def cross_back_kernel(slots, far, starts, *refs):
    shards, (stacked, *both_t), outers, (before, sent, high) = refs[:2], refs[2:5], refs[5:-3], refs[-3:]
    rows, wide = shards[0].shape
    half_width, lat = high.shape

    @pl.when(starts[starts.shape[0] - 1] != 0)
    def _():
        decoder = stacked[lat:, block_of(starts, far, wide)]
        last = 0.0
        for chain in range(2):
            error = shards[chain][...]
            last = last + jnp.dot(both_t[chain][lat:, :], error, preferred_element_type=F32)
            term = lax.dot_general(error, decoder, OVER_COLS, preferred_element_type=F32)
            sent[chain * rows:(chain + 1) * rows, :] = (before[chain, :, lat:] + term).astype(BF16)
        pieces = [(far, last)]
        for group, outer in zip(slots, outers):
            pieces += [(slot, outer[i, lat:]) for i, slot in enumerate(group)]
        for slot, piece in pieces:
            start = pl.multiple_of(starts[slot], wide)

            @pl.when(start < half_width)
            def _():
                for c in range(0, wide, lat):
                    sent[pl.ds(2 * rows + start + c, lat), :] = piece[:, c:c + lat].astype(BF16)

            @pl.when(start >= half_width)
            def _():
                for c in range(0, wide, lat):
                    high[pl.ds(start - half_width + c, lat), :] = piece[:, c:c + lat]


def own_back_kernel(slots, far, starts, *refs):
    shards, (stacked, *both_t), refs = refs[:2], refs[2:5], refs[5:]
    outers, (before, back_own, same, last, sems) = refs[:-5], refs[-5:]
    rows, wide = shards[0].shape
    lat = back_own.shape[1]
    blocks = []
    for group, outer in zip(slots, outers):
        blocks += [(slot, outer.at[i, :lat, :]) for i, slot in enumerate(group)]
    blocks.append((far, last))
    copies = []
    for i, (slot, block) in enumerate(blocks):
        copies.append(pltpu.make_async_copy(block, same.at[0, :, block_of(starts, slot, wide)], sems.at[i]))
    for copy in copies[:-1]:
        copy.start()
    decoder = stacked[:lat, block_of(starts, far, wide)]
    total = 0.0
    for chain in range(2):
        error = shards[chain][...]
        total = total + jnp.dot(both_t[chain][:lat, :], error, preferred_element_type=F32)
        term = lax.dot_general(error, decoder, OVER_COLS, preferred_element_type=F32)
        back_own[chain * rows:(chain + 1) * rows, :] = before[chain, :, :lat] + term
    last[...] = total
    copies[-1].start()
    for copy in copies:
        copy.wait()


def finish_kernel(
    starts, turned, preact, back_own, arrived, high, grad, bias, cross, stage, cross_stage, grad_sems, cross_sems
):
    pieces, height, lat = stage.shape
    rows = preact.shape[0]
    half_width = high.shape[0]
    copies = []
    first = starts[starts.shape[0] - 1] == 0

    @pl.when(first)
    def _():
        cross_stage[...] = arrived[rows:, :].astype(F32)

    @pl.when(jnp.logical_not(first))
    def _():
        cross_stage[...] = high[...]

    for c in range(half_width // lat):
        at = pl.ds(c * lat, lat)
        copies.append(pltpu.make_async_copy(cross_stage.at[at, :], cross.at[:, at], cross_sems.at[c]))
        copies[-1].start()
    value = jnp.where(preact[...] > 0, back_own[...] + arrived[:rows, :].astype(F32), 0.0).astype(BF16)
    for i in range(pieces):
        at = pl.ds(i * height, height)
        stage[i] = jnp.dot(turned[at, :], value, preferred_element_type=F32)
        copies.append(pltpu.make_async_copy(stage.at[i], grad.at[0, at, :], grad_sems.at[i]))
        copies[-1].start()
    bias[...] = jnp.sum(value.astype(F32), axis=0, keepdims=True)
    for copy in copies:
        copy.wait()


def ring_shards(residual_in, targets, enc_weight, enc_bias, dec_same, dec_cross):
    size = lax.axis_size("latent")
    reach = size // 2
    place = ring_place(lax.axis_index("latent"), size)
    layer = lax.axis_index("layer")
    sign = jnp.where(layer % 2 == 0, 1, -1)
    rows, wide = residual_in.shape[1:]
    half = rows // 2
    deep, lat = enc_weight.shape[1:]
    half_width = deep // 2
    err_scale = 1.0 / math.sqrt(rows)
    shape = jax.ShapeDtypeStruct
    unit = rows * wide * lat
    chains = (0, 1)

    def halves(array):
        return [array[:half], array[half:]]

    slot_p = {s: 2 * s - 1 for s in range(1, reach)}
    slot_q = {s: 2 * s for s in range(1, reach)}
    far = size - 1
    offsets = [0] * size
    offsets[far] = reach
    for s in range(1, reach):
        offsets[slot_p[s]] = -s
        offsets[slot_q[s]] = s
    starts = jnp.stack([ring_member(place + sign * offset, size) * wide for offset in offsets] + [layer])
    starts = starts.astype(jnp.int32)

    urgent, later = ((0, -1), (1, 1)), ((0, 1), (1, -1))

    def gather_step(found, s, ready=None):
        for chain, way in urgent + later if s < reach else urgent:
            slots = slot_p if way == 1 else slot_q
            shard = found[chain][slots[s - 1] if s > 1 else 0]
            if ready is not None and (chain, way) in later:
                shard = after(shard, ready[chain])
            found[chain][slots[s] if s < reach else far] = hop(shard, way)

    def both_chains(found, slots):
        return [found[chain][slot] for slot in slots for chain in chains]

    def encode(slots, before):
        first, last = slots[0] == 0, slots[-1] == far
        return call(
            functools.partial(encode_kernel, slots, first, last),
            [shape((rows, lat), F32)] + ([shape((rows, lat), BF16)] if last else []),
            2 * unit * len(slots),
            [starts] + both_chains(inputs, slots) + [enc_weight, before],
        )

    inputs = [[part] + [None] * (size - 1) for part in halves(residual_in[0])]
    turned_own = []
    for chain in chains:
        source = inputs[chain][0]
        turned_own += call(turn_own_kernel, [shape((wide, half), BF16)], 0, [starts, source])
    for s in range(1, reach + 1):
        gather_step(inputs, s, turned_own if s == 1 else None)
    low_cross = passed_along(after(dec_cross, inputs[0][slot_p.get(1, far)]), "layer", 1)
    stacked = jnp.concatenate([dec_same[0], jnp.concatenate([low_cross, dec_cross], axis=1)], axis=0)
    part = encode(tuple(range(far)), after(enc_bias, stacked))[0]
    preact, codes = encode((far,), part)
    earlier = passed_along(codes, "layer", 1)

    def spread(slots, dtypes, turned):
        outs = []
        for chain in chains:
            outs += [shape((half, wide), dtypes[chain].get(slot, F32)) for slot in slots]
            outs += [shape((2 * lat, half), BF16)] if turned else []
        found = call(
            functools.partial(spread_kernel, slots), outs, 4 * unit * len(slots), [starts, codes, earlier, stacked]
        )
        return found[:len(outs) // 2], found[len(outs) // 2:]

    rest = tuple(slot for slot in range(size) if slot != far)
    instant = tuple({far: BF16, (slot_q if way == 1 else slot_p).get(reach - 1): BF16} for _, way in later)
    block = lax.dynamic_slice_in_dim(stacked, starts[far], wide, 1)
    far_0, far_1 = [
        [(matmul(now, block[:lat]) + matmul(before, block[lat:])).astype(BF16)]
        for now, before in zip(halves(codes), halves(earlier))
    ]
    moving = {loop: hop(message, loop[1]) for loop, message in zip(urgent, (far_0[0], far_1[0]))}
    partial, both_t = [], []
    for pieces in spread(rest, instant, True):
        partial.append(dict(zip(rest, pieces)))
        both_t.append(pieces[-1])
    before = []
    for s in range(reach - 1, 0, -1):
        landed = [moving[loop] for loop in urgent]
        for chain, way in urgent + later:
            message = partial[chain][slot_q[s] if way == 1 else slot_p[s]]
            if (chain, way) in moving:
                message = (message + moving[chain, way].astype(F32)).astype(BF16)
            if (chain, way) in later and before:
                message = after(message, *before)
            moving[chain, way] = hop(message, way)
        before = landed
    errors = []
    for chain, wanted in zip(chains, halves(targets[0])):
        total = partial[chain][0]
        for way in (1, -1):
            if (chain, way) in moving:
                total = total + moving[chain, way].astype(F32)
        if chain == 1:
            wanted = after(wanted, codes)
        errors.append([((total - wanted.astype(F32)) * err_scale).astype(BF16)] + [None] * (size - 1))

    def back(slots, before):
        return call(
            functools.partial(back_kernel, slots, before is None),
            [shape((len(slots), 2 * lat, wide), F32), shape((2, half, 2 * lat), F32)],
            4 * unit * len(slots),
            [starts] + both_chains(errors, slots) + [stacked] + both_t + ([] if before is None else [before]),
        )

    groups, outers, acc, pending = [], [], None, [0]
    arrived = [after(inputs[0][1], errors[1][0])]
    turned = call(
        turn_kernel,
        [shape((deep, rows), BF16)],
        0,
        [starts] + turned_own + arrived + both_chains(inputs, range(1, size))[1:],
    )[0]
    groups = [group for group in ((0,), tuple(range(1, far))) if group]
    outer, acc = back(groups[0], None)
    outers = [outer]
    for s in range(1, reach + 1):
        gather_step(errors, s, (turned, acc) if s == 1 else None)
    for group in groups[1:]:
        outer, acc = back(group, acc)
        outers.append(outer)
    last = both_chains(errors, (far,)) + [stacked] + both_t + outers + [acc]
    sent, high = call(
        functools.partial(cross_back_kernel, groups, far),
        [shape((rows + half_width, lat), BF16), shape((half_width, lat), F32)],
        0,
        [starts] + last,
    )
    returned = passed_along(sent, "layer", -1)
    back_own, grad_same = call(
        functools.partial(own_back_kernel, groups, far),
        [shape((rows, lat), F32), shape((1, lat, deep), F32)],
        0,
        [starts] + last,
        out_spaces=[pltpu.VMEM, pl.ANY],
        scratch=[pltpu.VMEM((lat, wide), F32), pltpu.SemaphoreType.DMA((size,))],
    )
    height = deep // PIECES
    grad_enc, grad_bias, grad_cross = call(
        finish_kernel,
        [shape((1, deep, lat), F32), shape((1, lat), F32), shape((lat, half_width), F32)],
        2 * unit * size,
        [starts, turned, preact, back_own, returned, high],
        out_spaces=[pl.ANY, pltpu.VMEM, pl.ANY],
        scratch=[
            pltpu.VMEM((PIECES, height, lat), F32),
            pltpu.VMEM((half_width, lat), F32),
            pltpu.SemaphoreType.DMA((PIECES,)),
            pltpu.SemaphoreType.DMA((half_width // lat,)),
        ],
    )
    return (grad_enc, grad_bias, grad_same, grad_cross)


def wide_shards(residual_in, targets, enc_weight, enc_bias, dec_same, dec_cross):
    is_first = lax.axis_index("layer") == 0
    err_scale = 1.0 / math.sqrt(residual_in.shape[1])
    inputs = lax.all_gather(residual_in[0], "latent", axis=1, tiled=True)
    preact = matmul(inputs, enc_weight[0]) + enc_bias[0]
    codes_now = jnp.maximum(preact, 0.0).astype(BF16)
    earlier = passed_along(codes_now, "layer", 1)
    cross_full = lax.all_gather(dec_cross, "layer", axis=1, tiled=True)
    own_dec = dec_same[0]
    half_width = own_dec.shape[1] // 2
    recon_full = lax.psum(matmul(codes_now, own_dec) + matmul(earlier, cross_full), "latent")
    wanted = lax.all_gather(targets[0], "latent", axis=1, tiled=True)
    errors = ((recon_full - wanted.astype(F32)) * err_scale).astype(BF16)
    grad_same = matmul(codes_now, errors, OVER_ROWS)
    grad_full = matmul(earlier, errors, OVER_ROWS)
    returned = passed_along(grad_full[:, :half_width], "layer", -1)
    grad_cross = jnp.where(is_first, returned, grad_full[:, half_width:])
    from_next = passed_along(matmul(errors, cross_full, OVER_COLS), "layer", -1)
    grad_codes = matmul(errors, own_dec, OVER_COLS) + from_next
    grad_pre = jnp.where(preact > 0, grad_codes, 0.0).astype(BF16)
    grad_enc = matmul(inputs, grad_pre, OVER_ROWS)
    grad_bias = jnp.sum(grad_pre.astype(F32), axis=0)
    return (grad_enc[None], grad_bias[None], grad_same[None], grad_cross)


def solution(mesh):
    size = mesh.shape["latent"]
    placed = (
        P("layer", "groups", "latent"),
        P("layer", "groups", "latent"),
        P("layer", None, "latent"),
        P("layer", "latent"),
        P("layer", "latent", None),
        P("latent", "layer"),
    )
    return jax.shard_map(
        ring_shards if size % 2 == 0 and size <= RING_LIMIT else wide_shards,
        mesh=mesh,
        in_specs=placed,
        out_specs=(
            P(("groups", "layer"), None, "latent"),
            P(("groups", "layer"), "latent"),
            P(("groups", "layer"), "latent", None),
            P(("groups", "latent"), "layer"),
        ),
        check_vma=False,
    )
```

```python
import functools
import math

import jax
import jax.numpy as jnp
from jax import lax
from jax.experimental import pallas as pl
from jax.experimental.pallas import tpu as pltpu
from jax.sharding import PartitionSpec as P

F32 = jnp.float32
BF16 = jnp.bfloat16
OVER_ROWS = (((0,), (0,)), ((), ()))
OVER_COLS = (((1,), (1,)), ((), ()))
RING_LIMIT = 16
VMEM_BYTES = 24 * 1024 * 1024
PIECES = 8


def passed_along(shard, axis, by):
    size = lax.axis_size(axis)
    pairs = [(i, i + by) for i in range(size) if 0 <= i + by < size]
    return lax.ppermute(shard, axis, pairs)


def matmul(a, b, dims=(((1,), (0,)), ((), ()))):
    return lax.dot_general(a, b, dims, preferred_element_type=F32)


def ring_order(size):
    return [2 * p if p < size // 2 else 2 * (size - 1 - p) + 1 for p in range(size)]


def ring_member(place, size):
    place = lax.rem(place + 2 * size, size)
    return jnp.where(place < size // 2, 2 * place, 2 * (size - 1 - place) + 1)


def ring_place(member, size):
    return jnp.where(member % 2 == 0, member // 2, size - 1 - member // 2)


def hop(shard, way):
    size, layers = lax.axis_size("latent"), lax.axis_size("layer")
    order = ring_order(size)
    pairs = []
    for p in range(size):
        for layer in range(layers):
            by = way if layer % 2 == 0 else -way
            pairs.append((order[p] * layers + layer, order[(p + by) % size] * layers + layer))
    return lax.ppermute(shard, ("latent", "layer"), pairs)


def after(value, *others):
    return lax.optimization_barrier((value,) + others)[0]


def call(kernel, outs, flops, operands, spaces=None, out_spaces=None, scratch=(), aliases=None):
    def spec(space):
        return pl.BlockSpec(memory_space=space)

    spaces = spaces or [pltpu.VMEM] * (len(operands) - 1)
    out_spaces = out_spaces or [pltpu.VMEM] * len(outs)
    return pl.pallas_call(
        kernel,
        out_shape=outs,
        in_specs=[spec(pltpu.SMEM)] + [spec(space) for space in spaces],
        out_specs=[spec(space) for space in out_spaces],
        scratch_shapes=list(scratch),
        input_output_aliases=aliases or {},
        compiler_params=pltpu.CompilerParams(vmem_limit_bytes=VMEM_BYTES),
        cost_estimate=pl.CostEstimate(flops=flops, bytes_accessed=1024, transcendentals=0),
    )(*operands)


def block_of(starts, slot, wide):
    return pl.ds(pl.multiple_of(starts[slot], wide), wide)


def encode_kernel(slots, first, last, starts, *refs):
    count = 2 * len(slots)
    shards, (weight, before, *outs) = refs[:count], refs[count:]
    rows, wide = shards[0].shape
    for chain in range(2):
        at = slice(chain * rows, (chain + 1) * rows)
        total = jnp.broadcast_to(before[...], (rows, before.shape[1])) if first else before[at, :]
        for i, slot in enumerate(slots):
            block = weight[0, block_of(starts, slot, wide), :]
            total = total + jnp.dot(shards[2 * i + chain][...], block, preferred_element_type=F32)
        outs[0][at, :] = total
        if last:
            outs[1][at, :] = jnp.maximum(total, 0.0).astype(BF16)


def turn_own_kernel(starts, shard, *refs):
    refs[-1][...] = shard[...].T


def turn_kernel(starts, own_0, own_1, *refs):
    *shards, turned = refs
    rows, wide = shards[0].shape
    for chain, own in enumerate((own_0, own_1)):
        turned[block_of(starts, 0, wide), chain * rows:(chain + 1) * rows] = own[...]
    for k in range(len(shards) // 2):
        at = block_of(starts, k + 1, wide)
        for chain in range(2):
            turned[at, chain * rows:(chain + 1) * rows] = shards[2 * k + chain][...].T


def spread_kernel(slots, starts, codes, earlier, stacked, *outs):
    rows = codes.shape[0] // 2
    outs = list(outs)
    for chain in range(2):
        at = slice(chain * rows, (chain + 1) * rows)
        both = jnp.concatenate([codes[at, :], earlier[at, :]], axis=1)
        for slot in slots:
            partial = outs.pop(0)
            block = stacked[:, block_of(starts, slot, partial.shape[1])]
            partial[...] = jnp.dot(both, block, preferred_element_type=F32).astype(partial.dtype)
        if len(outs) > (1 - chain) * len(slots):
            outs.pop(0)[...] = both.T


def back_products(slots, starts, shards, stacked, both_t, before):
    wide = shards[0].shape[1]
    blocks, totals = [], [None, None] if before is None else [before[0], before[1]]
    for i, slot in enumerate(slots):
        decoder = stacked[:, block_of(starts, slot, wide)]
        block = 0.0
        for chain in range(2):
            error = shards[2 * i + chain][...]
            block = block + jnp.dot(both_t[chain][...], error, preferred_element_type=F32)
            term = lax.dot_general(error, decoder, OVER_COLS, preferred_element_type=F32)
            totals[chain] = term if totals[chain] is None else totals[chain] + term
        blocks.append(block)
    return blocks, totals


def back_kernel(slots, first, starts, *refs):
    count = 2 * len(slots)
    shards, (stacked, *both_t), (*before, outer, back) = refs[:count], refs[count:count + 3], refs[count + 3:]
    blocks, totals = back_products(slots, starts, shards, stacked, both_t, None if first else before[0])
    for i, block in enumerate(blocks):
        outer[i] = block
    for chain in range(2):
        back[chain] = totals[chain]


def cross_back_kernel(slots, far, starts, *refs):
    shards, (stacked, *both_t), outers, (before, sent, high) = refs[:2], refs[2:5], refs[5:-3], refs[-3:]
    rows, wide = shards[0].shape
    half_width, lat = high.shape

    @pl.when(starts[starts.shape[0] - 1] != 0)
    def _():
        decoder = stacked[lat:, block_of(starts, far, wide)]
        last = 0.0
        for chain in range(2):
            error = shards[chain][...]
            last = last + jnp.dot(both_t[chain][lat:, :], error, preferred_element_type=F32)
            term = lax.dot_general(error, decoder, OVER_COLS, preferred_element_type=F32)
            sent[chain * rows:(chain + 1) * rows, :] = (before[chain, :, lat:] + term).astype(BF16)
        pieces = [(far, last)]
        for group, outer in zip(slots, outers):
            pieces += [(slot, outer[i, lat:]) for i, slot in enumerate(group)]
        for slot, piece in pieces:
            start = pl.multiple_of(starts[slot], wide)

            @pl.when(start < half_width)
            def _():
                for c in range(0, wide, lat):
                    sent[pl.ds(2 * rows + start + c, lat), :] = piece[:, c:c + lat].astype(BF16)

            @pl.when(start >= half_width)
            def _():
                for c in range(0, wide, lat):
                    high[pl.ds(start - half_width + c, lat), :] = piece[:, c:c + lat]


def own_back_kernel(slots, far, starts, *refs):
    shards, (stacked, *both_t), refs = refs[:2], refs[2:5], refs[5:]
    outers, (before, back_own, same, last, sems) = refs[:-5], refs[-5:]
    rows, wide = shards[0].shape
    lat = back_own.shape[1]
    blocks = []
    for group, outer in zip(slots, outers):
        blocks += [(slot, outer.at[i, :lat, :]) for i, slot in enumerate(group)]
    blocks.append((far, last))
    copies = []
    for i, (slot, block) in enumerate(blocks):
        copies.append(pltpu.make_async_copy(block, same.at[0, :, block_of(starts, slot, wide)], sems.at[i]))
    for copy in copies[:-1]:
        copy.start()
    decoder = stacked[:lat, block_of(starts, far, wide)]
    total = 0.0
    for chain in range(2):
        error = shards[chain][...]
        total = total + jnp.dot(both_t[chain][:lat, :], error, preferred_element_type=F32)
        term = lax.dot_general(error, decoder, OVER_COLS, preferred_element_type=F32)
        back_own[chain * rows:(chain + 1) * rows, :] = before[chain, :, :lat] + term
    last[...] = total
    copies[-1].start()
    for copy in copies:
        copy.wait()


def finish_kernel(
    starts, turned, preact, back_own, arrived, high, grad, bias, cross, stage, cross_stage, grad_sems, cross_sem
):
    pieces, height, lat = stage.shape
    rows = preact.shape[0]
    half_width = high.shape[0]
    first = starts[starts.shape[0] - 1] == 0
    value = jnp.where(preact[...] > 0, back_own[...] + arrived[:rows, :].astype(F32), 0.0).astype(BF16)
    copies = []
    for i in range(pieces):
        at = pl.ds(i * height, height)
        stage[i] = jnp.dot(turned[at, :], value, preferred_element_type=F32)
        copies.append(pltpu.make_async_copy(stage.at[i], grad.at[0, at, :], grad_sems.at[i]))
        copies[-1].start()
        if i == 0:
            for c in range(0, half_width, lat):
                source = arrived[rows + c:rows + c + lat, :].astype(F32)
                cross_stage[:, c:c + lat] = jnp.where(first, source, high[c:c + lat, :])
            copies.append(pltpu.make_async_copy(cross_stage, cross, cross_sem))
            copies[-1].start()
    bias[...] = jnp.sum(value.astype(F32), axis=0, keepdims=True)
    for copy in copies:
        copy.wait()


def ring_shards(residual_in, targets, enc_weight, enc_bias, dec_same, dec_cross):
    size = lax.axis_size("latent")
    reach = size // 2
    place = ring_place(lax.axis_index("latent"), size)
    layer = lax.axis_index("layer")
    sign = jnp.where(layer % 2 == 0, 1, -1)
    rows, wide = residual_in.shape[1:]
    half = rows // 2
    deep, lat = enc_weight.shape[1:]
    half_width = deep // 2
    err_scale = 1.0 / math.sqrt(rows)
    shape = jax.ShapeDtypeStruct
    unit = rows * wide * lat
    chains = (0, 1)

    def halves(array):
        return [array[:half], array[half:]]

    slot_p = {s: 2 * s - 1 for s in range(1, reach)}
    slot_q = {s: 2 * s for s in range(1, reach)}
    far = size - 1
    offsets = [0] * size
    offsets[far] = reach
    for s in range(1, reach):
        offsets[slot_p[s]] = -s
        offsets[slot_q[s]] = s
    starts = jnp.stack([ring_member(place + sign * offset, size) * wide for offset in offsets] + [layer])
    starts = starts.astype(jnp.int32)

    urgent, later = ((0, -1), (1, 1)), ((0, 1), (1, -1))

    def gather_step(found, s, ready=None):
        for chain, way in urgent + later if s < reach else urgent:
            slots = slot_p if way == 1 else slot_q
            shard = found[chain][slots[s - 1] if s > 1 else 0]
            if ready is not None and (chain, way) in later:
                shard = after(shard, ready[chain])
            found[chain][slots[s] if s < reach else far] = hop(shard, way)

    def both_chains(found, slots):
        return [found[chain][slot] for slot in slots for chain in chains]

    def encode(slots, before):
        first, last = slots[0] == 0, slots[-1] == far
        return call(
            functools.partial(encode_kernel, slots, first, last),
            [shape((rows, lat), F32)] + ([shape((rows, lat), BF16)] if last else []),
            2 * unit * len(slots),
            [starts] + both_chains(inputs, slots) + [enc_weight, before],
        )

    inputs = [[part] + [None] * (size - 1) for part in halves(residual_in[0])]
    turned_own = []
    for chain in chains:
        source = inputs[chain][0]
        turned_own += call(turn_own_kernel, [shape((wide, half), BF16)], 0, [starts, source])
    for s in range(1, reach + 1):
        gather_step(inputs, s, turned_own if s == 1 else None)
    low_cross = passed_along(after(dec_cross, inputs[0][slot_p.get(1, far)]), "layer", 1)
    stacked = jnp.concatenate([dec_same[0], jnp.concatenate([low_cross, dec_cross], axis=1)], axis=0)
    part = encode(tuple(range(far)), after(enc_bias, stacked))[0]
    preact, codes = encode((far,), part)
    earlier = passed_along(codes, "layer", 1)

    def spread(slots, dtypes, turned):
        outs = []
        for chain in chains:
            outs += [shape((half, wide), dtypes[chain].get(slot, F32)) for slot in slots]
            outs += [shape((2 * lat, half), BF16)] if turned else []
        found = call(
            functools.partial(spread_kernel, slots), outs, 4 * unit * len(slots), [starts, codes, earlier, stacked]
        )
        return found[:len(outs) // 2], found[len(outs) // 2:]

    rest = tuple(slot for slot in range(size) if slot != far)
    instant = tuple({far: BF16, (slot_q if way == 1 else slot_p).get(reach - 1): BF16} for _, way in later)
    far_0, far_1 = spread((far,), instant, False)
    moving = {loop: hop(message, loop[1]) for loop, message in zip(urgent, (far_0[0], far_1[0]))}
    partial, both_t = [], []
    for pieces in spread(rest, instant, True):
        partial.append(dict(zip(rest, pieces)))
        both_t.append(pieces[-1])
    before = []
    for s in range(reach - 1, 0, -1):
        landed = [moving[loop] for loop in urgent]
        for chain, way in urgent + later:
            message = partial[chain][slot_q[s] if way == 1 else slot_p[s]]
            if (chain, way) in moving:
                message = (message + moving[chain, way].astype(F32)).astype(BF16)
            if (chain, way) in later and before:
                message = after(message, *before)
            moving[chain, way] = hop(message, way)
        before = landed
    errors = []
    for chain, wanted in zip(chains, halves(targets[0])):
        total = partial[chain][0]
        for way in (1, -1):
            if (chain, way) in moving:
                total = total + moving[chain, way].astype(F32)
        if chain == 1:
            wanted = after(wanted, codes)
        errors.append([((total - wanted.astype(F32)) * err_scale).astype(BF16)] + [None] * (size - 1))

    def back(slots, before):
        return call(
            functools.partial(back_kernel, slots, before is None),
            [shape((len(slots), 2 * lat, wide), F32), shape((2, half, 2 * lat), F32)],
            4 * unit * len(slots),
            [starts] + both_chains(errors, slots) + [stacked] + both_t + ([] if before is None else [before]),
        )

    groups, outers, acc, pending = [], [], None, [0]
    arrived = [after(inputs[0][1], errors[1][0])]
    turned = call(
        turn_kernel,
        [shape((deep, rows), BF16)],
        0,
        [starts] + turned_own + arrived + both_chains(inputs, range(1, size))[1:],
    )[0]
    for s in range(1, reach + 1):
        gather_step(errors, s, (turned, turned) if s == 2 else None)
    cut = 1 + 2 * min(1, reach - 1)
    groups = [group for group in (tuple(range(cut)), tuple(range(cut, far))) if group]
    outers, acc = [], None
    for group in groups:
        outer, acc = back(group, acc)
        outers.append(outer)
    last = both_chains(errors, (far,)) + [stacked] + both_t + outers + [acc]
    sent, high = call(
        functools.partial(cross_back_kernel, groups, far),
        [shape((rows + half_width, lat), BF16), shape((half_width, lat), F32)],
        0,
        [starts] + last,
    )
    returned = passed_along(sent, "layer", -1)
    back_own, grad_same = call(
        functools.partial(own_back_kernel, groups, far),
        [shape((rows, lat), F32), shape((1, lat, deep), F32)],
        0,
        [starts] + last,
        out_spaces=[pltpu.VMEM, pl.ANY],
        scratch=[pltpu.VMEM((lat, wide), F32), pltpu.SemaphoreType.DMA((size,))],
    )
    height = deep // PIECES
    grad_enc, grad_bias, grad_cross = call(
        finish_kernel,
        [shape((1, deep, lat), F32), shape((1, lat), F32), shape((lat, half_width), F32)],
        2 * unit * size,
        [starts, turned, preact, back_own, returned, high],
        out_spaces=[pl.ANY, pltpu.VMEM, pl.ANY],
        scratch=[
            pltpu.VMEM((PIECES, height, lat), F32),
            pltpu.VMEM((lat, half_width), F32),
            pltpu.SemaphoreType.DMA((PIECES,)),
            pltpu.SemaphoreType.DMA,
        ],
    )
    return (grad_enc, grad_bias, grad_same, grad_cross)


def wide_shards(residual_in, targets, enc_weight, enc_bias, dec_same, dec_cross):
    is_first = lax.axis_index("layer") == 0
    err_scale = 1.0 / math.sqrt(residual_in.shape[1])
    inputs = lax.all_gather(residual_in[0], "latent", axis=1, tiled=True)
    preact = matmul(inputs, enc_weight[0]) + enc_bias[0]
    codes_now = jnp.maximum(preact, 0.0).astype(BF16)
    earlier = passed_along(codes_now, "layer", 1)
    cross_full = lax.all_gather(dec_cross, "layer", axis=1, tiled=True)
    own_dec = dec_same[0]
    half_width = own_dec.shape[1] // 2
    recon_full = lax.psum(matmul(codes_now, own_dec) + matmul(earlier, cross_full), "latent")
    wanted = lax.all_gather(targets[0], "latent", axis=1, tiled=True)
    errors = ((recon_full - wanted.astype(F32)) * err_scale).astype(BF16)
    grad_same = matmul(codes_now, errors, OVER_ROWS)
    grad_full = matmul(earlier, errors, OVER_ROWS)
    returned = passed_along(grad_full[:, :half_width], "layer", -1)
    grad_cross = jnp.where(is_first, returned, grad_full[:, half_width:])
    from_next = passed_along(matmul(errors, cross_full, OVER_COLS), "layer", -1)
    grad_codes = matmul(errors, own_dec, OVER_COLS) + from_next
    grad_pre = jnp.where(preact > 0, grad_codes, 0.0).astype(BF16)
    grad_enc = matmul(inputs, grad_pre, OVER_ROWS)
    grad_bias = jnp.sum(grad_pre.astype(F32), axis=0)
    return (grad_enc[None], grad_bias[None], grad_same[None], grad_cross)


def solution(mesh):
    size = mesh.shape["latent"]
    placed = (
        P("layer", "groups", "latent"),
        P("layer", "groups", "latent"),
        P("layer", None, "latent"),
        P("layer", "latent"),
        P("layer", "latent", None),
        P("latent", "layer"),
    )
    return jax.shard_map(
        ring_shards if size % 2 == 0 and size <= RING_LIMIT else wide_shards,
        mesh=mesh,
        in_specs=placed,
        out_specs=(
            P(("groups", "layer"), None, "latent"),
            P(("groups", "layer"), "latent"),
            P(("groups", "layer"), "latent", None),
            P(("groups", "latent"), "layer"),
        ),
        check_vma=False,
    )
```

```python
import functools
import math

import jax
import jax.numpy as jnp
from jax import lax
from jax.experimental import pallas as pl
from jax.experimental.pallas import tpu as pltpu
from jax.sharding import PartitionSpec as P

F32 = jnp.float32
BF16 = jnp.bfloat16
OVER_ROWS = (((0,), (0,)), ((), ()))
OVER_COLS = (((1,), (1,)), ((), ()))
RING_LIMIT = 16
VMEM_BYTES = 24 * 1024 * 1024
PIECES = 8


def passed_along(shard, axis, by):
    size = lax.axis_size(axis)
    pairs = [(i, i + by) for i in range(size) if 0 <= i + by < size]
    return lax.ppermute(shard, axis, pairs)


def swapped(shard):
    size = lax.axis_size("layer")
    return lax.ppermute(shard, "layer", [(i, size - 1 - i) for i in range(size)])


def matmul(a, b, dims=(((1,), (0,)), ((), ()))):
    return lax.dot_general(a, b, dims, preferred_element_type=F32)


def ring_order(size):
    return [2 * p if p < size // 2 else 2 * (size - 1 - p) + 1 for p in range(size)]


def ring_member(place, size):
    place = lax.rem(place + 2 * size, size)
    return jnp.where(place < size // 2, 2 * place, 2 * (size - 1 - place) + 1)


def ring_place(member, size):
    return jnp.where(member % 2 == 0, member // 2, size - 1 - member // 2)


def hop(shard, way):
    size, layers = lax.axis_size("latent"), lax.axis_size("layer")
    order = ring_order(size)
    pairs = []
    for p in range(size):
        for layer in range(layers):
            by = way if layer % 2 == 0 else -way
            pairs.append((order[p] * layers + layer, order[(p + by) % size] * layers + layer))
    return lax.ppermute(shard, ("latent", "layer"), pairs)


def after(value, *others):
    return lax.optimization_barrier((value,) + others)[0]


def call(kernel, outs, flops, operands, spaces=None, out_spaces=None, scratch=(), aliases=None):
    def spec(space):
        return pl.BlockSpec(memory_space=space)

    spaces = spaces or [pltpu.VMEM] * (len(operands) - 1)
    out_spaces = out_spaces or [pltpu.VMEM] * len(outs)
    return pl.pallas_call(
        kernel,
        out_shape=outs,
        in_specs=[spec(pltpu.SMEM)] + [spec(space) for space in spaces],
        out_specs=[spec(space) for space in out_spaces],
        scratch_shapes=list(scratch),
        input_output_aliases=aliases or {},
        compiler_params=pltpu.CompilerParams(vmem_limit_bytes=VMEM_BYTES),
        cost_estimate=pl.CostEstimate(flops=flops, bytes_accessed=1024, transcendentals=0),
    )(*operands)


def block_of(starts, slot, wide):
    return pl.ds(pl.multiple_of(starts[slot], wide), wide)


def encode_kernel(slots, first, last, starts, *refs):
    count = 2 * len(slots)
    shards, (weight, before, *outs) = refs[:count], refs[count:]
    rows, wide = shards[0].shape
    for chain in range(2):
        at = slice(chain * rows, (chain + 1) * rows)
        total = jnp.broadcast_to(before[...], (rows, before.shape[1])) if first else before[at, :]
        for i, slot in enumerate(slots):
            block = weight[0, block_of(starts, slot, wide), :]
            total = total + jnp.dot(shards[2 * i + chain][...], block, preferred_element_type=F32)
        outs[0][at, :] = total
        if last:
            outs[1][at, :] = jnp.maximum(total, 0.0).astype(BF16)


def turn_own_kernel(starts, shard, *refs):
    refs[-1][...] = shard[...].T


def turn_kernel(starts, own_0, own_1, *refs):
    *shards, turned = refs
    rows, wide = shards[0].shape
    for chain, own in enumerate((own_0, own_1)):
        turned[block_of(starts, 0, wide), chain * rows:(chain + 1) * rows] = own[...]
    for k in range(len(shards) // 2):
        at = block_of(starts, k + 1, wide)
        for chain in range(2):
            turned[at, chain * rows:(chain + 1) * rows] = shards[2 * k + chain][...].T


def spread_kernel(slots, starts, codes, earlier, stacked, *outs):
    rows = codes.shape[0] // 2
    outs = list(outs)
    for chain in range(2):
        at = slice(chain * rows, (chain + 1) * rows)
        both = jnp.concatenate([codes[at, :], earlier[at, :]], axis=1)
        for slot in slots:
            partial = outs.pop(0)
            block = stacked[:, block_of(starts, slot, partial.shape[1])]
            partial[...] = jnp.dot(both, block, preferred_element_type=F32).astype(partial.dtype)
        if len(outs) > (1 - chain) * len(slots):
            outs.pop(0)[...] = both.T


def back_products(slots, starts, shards, stacked, both_t, before):
    wide = shards[0].shape[1]
    blocks, totals = [], [None, None] if before is None else [before[0], before[1]]
    for i, slot in enumerate(slots):
        decoder = stacked[:, block_of(starts, slot, wide)]
        block = 0.0
        for chain in range(2):
            error = shards[2 * i + chain][...]
            block = block + jnp.dot(both_t[chain][...], error, preferred_element_type=F32)
            term = lax.dot_general(error, decoder, OVER_COLS, preferred_element_type=F32)
            totals[chain] = term if totals[chain] is None else totals[chain] + term
        blocks.append(block)
    return blocks, totals


def back_kernel(slots, first, starts, *refs):
    count = 2 * len(slots)
    shards, (stacked, *both_t), (*before, outer, back) = refs[:count], refs[count:count + 3], refs[count + 3:]
    blocks, totals = back_products(slots, starts, shards, stacked, both_t, None if first else before[0])
    for i, block in enumerate(blocks):
        outer[i] = block
    for chain in range(2):
        back[chain] = totals[chain]


def cross_back_kernel(slots, far, starts, *refs):
    shards, (stacked, *both_t), outers, (before, sent, high) = refs[:2], refs[2:5], refs[5:-3], refs[-3:]
    rows, wide = shards[0].shape
    half_width, lat = high.shape

    @pl.when(starts[starts.shape[0] - 1] != 0)
    def _():
        decoder = stacked[lat:, block_of(starts, far, wide)]
        last = 0.0
        for chain in range(2):
            error = shards[chain][...]
            last = last + jnp.dot(both_t[chain][lat:, :], error, preferred_element_type=F32)
            term = lax.dot_general(error, decoder, OVER_COLS, preferred_element_type=F32)
            sent[chain * rows:(chain + 1) * rows, :] = (before[chain, :, lat:] + term).astype(BF16)
        pieces = [(far, last)]
        for group, outer in zip(slots, outers):
            pieces += [(slot, outer[i, lat:]) for i, slot in enumerate(group)]
        for slot, piece in pieces:
            start = pl.multiple_of(starts[slot], wide)

            @pl.when(start < half_width)
            def _():
                for c in range(0, wide, lat):
                    sent[pl.ds(2 * rows + start + c, lat), :] = piece[:, c:c + lat].astype(BF16)

            @pl.when(start >= half_width)
            def _():
                for c in range(0, wide, lat):
                    high[pl.ds(start - half_width + c, lat), :] = piece[:, c:c + lat]


def own_back_kernel(slots, far, starts, *refs):
    shards, (stacked, *both_t), refs = refs[:2], refs[2:5], refs[5:]
    outers, (before, back_own, same, last, sems) = refs[:-5], refs[-5:]
    rows, wide = shards[0].shape
    lat = back_own.shape[1]
    blocks = []
    for group, outer in zip(slots, outers):
        blocks += [(slot, outer.at[i, :lat, :]) for i, slot in enumerate(group)]
    blocks.append((far, last))
    copies = []
    for i, (slot, block) in enumerate(blocks):
        copies.append(pltpu.make_async_copy(block, same.at[0, :, block_of(starts, slot, wide)], sems.at[i]))
    for copy in copies[:-1]:
        copy.start()
    decoder = stacked[:lat, block_of(starts, far, wide)]
    total = 0.0
    for chain in range(2):
        error = shards[chain][...]
        total = total + jnp.dot(both_t[chain][:lat, :], error, preferred_element_type=F32)
        term = lax.dot_general(error, decoder, OVER_COLS, preferred_element_type=F32)
        back_own[chain * rows:(chain + 1) * rows, :] = before[chain, :, :lat] + term
    last[...] = total
    copies[-1].start()
    for copy in copies:
        copy.wait()


def finish_kernel(
    starts, turned, preact, back_own, arrived, high, grad, bias, cross, stage, cross_stage, grad_sems, cross_sem
):
    pieces, height, lat = stage.shape
    rows = preact.shape[0]
    half_width = high.shape[0]
    first = starts[starts.shape[0] - 1] == 0
    later = jnp.where(first, arrived[:rows, :].astype(F32), 0.0)
    value = jnp.where(preact[...] > 0, back_own[...] + later, 0.0).astype(BF16)
    copies = []
    for i in range(pieces):
        at = pl.ds(i * height, height)
        stage[i] = jnp.dot(turned[at, :], value, preferred_element_type=F32)
        copies.append(pltpu.make_async_copy(stage.at[i], grad.at[0, at, :], grad_sems.at[i]))
        copies[-1].start()
        if i == 0:
            for c in range(0, half_width, lat):
                source = arrived[rows + c:rows + c + lat, :].astype(F32)
                cross_stage[:, c:c + lat] = jnp.where(first, source, high[c:c + lat, :])
            copies.append(pltpu.make_async_copy(cross_stage, cross, cross_sem))
            copies[-1].start()
    bias[...] = jnp.sum(value.astype(F32), axis=0, keepdims=True)
    for copy in copies:
        copy.wait()


def ring_shards(residual_in, targets, enc_weight, enc_bias, dec_same, dec_cross):
    size = lax.axis_size("latent")
    reach = size // 2
    place = ring_place(lax.axis_index("latent"), size)
    layer = lax.axis_index("layer")
    sign = jnp.where(layer % 2 == 0, 1, -1)
    rows, wide = residual_in.shape[1:]
    half = rows // 2
    deep, lat = enc_weight.shape[1:]
    half_width = deep // 2
    err_scale = 1.0 / math.sqrt(rows)
    shape = jax.ShapeDtypeStruct
    unit = rows * wide * lat
    chains = (0, 1)

    def halves(array):
        return [array[:half], array[half:]]

    slot_p = {s: 2 * s - 1 for s in range(1, reach)}
    slot_q = {s: 2 * s for s in range(1, reach)}
    far = size - 1
    offsets = [0] * size
    offsets[far] = reach
    for s in range(1, reach):
        offsets[slot_p[s]] = -s
        offsets[slot_q[s]] = s
    starts = jnp.stack([ring_member(place + sign * offset, size) * wide for offset in offsets] + [layer])
    starts = starts.astype(jnp.int32)

    urgent, later = ((0, -1), (1, 1)), ((0, 1), (1, -1))

    def gather_step(found, s, ready=None):
        for chain, way in urgent + later if s < reach else urgent:
            slots = slot_p if way == 1 else slot_q
            shard = found[chain][slots[s - 1] if s > 1 else 0]
            if ready is not None and (chain, way) in later:
                shard = after(shard, ready[chain])
            found[chain][slots[s] if s < reach else far] = hop(shard, way)

    def both_chains(found, slots):
        return [found[chain][slot] for slot in slots for chain in chains]

    def encode(slots, before):
        first, last = slots[0] == 0, slots[-1] == far
        return call(
            functools.partial(encode_kernel, slots, first, last),
            [shape((rows, lat), F32)] + ([shape((rows, lat), BF16)] if last else []),
            2 * unit * len(slots),
            [starts] + both_chains(inputs, slots) + [enc_weight, before],
        )

    inputs = [[part] + [None] * (size - 1) for part in halves(residual_in[0])]
    turned_own = []
    for chain in chains:
        source = inputs[chain][0]
        turned_own += call(turn_own_kernel, [shape((wide, half), BF16)], 0, [starts, source])
    for s in range(1, reach + 1):
        gather_step(inputs, s, turned_own if s == 1 else None)
    low_cross = swapped(after(dec_cross, inputs[0][slot_p.get(1, far)]))
    cross = jnp.where(layer > 0, jnp.concatenate([low_cross, dec_cross], axis=1), jnp.zeros((), BF16))
    stacked = jnp.concatenate([dec_same[0], cross], axis=0)
    part = encode(tuple(range(far)), after(enc_bias, stacked))[0]
    preact, codes = encode((far,), part)
    earlier = swapped(codes)

    def spread(slots, dtypes, turned):
        outs = []
        for chain in chains:
            outs += [shape((half, wide), dtypes[chain].get(slot, F32)) for slot in slots]
            outs += [shape((2 * lat, half), BF16)] if turned else []
        found = call(
            functools.partial(spread_kernel, slots), outs, 4 * unit * len(slots), [starts, codes, earlier, stacked]
        )
        return found[:len(outs) // 2], found[len(outs) // 2:]

    rest = tuple(slot for slot in range(size) if slot != far)
    instant = tuple({far: BF16, (slot_q if way == 1 else slot_p).get(reach - 1): BF16} for _, way in later)
    far_0, far_1 = spread((far,), instant, False)
    moving = {loop: hop(message, loop[1]) for loop, message in zip(urgent, (far_0[0], far_1[0]))}
    partial, both_t = [], []
    for pieces in spread(rest, instant, True):
        partial.append(dict(zip(rest, pieces)))
        both_t.append(pieces[-1])
    before = []
    for s in range(reach - 1, 0, -1):
        landed = [moving[loop] for loop in urgent]
        for chain, way in urgent + later:
            message = partial[chain][slot_q[s] if way == 1 else slot_p[s]]
            if (chain, way) in moving:
                message = (message + moving[chain, way].astype(F32)).astype(BF16)
            if (chain, way) in later and before:
                message = after(message, *before)
            moving[chain, way] = hop(message, way)
        before = landed
    errors = []
    for chain, wanted in zip(chains, halves(targets[0])):
        total = partial[chain][0]
        for way in (1, -1):
            if (chain, way) in moving:
                total = total + moving[chain, way].astype(F32)
        if chain == 1:
            wanted = after(wanted, codes)
        errors.append([((total - wanted.astype(F32)) * err_scale).astype(BF16)] + [None] * (size - 1))

    def back(slots, before):
        return call(
            functools.partial(back_kernel, slots, before is None),
            [shape((len(slots), 2 * lat, wide), F32), shape((2, half, 2 * lat), F32)],
            4 * unit * len(slots),
            [starts] + both_chains(errors, slots) + [stacked] + both_t + ([] if before is None else [before]),
        )

    groups, outers, acc, pending = [], [], None, [0]
    arrived = [after(inputs[0][1], errors[1][0])]
    turned = call(
        turn_kernel,
        [shape((deep, rows), BF16)],
        0,
        [starts] + turned_own + arrived + both_chains(inputs, range(1, size))[1:],
    )[0]
    for s in range(1, reach + 1):
        gather_step(errors, s, (turned, turned) if s == 2 else None)
    cut = 1 + 2 * min(1, reach - 1)
    groups = [group for group in (tuple(range(cut)), tuple(range(cut, far))) if group]
    outers, acc = [], None
    for group in groups:
        outer, acc = back(group, acc)
        outers.append(outer)
    last = both_chains(errors, (far,)) + [stacked] + both_t + outers + [acc]
    sent, high = call(
        functools.partial(cross_back_kernel, groups, far),
        [shape((rows + half_width, lat), BF16), shape((half_width, lat), F32)],
        0,
        [starts] + last,
    )
    returned = swapped(sent)
    back_own, grad_same = call(
        functools.partial(own_back_kernel, groups, far),
        [shape((rows, lat), F32), shape((1, lat, deep), F32)],
        0,
        [starts] + last,
        out_spaces=[pltpu.VMEM, pl.ANY],
        scratch=[pltpu.VMEM((lat, wide), F32), pltpu.SemaphoreType.DMA((size,))],
    )
    height = deep // PIECES
    grad_enc, grad_bias, grad_cross = call(
        finish_kernel,
        [shape((1, deep, lat), F32), shape((1, lat), F32), shape((lat, half_width), F32)],
        2 * unit * size,
        [starts, turned, preact, back_own, returned, high],
        out_spaces=[pl.ANY, pltpu.VMEM, pl.ANY],
        scratch=[
            pltpu.VMEM((PIECES, height, lat), F32),
            pltpu.VMEM((lat, half_width), F32),
            pltpu.SemaphoreType.DMA((PIECES,)),
            pltpu.SemaphoreType.DMA,
        ],
    )
    return (grad_enc, grad_bias, grad_same, grad_cross)


def wide_shards(residual_in, targets, enc_weight, enc_bias, dec_same, dec_cross):
    is_first = lax.axis_index("layer") == 0
    err_scale = 1.0 / math.sqrt(residual_in.shape[1])
    inputs = lax.all_gather(residual_in[0], "latent", axis=1, tiled=True)
    preact = matmul(inputs, enc_weight[0]) + enc_bias[0]
    codes_now = jnp.maximum(preact, 0.0).astype(BF16)
    earlier = passed_along(codes_now, "layer", 1)
    cross_full = lax.all_gather(dec_cross, "layer", axis=1, tiled=True)
    own_dec = dec_same[0]
    half_width = own_dec.shape[1] // 2
    recon_full = lax.psum(matmul(codes_now, own_dec) + matmul(earlier, cross_full), "latent")
    wanted = lax.all_gather(targets[0], "latent", axis=1, tiled=True)
    errors = ((recon_full - wanted.astype(F32)) * err_scale).astype(BF16)
    grad_same = matmul(codes_now, errors, OVER_ROWS)
    grad_full = matmul(earlier, errors, OVER_ROWS)
    returned = passed_along(grad_full[:, :half_width], "layer", -1)
    grad_cross = jnp.where(is_first, returned, grad_full[:, half_width:])
    from_next = passed_along(matmul(errors, cross_full, OVER_COLS), "layer", -1)
    grad_codes = matmul(errors, own_dec, OVER_COLS) + from_next
    grad_pre = jnp.where(preact > 0, grad_codes, 0.0).astype(BF16)
    grad_enc = matmul(inputs, grad_pre, OVER_ROWS)
    grad_bias = jnp.sum(grad_pre.astype(F32), axis=0)
    return (grad_enc[None], grad_bias[None], grad_same[None], grad_cross)


def solution(mesh):
    size = mesh.shape["latent"]
    placed = (
        P("layer", "groups", "latent"),
        P("layer", "groups", "latent"),
        P("layer", None, "latent"),
        P("layer", "latent"),
        P("layer", "latent", None),
        P("latent", "layer"),
    )
    return jax.shard_map(
        ring_shards if size % 2 == 0 and size <= RING_LIMIT else wide_shards,
        mesh=mesh,
        in_specs=placed,
        out_specs=(
            P(("groups", "layer"), None, "latent"),
            P(("groups", "layer"), "latent"),
            P(("groups", "layer"), "latent", None),
            P(("groups", "latent"), "layer"),
        ),
        check_vma=False,
    )
```

```python
import functools
import math

import jax
import jax.numpy as jnp
from jax import lax
from jax.experimental import pallas as pl
from jax.experimental.pallas import tpu as pltpu
from jax.sharding import PartitionSpec as P

F32 = jnp.float32
BF16 = jnp.bfloat16
OVER_ROWS = (((0,), (0,)), ((), ()))
OVER_COLS = (((1,), (1,)), ((), ()))
RING_LIMIT = 16
VMEM_BYTES = 24 * 1024 * 1024
PIECES = 8


def passed_along(shard, axis, by):
    size = lax.axis_size(axis)
    pairs = [(i, i + by) for i in range(size) if 0 <= i + by < size]
    return lax.ppermute(shard, axis, pairs)


def swapped(shard):
    size = lax.axis_size("layer")
    return lax.ppermute(shard, "layer", [(i, size - 1 - i) for i in range(size)])


def matmul(a, b, dims=(((1,), (0,)), ((), ()))):
    return lax.dot_general(a, b, dims, preferred_element_type=F32)


def ring_order(size):
    return [2 * p if p < size // 2 else 2 * (size - 1 - p) + 1 for p in range(size)]


def ring_member(place, size):
    place = lax.rem(place + 2 * size, size)
    return jnp.where(place < size // 2, 2 * place, 2 * (size - 1 - place) + 1)


def ring_place(member, size):
    return jnp.where(member % 2 == 0, member // 2, size - 1 - member // 2)


def hop(shard, way):
    size, layers = lax.axis_size("latent"), lax.axis_size("layer")
    order = ring_order(size)
    pairs = []
    for p in range(size):
        for layer in range(layers):
            by = way if layer % 2 == 0 else -way
            pairs.append((order[p] * layers + layer, order[(p + by) % size] * layers + layer))
    return lax.ppermute(shard, ("latent", "layer"), pairs)


def after(value, *others):
    return lax.optimization_barrier((value,) + others)[0]


def call(kernel, outs, flops, operands, spaces=None, out_spaces=None, scratch=(), aliases=None):
    def spec(space):
        return pl.BlockSpec(memory_space=space)

    spaces = spaces or [pltpu.VMEM] * (len(operands) - 1)
    out_spaces = out_spaces or [pltpu.VMEM] * len(outs)
    return pl.pallas_call(
        kernel,
        out_shape=outs,
        in_specs=[spec(pltpu.SMEM)] + [spec(space) for space in spaces],
        out_specs=[spec(space) for space in out_spaces],
        scratch_shapes=list(scratch),
        input_output_aliases=aliases or {},
        compiler_params=pltpu.CompilerParams(vmem_limit_bytes=VMEM_BYTES),
        cost_estimate=pl.CostEstimate(flops=flops, bytes_accessed=1024, transcendentals=0),
    )(*operands)


def block_of(starts, slot, wide):
    return pl.ds(pl.multiple_of(starts[slot], wide), wide)


def encode_kernel(slots, first, last, starts, *refs):
    count = 2 * len(slots)
    shards, (weight, before, *outs) = refs[:count], refs[count:]
    rows, wide = shards[0].shape
    for chain in range(2):
        at = slice(chain * rows, (chain + 1) * rows)
        total = jnp.broadcast_to(before[...], (rows, before.shape[1])) if first else before[at, :]
        for i, slot in enumerate(slots):
            block = weight[0, block_of(starts, slot, wide), :]
            total = total + jnp.dot(shards[2 * i + chain][...], block, preferred_element_type=F32)
        outs[0][at, :] = total
        if last:
            outs[1][at, :] = jnp.maximum(total, 0.0).astype(BF16)


def turn_own_kernel(starts, shard, *refs):
    refs[-1][...] = shard[...].T


def turn_kernel(starts, own_0, own_1, *refs):
    *shards, turned = refs
    rows, wide = shards[0].shape
    for chain, own in enumerate((own_0, own_1)):
        turned[block_of(starts, 0, wide), chain * rows:(chain + 1) * rows] = own[...]
    for k in range(len(shards) // 2):
        at = block_of(starts, k + 1, wide)
        for chain in range(2):
            turned[at, chain * rows:(chain + 1) * rows] = shards[2 * k + chain][...].T


def spread_kernel(slots, starts, codes, earlier, stacked, *outs):
    rows = codes.shape[0] // 2
    outs = list(outs)
    for chain in range(2):
        at = slice(chain * rows, (chain + 1) * rows)
        both = jnp.concatenate([codes[at, :], earlier[at, :]], axis=1)
        for slot in slots:
            partial = outs.pop(0)
            block = stacked[:, block_of(starts, slot, partial.shape[1])]
            partial[...] = jnp.dot(both, block, preferred_element_type=F32).astype(partial.dtype)
        if len(outs) > (1 - chain) * len(slots):
            outs.pop(0)[...] = both.T


def back_products(slots, starts, shards, stacked, both_t, before):
    wide = shards[0].shape[1]
    blocks, totals = [], [None, None] if before is None else [before[0], before[1]]
    for i, slot in enumerate(slots):
        decoder = stacked[:, block_of(starts, slot, wide)]
        block = 0.0
        for chain in range(2):
            error = shards[2 * i + chain][...]
            block = block + jnp.dot(both_t[chain][...], error, preferred_element_type=F32)
            term = lax.dot_general(error, decoder, OVER_COLS, preferred_element_type=F32)
            totals[chain] = term if totals[chain] is None else totals[chain] + term
        blocks.append(block)
    return blocks, totals


def back_kernel(slots, first, starts, *refs):
    count = 2 * len(slots)
    shards, (stacked, *both_t), (*before, outer, back) = refs[:count], refs[count:count + 3], refs[count + 3:]
    blocks, totals = back_products(slots, starts, shards, stacked, both_t, None if first else before[0])
    for i, block in enumerate(blocks):
        outer[i] = block
    for chain in range(2):
        back[chain] = totals[chain]


def cross_back_kernel(slots, far, starts, *refs):
    shards, (stacked, *both_t), outers, (before, sent, high) = refs[:2], refs[2:5], refs[5:-3], refs[-3:]
    rows, wide = shards[0].shape
    half_width, lat = high.shape

    @pl.when(starts[starts.shape[0] - 1] != 0)
    def _():
        decoder = stacked[lat:, block_of(starts, far, wide)]
        last = 0.0
        for chain in range(2):
            error = shards[chain][...]
            last = last + jnp.dot(both_t[chain][lat:, :], error, preferred_element_type=F32)
            term = lax.dot_general(error, decoder, OVER_COLS, preferred_element_type=F32)
            sent[chain * rows:(chain + 1) * rows, :] = (before[chain, :, lat:] + term).astype(BF16)
        pieces = [(far, last)]
        for group, outer in zip(slots, outers):
            pieces += [(slot, outer[i, lat:]) for i, slot in enumerate(group)]
        for slot, piece in pieces:
            start = pl.multiple_of(starts[slot], wide)

            @pl.when(start < half_width)
            def _():
                for c in range(0, wide, lat):
                    sent[pl.ds(2 * rows + start + c, lat), :] = piece[:, c:c + lat].astype(BF16)

            @pl.when(start >= half_width)
            def _():
                for c in range(0, wide, lat):
                    high[pl.ds(start - half_width + c, lat), :] = piece[:, c:c + lat]


def own_back_kernel(slots, far, starts, *refs):
    shards, (stacked, *both_t), refs = refs[:2], refs[2:5], refs[5:]
    outers, (before, back_own, same, last, sems) = refs[:-5], refs[-5:]
    rows, wide = shards[0].shape
    lat = back_own.shape[1]
    blocks = []
    for group, outer in zip(slots, outers):
        blocks += [(slot, outer.at[i, :lat, :]) for i, slot in enumerate(group)]
    blocks.append((far, last))
    copies = []
    for i, (slot, block) in enumerate(blocks):
        copies.append(pltpu.make_async_copy(block, same.at[0, :, block_of(starts, slot, wide)], sems.at[i]))
    for copy in copies[:-1]:
        copy.start()
    decoder = stacked[:lat, block_of(starts, far, wide)]
    total = 0.0
    for chain in range(2):
        error = shards[chain][...]
        total = total + jnp.dot(both_t[chain][:lat, :], error, preferred_element_type=F32)
        term = lax.dot_general(error, decoder, OVER_COLS, preferred_element_type=F32)
        back_own[chain * rows:(chain + 1) * rows, :] = before[chain, :, :lat] + term
    last[...] = total
    copies[-1].start()
    for copy in copies:
        copy.wait()


def finish_kernel(
    starts, turned, preact, back_own, arrived, high, grad, bias, cross, stage, cross_stage, grad_sems, cross_sem
):
    pieces, height, lat = stage.shape
    rows = preact.shape[0]
    half_width = high.shape[0]
    first = starts[starts.shape[0] - 1] == 0
    later = jnp.where(first, arrived[:rows, :].astype(F32), 0.0)
    value = jnp.where(preact[...] > 0, back_own[...] + later, 0.0).astype(BF16)
    copies = []
    for i in range(pieces):
        at = pl.ds(i * height, height)
        stage[i] = jnp.dot(turned[at, :], value, preferred_element_type=F32)
        copies.append(pltpu.make_async_copy(stage.at[i], grad.at[0, at, :], grad_sems.at[i]))
        copies[-1].start()
        if i == 0:
            for c in range(0, half_width, lat):
                source = arrived[rows + c:rows + c + lat, :].astype(F32)
                cross_stage[:, c:c + lat] = jnp.where(first, source, high[c:c + lat, :])
            copies.append(pltpu.make_async_copy(cross_stage, cross, cross_sem))
            copies[-1].start()
    bias[...] = jnp.sum(value.astype(F32), axis=0, keepdims=True)
    for copy in copies:
        copy.wait()


def ring_shards(residual_in, targets, enc_weight, enc_bias, dec_same, dec_cross):
    size = lax.axis_size("latent")
    reach = size // 2
    place = ring_place(lax.axis_index("latent"), size)
    layer = lax.axis_index("layer")
    sign = jnp.where(layer % 2 == 0, 1, -1)
    rows, wide = residual_in.shape[1:]
    half = rows // 2
    deep, lat = enc_weight.shape[1:]
    half_width = deep // 2
    err_scale = 1.0 / math.sqrt(rows)
    shape = jax.ShapeDtypeStruct
    unit = rows * wide * lat
    chains = (0, 1)

    def halves(array):
        return [array[:half], array[half:]]

    slot_p = {s: 2 * s - 1 for s in range(1, reach)}
    slot_q = {s: 2 * s for s in range(1, reach)}
    far = size - 1
    offsets = [0] * size
    offsets[far] = reach
    for s in range(1, reach):
        offsets[slot_p[s]] = -s
        offsets[slot_q[s]] = s
    starts = jnp.stack([ring_member(place + sign * offset, size) * wide for offset in offsets] + [layer])
    starts = starts.astype(jnp.int32)

    urgent, later = ((0, -1), (1, 1)), ((0, 1), (1, -1))

    def gather_step(found, s, ready=None):
        for chain, way in urgent + later if s < reach else urgent:
            slots = slot_p if way == 1 else slot_q
            shard = found[chain][slots[s - 1] if s > 1 else 0]
            if ready is not None and (chain, way) in later:
                shard = after(shard, ready[chain])
            found[chain][slots[s] if s < reach else far] = hop(shard, way)

    def both_chains(found, slots):
        return [found[chain][slot] for slot in slots for chain in chains]

    def encode(slots, before):
        first, last = slots[0] == 0, slots[-1] == far
        return call(
            functools.partial(encode_kernel, slots, first, last),
            [shape((rows, lat), F32)] + ([shape((rows, lat), BF16)] if last else []),
            2 * unit * len(slots),
            [starts] + both_chains(inputs, slots) + [enc_weight, before],
        )

    inputs = [[part] + [None] * (size - 1) for part in halves(residual_in[0])]
    turned_own = []
    for chain in chains:
        source = inputs[chain][0]
        turned_own += call(turn_own_kernel, [shape((wide, half), BF16)], 0, [starts, source])
    for s in range(1, reach + 1):
        gather_step(inputs, s, turned_own if s == 1 else None)
    low_cross = swapped(after(dec_cross, inputs[0][slot_p.get(1, far)]))
    cross = jnp.where(layer > 0, jnp.concatenate([low_cross, dec_cross], axis=1), jnp.zeros((), BF16))
    stacked = jnp.concatenate([dec_same[0], cross], axis=0)
    part = encode(tuple(range(far)), after(enc_bias, stacked))[0]
    preact, codes = encode((far,), part)
    earlier = swapped(codes)

    def spread(slots, dtypes, turned):
        outs = []
        for chain in chains:
            outs += [shape((half, wide), dtypes[chain].get(slot, F32)) for slot in slots]
            outs += [shape((2 * lat, half), BF16)] if turned else []
        found = call(
            functools.partial(spread_kernel, slots), outs, 4 * unit * len(slots), [starts, codes, earlier, stacked]
        )
        return found[:len(outs) // 2], found[len(outs) // 2:]

    rest = tuple(slot for slot in range(size) if slot != far)
    instant = tuple({far: BF16, (slot_q if way == 1 else slot_p).get(reach - 1): BF16} for _, way in later)
    block = lax.dynamic_slice_in_dim(stacked, starts[far], wide, 1)
    far_0, far_1 = [
        [(matmul(now, block[:lat]) + matmul(before, block[lat:])).astype(BF16)]
        for now, before in zip(halves(codes), halves(earlier))
    ]
    moving = {loop: hop(message, loop[1]) for loop, message in zip(urgent, (far_0[0], far_1[0]))}
    partial, both_t = [], []
    for pieces in spread(rest, instant, True):
        partial.append(dict(zip(rest, pieces)))
        both_t.append(pieces[-1])
    before = []
    for s in range(reach - 1, 0, -1):
        landed = [moving[loop] for loop in urgent]
        for chain, way in urgent + later:
            message = partial[chain][slot_q[s] if way == 1 else slot_p[s]]
            if (chain, way) in moving:
                message = (message + moving[chain, way].astype(F32)).astype(BF16)
            if (chain, way) in later and before:
                message = after(message, *before)
            moving[chain, way] = hop(message, way)
        before = landed
    errors = []
    for chain, wanted in zip(chains, halves(targets[0])):
        total = partial[chain][0]
        for way in (1, -1):
            if (chain, way) in moving:
                total = total + moving[chain, way].astype(F32)
        if chain == 1:
            wanted = after(wanted, codes)
        errors.append([((total - wanted.astype(F32)) * err_scale).astype(BF16)] + [None] * (size - 1))

    def back(slots, before):
        return call(
            functools.partial(back_kernel, slots, before is None),
            [shape((len(slots), 2 * lat, wide), F32), shape((2, half, 2 * lat), F32)],
            4 * unit * len(slots),
            [starts] + both_chains(errors, slots) + [stacked] + both_t + ([] if before is None else [before]),
        )

    groups, outers, acc, pending = [], [], None, [0]
    arrived = [after(inputs[0][1], errors[1][0])]
    turned = call(
        turn_kernel,
        [shape((deep, rows), BF16)],
        0,
        [starts] + turned_own + arrived + both_chains(inputs, range(1, size))[1:],
    )[0]
    groups = [group for group in ((0,), tuple(range(1, far))) if group]
    outer, acc = back(groups[0], None)
    outers = [outer]
    for s in range(1, reach + 1):
        gather_step(errors, s, (turned, acc) if s == 1 else None)
    for group in groups[1:]:
        outer, acc = back(group, acc)
        outers.append(outer)
    last = both_chains(errors, (far,)) + [stacked] + both_t + outers + [acc]
    sent, high = call(
        functools.partial(cross_back_kernel, groups, far),
        [shape((rows + half_width, lat), BF16), shape((half_width, lat), F32)],
        0,
        [starts] + last,
    )
    returned = swapped(sent)
    back_own, grad_same = call(
        functools.partial(own_back_kernel, groups, far),
        [shape((rows, lat), F32), shape((1, lat, deep), F32)],
        0,
        [starts] + last,
        out_spaces=[pltpu.VMEM, pl.ANY],
        scratch=[pltpu.VMEM((lat, wide), F32), pltpu.SemaphoreType.DMA((size,))],
    )
    height = deep // PIECES
    grad_enc, grad_bias, grad_cross = call(
        finish_kernel,
        [shape((1, deep, lat), F32), shape((1, lat), F32), shape((lat, half_width), F32)],
        2 * unit * size,
        [starts, turned, preact, back_own, returned, high],
        out_spaces=[pl.ANY, pltpu.VMEM, pl.ANY],
        scratch=[
            pltpu.VMEM((PIECES, height, lat), F32),
            pltpu.VMEM((lat, half_width), F32),
            pltpu.SemaphoreType.DMA((PIECES,)),
            pltpu.SemaphoreType.DMA,
        ],
    )
    return (grad_enc, grad_bias, grad_same, grad_cross)


def wide_shards(residual_in, targets, enc_weight, enc_bias, dec_same, dec_cross):
    is_first = lax.axis_index("layer") == 0
    err_scale = 1.0 / math.sqrt(residual_in.shape[1])
    inputs = lax.all_gather(residual_in[0], "latent", axis=1, tiled=True)
    preact = matmul(inputs, enc_weight[0]) + enc_bias[0]
    codes_now = jnp.maximum(preact, 0.0).astype(BF16)
    earlier = passed_along(codes_now, "layer", 1)
    cross_full = lax.all_gather(dec_cross, "layer", axis=1, tiled=True)
    own_dec = dec_same[0]
    half_width = own_dec.shape[1] // 2
    recon_full = lax.psum(matmul(codes_now, own_dec) + matmul(earlier, cross_full), "latent")
    wanted = lax.all_gather(targets[0], "latent", axis=1, tiled=True)
    errors = ((recon_full - wanted.astype(F32)) * err_scale).astype(BF16)
    grad_same = matmul(codes_now, errors, OVER_ROWS)
    grad_full = matmul(earlier, errors, OVER_ROWS)
    returned = passed_along(grad_full[:, :half_width], "layer", -1)
    grad_cross = jnp.where(is_first, returned, grad_full[:, half_width:])
    from_next = passed_along(matmul(errors, cross_full, OVER_COLS), "layer", -1)
    grad_codes = matmul(errors, own_dec, OVER_COLS) + from_next
    grad_pre = jnp.where(preact > 0, grad_codes, 0.0).astype(BF16)
    grad_enc = matmul(inputs, grad_pre, OVER_ROWS)
    grad_bias = jnp.sum(grad_pre.astype(F32), axis=0)
    return (grad_enc[None], grad_bias[None], grad_same[None], grad_cross)


def solution(mesh):
    size = mesh.shape["latent"]
    placed = (
        P("layer", "groups", "latent"),
        P("layer", "groups", "latent"),
        P("layer", None, "latent"),
        P("layer", "latent"),
        P("layer", "latent", None),
        P("latent", "layer"),
    )
    return jax.shard_map(
        ring_shards if size % 2 == 0 and size <= RING_LIMIT else wide_shards,
        mesh=mesh,
        in_specs=placed,
        out_specs=(
            P(("groups", "layer"), None, "latent"),
            P(("groups", "layer"), "latent"),
            P(("groups", "layer"), "latent", None),
            P(("groups", "latent"), "layer"),
        ),
        check_vma=False,
    )
```

```python
import functools
import math

import jax
import jax.numpy as jnp
from jax import lax
from jax.experimental import pallas as pl
from jax.experimental.pallas import tpu as pltpu
from jax.sharding import PartitionSpec as P

F32 = jnp.float32
BF16 = jnp.bfloat16
OVER_ROWS = (((0,), (0,)), ((), ()))
OVER_COLS = (((1,), (1,)), ((), ()))
RING_LIMIT = 16
VMEM_BYTES = 24 * 1024 * 1024
PIECES = 16


def passed_along(shard, axis, by):
    size = lax.axis_size(axis)
    pairs = [(i, i + by) for i in range(size) if 0 <= i + by < size]
    return lax.ppermute(shard, axis, pairs)


def swapped(shard):
    size = lax.axis_size("layer")
    return lax.ppermute(shard, "layer", [(i, size - 1 - i) for i in range(size)])


def matmul(a, b, dims=(((1,), (0,)), ((), ()))):
    return lax.dot_general(a, b, dims, preferred_element_type=F32)


def ring_order(size):
    return [2 * p if p < size // 2 else 2 * (size - 1 - p) + 1 for p in range(size)]


def ring_member(place, size):
    place = lax.rem(place + 2 * size, size)
    return jnp.where(place < size // 2, 2 * place, 2 * (size - 1 - place) + 1)


def ring_place(member, size):
    return jnp.where(member % 2 == 0, member // 2, size - 1 - member // 2)


def hop(shard, way):
    size, layers = lax.axis_size("latent"), lax.axis_size("layer")
    order = ring_order(size)
    pairs = []
    for p in range(size):
        for layer in range(layers):
            by = way if layer % 2 == 0 else -way
            pairs.append((order[p] * layers + layer, order[(p + by) % size] * layers + layer))
    return lax.ppermute(shard, ("latent", "layer"), pairs)


def after(value, *others):
    return lax.optimization_barrier((value,) + others)[0]


def call(kernel, outs, flops, operands, spaces=None, out_spaces=None, scratch=(), aliases=None):
    def spec(space):
        return pl.BlockSpec(memory_space=space)

    spaces = spaces or [pltpu.VMEM] * (len(operands) - 1)
    out_spaces = out_spaces or [pltpu.VMEM] * len(outs)
    return pl.pallas_call(
        kernel,
        out_shape=outs,
        in_specs=[spec(pltpu.SMEM)] + [spec(space) for space in spaces],
        out_specs=[spec(space) for space in out_spaces],
        scratch_shapes=list(scratch),
        input_output_aliases=aliases or {},
        compiler_params=pltpu.CompilerParams(vmem_limit_bytes=VMEM_BYTES),
        cost_estimate=pl.CostEstimate(flops=flops, bytes_accessed=1024, transcendentals=0),
    )(*operands)


def block_of(starts, slot, wide):
    return pl.ds(pl.multiple_of(starts[slot], wide), wide)


def encode_kernel(slots, first, last, starts, *refs):
    count = 2 * len(slots)
    shards, (weight, before, *outs) = refs[:count], refs[count:]
    rows, wide = shards[0].shape
    for chain in range(2):
        at = slice(chain * rows, (chain + 1) * rows)
        total = jnp.broadcast_to(before[...], (rows, before.shape[1])) if first else before[at, :]
        for i, slot in enumerate(slots):
            block = weight[0, block_of(starts, slot, wide), :]
            total = total + jnp.dot(shards[2 * i + chain][...], block, preferred_element_type=F32)
        outs[0][at, :] = total
        if last:
            outs[1][at, :] = jnp.maximum(total, 0.0).astype(BF16)


def turn_own_kernel(starts, shard, *refs):
    refs[-1][...] = shard[...].T


def turn_kernel(starts, own_0, own_1, *refs):
    *shards, turned = refs
    rows, wide = shards[0].shape
    for chain, own in enumerate((own_0, own_1)):
        turned[block_of(starts, 0, wide), chain * rows:(chain + 1) * rows] = own[...]
    for k in range(len(shards) // 2):
        at = block_of(starts, k + 1, wide)
        for chain in range(2):
            turned[at, chain * rows:(chain + 1) * rows] = shards[2 * k + chain][...].T


def spread_kernel(slots, starts, codes, earlier, stacked, *outs):
    rows = codes.shape[0] // 2
    outs = list(outs)
    for chain in range(2):
        at = slice(chain * rows, (chain + 1) * rows)
        before = jnp.where(starts[starts.shape[0] - 1] > 0, earlier[at, :], jnp.zeros((), BF16))
        both = jnp.concatenate([codes[at, :], before], axis=1)
        for slot in slots:
            partial = outs.pop(0)
            block = stacked[:, block_of(starts, slot, partial.shape[1])]
            partial[...] = jnp.dot(both, block, preferred_element_type=F32).astype(partial.dtype)
        if len(outs) > (1 - chain) * len(slots):
            outs.pop(0)[...] = both.T


def back_products(slots, starts, shards, stacked, both_t, before):
    wide = shards[0].shape[1]
    blocks, totals = [], [None, None] if before is None else [before[0], before[1]]
    for i, slot in enumerate(slots):
        decoder = stacked[:, block_of(starts, slot, wide)]
        block = 0.0
        for chain in range(2):
            error = shards[2 * i + chain][...]
            block = block + jnp.dot(both_t[chain][...], error, preferred_element_type=F32)
            term = lax.dot_general(error, decoder, OVER_COLS, preferred_element_type=F32)
            totals[chain] = term if totals[chain] is None else totals[chain] + term
        blocks.append(block)
    return blocks, totals


def back_kernel(slots, first, starts, *refs):
    count = 2 * len(slots)
    shards, (stacked, *both_t), (*before, outer, back) = refs[:count], refs[count:count + 3], refs[count + 3:]
    blocks, totals = back_products(slots, starts, shards, stacked, both_t, None if first else before[0])
    for i, block in enumerate(blocks):
        outer[i] = block
    for chain in range(2):
        back[chain] = totals[chain]


def cross_back_kernel(slots, far, starts, *refs):
    shards, (stacked, *both_t), outers, (before, sent, high) = refs[:2], refs[2:5], refs[5:-3], refs[-3:]
    rows, wide = shards[0].shape
    half_width, lat = high.shape

    @pl.when(starts[starts.shape[0] - 1] != 0)
    def _():
        decoder = stacked[lat:, block_of(starts, far, wide)]
        last = 0.0
        for chain in range(2):
            error = shards[chain][...]
            last = last + jnp.dot(both_t[chain][lat:, :], error, preferred_element_type=F32)
            term = lax.dot_general(error, decoder, OVER_COLS, preferred_element_type=F32)
            sent[chain * rows:(chain + 1) * rows, :] = (before[chain, :, lat:] + term).astype(BF16)
        pieces = [(far, last)]
        for group, outer in zip(slots, outers):
            pieces += [(slot, outer[i, lat:]) for i, slot in enumerate(group)]
        for slot, piece in pieces:
            start = pl.multiple_of(starts[slot], wide)

            @pl.when(start < half_width)
            def _():
                for c in range(0, wide, lat):
                    sent[pl.ds(2 * rows + start + c, lat), :] = piece[:, c:c + lat].astype(BF16)

            @pl.when(start >= half_width)
            def _():
                for c in range(0, wide, lat):
                    high[pl.ds(start - half_width + c, lat), :] = piece[:, c:c + lat]


def own_back_kernel(slots, far, starts, *refs):
    shards, (stacked, *both_t), refs = refs[:2], refs[2:5], refs[5:]
    outers, (before, back_own, same, last, sems) = refs[:-5], refs[-5:]
    rows, wide = shards[0].shape
    lat = back_own.shape[1]
    blocks = []
    for group, outer in zip(slots, outers):
        blocks += [(slot, outer.at[i, :lat, :]) for i, slot in enumerate(group)]
    blocks.append((far, last))
    copies = []
    for i, (slot, block) in enumerate(blocks):
        copies.append(pltpu.make_async_copy(block, same.at[0, :, block_of(starts, slot, wide)], sems.at[i]))
    for copy in copies[:-1]:
        copy.start()
    decoder = stacked[:lat, block_of(starts, far, wide)]
    total = 0.0
    for chain in range(2):
        error = shards[chain][...]
        total = total + jnp.dot(both_t[chain][:lat, :], error, preferred_element_type=F32)
        term = lax.dot_general(error, decoder, OVER_COLS, preferred_element_type=F32)
        back_own[chain * rows:(chain + 1) * rows, :] = before[chain, :, :lat] + term
    last[...] = total
    copies[-1].start()
    for copy in copies:
        copy.wait()


def finish_kernel(
    starts, turned, preact, back_own, arrived, high, grad, bias, cross, stage, cross_stage, grad_sems, cross_sem
):
    pieces, height, lat = stage.shape
    rows = preact.shape[0]
    half_width = high.shape[0]
    first = starts[starts.shape[0] - 1] == 0
    later = jnp.where(first, arrived[:rows, :].astype(F32), 0.0)
    value = jnp.where(preact[...] > 0, back_own[...] + later, 0.0).astype(BF16)
    copies = []
    for i in range(pieces):
        at = pl.ds(i * height, height)
        stage[i] = jnp.dot(turned[at, :], value, preferred_element_type=F32)
        copies.append(pltpu.make_async_copy(stage.at[i], grad.at[0, at, :], grad_sems.at[i]))
        copies[-1].start()
        if i == 0:
            for c in range(0, half_width, lat):
                source = arrived[rows + c:rows + c + lat, :].astype(F32)
                cross_stage[:, c:c + lat] = jnp.where(first, source, high[c:c + lat, :])
            copies.append(pltpu.make_async_copy(cross_stage, cross, cross_sem))
            copies[-1].start()
    bias[...] = jnp.sum(value.astype(F32), axis=0, keepdims=True)
    for copy in copies:
        copy.wait()


def ring_shards(residual_in, targets, enc_weight, enc_bias, dec_same, dec_cross):
    size = lax.axis_size("latent")
    reach = size // 2
    place = ring_place(lax.axis_index("latent"), size)
    layer = lax.axis_index("layer")
    sign = jnp.where(layer % 2 == 0, 1, -1)
    rows, wide = residual_in.shape[1:]
    half = rows // 2
    deep, lat = enc_weight.shape[1:]
    half_width = deep // 2
    err_scale = 1.0 / math.sqrt(rows)
    shape = jax.ShapeDtypeStruct
    unit = rows * wide * lat
    chains = (0, 1)

    def halves(array):
        return [array[:half], array[half:]]

    slot_p = {s: 2 * s - 1 for s in range(1, reach)}
    slot_q = {s: 2 * s for s in range(1, reach)}
    far = size - 1
    offsets = [0] * size
    offsets[far] = reach
    for s in range(1, reach):
        offsets[slot_p[s]] = -s
        offsets[slot_q[s]] = s
    starts = jnp.stack([ring_member(place + sign * offset, size) * wide for offset in offsets] + [layer])
    starts = starts.astype(jnp.int32)

    urgent, later = ((0, -1), (1, 1)), ((0, 1), (1, -1))

    def gather_step(found, s, ready=None):
        for chain, way in urgent + later if s < reach else urgent:
            slots = slot_p if way == 1 else slot_q
            shard = found[chain][slots[s - 1] if s > 1 else 0]
            if ready is not None and (chain, way) in later:
                shard = after(shard, ready[chain])
            found[chain][slots[s] if s < reach else far] = hop(shard, way)

    def both_chains(found, slots):
        return [found[chain][slot] for slot in slots for chain in chains]

    def encode(slots, before):
        first, last = slots[0] == 0, slots[-1] == far
        return call(
            functools.partial(encode_kernel, slots, first, last),
            [shape((rows, lat), F32)] + ([shape((rows, lat), BF16)] if last else []),
            2 * unit * len(slots),
            [starts] + both_chains(inputs, slots) + [enc_weight, before],
        )

    inputs = [[part] + [None] * (size - 1) for part in halves(residual_in[0])]
    turned_own = []
    for chain in chains:
        source = inputs[chain][0]
        turned_own += call(turn_own_kernel, [shape((wide, half), BF16)], 0, [starts, source])
    for s in range(1, reach + 1):
        gather_step(inputs, s, turned_own if s == 1 else None)
    low_cross = swapped(after(dec_cross, inputs[0][slot_p.get(1, far)]))
    stacked = jnp.concatenate([dec_same[0], jnp.concatenate([low_cross, dec_cross], axis=1)], axis=0)
    part = encode(tuple(range(far)), after(enc_bias, stacked))[0]
    preact, codes = encode((far,), part)
    earlier = swapped(codes)

    def spread(slots, dtypes, turned):
        outs = []
        for chain in chains:
            outs += [shape((half, wide), dtypes[chain].get(slot, F32)) for slot in slots]
            outs += [shape((2 * lat, half), BF16)] if turned else []
        found = call(
            functools.partial(spread_kernel, slots), outs, 4 * unit * len(slots), [starts, codes, earlier, stacked]
        )
        return found[:len(outs) // 2], found[len(outs) // 2:]

    rest = tuple(slot for slot in range(size) if slot != far)
    instant = tuple({far: BF16, (slot_q if way == 1 else slot_p).get(reach - 1): BF16} for _, way in later)
    far_0, far_1 = spread((far,), instant, False)
    moving = {loop: hop(message, loop[1]) for loop, message in zip(urgent, (far_0[0], far_1[0]))}
    partial, both_t = [], []
    for pieces in spread(rest, instant, True):
        partial.append(dict(zip(rest, pieces)))
        both_t.append(pieces[-1])
    before = []
    for s in range(reach - 1, 0, -1):
        landed = [moving[loop] for loop in urgent]
        for chain, way in urgent + later:
            message = partial[chain][slot_q[s] if way == 1 else slot_p[s]]
            if (chain, way) in moving:
                message = (message + moving[chain, way].astype(F32)).astype(BF16)
            if (chain, way) in later and before:
                message = after(message, *before)
            moving[chain, way] = hop(message, way)
        before = landed
    errors = []
    for chain, wanted in zip(chains, halves(targets[0])):
        total = partial[chain][0]
        for way in (1, -1):
            if (chain, way) in moving:
                total = total + moving[chain, way].astype(F32)
        if chain == 1:
            wanted = after(wanted, codes)
        errors.append([((total - wanted.astype(F32)) * err_scale).astype(BF16)] + [None] * (size - 1))

    def back(slots, before):
        return call(
            functools.partial(back_kernel, slots, before is None),
            [shape((len(slots), 2 * lat, wide), F32), shape((2, half, 2 * lat), F32)],
            4 * unit * len(slots),
            [starts] + both_chains(errors, slots) + [stacked] + both_t + ([] if before is None else [before]),
        )

    groups, outers, acc, pending = [], [], None, [0]
    arrived = [after(inputs[0][1], errors[1][0])]
    turned = call(
        turn_kernel,
        [shape((deep, rows), BF16)],
        0,
        [starts] + turned_own + arrived + both_chains(inputs, range(1, size))[1:],
    )[0]
    for s in range(1, reach + 1):
        gather_step(errors, s, (turned, turned) if s == 2 else None)
    cut = 1 + 2 * min(1, reach - 1)
    groups = [group for group in (tuple(range(cut)), tuple(range(cut, far))) if group]
    outers, acc = [], None
    for group in groups:
        outer, acc = back(group, acc)
        outers.append(outer)
    last = both_chains(errors, (far,)) + [stacked] + both_t + outers + [acc]
    sent, high = call(
        functools.partial(cross_back_kernel, groups, far),
        [shape((rows + half_width, lat), BF16), shape((half_width, lat), F32)],
        0,
        [starts] + last,
    )
    returned = swapped(sent)
    back_own, grad_same = call(
        functools.partial(own_back_kernel, groups, far),
        [shape((rows, lat), F32), shape((1, lat, deep), F32)],
        0,
        [starts] + last,
        out_spaces=[pltpu.VMEM, pl.ANY],
        scratch=[pltpu.VMEM((lat, wide), F32), pltpu.SemaphoreType.DMA((size,))],
    )
    height = deep // PIECES
    grad_enc, grad_bias, grad_cross = call(
        finish_kernel,
        [shape((1, deep, lat), F32), shape((1, lat), F32), shape((lat, half_width), F32)],
        2 * unit * size,
        [starts, turned, preact, back_own, returned, high],
        out_spaces=[pl.ANY, pltpu.VMEM, pl.ANY],
        scratch=[
            pltpu.VMEM((PIECES, height, lat), F32),
            pltpu.VMEM((lat, half_width), F32),
            pltpu.SemaphoreType.DMA((PIECES,)),
            pltpu.SemaphoreType.DMA,
        ],
    )
    return (grad_enc, grad_bias, grad_same, grad_cross)


def wide_shards(residual_in, targets, enc_weight, enc_bias, dec_same, dec_cross):
    is_first = lax.axis_index("layer") == 0
    err_scale = 1.0 / math.sqrt(residual_in.shape[1])
    inputs = lax.all_gather(residual_in[0], "latent", axis=1, tiled=True)
    preact = matmul(inputs, enc_weight[0]) + enc_bias[0]
    codes_now = jnp.maximum(preact, 0.0).astype(BF16)
    earlier = passed_along(codes_now, "layer", 1)
    cross_full = lax.all_gather(dec_cross, "layer", axis=1, tiled=True)
    own_dec = dec_same[0]
    half_width = own_dec.shape[1] // 2
    recon_full = lax.psum(matmul(codes_now, own_dec) + matmul(earlier, cross_full), "latent")
    wanted = lax.all_gather(targets[0], "latent", axis=1, tiled=True)
    errors = ((recon_full - wanted.astype(F32)) * err_scale).astype(BF16)
    grad_same = matmul(codes_now, errors, OVER_ROWS)
    grad_full = matmul(earlier, errors, OVER_ROWS)
    returned = passed_along(grad_full[:, :half_width], "layer", -1)
    grad_cross = jnp.where(is_first, returned, grad_full[:, half_width:])
    from_next = passed_along(matmul(errors, cross_full, OVER_COLS), "layer", -1)
    grad_codes = matmul(errors, own_dec, OVER_COLS) + from_next
    grad_pre = jnp.where(preact > 0, grad_codes, 0.0).astype(BF16)
    grad_enc = matmul(inputs, grad_pre, OVER_ROWS)
    grad_bias = jnp.sum(grad_pre.astype(F32), axis=0)
    return (grad_enc[None], grad_bias[None], grad_same[None], grad_cross)


def solution(mesh):
    size = mesh.shape["latent"]
    placed = (
        P("layer", "groups", "latent"),
        P("layer", "groups", "latent"),
        P("layer", None, "latent"),
        P("layer", "latent"),
        P("layer", "latent", None),
        P("latent", "layer"),
    )
    return jax.shard_map(
        ring_shards if size % 2 == 0 and size <= RING_LIMIT else wide_shards,
        mesh=mesh,
        in_specs=placed,
        out_specs=(
            P(("groups", "layer"), None, "latent"),
            P(("groups", "layer"), "latent"),
            P(("groups", "layer"), "latent", None),
            P(("groups", "latent"), "layer"),
        ),
        check_vma=False,
    )
```

```python
import functools
import math

import jax
import jax.numpy as jnp
from jax import lax
from jax.experimental import pallas as pl
from jax.experimental.pallas import tpu as pltpu
from jax.sharding import PartitionSpec as P

F32 = jnp.float32
BF16 = jnp.bfloat16
OVER_ROWS = (((0,), (0,)), ((), ()))
OVER_COLS = (((1,), (1,)), ((), ()))
RING_LIMIT = 16
VMEM_BYTES = 24 * 1024 * 1024
PIECES = 8


def passed_along(shard, axis, by):
    size = lax.axis_size(axis)
    pairs = [(i, i + by) for i in range(size) if 0 <= i + by < size]
    return lax.ppermute(shard, axis, pairs)


def swapped(shard):
    size = lax.axis_size("layer")
    return lax.ppermute(shard, "layer", [(i, size - 1 - i) for i in range(size)])


def matmul(a, b, dims=(((1,), (0,)), ((), ()))):
    return lax.dot_general(a, b, dims, preferred_element_type=F32)


def ring_order(size):
    return [2 * p if p < size // 2 else 2 * (size - 1 - p) + 1 for p in range(size)]


def ring_member(place, size):
    place = lax.rem(place + 2 * size, size)
    return jnp.where(place < size // 2, 2 * place, 2 * (size - 1 - place) + 1)


def ring_place(member, size):
    return jnp.where(member % 2 == 0, member // 2, size - 1 - member // 2)


def hop(shard, way):
    size = lax.axis_size("latent")
    order = ring_order(size)
    return lax.ppermute(shard, "latent", [(order[p], order[(p + way) % size]) for p in range(size)])


def after(value, *others):
    return lax.optimization_barrier((value,) + others)[0]


def call(kernel, outs, flops, operands, spaces=None, out_spaces=None, scratch=(), aliases=None):
    def spec(space):
        return pl.BlockSpec(memory_space=space)

    spaces = spaces or [pltpu.VMEM] * (len(operands) - 1)
    out_spaces = out_spaces or [pltpu.VMEM] * len(outs)
    return pl.pallas_call(
        kernel,
        out_shape=outs,
        in_specs=[spec(pltpu.SMEM)] + [spec(space) for space in spaces],
        out_specs=[spec(space) for space in out_spaces],
        scratch_shapes=list(scratch),
        input_output_aliases=aliases or {},
        compiler_params=pltpu.CompilerParams(vmem_limit_bytes=VMEM_BYTES),
        cost_estimate=pl.CostEstimate(flops=flops, bytes_accessed=1024, transcendentals=0),
    )(*operands)


def block_of(starts, slot, wide):
    return pl.ds(pl.multiple_of(starts[slot], wide), wide)


def encode_kernel(slots, first, last, starts, *refs):
    count = 2 * len(slots)
    shards, (weight, before, *outs) = refs[:count], refs[count:]
    rows, wide = shards[0].shape
    for chain in range(2):
        at = slice(chain * rows, (chain + 1) * rows)
        total = jnp.broadcast_to(before[...], (rows, before.shape[1])) if first else before[at, :]
        for i, slot in enumerate(slots):
            block = weight[0, block_of(starts, slot, wide), :]
            total = total + jnp.dot(shards[2 * i + chain][...], block, preferred_element_type=F32)
        outs[0][at, :] = total
        if last:
            outs[1][at, :] = jnp.maximum(total, 0.0).astype(BF16)


def turn_own_kernel(starts, shard, *refs):
    refs[-1][...] = shard[...].T


def turn_kernel(starts, own_0, own_1, *refs):
    *shards, turned = refs
    rows, wide = shards[0].shape
    for chain, own in enumerate((own_0, own_1)):
        turned[block_of(starts, 0, wide), chain * rows:(chain + 1) * rows] = own[...]
    for k in range(len(shards) // 2):
        at = block_of(starts, k + 1, wide)
        for chain in range(2):
            turned[at, chain * rows:(chain + 1) * rows] = shards[2 * k + chain][...].T


def spread_kernel(slots, starts, codes, earlier, stacked, *outs):
    rows = codes.shape[0] // 2
    outs = list(outs)
    for chain in range(2):
        at = slice(chain * rows, (chain + 1) * rows)
        both = jnp.concatenate([codes[at, :], earlier[at, :]], axis=1)
        for slot in slots:
            partial = outs.pop(0)
            block = stacked[:, block_of(starts, slot, partial.shape[1])]
            partial[...] = jnp.dot(both, block, preferred_element_type=F32).astype(partial.dtype)
        if len(outs) > (1 - chain) * len(slots):
            outs.pop(0)[...] = both.T


def back_products(slots, starts, shards, stacked, both_t, before):
    wide = shards[0].shape[1]
    blocks, totals = [], [None, None] if before is None else [before[0], before[1]]
    for i, slot in enumerate(slots):
        decoder = stacked[:, block_of(starts, slot, wide)]
        block = 0.0
        for chain in range(2):
            error = shards[2 * i + chain][...]
            block = block + jnp.dot(both_t[chain][...], error, preferred_element_type=F32)
            term = lax.dot_general(error, decoder, OVER_COLS, preferred_element_type=F32)
            totals[chain] = term if totals[chain] is None else totals[chain] + term
        blocks.append(block)
    return blocks, totals


def back_kernel(slots, first, starts, *refs):
    count = 2 * len(slots)
    shards, (stacked, *both_t), (*before, outer, back) = refs[:count], refs[count:count + 3], refs[count + 3:]
    blocks, totals = back_products(slots, starts, shards, stacked, both_t, None if first else before[0])
    for i, block in enumerate(blocks):
        outer[i] = block
    for chain in range(2):
        back[chain] = totals[chain]


def cross_back_kernel(slots, far, starts, *refs):
    shards, (stacked, *both_t), outers, (before, sent, high) = refs[:2], refs[2:5], refs[5:-3], refs[-3:]
    rows, wide = shards[0].shape
    half_width, lat = high.shape

    @pl.when(starts[starts.shape[0] - 1] != 0)
    def _():
        decoder = stacked[lat:, block_of(starts, far, wide)]
        last = 0.0
        for chain in range(2):
            error = shards[chain][...]
            last = last + jnp.dot(both_t[chain][lat:, :], error, preferred_element_type=F32)
            term = lax.dot_general(error, decoder, OVER_COLS, preferred_element_type=F32)
            sent[chain * rows:(chain + 1) * rows, :] = (before[chain, :, lat:] + term).astype(BF16)
        pieces = [(far, last)]
        for group, outer in zip(slots, outers):
            pieces += [(slot, outer[i, lat:]) for i, slot in enumerate(group)]
        for slot, piece in pieces:
            start = pl.multiple_of(starts[slot], wide)

            @pl.when(start < half_width)
            def _():
                for c in range(0, wide, lat):
                    sent[pl.ds(2 * rows + start + c, lat), :] = piece[:, c:c + lat].astype(BF16)

            @pl.when(start >= half_width)
            def _():
                for c in range(0, wide, lat):
                    high[pl.ds(start - half_width + c, lat), :] = piece[:, c:c + lat]


def own_back_kernel(slots, far, starts, *refs):
    shards, (stacked, *both_t), refs = refs[:2], refs[2:5], refs[5:]
    outers, (before, back_own, same, last, sems) = refs[:-5], refs[-5:]
    rows, wide = shards[0].shape
    lat = back_own.shape[1]
    blocks = []
    for group, outer in zip(slots, outers):
        blocks += [(slot, outer.at[i, :lat, :]) for i, slot in enumerate(group)]
    blocks.append((far, last))
    copies = []
    for i, (slot, block) in enumerate(blocks):
        copies.append(pltpu.make_async_copy(block, same.at[0, :, block_of(starts, slot, wide)], sems.at[i]))
    for copy in copies[:-1]:
        copy.start()
    decoder = stacked[:lat, block_of(starts, far, wide)]
    total = 0.0
    for chain in range(2):
        error = shards[chain][...]
        total = total + jnp.dot(both_t[chain][:lat, :], error, preferred_element_type=F32)
        term = lax.dot_general(error, decoder, OVER_COLS, preferred_element_type=F32)
        back_own[chain * rows:(chain + 1) * rows, :] = before[chain, :, :lat] + term
    last[...] = total
    copies[-1].start()
    for copy in copies:
        copy.wait()


def finish_kernel(
    starts, turned, preact, back_own, arrived, high, grad, bias, cross, stage, cross_stage, grad_sems, cross_sem
):
    pieces, height, lat = stage.shape
    rows = preact.shape[0]
    half_width = high.shape[0]
    first = starts[starts.shape[0] - 1] == 0
    later = jnp.where(first, arrived[:rows, :].astype(F32), 0.0)
    value = jnp.where(preact[...] > 0, back_own[...] + later, 0.0).astype(BF16)
    copies = []
    for i in range(pieces):
        at = pl.ds(i * height, height)
        stage[i] = jnp.dot(turned[at, :], value, preferred_element_type=F32)
        copies.append(pltpu.make_async_copy(stage.at[i], grad.at[0, at, :], grad_sems.at[i]))
        copies[-1].start()
        if i == 0:
            for c in range(0, half_width, lat):
                source = arrived[rows + c:rows + c + lat, :].astype(F32)
                cross_stage[:, c:c + lat] = jnp.where(first, source, high[c:c + lat, :])
            copies.append(pltpu.make_async_copy(cross_stage, cross, cross_sem))
            copies[-1].start()
    bias[...] = jnp.sum(value.astype(F32), axis=0, keepdims=True)
    for copy in copies:
        copy.wait()


def ring_shards(residual_in, targets, enc_weight, enc_bias, dec_same, dec_cross):
    size = lax.axis_size("latent")
    reach = size // 2
    place = ring_place(lax.axis_index("latent"), size)
    layer = lax.axis_index("layer")
    rows, wide = residual_in.shape[1:]
    half = rows // 2
    deep, lat = enc_weight.shape[1:]
    half_width = deep // 2
    err_scale = 1.0 / math.sqrt(rows)
    shape = jax.ShapeDtypeStruct
    unit = rows * wide * lat
    chains = (0, 1)

    def halves(array):
        return [array[:half], array[half:]]

    slot_p = {s: 2 * s - 1 for s in range(1, reach)}
    slot_q = {s: 2 * s for s in range(1, reach)}
    far = size - 1
    offsets = [0] * size
    offsets[far] = reach
    for s in range(1, reach):
        offsets[slot_p[s]] = -s
        offsets[slot_q[s]] = s
    starts = jnp.stack([ring_member(place + offset, size) * wide for offset in offsets] + [layer])
    starts = starts.astype(jnp.int32)

    urgent, later = ((0, -1), (1, 1)), ((0, 1), (1, -1))

    def gather_step(found, s, ready=None):
        for chain, way in urgent + later if s < reach else urgent:
            slots = slot_p if way == 1 else slot_q
            shard = found[chain][slots[s - 1] if s > 1 else 0]
            if ready is not None and (chain, way) in later:
                shard = after(shard, ready[chain])
            found[chain][slots[s] if s < reach else far] = hop(shard, way)

    def both_chains(found, slots):
        return [found[chain][slot] for slot in slots for chain in chains]

    def encode(slots, before):
        first, last = slots[0] == 0, slots[-1] == far
        return call(
            functools.partial(encode_kernel, slots, first, last),
            [shape((rows, lat), F32)] + ([shape((rows, lat), BF16)] if last else []),
            2 * unit * len(slots),
            [starts] + both_chains(inputs, slots) + [enc_weight, before],
        )

    inputs = [[part] + [None] * (size - 1) for part in halves(residual_in[0])]
    turned_own = []
    for chain in chains:
        source = inputs[chain][0]
        turned_own += call(turn_own_kernel, [shape((wide, half), BF16)], 0, [starts, source])
    for s in range(1, reach + 1):
        gather_step(inputs, s, turned_own if s == 1 else None)
    low_cross = swapped(after(dec_cross, inputs[0][slot_p.get(1, far)]))
    cross = jnp.where(layer > 0, jnp.concatenate([low_cross, dec_cross], axis=1), jnp.zeros((), BF16))
    stacked = jnp.concatenate([dec_same[0], cross], axis=0)
    part = encode(tuple(range(far)), after(enc_bias, stacked))[0]
    preact, codes = encode((far,), part)
    earlier = swapped(codes)

    def spread(slots, dtypes, turned):
        outs = []
        for chain in chains:
            outs += [shape((half, wide), dtypes[chain].get(slot, F32)) for slot in slots]
            outs += [shape((2 * lat, half), BF16)] if turned else []
        found = call(
            functools.partial(spread_kernel, slots), outs, 4 * unit * len(slots), [starts, codes, earlier, stacked]
        )
        return found[:len(outs) // 2], found[len(outs) // 2:]

    rest = tuple(slot for slot in range(size) if slot != far)
    instant = tuple({far: BF16, (slot_q if way == 1 else slot_p).get(reach - 1): BF16} for _, way in later)
    far_0, far_1 = spread((far,), instant, False)
    moving = {loop: hop(message, loop[1]) for loop, message in zip(urgent, (far_0[0], far_1[0]))}
    partial, both_t = [], []
    for pieces in spread(rest, instant, True):
        partial.append(dict(zip(rest, pieces)))
        both_t.append(pieces[-1])
    before = []
    for s in range(reach - 1, 0, -1):
        landed = [moving[loop] for loop in urgent]
        for chain, way in urgent + later:
            message = partial[chain][slot_q[s] if way == 1 else slot_p[s]]
            if (chain, way) in moving:
                message = (message + moving[chain, way].astype(F32)).astype(BF16)
            if (chain, way) in later and before:
                message = after(message, *before)
            moving[chain, way] = hop(message, way)
        before = landed
    errors = []
    for chain, wanted in zip(chains, halves(targets[0])):
        total = partial[chain][0]
        for way in (1, -1):
            if (chain, way) in moving:
                total = total + moving[chain, way].astype(F32)
        if chain == 1:
            wanted = after(wanted, codes)
        errors.append([((total - wanted.astype(F32)) * err_scale).astype(BF16)] + [None] * (size - 1))

    def back(slots, before):
        return call(
            functools.partial(back_kernel, slots, before is None),
            [shape((len(slots), 2 * lat, wide), F32), shape((2, half, 2 * lat), F32)],
            4 * unit * len(slots),
            [starts] + both_chains(errors, slots) + [stacked] + both_t + ([] if before is None else [before]),
        )

    groups, outers, acc, pending = [], [], None, [0]
    arrived = [after(inputs[0][1], errors[1][0])]
    turned = call(
        turn_kernel,
        [shape((deep, rows), BF16)],
        0,
        [starts] + turned_own + arrived + both_chains(inputs, range(1, size))[1:],
    )[0]
    for s in range(1, reach + 1):
        gather_step(errors, s, (turned, turned) if s == 2 else None)
    cut = 1 + 2 * min(1, reach - 1)
    groups = [group for group in (tuple(range(cut)), tuple(range(cut, far))) if group]
    outers, acc = [], None
    for group in groups:
        outer, acc = back(group, acc)
        outers.append(outer)
    last = both_chains(errors, (far,)) + [stacked] + both_t + outers + [acc]
    sent, high = call(
        functools.partial(cross_back_kernel, groups, far),
        [shape((rows + half_width, lat), BF16), shape((half_width, lat), F32)],
        0,
        [starts] + last,
    )
    returned = swapped(sent)
    back_own, grad_same = call(
        functools.partial(own_back_kernel, groups, far),
        [shape((rows, lat), F32), shape((1, lat, deep), F32)],
        0,
        [starts] + last,
        out_spaces=[pltpu.VMEM, pl.ANY],
        scratch=[pltpu.VMEM((lat, wide), F32), pltpu.SemaphoreType.DMA((size,))],
    )
    height = deep // PIECES
    grad_enc, grad_bias, grad_cross = call(
        finish_kernel,
        [shape((1, deep, lat), F32), shape((1, lat), F32), shape((lat, half_width), F32)],
        2 * unit * size,
        [starts, turned, preact, back_own, returned, high],
        out_spaces=[pl.ANY, pltpu.VMEM, pl.ANY],
        scratch=[
            pltpu.VMEM((PIECES, height, lat), F32),
            pltpu.VMEM((lat, half_width), F32),
            pltpu.SemaphoreType.DMA((PIECES,)),
            pltpu.SemaphoreType.DMA,
        ],
    )
    return (grad_enc, grad_bias, grad_same, grad_cross)


def wide_shards(residual_in, targets, enc_weight, enc_bias, dec_same, dec_cross):
    is_first = lax.axis_index("layer") == 0
    err_scale = 1.0 / math.sqrt(residual_in.shape[1])
    inputs = lax.all_gather(residual_in[0], "latent", axis=1, tiled=True)
    preact = matmul(inputs, enc_weight[0]) + enc_bias[0]
    codes_now = jnp.maximum(preact, 0.0).astype(BF16)
    earlier = passed_along(codes_now, "layer", 1)
    cross_full = lax.all_gather(dec_cross, "layer", axis=1, tiled=True)
    own_dec = dec_same[0]
    half_width = own_dec.shape[1] // 2
    recon_full = lax.psum(matmul(codes_now, own_dec) + matmul(earlier, cross_full), "latent")
    wanted = lax.all_gather(targets[0], "latent", axis=1, tiled=True)
    errors = ((recon_full - wanted.astype(F32)) * err_scale).astype(BF16)
    grad_same = matmul(codes_now, errors, OVER_ROWS)
    grad_full = matmul(earlier, errors, OVER_ROWS)
    returned = passed_along(grad_full[:, :half_width], "layer", -1)
    grad_cross = jnp.where(is_first, returned, grad_full[:, half_width:])
    from_next = passed_along(matmul(errors, cross_full, OVER_COLS), "layer", -1)
    grad_codes = matmul(errors, own_dec, OVER_COLS) + from_next
    grad_pre = jnp.where(preact > 0, grad_codes, 0.0).astype(BF16)
    grad_enc = matmul(inputs, grad_pre, OVER_ROWS)
    grad_bias = jnp.sum(grad_pre.astype(F32), axis=0)
    return (grad_enc[None], grad_bias[None], grad_same[None], grad_cross)


def solution(mesh):
    size = mesh.shape["latent"]
    placed = (
        P("layer", "groups", "latent"),
        P("layer", "groups", "latent"),
        P("layer", None, "latent"),
        P("layer", "latent"),
        P("layer", "latent", None),
        P("latent", "layer"),
    )
    return jax.shard_map(
        ring_shards if size % 2 == 0 and size <= RING_LIMIT else wide_shards,
        mesh=mesh,
        in_specs=placed,
        out_specs=(
            P(("groups", "layer"), None, "latent"),
            P(("groups", "layer"), "latent"),
            P(("groups", "layer"), "latent", None),
            P(("groups", "latent"), "layer"),
        ),
        check_vma=False,
    )
```

```python
import functools
import math

import jax
import jax.numpy as jnp
from jax import lax
from jax.experimental import pallas as pl
from jax.experimental.pallas import tpu as pltpu
from jax.sharding import PartitionSpec as P

F32 = jnp.float32
BF16 = jnp.bfloat16
OVER_ROWS = (((0,), (0,)), ((), ()))
OVER_COLS = (((1,), (1,)), ((), ()))
RING_LIMIT = 16
VMEM_BYTES = 24 * 1024 * 1024
PIECES = 8


def passed_along(shard, axis, by):
    size = lax.axis_size(axis)
    pairs = [(i, i + by) for i in range(size) if 0 <= i + by < size]
    return lax.ppermute(shard, axis, pairs)


def swapped(shard):
    size = lax.axis_size("layer")
    return lax.ppermute(shard, "layer", [(i, size - 1 - i) for i in range(size)])


def matmul(a, b, dims=(((1,), (0,)), ((), ()))):
    return lax.dot_general(a, b, dims, preferred_element_type=F32)


def ring_order(size):
    return [2 * p if p < size // 2 else 2 * (size - 1 - p) + 1 for p in range(size)]


def ring_member(place, size):
    place = lax.rem(place + 2 * size, size)
    return jnp.where(place < size // 2, 2 * place, 2 * (size - 1 - place) + 1)


def ring_place(member, size):
    return jnp.where(member % 2 == 0, member // 2, size - 1 - member // 2)


def hop(shard, way):
    size, layers = lax.axis_size("latent"), lax.axis_size("layer")
    order = ring_order(size)
    pairs = []
    for p in range(size):
        for layer in range(layers):
            by = way if layer % 2 == 0 else -way
            pairs.append((order[p] * layers + layer, order[(p + by) % size] * layers + layer))
    return lax.ppermute(shard, ("latent", "layer"), pairs)


def after(value, *others):
    return lax.optimization_barrier((value,) + others)[0]


def call(kernel, outs, flops, operands, spaces=None, out_spaces=None, scratch=(), aliases=None):
    def spec(space):
        return pl.BlockSpec(memory_space=space)

    spaces = spaces or [pltpu.VMEM] * (len(operands) - 1)
    out_spaces = out_spaces or [pltpu.VMEM] * len(outs)
    return pl.pallas_call(
        kernel,
        out_shape=outs,
        in_specs=[spec(pltpu.SMEM)] + [spec(space) for space in spaces],
        out_specs=[spec(space) for space in out_spaces],
        scratch_shapes=list(scratch),
        input_output_aliases=aliases or {},
        compiler_params=pltpu.CompilerParams(vmem_limit_bytes=VMEM_BYTES),
        cost_estimate=pl.CostEstimate(flops=flops, bytes_accessed=1024, transcendentals=0),
    )(*operands)


def block_of(starts, slot, wide):
    return pl.ds(pl.multiple_of(starts[slot], wide), wide)


def encode_kernel(slots, first, last, starts, *refs):
    count = 2 * len(slots)
    shards, (weight, before, *outs) = refs[:count], refs[count:]
    rows, wide = shards[0].shape
    for chain in range(2):
        at = slice(chain * rows, (chain + 1) * rows)
        total = jnp.broadcast_to(before[...], (rows, before.shape[1])) if first else before[at, :]
        for i, slot in enumerate(slots):
            block = weight[0, block_of(starts, slot, wide), :]
            total = total + jnp.dot(shards[2 * i + chain][...], block, preferred_element_type=F32)
        outs[0][at, :] = total
        if last:
            outs[1][at, :] = jnp.maximum(total, 0.0).astype(BF16)


def turn_own_kernel(starts, shard, *refs):
    refs[-1][...] = shard[...].T


def turn_kernel(starts, own_0, own_1, *refs):
    *shards, turned = refs
    rows, wide = shards[0].shape
    for chain, own in enumerate((own_0, own_1)):
        turned[block_of(starts, 0, wide), chain * rows:(chain + 1) * rows] = own[...]
    for k in range(len(shards) // 2):
        at = block_of(starts, k + 1, wide)
        for chain in range(2):
            turned[at, chain * rows:(chain + 1) * rows] = shards[2 * k + chain][...].T


def spread_kernel(slots, starts, codes, earlier, stacked, *outs):
    rows = codes.shape[0] // 2
    outs = list(outs)
    for chain in range(2):
        at = slice(chain * rows, (chain + 1) * rows)
        both = jnp.concatenate([codes[at, :], earlier[at, :]], axis=1)
        for slot in slots:
            partial = outs.pop(0)
            block = stacked[:, block_of(starts, slot, partial.shape[1])]
            partial[...] = jnp.dot(both, block, preferred_element_type=F32).astype(partial.dtype)
        if len(outs) > (1 - chain) * len(slots):
            outs.pop(0)[...] = both.T


def back_products(slots, starts, shards, stacked, both_t, before):
    wide = shards[0].shape[1]
    blocks, totals = [], [None, None] if before is None else [before[0], before[1]]
    for i, slot in enumerate(slots):
        decoder = stacked[:, block_of(starts, slot, wide)]
        block = 0.0
        for chain in range(2):
            error = shards[2 * i + chain][...]
            block = block + jnp.dot(both_t[chain][...], error, preferred_element_type=F32)
            term = lax.dot_general(error, decoder, OVER_COLS, preferred_element_type=F32)
            totals[chain] = term if totals[chain] is None else totals[chain] + term
        blocks.append(block)
    return blocks, totals


def back_kernel(slots, first, starts, *refs):
    count = 2 * len(slots)
    shards, (stacked, *both_t), (*before, outer, back) = refs[:count], refs[count:count + 3], refs[count + 3:]
    blocks, totals = back_products(slots, starts, shards, stacked, both_t, None if first else before[0])
    for i, block in enumerate(blocks):
        outer[i] = block
    for chain in range(2):
        back[chain] = totals[chain]


def near_back_kernel(groups, starts, *refs):
    count = 2 * len(groups[-1])
    shards, (stacked, *both_t), refs = refs[:count], refs[count:count + 3], refs[count + 3:]
    *outers, before, outer, back, same, sems = refs
    wide = shards[0].shape[1]
    lat = stacked.shape[0] // 2
    copies = []

    def send(slots, blocks):
        for i, slot in enumerate(slots):
            there = same.at[0, :, block_of(starts, slot, wide)]
            copies.append(pltpu.make_async_copy(blocks.at[i, :lat, :], there, sems.at[len(copies)]))
            copies[-1].start()

    for slots, blocks in zip(groups[:-1], outers):
        send(slots, blocks)
    found, totals = back_products(groups[-1], starts, shards, stacked, both_t, before)
    for i, block in enumerate(found):
        outer[i] = block
    send(groups[-1], outer)
    for chain in range(2):
        back[chain] = totals[chain]
    for copy in copies:
        copy.wait()


def cross_back_kernel(slots, far, starts, *refs):
    shards, (stacked, *both_t), outers, (before, sent, high) = refs[:2], refs[2:5], refs[5:-3], refs[-3:]
    rows, wide = shards[0].shape
    half_width, lat = high.shape

    @pl.when(starts[starts.shape[0] - 1] != 0)
    def _():
        decoder = stacked[lat:, block_of(starts, far, wide)]
        last = 0.0
        for chain in range(2):
            error = shards[chain][...]
            last = last + jnp.dot(both_t[chain][lat:, :], error, preferred_element_type=F32)
            term = lax.dot_general(error, decoder, OVER_COLS, preferred_element_type=F32)
            sent[chain * rows:(chain + 1) * rows, :] = (before[chain, :, lat:] + term).astype(BF16)
        pieces = [(far, last)]
        for group, outer in zip(slots, outers):
            pieces += [(slot, outer[i, lat:]) for i, slot in enumerate(group)]
        for slot, piece in pieces:
            start = pl.multiple_of(starts[slot], wide)

            @pl.when(start < half_width)
            def _():
                for c in range(0, wide, lat):
                    sent[pl.ds(2 * rows + start + c, lat), :] = piece[:, c:c + lat].astype(BF16)

            @pl.when(start >= half_width)
            def _():
                for c in range(0, wide, lat):
                    high[pl.ds(start - half_width + c, lat), :] = piece[:, c:c + lat]


def own_back_kernel(far, starts, *refs):
    shards, (stacked, *both_t), (before, back_own, last) = refs[:2], refs[2:5], refs[5:]
    rows, wide = shards[0].shape
    lat = back_own.shape[1]
    decoder = stacked[:lat, block_of(starts, far, wide)]
    total = 0.0
    for chain in range(2):
        error = shards[chain][...]
        total = total + jnp.dot(both_t[chain][:lat, :], error, preferred_element_type=F32)
        term = lax.dot_general(error, decoder, OVER_COLS, preferred_element_type=F32)
        back_own[chain * rows:(chain + 1) * rows, :] = before[chain, :, :lat] + term
    last[...] = total


def finish_kernel(
    far, starts, turned, preact, back_own, arrived, high, last, same_before, grad, bias, cross, same,
    stage, cross_stage, grad_sems, cross_sem, same_sem
):
    same_copy = pltpu.make_async_copy(last, same.at[0, :, block_of(starts, far, last.shape[1])], same_sem)
    same_copy.start()
    pieces, height, lat = stage.shape
    rows = preact.shape[0]
    half_width = high.shape[0]
    first = starts[starts.shape[0] - 1] == 0
    later = jnp.where(first, arrived[:rows, :].astype(F32), 0.0)
    value = jnp.where(preact[...] > 0, back_own[...] + later, 0.0).astype(BF16)
    copies = []
    for i in range(pieces):
        at = pl.ds(i * height, height)
        stage[i] = jnp.dot(turned[at, :], value, preferred_element_type=F32)
        copies.append(pltpu.make_async_copy(stage.at[i], grad.at[0, at, :], grad_sems.at[i]))
        copies[-1].start()
        if i == 0:
            for c in range(0, half_width, lat):
                source = arrived[rows + c:rows + c + lat, :].astype(F32)
                cross_stage[:, c:c + lat] = jnp.where(first, source, high[c:c + lat, :])
            copies.append(pltpu.make_async_copy(cross_stage, cross, cross_sem))
            copies[-1].start()
    bias[...] = jnp.sum(value.astype(F32), axis=0, keepdims=True)
    same_copy.wait()
    for copy in copies:
        copy.wait()


def ring_shards(residual_in, targets, enc_weight, enc_bias, dec_same, dec_cross):
    size = lax.axis_size("latent")
    reach = size // 2
    place = ring_place(lax.axis_index("latent"), size)
    layer = lax.axis_index("layer")
    sign = jnp.where(layer % 2 == 0, 1, -1)
    rows, wide = residual_in.shape[1:]
    half = rows // 2
    deep, lat = enc_weight.shape[1:]
    half_width = deep // 2
    err_scale = 1.0 / math.sqrt(rows)
    shape = jax.ShapeDtypeStruct
    unit = rows * wide * lat
    chains = (0, 1)

    def halves(array):
        return [array[:half], array[half:]]

    slot_p = {s: 2 * s - 1 for s in range(1, reach)}
    slot_q = {s: 2 * s for s in range(1, reach)}
    far = size - 1
    offsets = [0] * size
    offsets[far] = reach
    for s in range(1, reach):
        offsets[slot_p[s]] = -s
        offsets[slot_q[s]] = s
    starts = jnp.stack([ring_member(place + sign * offset, size) * wide for offset in offsets] + [layer])
    starts = starts.astype(jnp.int32)

    urgent, later = ((0, -1), (1, 1)), ((0, 1), (1, -1))

    def gather_step(found, s, ready=None):
        for chain, way in urgent + later if s < reach else urgent:
            slots = slot_p if way == 1 else slot_q
            shard = found[chain][slots[s - 1] if s > 1 else 0]
            if ready is not None and (chain, way) in later:
                shard = after(shard, ready[chain])
            found[chain][slots[s] if s < reach else far] = hop(shard, way)

    def both_chains(found, slots):
        return [found[chain][slot] for slot in slots for chain in chains]

    def encode(slots, before):
        first, last = slots[0] == 0, slots[-1] == far
        return call(
            functools.partial(encode_kernel, slots, first, last),
            [shape((rows, lat), F32)] + ([shape((rows, lat), BF16)] if last else []),
            2 * unit * len(slots),
            [starts] + both_chains(inputs, slots) + [enc_weight, before],
        )

    inputs = [[part] + [None] * (size - 1) for part in halves(residual_in[0])]
    turned_own = []
    for chain in chains:
        source = inputs[chain][0]
        turned_own += call(turn_own_kernel, [shape((wide, half), BF16)], 0, [starts, source])
    for s in range(1, reach + 1):
        gather_step(inputs, s, turned_own if s == 1 else None)
    low_cross = swapped(after(dec_cross, inputs[0][slot_p.get(1, far)]))
    cross = jnp.where(layer > 0, jnp.concatenate([low_cross, dec_cross], axis=1), jnp.zeros((), BF16))
    stacked = jnp.concatenate([dec_same[0], cross], axis=0)
    part = encode(tuple(range(far)), after(enc_bias, stacked))[0]
    preact, codes = encode((far,), part)
    earlier = swapped(codes)

    def spread(slots, dtypes, turned):
        outs = []
        for chain in chains:
            outs += [shape((half, wide), dtypes[chain].get(slot, F32)) for slot in slots]
            outs += [shape((2 * lat, half), BF16)] if turned else []
        found = call(
            functools.partial(spread_kernel, slots), outs, 4 * unit * len(slots), [starts, codes, earlier, stacked]
        )
        return found[:len(outs) // 2], found[len(outs) // 2:]

    rest = tuple(slot for slot in range(size) if slot != far)
    instant = tuple({far: BF16, (slot_q if way == 1 else slot_p).get(reach - 1): BF16} for _, way in later)
    far_0, far_1 = spread((far,), instant, False)
    moving = {loop: hop(message, loop[1]) for loop, message in zip(urgent, (far_0[0], far_1[0]))}
    partial, both_t = [], []
    for pieces in spread(rest, instant, True):
        partial.append(dict(zip(rest, pieces)))
        both_t.append(pieces[-1])
    before = []
    for s in range(reach - 1, 0, -1):
        landed = [moving[loop] for loop in urgent]
        for chain, way in urgent + later:
            message = partial[chain][slot_q[s] if way == 1 else slot_p[s]]
            if (chain, way) in moving:
                message = (message + moving[chain, way].astype(F32)).astype(BF16)
            if (chain, way) in later and before:
                message = after(message, *before)
            moving[chain, way] = hop(message, way)
        before = landed
    errors = []
    for chain, wanted in zip(chains, halves(targets[0])):
        total = partial[chain][0]
        for way in (1, -1):
            if (chain, way) in moving:
                total = total + moving[chain, way].astype(F32)
        if chain == 1:
            wanted = after(wanted, codes)
        errors.append([((total - wanted.astype(F32)) * err_scale).astype(BF16)] + [None] * (size - 1))

    def back(slots, before):
        return call(
            functools.partial(back_kernel, slots, before is None),
            [shape((len(slots), 2 * lat, wide), F32), shape((2, half, 2 * lat), F32)],
            4 * unit * len(slots),
            [starts] + both_chains(errors, slots) + [stacked] + both_t + ([] if before is None else [before]),
        )

    groups, outers, acc, pending = [], [], None, [0]
    arrived = [after(inputs[0][1], errors[1][0])]
    turned = call(
        turn_kernel,
        [shape((deep, rows), BF16)],
        0,
        [starts] + turned_own + arrived + both_chains(inputs, range(1, size))[1:],
    )[0]
    for s in range(1, reach + 1):
        gather_step(errors, s, (turned, turned) if s == 1 else None)
    cut = 1 + 2 * min(1, reach - 1)
    groups = [group for group in (tuple(range(cut)), tuple(range(cut, far))) if group]
    outers, acc = [], None
    for group in groups[:-1]:
        outer, acc = back(group, acc)
        outers.append(outer)
    before = [jnp.zeros((2, half, 2 * lat), F32)] if acc is None else [acc]
    outer, acc, same = call(
        functools.partial(near_back_kernel, groups),
        [
            shape((len(groups[-1]), 2 * lat, wide), F32),
            shape((2, half, 2 * lat), F32),
            shape((1, lat, deep), F32),
        ],
        0,
        [starts] + both_chains(errors, groups[-1]) + [stacked] + both_t + outers + before,
        out_spaces=[pltpu.VMEM, pltpu.VMEM, pl.ANY],
        scratch=[pltpu.SemaphoreType.DMA((far,))],
    )
    outers.append(outer)
    last = both_chains(errors, (far,)) + [stacked] + both_t + outers + [acc]
    sent, high = call(
        functools.partial(cross_back_kernel, groups, far),
        [shape((rows + half_width, lat), BF16), shape((half_width, lat), F32)],
        0,
        [starts] + last,
    )
    returned = swapped(sent)
    back_own, last_same = call(
        functools.partial(own_back_kernel, far),
        [shape((rows, lat), F32), shape((lat, wide), F32)],
        0,
        [starts] + both_chains(errors, (far,)) + [stacked] + both_t + [acc],
    )
    height = deep // PIECES
    grad_enc, grad_bias, grad_cross, grad_same = call(
        functools.partial(finish_kernel, far),
        [shape((1, deep, lat), F32), shape((1, lat), F32), shape((lat, half_width), F32), shape((1, lat, deep), F32)],
        2 * unit * size,
        [starts, turned, preact, back_own, returned, high, last_same, same],
        spaces=[pltpu.VMEM] * 6 + [pl.ANY],
        out_spaces=[pl.ANY, pltpu.VMEM, pl.ANY, pl.ANY],
        aliases={7: 3},
        scratch=[
            pltpu.VMEM((PIECES, height, lat), F32),
            pltpu.VMEM((lat, half_width), F32),
            pltpu.SemaphoreType.DMA((PIECES,)),
            pltpu.SemaphoreType.DMA,
            pltpu.SemaphoreType.DMA,
        ],
    )
    return (grad_enc, grad_bias, grad_same, grad_cross)


def wide_shards(residual_in, targets, enc_weight, enc_bias, dec_same, dec_cross):
    is_first = lax.axis_index("layer") == 0
    err_scale = 1.0 / math.sqrt(residual_in.shape[1])
    inputs = lax.all_gather(residual_in[0], "latent", axis=1, tiled=True)
    preact = matmul(inputs, enc_weight[0]) + enc_bias[0]
    codes_now = jnp.maximum(preact, 0.0).astype(BF16)
    earlier = passed_along(codes_now, "layer", 1)
    cross_full = lax.all_gather(dec_cross, "layer", axis=1, tiled=True)
    own_dec = dec_same[0]
    half_width = own_dec.shape[1] // 2
    recon_full = lax.psum(matmul(codes_now, own_dec) + matmul(earlier, cross_full), "latent")
    wanted = lax.all_gather(targets[0], "latent", axis=1, tiled=True)
    errors = ((recon_full - wanted.astype(F32)) * err_scale).astype(BF16)
    grad_same = matmul(codes_now, errors, OVER_ROWS)
    grad_full = matmul(earlier, errors, OVER_ROWS)
    returned = passed_along(grad_full[:, :half_width], "layer", -1)
    grad_cross = jnp.where(is_first, returned, grad_full[:, half_width:])
    from_next = passed_along(matmul(errors, cross_full, OVER_COLS), "layer", -1)
    grad_codes = matmul(errors, own_dec, OVER_COLS) + from_next
    grad_pre = jnp.where(preact > 0, grad_codes, 0.0).astype(BF16)
    grad_enc = matmul(inputs, grad_pre, OVER_ROWS)
    grad_bias = jnp.sum(grad_pre.astype(F32), axis=0)
    return (grad_enc[None], grad_bias[None], grad_same[None], grad_cross)


def solution(mesh):
    size = mesh.shape["latent"]
    placed = (
        P("layer", "groups", "latent"),
        P("layer", "groups", "latent"),
        P("layer", None, "latent"),
        P("layer", "latent"),
        P("layer", "latent", None),
        P("latent", "layer"),
    )
    return jax.shard_map(
        ring_shards if size % 2 == 0 and size <= RING_LIMIT else wide_shards,
        mesh=mesh,
        in_specs=placed,
        out_specs=(
            P(("groups", "layer"), None, "latent"),
            P(("groups", "layer"), "latent"),
            P(("groups", "layer"), "latent", None),
            P(("groups", "latent"), "layer"),
        ),
        check_vma=False,
    )
```

```python
import functools
import math

import jax
import jax.numpy as jnp
from jax import lax
from jax.experimental import pallas as pl
from jax.experimental.pallas import tpu as pltpu
from jax.sharding import PartitionSpec as P

F32 = jnp.float32
BF16 = jnp.bfloat16
OVER_ROWS = (((0,), (0,)), ((), ()))
OVER_COLS = (((1,), (1,)), ((), ()))
RING_LIMIT = 16
VMEM_BYTES = 24 * 1024 * 1024
PIECES = 8


def passed_along(shard, axis, by):
    size = lax.axis_size(axis)
    pairs = [(i, i + by) for i in range(size) if 0 <= i + by < size]
    return lax.ppermute(shard, axis, pairs)


def swapped(shard):
    size = lax.axis_size("layer")
    return lax.ppermute(shard, "layer", [(i, size - 1 - i) for i in range(size)])


def matmul(a, b, dims=(((1,), (0,)), ((), ()))):
    return lax.dot_general(a, b, dims, preferred_element_type=F32)


def ring_order(size):
    return [2 * p if p < size // 2 else 2 * (size - 1 - p) + 1 for p in range(size)]


def ring_member(place, size):
    place = lax.rem(place + 2 * size, size)
    return jnp.where(place < size // 2, 2 * place, 2 * (size - 1 - place) + 1)


def ring_place(member, size):
    return jnp.where(member % 2 == 0, member // 2, size - 1 - member // 2)


def hop(shard, way):
    size, layers = lax.axis_size("latent"), lax.axis_size("layer")
    order = ring_order(size)
    pairs = []
    for p in range(size):
        for layer in range(layers):
            by = way if layer % 2 == 0 else -way
            pairs.append((order[p] * layers + layer, order[(p + by) % size] * layers + layer))
    return lax.ppermute(shard, ("latent", "layer"), pairs)


def after(value, *others):
    return lax.optimization_barrier((value,) + others)[0]


def call(kernel, outs, flops, operands, spaces=None, out_spaces=None, scratch=(), aliases=None):
    def spec(space):
        return pl.BlockSpec(memory_space=space)

    spaces = spaces or [pltpu.VMEM] * (len(operands) - 1)
    out_spaces = out_spaces or [pltpu.VMEM] * len(outs)
    return pl.pallas_call(
        kernel,
        out_shape=outs,
        in_specs=[spec(pltpu.SMEM)] + [spec(space) for space in spaces],
        out_specs=[spec(space) for space in out_spaces],
        scratch_shapes=list(scratch),
        input_output_aliases=aliases or {},
        compiler_params=pltpu.CompilerParams(vmem_limit_bytes=VMEM_BYTES),
        cost_estimate=pl.CostEstimate(flops=flops, bytes_accessed=1024, transcendentals=0),
    )(*operands)


def block_of(starts, slot, wide):
    return pl.ds(pl.multiple_of(starts[slot], wide), wide)


def encode_kernel(slots, first, last, starts, *refs):
    count = 2 * len(slots)
    shards, (weight, before, *outs) = refs[:count], refs[count:]
    rows, wide = shards[0].shape
    for chain in range(2):
        at = slice(chain * rows, (chain + 1) * rows)
        total = jnp.broadcast_to(before[...], (rows, before.shape[1])) if first else before[at, :]
        for i, slot in enumerate(slots):
            block = weight[0, block_of(starts, slot, wide), :]
            total = total + jnp.dot(shards[2 * i + chain][...], block, preferred_element_type=F32)
        outs[0][at, :] = total
        if last:
            outs[1][at, :] = jnp.maximum(total, 0.0).astype(BF16)


def turn_own_kernel(starts, shard, *refs):
    refs[-1][...] = shard[...].T


def turn_kernel(starts, own_0, own_1, *refs):
    *shards, turned = refs
    rows, wide = shards[0].shape
    for chain, own in enumerate((own_0, own_1)):
        turned[block_of(starts, 0, wide), chain * rows:(chain + 1) * rows] = own[...]
    for k in range(len(shards) // 2):
        at = block_of(starts, k + 1, wide)
        for chain in range(2):
            turned[at, chain * rows:(chain + 1) * rows] = shards[2 * k + chain][...].T


def spread_kernel(slots, starts, codes, earlier, stacked, *outs):
    rows = codes.shape[0] // 2
    outs = list(outs)
    for chain in range(2):
        at = slice(chain * rows, (chain + 1) * rows)
        both = jnp.concatenate([codes[at, :], earlier[at, :]], axis=1)
        for slot in slots:
            partial = outs.pop(0)
            block = stacked[:, block_of(starts, slot, partial.shape[1])]
            partial[...] = jnp.dot(both, block, preferred_element_type=F32).astype(partial.dtype)
        if len(outs) > (1 - chain) * len(slots):
            outs.pop(0)[...] = both.T


def back_products(slots, starts, shards, stacked, both_t, before):
    wide = shards[0].shape[1]
    blocks, totals = [], [None, None] if before is None else [before[0], before[1]]
    for i, slot in enumerate(slots):
        decoder = stacked[:, block_of(starts, slot, wide)]
        block = 0.0
        for chain in range(2):
            error = shards[2 * i + chain][...]
            block = block + jnp.dot(both_t[chain][...], error, preferred_element_type=F32)
            term = lax.dot_general(error, decoder, OVER_COLS, preferred_element_type=F32)
            totals[chain] = term if totals[chain] is None else totals[chain] + term
        blocks.append(block)
    return blocks, totals


def back_kernel(slots, first, starts, *refs):
    count = 2 * len(slots)
    shards, (stacked, *both_t), (*before, outer, back) = refs[:count], refs[count:count + 3], refs[count + 3:]
    blocks, totals = back_products(slots, starts, shards, stacked, both_t, None if first else before[0])
    for i, block in enumerate(blocks):
        outer[i] = block
    for chain in range(2):
        back[chain] = totals[chain]


def cross_back_kernel(slots, far, starts, *refs):
    shards, (stacked, *both_t), outers, (before, sent, high) = refs[:2], refs[2:5], refs[5:-3], refs[-3:]
    rows, wide = shards[0].shape
    half_width, lat = high.shape

    @pl.when(starts[starts.shape[0] - 1] != 0)
    def _():
        decoder = stacked[lat:, block_of(starts, far, wide)]
        last = 0.0
        for chain in range(2):
            error = shards[chain][...]
            last = last + jnp.dot(both_t[chain][lat:, :], error, preferred_element_type=F32)
            term = lax.dot_general(error, decoder, OVER_COLS, preferred_element_type=F32)
            sent[chain * rows:(chain + 1) * rows, :] = (before[chain, :, lat:] + term).astype(BF16)
        pieces = [(far, last)]
        for group, outer in zip(slots, outers):
            pieces += [(slot, outer[i, lat:]) for i, slot in enumerate(group)]
        for slot, piece in pieces:
            start = pl.multiple_of(starts[slot], wide)

            @pl.when(start < half_width)
            def _():
                for c in range(0, wide, lat):
                    sent[pl.ds(2 * rows + start + c, lat), :] = piece[:, c:c + lat].astype(BF16)

            @pl.when(start >= half_width)
            def _():
                for c in range(0, wide, lat):
                    high[pl.ds(start - half_width + c, lat), :] = piece[:, c:c + lat]


def own_back_kernel(slots, far, starts, *refs):
    shards, (stacked, *both_t), refs = refs[:2], refs[2:5], refs[5:]
    outers, (before, back_own, same, last, sems) = refs[:-5], refs[-5:]
    rows, wide = shards[0].shape
    lat = back_own.shape[1]
    blocks = []
    for group, outer in zip(slots, outers):
        blocks += [(slot, outer.at[i, :lat, :]) for i, slot in enumerate(group)]
    blocks.append((far, last))
    copies = []
    for i, (slot, block) in enumerate(blocks):
        copies.append(pltpu.make_async_copy(block, same.at[0, :, block_of(starts, slot, wide)], sems.at[i]))
    for copy in copies[:-1]:
        copy.start()
    decoder = stacked[:lat, block_of(starts, far, wide)]
    total = 0.0
    for chain in range(2):
        error = shards[chain][...]
        total = total + jnp.dot(both_t[chain][:lat, :], error, preferred_element_type=F32)
        term = lax.dot_general(error, decoder, OVER_COLS, preferred_element_type=F32)
        back_own[chain * rows:(chain + 1) * rows, :] = before[chain, :, :lat] + term
    last[...] = total
    copies[-1].start()
    for copy in copies:
        copy.wait()


def finish_kernel(
    starts, turned, preact, back_own, arrived, high, grad, bias, cross, stage, cross_stage, grad_sems, cross_sem
):
    pieces, height, lat = stage.shape
    rows = preact.shape[0]
    half_width = high.shape[0]
    first = starts[starts.shape[0] - 1] == 0
    later = jnp.where(first, arrived[:rows, :].astype(F32), 0.0)
    value = jnp.where(preact[...] > 0, back_own[...] + later, 0.0).astype(BF16)
    copies = []
    for i in range(pieces):
        at = pl.ds(i * height, height)
        stage[i] = jnp.dot(turned[at, :], value, preferred_element_type=F32)
        copies.append(pltpu.make_async_copy(stage.at[i], grad.at[0, at, :], grad_sems.at[i]))
        copies[-1].start()
        if i == 0:
            for c in range(0, half_width, lat):
                source = arrived[rows + c:rows + c + lat, :].astype(F32)
                cross_stage[:, c:c + lat] = jnp.where(first, source, high[c:c + lat, :])
            copies.append(pltpu.make_async_copy(cross_stage, cross, cross_sem))
            copies[-1].start()
    bias[...] = jnp.sum(value.astype(F32), axis=0, keepdims=True)
    for copy in copies:
        copy.wait()


def ring_shards(residual_in, targets, enc_weight, enc_bias, dec_same, dec_cross):
    size = lax.axis_size("latent")
    reach = size // 2
    place = ring_place(lax.axis_index("latent"), size)
    layer = lax.axis_index("layer")
    sign = jnp.where(layer % 2 == 0, 1, -1)
    rows, wide = residual_in.shape[1:]
    half = rows // 2
    deep, lat = enc_weight.shape[1:]
    half_width = deep // 2
    err_scale = 1.0 / math.sqrt(rows)
    shape = jax.ShapeDtypeStruct
    unit = rows * wide * lat
    chains = (0, 1)

    def halves(array):
        return [array[:half], array[half:]]

    slot_p = {s: 2 * s - 1 for s in range(1, reach)}
    slot_q = {s: 2 * s for s in range(1, reach)}
    far = size - 1
    offsets = [0] * size
    offsets[far] = reach
    for s in range(1, reach):
        offsets[slot_p[s]] = -s
        offsets[slot_q[s]] = s
    starts = jnp.stack([ring_member(place + sign * offset, size) * wide for offset in offsets] + [layer])
    starts = starts.astype(jnp.int32)

    urgent, later = ((0, -1), (1, 1)), ((0, 1), (1, -1))

    def gather_step(found, s, ready=None):
        for chain, way in urgent + later if s < reach else urgent:
            slots = slot_p if way == 1 else slot_q
            shard = found[chain][slots[s - 1] if s > 1 else 0]
            if ready is not None and (chain, way) in later:
                shard = after(shard, ready[chain])
            found[chain][slots[s] if s < reach else far] = hop(shard, way)

    def both_chains(found, slots):
        return [found[chain][slot] for slot in slots for chain in chains]

    def encode(slots, before):
        first, last = slots[0] == 0, slots[-1] == far
        return call(
            functools.partial(encode_kernel, slots, first, last),
            [shape((rows, lat), F32)] + ([shape((rows, lat), BF16)] if last else []),
            2 * unit * len(slots),
            [starts] + both_chains(inputs, slots) + [enc_weight, before],
        )

    inputs = [[part] + [None] * (size - 1) for part in halves(residual_in[0])]
    turned_own = []
    for chain in chains:
        source = inputs[chain][0]
        turned_own += call(turn_own_kernel, [shape((wide, half), BF16)], 0, [starts, source])
    for s in range(1, reach + 1):
        gather_step(inputs, s, turned_own if s == 1 else None)
    low_cross = swapped(after(dec_cross, inputs[0][slot_p.get(1, far)]))
    cross = jnp.where(layer > 0, jnp.concatenate([low_cross, dec_cross], axis=1), jnp.zeros((), BF16))
    stacked = jnp.concatenate([dec_same[0], cross], axis=0)
    part = encode(tuple(range(far)), after(enc_bias, stacked))[0]
    preact, codes = encode((far,), part)
    earlier = swapped(codes)

    def spread(slots, dtypes, turned):
        outs = []
        for chain in chains:
            outs += [shape((half, wide), dtypes[chain].get(slot, F32)) for slot in slots]
            outs += [shape((2 * lat, half), BF16)] if turned else []
        found = call(
            functools.partial(spread_kernel, slots), outs, 4 * unit * len(slots), [starts, codes, earlier, stacked]
        )
        return found[:len(outs) // 2], found[len(outs) // 2:]

    rest = tuple(slot for slot in range(size) if slot != far)
    instant = tuple({far: BF16, (slot_q if way == 1 else slot_p).get(reach - 1): BF16} for _, way in later)
    far_0, far_1 = spread((far,), instant, False)
    moving = {loop: hop(message, loop[1]) for loop, message in zip(urgent, (far_0[0], far_1[0]))}
    partial, both_t = [], []
    for pieces in spread(rest, instant, True):
        partial.append(dict(zip(rest, pieces)))
        both_t.append(pieces[-1])
    before = []
    for s in range(reach - 1, 0, -1):
        landed = [moving[loop] for loop in urgent]
        for chain, way in urgent + later:
            message = partial[chain][slot_q[s] if way == 1 else slot_p[s]]
            if (chain, way) in moving:
                message = (message + moving[chain, way].astype(F32)).astype(BF16)
            if (chain, way) in later and before:
                message = after(message, *before)
            moving[chain, way] = hop(message, way)
        before = landed
    errors = []
    for chain, wanted in zip(chains, halves(targets[0])):
        total = partial[chain][0]
        for way in (1, -1):
            if (chain, way) in moving:
                total = total + moving[chain, way].astype(F32)
        if chain == 1:
            wanted = after(wanted, errors[0][0])
        errors.append([((total - wanted.astype(F32)) * err_scale).astype(BF16)] + [None] * (size - 1))

    def back(slots, before):
        return call(
            functools.partial(back_kernel, slots, before is None),
            [shape((len(slots), 2 * lat, wide), F32), shape((2, half, 2 * lat), F32)],
            4 * unit * len(slots),
            [starts] + both_chains(errors, slots) + [stacked] + both_t + ([] if before is None else [before]),
        )

    groups, outers, acc, pending = [], [], None, [0]
    arrived = [after(inputs[0][1], errors[1][0])]
    turned = call(
        turn_kernel,
        [shape((deep, rows), BF16)],
        0,
        [starts] + turned_own + arrived + both_chains(inputs, range(1, size))[1:],
    )[0]
    for s in range(1, reach + 1):
        gather_step(errors, s, (turned, turned) if s == 1 else None)
    cut = 1 + 2 * min(1, reach - 1)
    groups = [group for group in (tuple(range(cut)), tuple(range(cut, far))) if group]
    outers, acc = [], None
    for group in groups:
        outer, acc = back(group, acc)
        outers.append(outer)
    last = both_chains(errors, (far,)) + [stacked] + both_t + outers + [acc]
    sent, high = call(
        functools.partial(cross_back_kernel, groups, far),
        [shape((rows + half_width, lat), BF16), shape((half_width, lat), F32)],
        0,
        [starts] + last,
    )
    returned = swapped(sent)
    back_own, grad_same = call(
        functools.partial(own_back_kernel, groups, far),
        [shape((rows, lat), F32), shape((1, lat, deep), F32)],
        0,
        [starts] + last,
        out_spaces=[pltpu.VMEM, pl.ANY],
        scratch=[pltpu.VMEM((lat, wide), F32), pltpu.SemaphoreType.DMA((size,))],
    )
    height = deep // PIECES
    grad_enc, grad_bias, grad_cross = call(
        finish_kernel,
        [shape((1, deep, lat), F32), shape((1, lat), F32), shape((lat, half_width), F32)],
        2 * unit * size,
        [starts, turned, preact, back_own, returned, high],
        out_spaces=[pl.ANY, pltpu.VMEM, pl.ANY],
        scratch=[
            pltpu.VMEM((PIECES, height, lat), F32),
            pltpu.VMEM((lat, half_width), F32),
            pltpu.SemaphoreType.DMA((PIECES,)),
            pltpu.SemaphoreType.DMA,
        ],
    )
    return (grad_enc, grad_bias, grad_same, grad_cross)


def wide_shards(residual_in, targets, enc_weight, enc_bias, dec_same, dec_cross):
    is_first = lax.axis_index("layer") == 0
    err_scale = 1.0 / math.sqrt(residual_in.shape[1])
    inputs = lax.all_gather(residual_in[0], "latent", axis=1, tiled=True)
    preact = matmul(inputs, enc_weight[0]) + enc_bias[0]
    codes_now = jnp.maximum(preact, 0.0).astype(BF16)
    earlier = passed_along(codes_now, "layer", 1)
    cross_full = lax.all_gather(dec_cross, "layer", axis=1, tiled=True)
    own_dec = dec_same[0]
    half_width = own_dec.shape[1] // 2
    recon_full = lax.psum(matmul(codes_now, own_dec) + matmul(earlier, cross_full), "latent")
    wanted = lax.all_gather(targets[0], "latent", axis=1, tiled=True)
    errors = ((recon_full - wanted.astype(F32)) * err_scale).astype(BF16)
    grad_same = matmul(codes_now, errors, OVER_ROWS)
    grad_full = matmul(earlier, errors, OVER_ROWS)
    returned = passed_along(grad_full[:, :half_width], "layer", -1)
    grad_cross = jnp.where(is_first, returned, grad_full[:, half_width:])
    from_next = passed_along(matmul(errors, cross_full, OVER_COLS), "layer", -1)
    grad_codes = matmul(errors, own_dec, OVER_COLS) + from_next
    grad_pre = jnp.where(preact > 0, grad_codes, 0.0).astype(BF16)
    grad_enc = matmul(inputs, grad_pre, OVER_ROWS)
    grad_bias = jnp.sum(grad_pre.astype(F32), axis=0)
    return (grad_enc[None], grad_bias[None], grad_same[None], grad_cross)


def solution(mesh):
    size = mesh.shape["latent"]
    placed = (
        P("layer", "groups", "latent"),
        P("layer", "groups", "latent"),
        P("layer", None, "latent"),
        P("layer", "latent"),
        P("layer", "latent", None),
        P("latent", "layer"),
    )
    return jax.shard_map(
        ring_shards if size % 2 == 0 and size <= RING_LIMIT else wide_shards,
        mesh=mesh,
        in_specs=placed,
        out_specs=(
            P(("groups", "layer"), None, "latent"),
            P(("groups", "layer"), "latent"),
            P(("groups", "layer"), "latent", None),
            P(("groups", "latent"), "layer"),
        ),
        check_vma=False,
    )
```

```python
import functools
import math

import jax
import jax.numpy as jnp
from jax import lax
from jax.experimental import pallas as pl
from jax.experimental.pallas import tpu as pltpu
from jax.sharding import PartitionSpec as P

F32 = jnp.float32
BF16 = jnp.bfloat16
OVER_ROWS = (((0,), (0,)), ((), ()))
OVER_COLS = (((1,), (1,)), ((), ()))
RING_LIMIT = 16
VMEM_BYTES = 24 * 1024 * 1024
PIECES = 8


def passed_along(shard, axis, by):
    size = lax.axis_size(axis)
    pairs = [(i, i + by) for i in range(size) if 0 <= i + by < size]
    return lax.ppermute(shard, axis, pairs)


def swapped(shard):
    size = lax.axis_size("layer")
    return lax.ppermute(shard, "layer", [(i, size - 1 - i) for i in range(size)])


def matmul(a, b, dims=(((1,), (0,)), ((), ()))):
    return lax.dot_general(a, b, dims, preferred_element_type=F32)


def ring_order(size):
    return [2 * p if p < size // 2 else 2 * (size - 1 - p) + 1 for p in range(size)]


def ring_member(place, size):
    place = lax.rem(place + 2 * size, size)
    return jnp.where(place < size // 2, 2 * place, 2 * (size - 1 - place) + 1)


def ring_place(member, size):
    return jnp.where(member % 2 == 0, member // 2, size - 1 - member // 2)


def hop(shard, way):
    size, layers = lax.axis_size("latent"), lax.axis_size("layer")
    order = ring_order(size)
    pairs = []
    for p in range(size):
        for layer in range(layers):
            by = way if layer % 2 == 0 else -way
            pairs.append((order[p] * layers + layer, order[(p + by) % size] * layers + layer))
    return lax.ppermute(shard, ("latent", "layer"), pairs)


def after(value, *others):
    return lax.optimization_barrier((value,) + others)[0]


def call(kernel, outs, flops, operands, spaces=None, out_spaces=None, scratch=(), aliases=None):
    def spec(space):
        return pl.BlockSpec(memory_space=space)

    spaces = spaces or [pltpu.VMEM] * (len(operands) - 1)
    out_spaces = out_spaces or [pltpu.VMEM] * len(outs)
    return pl.pallas_call(
        kernel,
        out_shape=outs,
        in_specs=[spec(pltpu.SMEM)] + [spec(space) for space in spaces],
        out_specs=[spec(space) for space in out_spaces],
        scratch_shapes=list(scratch),
        input_output_aliases=aliases or {},
        compiler_params=pltpu.CompilerParams(vmem_limit_bytes=VMEM_BYTES),
        cost_estimate=pl.CostEstimate(flops=flops, bytes_accessed=1024, transcendentals=0),
    )(*operands)


def block_of(starts, slot, wide):
    return pl.ds(pl.multiple_of(starts[slot], wide), wide)


def encode_kernel(slots, first, last, starts, *refs):
    count = 2 * len(slots)
    shards, (weight, before, *outs) = refs[:count], refs[count:]
    rows, wide = shards[0].shape
    for chain in range(2):
        at = slice(chain * rows, (chain + 1) * rows)
        total = jnp.broadcast_to(before[...], (rows, before.shape[1])) if first else before[at, :]
        for i, slot in enumerate(slots):
            block = weight[0, block_of(starts, slot, wide), :]
            total = total + jnp.dot(shards[2 * i + chain][...], block, preferred_element_type=F32)
        outs[0][at, :] = total
        if last:
            outs[1][at, :] = jnp.maximum(total, 0.0).astype(BF16)


def turn_own_kernel(starts, shard, *refs):
    refs[-1][...] = shard[...].T


def turn_kernel(starts, own_0, own_1, *refs):
    *shards, turned = refs
    rows, wide = shards[0].shape
    for chain, own in enumerate((own_0, own_1)):
        turned[block_of(starts, 0, wide), chain * rows:(chain + 1) * rows] = own[...]
    for k in range(len(shards) // 2):
        at = block_of(starts, k + 1, wide)
        for chain in range(2):
            turned[at, chain * rows:(chain + 1) * rows] = shards[2 * k + chain][...].T


def spread_kernel(slots, starts, codes, earlier, stacked, *outs):
    rows = codes.shape[0] // 2
    outs = list(outs)
    for chain in range(2):
        at = slice(chain * rows, (chain + 1) * rows)
        both = jnp.concatenate([codes[at, :], earlier[at, :]], axis=1)
        for slot in slots:
            partial = outs.pop(0)
            block = stacked[:, block_of(starts, slot, partial.shape[1])]
            partial[...] = jnp.dot(both, block, preferred_element_type=F32).astype(partial.dtype)
        if len(outs) > (1 - chain) * len(slots):
            outs.pop(0)[...] = both.T


def back_products(slots, starts, shards, stacked, both_t, before):
    wide = shards[0].shape[1]
    blocks, totals = [], [None, None] if before is None else [before[0], before[1]]
    for i, slot in enumerate(slots):
        decoder = stacked[:, block_of(starts, slot, wide)]
        block = 0.0
        for chain in range(2):
            error = shards[2 * i + chain][...]
            block = block + jnp.dot(both_t[chain][...], error, preferred_element_type=F32)
            term = lax.dot_general(error, decoder, OVER_COLS, preferred_element_type=F32)
            totals[chain] = term if totals[chain] is None else totals[chain] + term
        blocks.append(block)
    return blocks, totals


def back_kernel(slots, first, starts, *refs):
    count = 2 * len(slots)
    shards, (stacked, *both_t), (*before, outer, back) = refs[:count], refs[count:count + 3], refs[count + 3:]
    blocks, totals = back_products(slots, starts, shards, stacked, both_t, None if first else before[0])
    for i, block in enumerate(blocks):
        outer[i] = block
    for chain in range(2):
        back[chain] = totals[chain]


def cross_back_kernel(slots, far, starts, *refs):
    shards, (stacked, *both_t), outers, (before, sent, high) = refs[:2], refs[2:5], refs[5:-3], refs[-3:]
    rows, wide = shards[0].shape
    half_width, lat = high.shape

    @pl.when(starts[starts.shape[0] - 1] != 0)
    def _():
        decoder = stacked[lat:, block_of(starts, far, wide)]
        last = 0.0
        for chain in range(2):
            error = shards[chain][...]
            last = last + jnp.dot(both_t[chain][lat:, :], error, preferred_element_type=F32)
            term = lax.dot_general(error, decoder, OVER_COLS, preferred_element_type=F32)
            sent[chain * rows:(chain + 1) * rows, :] = before[chain, :, lat:] + term
        pieces = [(far, last)]
        for group, outer in zip(slots, outers):
            pieces += [(slot, outer[i, lat:]) for i, slot in enumerate(group)]
        for slot, piece in pieces:
            start = pl.multiple_of(starts[slot], wide)

            @pl.when(start < half_width)
            def _():
                for c in range(0, wide, lat):
                    sent[pl.ds(2 * rows + start + c, lat), :] = piece[:, c:c + lat]

            @pl.when(start >= half_width)
            def _():
                for c in range(0, wide, lat):
                    high[pl.ds(start - half_width + c, lat), :] = piece[:, c:c + lat]


def own_back_kernel(slots, far, starts, *refs):
    shards, (stacked, *both_t), refs = refs[:2], refs[2:5], refs[5:]
    outers, (before, back_own, same, last, sems) = refs[:-5], refs[-5:]
    rows, wide = shards[0].shape
    lat = back_own.shape[1]
    blocks = []
    for group, outer in zip(slots, outers):
        blocks += [(slot, outer.at[i, :lat, :]) for i, slot in enumerate(group)]
    blocks.append((far, last))
    copies = []
    for i, (slot, block) in enumerate(blocks):
        copies.append(pltpu.make_async_copy(block, same.at[0, :, block_of(starts, slot, wide)], sems.at[i]))
    for copy in copies[:-1]:
        copy.start()
    decoder = stacked[:lat, block_of(starts, far, wide)]
    total = 0.0
    for chain in range(2):
        error = shards[chain][...]
        total = total + jnp.dot(both_t[chain][:lat, :], error, preferred_element_type=F32)
        term = lax.dot_general(error, decoder, OVER_COLS, preferred_element_type=F32)
        back_own[chain * rows:(chain + 1) * rows, :] = before[chain, :, :lat] + term
    last[...] = total
    copies[-1].start()
    for copy in copies:
        copy.wait()


def finish_kernel(
    starts, turned, preact, back_own, arrived, high, grad, bias, cross, stage, cross_stage, grad_sems, cross_sem
):
    pieces, height, lat = stage.shape
    rows = preact.shape[0]
    half_width = high.shape[0]
    first = starts[starts.shape[0] - 1] == 0
    later = jnp.where(first, arrived[:rows, :].astype(F32), 0.0)
    value = jnp.where(preact[...] > 0, back_own[...] + later, 0.0).astype(BF16)
    copies = []
    for i in range(pieces):
        at = pl.ds(i * height, height)
        stage[i] = jnp.dot(turned[at, :], value, preferred_element_type=F32)
        copies.append(pltpu.make_async_copy(stage.at[i], grad.at[0, at, :], grad_sems.at[i]))
        copies[-1].start()
        if i == 0:
            for c in range(0, half_width, lat):
                source = arrived[rows + c:rows + c + lat, :].astype(F32)
                cross_stage[:, c:c + lat] = jnp.where(first, source, high[c:c + lat, :])
            copies.append(pltpu.make_async_copy(cross_stage, cross, cross_sem))
            copies[-1].start()
    bias[...] = jnp.sum(value.astype(F32), axis=0, keepdims=True)
    for copy in copies:
        copy.wait()


def ring_shards(residual_in, targets, enc_weight, enc_bias, dec_same, dec_cross):
    size = lax.axis_size("latent")
    reach = size // 2
    place = ring_place(lax.axis_index("latent"), size)
    layer = lax.axis_index("layer")
    sign = jnp.where(layer % 2 == 0, 1, -1)
    rows, wide = residual_in.shape[1:]
    half = rows // 2
    deep, lat = enc_weight.shape[1:]
    half_width = deep // 2
    err_scale = 1.0 / math.sqrt(rows)
    shape = jax.ShapeDtypeStruct
    unit = rows * wide * lat
    chains = (0, 1)

    def halves(array):
        return [array[:half], array[half:]]

    slot_p = {s: 2 * s - 1 for s in range(1, reach)}
    slot_q = {s: 2 * s for s in range(1, reach)}
    far = size - 1
    offsets = [0] * size
    offsets[far] = reach
    for s in range(1, reach):
        offsets[slot_p[s]] = -s
        offsets[slot_q[s]] = s
    starts = jnp.stack([ring_member(place + sign * offset, size) * wide for offset in offsets] + [layer])
    starts = starts.astype(jnp.int32)

    urgent, later = ((0, -1), (1, 1)), ((0, 1), (1, -1))

    def gather_step(found, s, ready=None):
        for chain, way in urgent + later if s < reach else urgent:
            slots = slot_p if way == 1 else slot_q
            shard = found[chain][slots[s - 1] if s > 1 else 0]
            if ready is not None and (chain, way) in later:
                shard = after(shard, ready[chain])
            found[chain][slots[s] if s < reach else far] = hop(shard, way)

    def both_chains(found, slots):
        return [found[chain][slot] for slot in slots for chain in chains]

    def encode(slots, before):
        first, last = slots[0] == 0, slots[-1] == far
        return call(
            functools.partial(encode_kernel, slots, first, last),
            [shape((rows, lat), F32)] + ([shape((rows, lat), BF16)] if last else []),
            2 * unit * len(slots),
            [starts] + both_chains(inputs, slots) + [enc_weight, before],
        )

    inputs = [[part] + [None] * (size - 1) for part in halves(residual_in[0])]
    turned_own = []
    for chain in chains:
        source = inputs[chain][0]
        turned_own += call(turn_own_kernel, [shape((wide, half), BF16)], 0, [starts, source])
    for s in range(1, reach + 1):
        gather_step(inputs, s, turned_own if s == 1 else None)
    low_cross = swapped(after(dec_cross, inputs[0][slot_p.get(1, far)]))
    cross = jnp.where(layer > 0, jnp.concatenate([low_cross, dec_cross], axis=1), jnp.zeros((), BF16))
    stacked = jnp.concatenate([dec_same[0], cross], axis=0)
    part = encode(tuple(range(far)), after(enc_bias, stacked))[0]
    preact, codes = encode((far,), part)
    earlier = swapped(codes)

    def spread(slots, dtypes, turned):
        outs = []
        for chain in chains:
            outs += [shape((half, wide), dtypes[chain].get(slot, F32)) for slot in slots]
            outs += [shape((2 * lat, half), BF16)] if turned else []
        found = call(
            functools.partial(spread_kernel, slots), outs, 4 * unit * len(slots), [starts, codes, earlier, stacked]
        )
        return found[:len(outs) // 2], found[len(outs) // 2:]

    rest = tuple(slot for slot in range(size) if slot != far)
    instant = tuple({far: BF16, (slot_q if way == 1 else slot_p).get(reach - 1): BF16} for _, way in later)
    far_0, far_1 = spread((far,), instant, False)
    moving = {loop: hop(message, loop[1]) for loop, message in zip(urgent, (far_0[0], far_1[0]))}
    partial, both_t = [], []
    for pieces in spread(rest, instant, True):
        partial.append(dict(zip(rest, pieces)))
        both_t.append(pieces[-1])
    before = []
    for s in range(reach - 1, 0, -1):
        landed = [moving[loop] for loop in urgent]
        for chain, way in urgent + later:
            message = partial[chain][slot_q[s] if way == 1 else slot_p[s]]
            if (chain, way) in moving:
                message = (message + moving[chain, way].astype(F32)).astype(BF16)
            if (chain, way) in later and before:
                message = after(message, *before)
            moving[chain, way] = hop(message, way)
        before = landed
    errors = []
    for chain, wanted in zip(chains, halves(targets[0])):
        total = partial[chain][0]
        for way in (1, -1):
            if (chain, way) in moving:
                total = total + moving[chain, way].astype(F32)
        if chain == 1:
            wanted = after(wanted, codes)
        errors.append([((total - wanted.astype(F32)) * err_scale).astype(BF16)] + [None] * (size - 1))

    def back(slots, before):
        return call(
            functools.partial(back_kernel, slots, before is None),
            [shape((len(slots), 2 * lat, wide), F32), shape((2, half, 2 * lat), F32)],
            4 * unit * len(slots),
            [starts] + both_chains(errors, slots) + [stacked] + both_t + ([] if before is None else [before]),
        )

    groups, outers, acc, pending = [], [], None, [0]
    arrived = [after(inputs[0][1], errors[1][0])]
    turned = call(
        turn_kernel,
        [shape((deep, rows), BF16)],
        0,
        [starts] + turned_own + arrived + both_chains(inputs, range(1, size))[1:],
    )[0]
    for s in range(1, reach + 1):
        gather_step(errors, s, (turned, turned) if s == 2 else None)
    cut = 1 + 2 * min(1, reach - 1)
    groups = [group for group in (tuple(range(cut)), tuple(range(cut, far))) if group]
    outers, acc = [], None
    for group in groups:
        outer, acc = back(group, acc)
        outers.append(outer)
    last = both_chains(errors, (far,)) + [stacked] + both_t + outers + [acc]
    sent, high = call(
        functools.partial(cross_back_kernel, groups, far),
        [shape((rows + half_width, lat), F32), shape((half_width, lat), F32)],
        0,
        [starts] + last,
    )
    returned = swapped(sent)
    back_own, grad_same = call(
        functools.partial(own_back_kernel, groups, far),
        [shape((rows, lat), F32), shape((1, lat, deep), F32)],
        0,
        [starts] + last,
        out_spaces=[pltpu.VMEM, pl.ANY],
        scratch=[pltpu.VMEM((lat, wide), F32), pltpu.SemaphoreType.DMA((size,))],
    )
    height = deep // PIECES
    grad_enc, grad_bias, grad_cross = call(
        finish_kernel,
        [shape((1, deep, lat), F32), shape((1, lat), F32), shape((lat, half_width), F32)],
        2 * unit * size,
        [starts, turned, preact, back_own, returned, high],
        out_spaces=[pl.ANY, pltpu.VMEM, pl.ANY],
        scratch=[
            pltpu.VMEM((PIECES, height, lat), F32),
            pltpu.VMEM((lat, half_width), F32),
            pltpu.SemaphoreType.DMA((PIECES,)),
            pltpu.SemaphoreType.DMA,
        ],
    )
    return (grad_enc, grad_bias, grad_same, grad_cross)


def wide_shards(residual_in, targets, enc_weight, enc_bias, dec_same, dec_cross):
    is_first = lax.axis_index("layer") == 0
    err_scale = 1.0 / math.sqrt(residual_in.shape[1])
    inputs = lax.all_gather(residual_in[0], "latent", axis=1, tiled=True)
    preact = matmul(inputs, enc_weight[0]) + enc_bias[0]
    codes_now = jnp.maximum(preact, 0.0).astype(BF16)
    earlier = passed_along(codes_now, "layer", 1)
    cross_full = lax.all_gather(dec_cross, "layer", axis=1, tiled=True)
    own_dec = dec_same[0]
    half_width = own_dec.shape[1] // 2
    recon_full = lax.psum(matmul(codes_now, own_dec) + matmul(earlier, cross_full), "latent")
    wanted = lax.all_gather(targets[0], "latent", axis=1, tiled=True)
    errors = ((recon_full - wanted.astype(F32)) * err_scale).astype(BF16)
    grad_same = matmul(codes_now, errors, OVER_ROWS)
    grad_full = matmul(earlier, errors, OVER_ROWS)
    returned = passed_along(grad_full[:, :half_width], "layer", -1)
    grad_cross = jnp.where(is_first, returned, grad_full[:, half_width:])
    from_next = passed_along(matmul(errors, cross_full, OVER_COLS), "layer", -1)
    grad_codes = matmul(errors, own_dec, OVER_COLS) + from_next
    grad_pre = jnp.where(preact > 0, grad_codes, 0.0).astype(BF16)
    grad_enc = matmul(inputs, grad_pre, OVER_ROWS)
    grad_bias = jnp.sum(grad_pre.astype(F32), axis=0)
    return (grad_enc[None], grad_bias[None], grad_same[None], grad_cross)


def solution(mesh):
    size = mesh.shape["latent"]
    placed = (
        P("layer", "groups", "latent"),
        P("layer", "groups", "latent"),
        P("layer", None, "latent"),
        P("layer", "latent"),
        P("layer", "latent", None),
        P("latent", "layer"),
    )
    return jax.shard_map(
        ring_shards if size % 2 == 0 and size <= RING_LIMIT else wide_shards,
        mesh=mesh,
        in_specs=placed,
        out_specs=(
            P(("groups", "layer"), None, "latent"),
            P(("groups", "layer"), "latent"),
            P(("groups", "layer"), "latent", None),
            P(("groups", "latent"), "layer"),
        ),
        check_vma=False,
    )
```
